32 devices in a mesh: dp: 8 (over y, x, core), tensor: 4 (over z).
Axes of the slice: x: 2, y: 2, z: 4, core: 2. Of those that a mesh axis runs over, the one named last changes fastest.
Arguments:
- tokens: bfloat16 [2048, 8192], P('dp', 'tensor'), may hold values from -6 to 6
- queries: bfloat16 [2048, 4096], P('dp', 'tensor'), may hold values from -400 to 400
- d_out: bfloat16 [2048, 4096], P('dp', 'tensor'), may hold values from -6 to 6
- segments: int32 [8, 256], P('dp'), may hold values from 0 to 3, never falling along the last dimension, each value on 1 to 128 neighbouring positions
- cached: bfloat16 [8192, 1024], P(None, 'tensor'), may hold values from -0.0625 to 0.0625
- master: float32 [8192, 1024], P('dp', 'tensor'), may hold values from -0.0625 to 0.0625
- moment: float32 [8192, 1024], P('dp', 'tensor'), may hold values from -4 to 4
- second: float32 [8192, 1024], P('dp', 'tensor'), may hold values from 0.05 to 2
- grad: float32 [8192, 1024], P('dp', 'tensor'), may hold values from -6 to 6
Outputs:
- master_new: float32 [8192, 1024], P('dp', 'tensor')
- moment_new: float32 [8192, 1024], P('dp', 'tensor')
- second_new: float32 [8192, 1024], P('dp', 'tensor')
- new_cache: bfloat16 [8192, 1024], P(None, 'tensor')
- new_grad: float32 [8192, 1024], P('dp', 'tensor')
- d_queries: bfloat16 [2048, 4096], P('dp', 'tensor')
- d_tokens: bfloat16 [2048, 8192], P('dp', 'tensor')
The draws below stay inside these ranges and needn't reach their ends.
Inputs may be any that keep to these rules, and one draw needn't show every extreme that they name: `segments`: document numbers within a pack never fall.
All inputs are finite; a program needn't handle non-finite values.
Results may differ from the reference program's by a relative error of at most 0.0091.
Values may be sent and summed in bfloat16 or wider, within the bound.
No kernel may reach another device: no remote copies, remote signals or barrier semaphores. Data moves between devices by JAX's collectives and lax.ppermute only.
A program may use at most 128 MiB of HBM per device.

```python
import math
import jax
import jax.numpy as jnp
import numpy as np
from jax import lax

D = 8192
HD = 128
GROUP = 8
DOCS = 4
TOK_DEV = 256
KVH = 4
QH = 32
PACKS = 8
TOKENS = 2048


def draw_queries(key, part):
    key = jax.random.fold_in(key, 11)
    normal_part = jax.random.normal(key, (TOKENS, QH * HD), jnp.float32)
    return normal_part.astype(jnp.bfloat16)


def draw_d_out(key, part):
    key = jax.random.fold_in(key, 23)
    normal_part = jnp.clip(jax.random.normal(key, (TOKENS, QH * HD), jnp.float32), -6.0, 6.0)
    return normal_part.astype(jnp.bfloat16)


def raised(entries, rng, source, target, parts, factor):
    owner, partner = [(jnp.arange(entries.shape[dim]) // (entries.shape[dim] // parts)).reshape([-1 if axis == dim else 1 for axis in range(entries.ndim)]) for dim in (source, target)]
    chosen = jax.random.permutation(rng, parts)[partner]
    strong = (owner == chosen) | (owner == (partner + parts // 2) % parts)
    return jnp.where(strong, factor * entries, entries)


def steps_of(rng, dims, cuts, least, largest):
    factor_of, own = 1.0, jax.random.fold_in(rng, 6)
    for dim, parts in cuts:
        draws = jnp.exp(jax.random.uniform(jax.random.fold_in(own, dim), (parts,), jnp.float32, least / len(cuts), largest / len(cuts)))
        factor_of = factor_of * jnp.repeat(draws, dims[dim] // parts).reshape([-1 if axis == dim else 1 for axis in range(len(dims))])
    return factor_of


def length_profile(count, total, bound, slope):
    loads = [(1 << 20) // math.isqrt(grade ** slope) + 1 for grade in range(2, count + 1)]
    surplus, given = total - bound - (count - 1), [1] * (count - 1)
    while surplus > 0:
        movable = [i for i in range(count - 1) if given[i] < bound]
        mass, left = sum([loads[i] for i in movable]), surplus
        for i in movable:
            more = min(bound - given[i], max(1, left * loads[i] // mass), surplus)
            given[i] = given[i] + more
            surplus = surplus - more
    return np.array([bound] + given)


def uneven_parts(stream_key, count, total, limit, slope):
    if count == 2:
        one = jax.random.randint(stream_key, (), max(1, total - limit), min(limit, total - 1) + 1)
        return jnp.stack([one, total - one])
    sizes = jnp.asarray(length_profile(count, total, limit, slope), jnp.int32)
    twos = (count - 1) // 2
    source_of, sink = sizes[1:1 + 2 * twos:2], sizes[2:2 + 2 * twos:2]
    room = jnp.minimum(source_of - 1, limit - sink)
    moved = jax.random.randint(jax.random.fold_in(stream_key, 1), (twos,), 0, 1 << 20) % (room + 1)
    sizes = sizes.at[1:1 + 2 * twos:2].set(source_of - moved).at[2:2 + 2 * twos:2].set(sink + moved)
    return sizes[jax.random.permutation(jax.random.fold_in(stream_key, 2), count)]


def normal_values(key, shape, spread, limit, split=(), held_as=jnp.bfloat16):
    array = spread * jax.random.normal(key, shape, jnp.float32)
    if split:
        array = array * steps_of(key, shape, split, -0.22, 0.18)
    return jnp.clip(array, -limit, limit).astype(held_as)


def bell_draw_with(rng, shape, deviation, reach, shards, heavy, dtype=jnp.bfloat16):
    array = deviation * jax.random.normal(rng, shape, jnp.float32)
    if shards:
        array = array * steps_of(rng, shape, shards, -0.22, 0.18)
    return jnp.clip(raised(array, jax.random.fold_in(rng, 3), *heavy), -reach, reach).astype(dtype)


def setup_inputs(seed: int = 0) -> dict:
    splits = jax.random.split(jax.random.key(seed), 10)
    tokens = bell_draw_with(splits[0], (TOKENS, D), 1.0, 6.0, ((0, 8), (1, 4)), (0, 1, 8, 2.0))
    queries = draw_queries(jax.random.fold_in(splits[9], 71), 0)
    d_out = draw_d_out(jax.random.fold_in(splits[9], 71), 0)
    segments = jax.vmap(lambda own: jnp.searchsorted(jnp.cumsum(uneven_parts(own, DOCS, TOK_DEV, TOK_DEV // 2, 2)), jnp.arange(TOK_DEV), side="right"))(jax.random.split(splits[3], PACKS)).reshape((PACKS, TOK_DEV)).astype(jnp.int32)
    cached = normal_values(splits[4], (D, 2 * KVH * HD), D ** -0.5, 0.0625, ((1, 4),))
    master = normal_values(splits[5], (D, 2 * KVH * HD), D ** -0.5, 0.0625, ((0, 8), (1, 4)), jnp.float32)
    moment = normal_values(splits[6], (D, 2 * KVH * HD), 0.5, 4.0, ((0, 8), (1, 4)), jnp.float32)
    second = jnp.clip(jnp.exp(math.log(2.0) - 3.6888794 * jax.random.uniform(splits[7], (D, 2 * KVH * HD), jnp.float32) ** steps_of(splits[7], (D, 2 * KVH * HD), ((0, 8), (1, 4)), -0.2, 0.2)), 0.05, 2.0)
    grad = normal_values(splits[8], (D, 2 * KVH * HD), 1.0, 6.0, ((0, 8), (1, 4)), jnp.float32)
    return dict(tokens=tokens, queries=queries, d_out=d_out, segments=segments, cached=cached, master=master, moment=moment, second=second, grad=grad)


beta_first = 0.9
beta_second = 0.95
learn_rate = 0.0003
weight_decay = 0.1
adam_epsilon = 1e-08
first_fix = 1.0 - 0.9 ** 40
second_fix = 1.0 - 0.95 ** 40

def pack_backward(pieces):
    heads, query_heads, grads_out, doc_ids = pieces
    keys = heads[:, :, 0].astype(jnp.float32)
    values = heads[:, :, 1].astype(jnp.float32)
    query_float = query_heads.astype(jnp.float32)
    grads_float = grads_out.astype(jnp.float32)
    factor = 1.0 / math.sqrt(HD)
    scores = jnp.einsum('qhgd,khd->hgqk', query_float, keys) * factor
    position = jnp.arange(TOK_DEV)
    allowed = (doc_ids[:, None] == doc_ids[None, :]) & (position[None, :] <= position[:, None])
    scores = jnp.where(allowed, scores, -1e+30)
    highest = lax.optimization_barrier(jnp.max(scores, axis=-1, keepdims=True))
    weights = jnp.exp(scores - highest)
    probs = weights / lax.optimization_barrier(jnp.sum(weights, axis=-1, keepdims=True))
    probs_low = lax.optimization_barrier(probs.astype(jnp.bfloat16)).astype(jnp.float32)
    attended = jnp.einsum('hgqk,khd->qhgd', probs_low, values)
    rowdot = lax.optimization_barrier(jnp.sum(grads_float * attended, axis=-1))
    d_probs = jnp.einsum('qhgd,khd->hgqk', grads_float, values)
    d_scores = probs * (d_probs - jnp.transpose(rowdot, (1, 2, 0))[..., None]) * factor
    d_scores_low = lax.optimization_barrier(d_scores.astype(jnp.bfloat16)).astype(jnp.float32)
    d_query = jnp.einsum('hgqk,khd->qhgd', d_scores_low, keys).astype(jnp.bfloat16)
    d_keys = jnp.einsum('hgqk,qhgd->khd', d_scores_low, query_float)
    d_values = jnp.einsum('hgqk,qhgd->khd', probs_low, grads_float)
    d_heads = jnp.stack([d_keys, d_values], axis=2).astype(jnp.bfloat16)
    return (d_query, d_heads)

def reference(tokens, queries, d_out, segments, cached, master, moment, second, grad):
    moment_new = beta_first * moment + (1.0 - beta_first) * grad
    second_new = beta_second * second + (1.0 - beta_second) * grad * grad
    update = moment_new / first_fix / (jnp.sqrt(second_new / second_fix) + adam_epsilon)
    master_new = master - learn_rate * (update + weight_decay * master)
    cached_float = cached.astype(jnp.float32)
    delta = master_new - cached_float
    blocks = delta.reshape(D, -1, HD)
    block_scale = (lax.optimization_barrier(jnp.max(jnp.abs(blocks), axis=2)) + 1e-06).astype(jnp.bfloat16)
    scale_float = block_scale.astype(jnp.float32)[:, :, None]
    codes = (blocks / scale_float).astype(jnp.bfloat16)
    new_cache = (cached_float + (codes.astype(jnp.float32) * scale_float).reshape(D, -1)).astype(jnp.bfloat16)
    projected = jnp.dot(tokens, cached, preferred_element_type=jnp.float32).astype(jnp.bfloat16)
    heads = projected.reshape(PACKS, TOK_DEV, KVH, 2, HD)
    query_heads = queries.reshape(PACKS, TOK_DEV, KVH, GROUP, HD)
    grads_out = d_out.reshape(PACKS, TOK_DEV, KVH, GROUP, HD)
    d_query, d_heads = lax.map(pack_backward, (heads, query_heads, grads_out, segments))
    d_queries = d_query.reshape(TOKENS, QH * HD)
    d_projected = d_heads.reshape(TOKENS, 2 * KVH * HD)
    new_grad = lax.dot_general(tokens, d_projected, (((0,), (0,)), ((), ())), preferred_element_type=jnp.float32)
    d_tokens = lax.dot_general(d_projected, cached, (((1,), (1,)), ((), ())), preferred_element_type=jnp.float32).astype(jnp.bfloat16)
    return (master_new, moment_new, second_new, new_cache, new_grad, d_queries, d_tokens)
```

```python
import math

import jax
import jax.numpy as jnp
from jax import lax
from jax.sharding import PartitionSpec as P

HD = 128


beta_first = 0.9
beta_second = 0.95
learn_rate = 0.0003
weight_decay = 0.1
adam_epsilon = 1e-08
first_fix = 1.0 - 0.9**40
second_fix = 1.0 - 0.95**40


def optimizer(cached, master, moment, second, grad):
    rows_here = master.shape[0]
    first_row = lax.axis_index("dp") * rows_here
    moment_new = beta_first * moment + (1.0 - beta_first) * grad
    second_new = beta_second * second + (1.0 - beta_second) * grad * grad
    update = moment_new / first_fix / (jnp.sqrt(second_new / second_fix) + adam_epsilon)
    master_new = master - learn_rate * (update + weight_decay * master)
    own_cache = lax.dynamic_slice_in_dim(cached, first_row, rows_here, 0).astype(jnp.float32)
    blocks = (master_new - own_cache).reshape(rows_here, -1, HD)
    block_scale = (jnp.max(jnp.abs(blocks), axis=2, keepdims=True) + 1e-06).astype(jnp.bfloat16)
    scale = block_scale.astype(jnp.float32)
    codes = (blocks / scale).astype(jnp.bfloat16)
    scaled = codes.astype(jnp.float32) * scale
    own_new = (own_cache + scaled.reshape(rows_here, -1)).astype(jnp.bfloat16)
    return master_new, moment_new, second_new, own_new


def attention_backward(projected, queries, d_out, doc_ids):
    length = projected.shape[0]
    heads = projected.reshape(length, -1, 2, HD)
    keys = heads[:, :, 0]
    values = heads[:, :, 1]
    query_heads = queries.reshape(length, keys.shape[1], -1, HD)
    grads_out = d_out.reshape(length, keys.shape[1], -1, HD)
    factor = 1.0 / math.sqrt(HD)
    scores = (
        jnp.einsum("qhgd,khd->hgqk", query_heads, keys, preferred_element_type=jnp.float32) * factor
    )
    position = jnp.arange(length)
    allowed = (doc_ids[:, None] == doc_ids[None, :]) & (position[None, :] <= position[:, None])
    scores = jnp.where(allowed, scores, -1e30)
    highest = jnp.max(scores, axis=-1, keepdims=True)
    weights = jnp.exp(scores - highest)
    probs = weights / jnp.sum(weights, axis=-1, keepdims=True)
    probs_low = probs.astype(jnp.bfloat16)
    attended = jnp.einsum("hgqk,khd->qhgd", probs_low, values, preferred_element_type=jnp.float32)
    rowdot = jnp.sum(grads_out.astype(jnp.float32) * attended, axis=-1)
    d_probs = jnp.einsum("qhgd,khd->hgqk", grads_out, values, preferred_element_type=jnp.float32)
    d_scores = (probs * (d_probs - jnp.transpose(rowdot, (1, 2, 0))[..., None]) * factor).astype(
        jnp.bfloat16
    )
    d_queries = (
        jnp.einsum("hgqk,khd->qhgd", d_scores, keys, preferred_element_type=jnp.float32)
        .astype(jnp.bfloat16)
        .reshape(length, -1)
    )
    d_keys = jnp.einsum("hgqk,qhgd->khd", d_scores, query_heads, preferred_element_type=jnp.float32)
    d_values = jnp.einsum(
        "hgqk,qhgd->khd", probs_low, grads_out, preferred_element_type=jnp.float32
    )
    d_projected = jnp.stack([d_keys, d_values], axis=2).astype(jnp.bfloat16).reshape(length, -1)
    return d_queries, d_projected


def make_body(n_dp, n_z):
    ring = [[(z, (z + s) % n_z) for z in range(n_z)] for s in range(n_z)]
    up = [(z, z + 1) for z in range(n_z - 1)]
    down = [(z + 1, z) for z in range(n_z - 1)]

    def body(tokens, queries, d_out, segments, cached, master, moment, second, grad):
        me_dp = lax.axis_index("dp")
        me_z = lax.axis_index("tensor")
        length, feats = tokens.shape
        cols = cached.shape[1]

        def part(chunk, index):
            rows = lax.dynamic_slice_in_dim(cached, jnp.clip(index, 0, n_z - 1) * feats, feats, 0)
            return jnp.dot(chunk, rows, preferred_element_type=jnp.float32)

        projected = part(tokens, me_z)
        held = jnp.zeros((n_z + 1, length, feats), tokens.dtype)
        held = lax.dynamic_update_slice(held, tokens[None], (me_z, 0, 0))
        from_low, from_high = tokens, tokens
        for s in range(1, n_z):
            from_low = lax.ppermute(from_low, "tensor", up)
            from_high = lax.ppermute(from_high, "tensor", down)
            low, high = me_z - s, me_z + s
            projected = projected + part(from_low, low) + part(from_high, high)
            held = lax.dynamic_update_slice(
                held, from_low[None], (jnp.where(low >= 0, low, n_z), 0, 0)
            )
            held = lax.dynamic_update_slice(
                held, from_high[None], (jnp.where(high < n_z, high, n_z), 0, 0)
            )
        projected = projected.astype(jnp.bfloat16)

        master_new, moment_new, second_new, own_new = optimizer(
            cached, master, moment, second, grad
        )
        new_cache = lax.all_gather(own_new, "dp", axis=0, tiled=True)

        share = feats // n_dp

        def block_for(z):
            return lax.dynamic_slice_in_dim(cached, z * feats + me_dp * share, share, 0)

        blocks = [block_for(me_z)]
        for s in range(1, n_z):
            blocks.append(lax.ppermute(block_for((me_z + s) % n_z), "tensor", ring[s]))
        feature_rows = lax.all_gather(jnp.concatenate(blocks, axis=1), "dp", axis=0, tiled=True)

        d_queries, d_projected = attention_backward(projected, queries, d_out, segments[0])

        partial = lax.dot_general(
            held[:n_z],
            d_projected,
            (((1,), (0,)), ((), ())),
            preferred_element_type=jnp.float32,
        ).reshape(n_z * feats, cols)
        new_grad = lax.psum_scatter(
            partial.astype(jnp.bfloat16), "dp", scatter_dimension=0, tiled=True
        ).astype(jnp.float32)

        pieces = [d_projected] + [
            lax.ppermute(d_projected, "tensor", ring[s]) for s in range(1, n_z)
        ]
        d_tokens = lax.dot_general(
            jnp.concatenate(pieces, axis=1),
            feature_rows,
            (((1,), (1,)), ((), ())),
            preferred_element_type=jnp.float32,
        ).astype(jnp.bfloat16)
        return (master_new, moment_new, second_new, new_cache, new_grad, d_queries, d_tokens)

    return body


def solution(mesh):
    in_specs = (
        P("dp", "tensor"),
        P("dp", "tensor"),
        P("dp", "tensor"),
        P("dp", None),
        P(None, "tensor"),
        P("dp", "tensor"),
        P("dp", "tensor"),
        P("dp", "tensor"),
        P("dp", "tensor"),
    )
    out_specs = (
        P("dp", "tensor"),
        P("dp", "tensor"),
        P("dp", "tensor"),
        P(None, "tensor"),
        P("dp", "tensor"),
        P("dp", "tensor"),
        P("dp", "tensor"),
    )
    body = make_body(mesh.shape["dp"], mesh.shape["tensor"])
    return jax.shard_map(body, mesh=mesh, in_specs=in_specs, out_specs=out_specs, check_vma=False)
```

```python
import math

import jax
import jax.numpy as jnp
from jax import lax
from jax.experimental import pallas as pl
from jax.experimental.pallas import tpu as pltpu
from jax.sharding import PartitionSpec as P

HD = 128


beta_first = 0.9
beta_second = 0.95
learn_rate = 0.0003
weight_decay = 0.1
adam_epsilon = 1e-08
first_fix = 1.0 - 0.9**40
second_fix = 1.0 - 0.95**40


def optimizer_kernel(
    place, cached, master, moment, second, grad, master_out, moment_out, second_out, cache_out
):
    moment_new = beta_first * moment[...] + (1.0 - beta_first) * grad[...]
    second_new = beta_second * second[...] + (1.0 - beta_second) * grad[...] * grad[...]
    update = moment_new / first_fix / (jnp.sqrt(second_new / second_fix) + adam_epsilon)
    master_new = master[...] - learn_rate * (update + weight_decay * master[...])
    moment_out[...] = moment_new
    second_out[...] = second_new
    master_out[...] = master_new
    for start in range(0, cached.shape[1], HD):
        block = slice(start, start + HD)
        own_cache = cached[:, block].astype(jnp.float32)
        delta = master_new[:, block] - own_cache
        largest = jnp.max(jnp.abs(delta), axis=1, keepdims=True)
        scale = (largest + 1e-06).astype(jnp.bfloat16).astype(jnp.float32)
        codes = (delta / scale).astype(jnp.bfloat16)
        cache_out[:, block] = (own_cache + codes.astype(jnp.float32) * scale).astype(jnp.bfloat16)


def optimizer(cached, master, moment, second, grad):
    rows, cols = master.shape
    step = min(rows, 256)
    steps = rows // step
    own = pl.BlockSpec((step, cols), lambda i, place: (i, 0))
    full = jax.ShapeDtypeStruct((rows, cols), jnp.float32)
    return pl.pallas_call(
        optimizer_kernel,
        grid_spec=pltpu.PrefetchScalarGridSpec(
            num_scalar_prefetch=1,
            grid=(steps,),
            in_specs=[pl.BlockSpec((step, cols), lambda i, place: (place[0] * steps + i, 0))]
            + [own] * 4,
            out_specs=[own] * 4,
        ),
        out_shape=[full, full, full, jax.ShapeDtypeStruct((rows, cols), jnp.bfloat16)],
        cost_estimate=pl.CostEstimate(
            flops=40 * rows * cols, bytes_accessed=32 * rows * cols, transcendentals=rows * cols
        ),
        compiler_params=pltpu.CompilerParams(vmem_limit_bytes=32 * 1024 * 1024),
        name="optimizer",
    )(lax.axis_index("dp").astype(jnp.int32).reshape(1), cached, master, moment, second, grad)


def attention_backward(projected, queries, d_out, doc_ids):
    length = projected.shape[0]
    heads = projected.reshape(length, -1, 2, HD)
    keys = heads[:, :, 0]
    values = heads[:, :, 1]
    query_heads = queries.reshape(length, keys.shape[1], -1, HD)
    grads_out = d_out.reshape(length, keys.shape[1], -1, HD)
    factor = 1.0 / math.sqrt(HD)
    scores = (
        jnp.einsum("qhgd,khd->hgqk", query_heads, keys, preferred_element_type=jnp.float32) * factor
    )
    position = jnp.arange(length)
    allowed = (doc_ids[:, None] == doc_ids[None, :]) & (position[None, :] <= position[:, None])
    scores = jnp.where(allowed, scores, -1e30)
    highest = jnp.max(scores, axis=-1, keepdims=True)
    weights = jnp.exp(scores - highest)
    probs = weights / jnp.sum(weights, axis=-1, keepdims=True)
    probs_low = probs.astype(jnp.bfloat16)
    attended = jnp.einsum("hgqk,khd->qhgd", probs_low, values, preferred_element_type=jnp.float32)
    rowdot = jnp.sum(grads_out.astype(jnp.float32) * attended, axis=-1)
    d_probs = jnp.einsum("qhgd,khd->hgqk", grads_out, values, preferred_element_type=jnp.float32)
    d_scores = (probs * (d_probs - jnp.transpose(rowdot, (1, 2, 0))[..., None]) * factor).astype(
        jnp.bfloat16
    )
    d_queries = (
        jnp.einsum("hgqk,khd->qhgd", d_scores, keys, preferred_element_type=jnp.float32)
        .astype(jnp.bfloat16)
        .reshape(length, -1)
    )
    d_keys = jnp.einsum("hgqk,qhgd->khd", d_scores, query_heads, preferred_element_type=jnp.float32)
    d_values = jnp.einsum(
        "hgqk,qhgd->khd", probs_low, grads_out, preferred_element_type=jnp.float32
    )
    d_projected = jnp.stack([d_keys, d_values], axis=2).astype(jnp.bfloat16).reshape(length, -1)
    return d_queries, d_projected


def weight_kernel(place, chunk_a, chunk_b, d_projected, *refs):
    *added, out_a, out_b = refs
    half = out_a.shape[-1]
    for side, (chunk, out) in enumerate(((chunk_a, out_a), (chunk_b, out_b))):
        columns = d_projected[:, side * half : (side + 1) * half]
        total = lax.dot_general(
            chunk[0], columns, (((0,), (0,)), ((), ())), preferred_element_type=jnp.float32
        )
        if added:
            total = total + added[side][0].astype(jnp.float32)
        out[0] = total.astype(out.dtype)


def weight_parts(held, d_projected, place, added, dtype, name):
    length, cols = d_projected.shape
    rows = held.shape[2] // 2
    half = cols // 2
    out = pl.BlockSpec((1, rows, half), lambda k, place: (k, 0, 0))
    shape = jax.ShapeDtypeStruct((2, rows, half), dtype)
    return pl.pallas_call(
        weight_kernel,
        grid_spec=pltpu.PrefetchScalarGridSpec(
            num_scalar_prefetch=1,
            grid=(2,),
            in_specs=[
                pl.BlockSpec((1, length, rows), lambda k, place: (place[k], 0, place[4])),
                pl.BlockSpec((1, length, rows), lambda k, place: (place[2 + k], 0, place[4])),
                pl.BlockSpec((length, cols), lambda k, place: (0, 0)),
            ]
            + [out] * len(added),
            out_specs=[out, out],
        ),
        out_shape=[shape, shape],
        cost_estimate=pl.CostEstimate(
            flops=4 * length * rows * cols, bytes_accessed=8 * rows * cols, transcendentals=0
        ),
        compiler_params=pltpu.CompilerParams(vmem_limit_bytes=32 * 1024 * 1024),
        name=name,
    )(place, held, held, d_projected, *added)


def weight_sum(held, d_projected):
    index = lax.axis_index("dp").astype(jnp.int32)
    core, x, y = index % 2, (index // 2) % 2, index // 4

    def swap(value, bit):
        return lax.ppermute(value, "dp", [(i, i ^ bit) for i in range(8)])

    zero = jnp.zeros_like(x)
    send = [1 - x, 3 - x, 2 - 2 * y, 3 - 2 * y]
    keep = [x, 2 + x, 2 * y, 2 * y + 1]

    def parts(chunks, which, added, dtype, name):
        place = jnp.stack(chunks + [which + zero])
        return weight_parts(held, d_projected, place, added, dtype, name)

    theirs = parts(send, 1 - core, [], jnp.bfloat16, "weight_send_other")
    theirs = [swap(part, 1) for part in theirs]
    rest = parts(keep, 1 - core, [], jnp.bfloat16, "weight_keep_other")
    rest = [swap(part, 1) for part in rest]
    send_a, send_b = parts(send, core, theirs, jnp.bfloat16, "weight_send")
    got_a, got_b = swap(send_a, 2), swap(send_b, 4)
    keep_a, keep_b = parts(keep, core, rest, jnp.float32, "weight_keep")

    def pick(keep, got, which):
        return lax.dynamic_index_in_dim(keep, which, 0, False) + lax.dynamic_index_in_dim(
            got, which, 0, False
        ).astype(jnp.float32)

    last_a = swap(pick(keep_a, got_a, 1 - y).astype(jnp.bfloat16), 4)
    last_b = swap(pick(keep_b, got_b, 1 - x).astype(jnp.bfloat16), 2)
    sum_a = pick(keep_a, got_a, y) + last_a.astype(jnp.float32)
    sum_b = pick(keep_b, got_b, x) + last_b.astype(jnp.float32)
    return jnp.concatenate([sum_a, sum_b], axis=1)


def make_body(n_dp, n_z):
    ring = [[(z, (z + s) % n_z) for z in range(n_z)] for s in range(n_z)]

    def body(tokens, queries, d_out, segments, cached, master, moment, second, grad):
        me_dp = lax.axis_index("dp")
        me_z = lax.axis_index("tensor")
        length, feats = tokens.shape
        cols = cached.shape[1]

        def part(chunk, index):
            rows = lax.dynamic_slice_in_dim(cached, jnp.clip(index, 0, n_z - 1) * feats, feats, 0)
            return jnp.dot(chunk, rows, preferred_element_type=jnp.float32)

        def hold(held, chunk, index):
            slot = jnp.where((index >= 0) & (index < n_z), index, n_z)
            return lax.dynamic_update_slice(held, chunk[None], (slot, 0, 0))

        projected = part(tokens, me_z)
        held = hold(jnp.zeros((n_z + 1, length, feats), tokens.dtype), tokens, me_z)
        from_low, from_high, merged = tokens, tokens, None
        for s in range(1, n_z):
            up = [(z, z + 1) for z in range(s - 1, n_z - 1)]
            down = [(z + 1, z) for z in range(n_z - s)]
            low, high = me_z - s, me_z + s
            if merged is None:
                from_low = lax.ppermute(from_low, "tensor", up)
                from_high = lax.ppermute(from_high, "tensor", down)
            else:
                merged = lax.ppermute(merged, "tensor", up + down)
            if merged is None and 2 * s >= n_z:
                merged = jnp.where(me_z >= s, from_low, from_high)
            if merged is None:
                projected = projected + part(from_low, low) + part(from_high, high)
                held = hold(hold(held, from_low, low), from_high, high)
            else:
                origin = jnp.where(me_z >= s, low, high)
                projected = projected + part(merged, origin)
                held = hold(held, merged, origin)
        projected = projected.astype(jnp.bfloat16)

        master_new, moment_new, second_new, own_new = optimizer(
            cached, master, moment, second, grad
        )
        new_cache = lax.all_gather(own_new, "dp", axis=0, tiled=True)

        share = feats // n_dp

        def block_for(z):
            return lax.dynamic_slice_in_dim(cached, z * feats + me_dp * share, share, 0)

        blocks = [block_for(me_z)]
        for s in range(1, n_z):
            blocks.append(lax.ppermute(block_for((me_z + s) % n_z), "tensor", ring[s]))
        feature_rows = lax.all_gather(jnp.concatenate(blocks, axis=1), "dp", axis=0, tiled=True)

        d_queries, d_projected = attention_backward(projected, queries, d_out, segments[0])

        if n_dp == 8 and n_z == 4:
            new_grad = weight_sum(held, d_projected)
        else:
            partial = lax.dot_general(
                held[:n_z],
                d_projected,
                (((1,), (0,)), ((), ())),
                preferred_element_type=jnp.float32,
            ).reshape(n_z * feats, cols)
            new_grad = lax.psum_scatter(
                partial.astype(jnp.bfloat16), "dp", scatter_dimension=0, tiled=True
            ).astype(jnp.float32)

        pieces = [d_projected] + [
            lax.ppermute(d_projected, "tensor", ring[s]) for s in range(1, n_z)
        ]
        d_tokens = lax.dot_general(
            jnp.concatenate(pieces, axis=1),
            feature_rows,
            (((1,), (1,)), ((), ())),
            preferred_element_type=jnp.float32,
        ).astype(jnp.bfloat16)
        return (master_new, moment_new, second_new, new_cache, new_grad, d_queries, d_tokens)

    return body


def solution(mesh):
    in_specs = (
        P("dp", "tensor"),
        P("dp", "tensor"),
        P("dp", "tensor"),
        P("dp", None),
        P(None, "tensor"),
        P("dp", "tensor"),
        P("dp", "tensor"),
        P("dp", "tensor"),
        P("dp", "tensor"),
    )
    out_specs = (
        P("dp", "tensor"),
        P("dp", "tensor"),
        P("dp", "tensor"),
        P(None, "tensor"),
        P("dp", "tensor"),
        P("dp", "tensor"),
        P("dp", "tensor"),
    )
    body = make_body(mesh.shape["dp"], mesh.shape["tensor"])
    return jax.shard_map(body, mesh=mesh, in_specs=in_specs, out_specs=out_specs, check_vma=False)
```

```python
import functools
import math

import jax
import jax.numpy as jnp
from jax import lax
from jax.experimental import pallas as pl
from jax.experimental.pallas import tpu as pltpu
from jax.sharding import PartitionSpec as P

HD = 128
VMEM_STREAM = 56 * 1024 * 1024
VMEM_WHOLE = 24 * 1024 * 1024


beta_first = 0.9
beta_second = 0.95
learn_rate = 0.0003
weight_decay = 0.1
adam_epsilon = 1e-08
first_fix = 1.0 - 0.9**40
second_fix = 1.0 - 0.95**40


def optimizer_kernel(
    place, cached, master, moment, second, grad, master_out, moment_out, second_out, cache_out
):
    moment_new = beta_first * moment[...] + (1.0 - beta_first) * grad[...]
    second_new = beta_second * second[...] + (1.0 - beta_second) * grad[...] * grad[...]
    update = moment_new / first_fix / (jnp.sqrt(second_new / second_fix) + adam_epsilon)
    master_new = master[...] - learn_rate * (update + weight_decay * master[...])
    moment_out[...] = moment_new
    second_out[...] = second_new
    master_out[...] = master_new
    for start in range(0, cached.shape[1], HD):
        block = slice(start, start + HD)
        own_cache = cached[:, block].astype(jnp.float32)
        delta = master_new[:, block] - own_cache
        largest = jnp.max(jnp.abs(delta), axis=1, keepdims=True)
        scale = (largest + 1e-06).astype(jnp.bfloat16).astype(jnp.float32)
        codes = (delta / scale).astype(jnp.bfloat16)
        cache_out[:, block] = (own_cache + codes.astype(jnp.float32) * scale).astype(jnp.bfloat16)


def optimizer(cached, master, moment, second, grad):
    rows, cols = master.shape
    step = min(rows, 256)
    steps = rows // step
    own = pl.BlockSpec((step, cols), lambda i, place: (i, 0))
    full = jax.ShapeDtypeStruct((rows, cols), jnp.float32)
    return pl.pallas_call(
        optimizer_kernel,
        grid_spec=pltpu.PrefetchScalarGridSpec(
            num_scalar_prefetch=1,
            grid=(steps,),
            in_specs=[pl.BlockSpec((step, cols), lambda i, place: (place[0] * steps + i, 0))]
            + [own] * 4,
            out_specs=[own] * 4,
        ),
        out_shape=[full, full, full, jax.ShapeDtypeStruct((rows, cols), jnp.bfloat16)],
        cost_estimate=pl.CostEstimate(
            flops=40 * rows * cols, bytes_accessed=32 * rows * cols, transcendentals=rows * cols
        ),
        compiler_params=pltpu.CompilerParams(vmem_limit_bytes=VMEM_STREAM),
        name="optimizer",
    )(lax.axis_index("dp").astype(jnp.int32).reshape(1), cached, master, moment, second, grad)


def attention_backward(projected, queries, d_out, doc_ids):
    length = projected.shape[0]
    heads = projected.reshape(length, -1, 2, HD)
    keys = heads[:, :, 0]
    values = heads[:, :, 1]
    query_heads = queries.reshape(length, keys.shape[1], -1, HD)
    grads_out = d_out.reshape(length, keys.shape[1], -1, HD)
    factor = 1.0 / math.sqrt(HD)
    scores = (
        jnp.einsum("qhgd,khd->hgqk", query_heads, keys, preferred_element_type=jnp.float32) * factor
    )
    position = jnp.arange(length)
    allowed = (doc_ids[:, None] == doc_ids[None, :]) & (position[None, :] <= position[:, None])
    scores = jnp.where(allowed, scores, -1e30)
    highest = jnp.max(scores, axis=-1, keepdims=True)
    weights = jnp.exp(scores - highest)
    probs = weights / jnp.sum(weights, axis=-1, keepdims=True)
    probs_low = probs.astype(jnp.bfloat16)
    attended = jnp.einsum("hgqk,khd->qhgd", probs_low, values, preferred_element_type=jnp.float32)
    rowdot = jnp.sum(grads_out.astype(jnp.float32) * attended, axis=-1)
    d_probs = jnp.einsum("qhgd,khd->hgqk", grads_out, values, preferred_element_type=jnp.float32)
    d_scores = (probs * (d_probs - jnp.transpose(rowdot, (1, 2, 0))[..., None]) * factor).astype(
        jnp.bfloat16
    )
    d_queries = (
        jnp.einsum("hgqk,khd->qhgd", d_scores, keys, preferred_element_type=jnp.float32)
        .astype(jnp.bfloat16)
        .reshape(length, -1)
    )
    d_keys = jnp.einsum("hgqk,qhgd->khd", d_scores, query_heads, preferred_element_type=jnp.float32)
    d_values = jnp.einsum(
        "hgqk,qhgd->khd", probs_low, grads_out, preferred_element_type=jnp.float32
    )
    d_projected = jnp.stack([d_keys, d_values], axis=2).astype(jnp.bfloat16).reshape(length, -1)
    return d_queries, d_projected


def on_chip(kernel, place, arrays, out_shape, flops, name):
    vmem = pl.BlockSpec(memory_space=pltpu.VMEM)
    size = sum(a.size * a.dtype.itemsize for a in arrays)
    size += sum(s.size * s.dtype.itemsize for s in out_shape)
    return pl.pallas_call(
        kernel,
        in_specs=[pl.BlockSpec(memory_space=pltpu.SMEM)] + [vmem] * len(arrays),
        out_specs=[vmem] * len(out_shape),
        out_shape=out_shape,
        cost_estimate=pl.CostEstimate(flops=flops, bytes_accessed=size, transcendentals=0),
        compiler_params=pltpu.CompilerParams(vmem_limit_bytes=VMEM_WHOLE),
        name=name,
    )(place, *arrays)


def split_kernel(place, whole, *pieces):
    rows = pieces[0].shape[0]
    for p, piece in enumerate(pieces):
        piece[...] = whole[p * rows : (p + 1) * rows, :]


def weight_kernel(n_slots, n_pieces, n_chunks, keep, place, *refs):
    n = n_slots * n_pieces
    d_projected, added, outs = refs[n], refs[n + 1 : -2], refs[-2:]
    _, half, rows = outs[0].shape
    start = pl.multiple_of(place[0] * rows, rows)
    for j in range(n_slots):
        chunk = place[3 + j]
        bits = (chunk & 1, (chunk >> 1) & 1)
        inside = (chunk >= 0) & (chunk < n_chunks)
        for side in range(2):
            same = bits[side] == place[1 + side]
            wanted = inside & (same if keep else jnp.logical_not(same))
            position = bits[1 - side]

            @pl.when(wanted)
            def _():
                total = jnp.zeros((half, rows), jnp.float32)
                for p in range(n_pieces):
                    piece = refs[j * n_pieces + p]
                    height = piece.shape[0]
                    columns = d_projected[
                        p * height : (p + 1) * height, side * half : (side + 1) * half
                    ]
                    total = total + lax.dot_general(
                        columns,
                        piece[:, pl.ds(start, rows)],
                        (((0,), (0,)), ((), ())),
                        preferred_element_type=jnp.float32,
                    )
                if added:
                    total = total + added[side][position].astype(jnp.float32)
                outs[side][position] = total.astype(outs[side].dtype)


def combine_kernel(place, keep_a, got_a, keep_b, got_b, out_a, out_b):
    sides = ((keep_a, got_a, out_a), (keep_b, got_b, out_b))
    for side, (keep, got, out) in enumerate(sides):
        which = place[side]
        out[...] = (keep[which] + got[which].astype(jnp.float32)).astype(out.dtype)


def finish_kernel(place, keep_a, got_a, keep_b, got_b, last_a, last_b, out):
    half = last_a.shape[0]
    sides = ((keep_a, got_a, last_a), (keep_b, got_b, last_b))
    for side, (keep, got, last) in enumerate(sides):
        which = place[side]
        total = keep[which] + got[which].astype(jnp.float32) + last[...].astype(jnp.float32)
        out[:, side * half : (side + 1) * half] = total.T


def weight_sum(slots, d_projected, n_chunks):
    index = lax.axis_index("dp").astype(jnp.int32)
    core, x, y = index % 2, (index // 2) % 2, index // 4
    pieces = [piece for _, held in slots for piece in held]
    n_pieces = len(slots[0][1])
    length, cols = d_projected.shape
    half, rows = cols // 2, pieces[0].shape[1] // 2

    def swap(value, bit):
        return lax.ppermute(value, "dp", [(i, i ^ bit) for i in range(8)])

    def parts(which, keep, added, dtype, name):
        place = jnp.stack([which, x, y] + [chunk for chunk, _ in slots])
        kernel = functools.partial(weight_kernel, len(slots), n_pieces, n_chunks, keep)
        shape = jax.ShapeDtypeStruct((2, half, rows), dtype)
        arrays = pieces + [d_projected] + added
        return on_chip(kernel, place, arrays, [shape, shape], 4 * length * rows * cols, name)

    theirs = parts(1 - core, False, [], jnp.bfloat16, "weight_send_other")
    theirs = [swap(part, 1) for part in theirs]
    rest = parts(1 - core, True, [], jnp.bfloat16, "weight_keep_other")
    rest = [swap(part, 1) for part in rest]
    send_a, send_b = parts(core, False, theirs, jnp.bfloat16, "weight_send")
    got_a, got_b = swap(send_a, 2), swap(send_b, 4)
    keep_a, keep_b = parts(core, True, rest, jnp.float32, "weight_keep")

    small = jax.ShapeDtypeStruct((half, rows), jnp.bfloat16)
    arrays = [keep_a, got_a, keep_b, got_b]
    last_a, last_b = on_chip(
        combine_kernel, jnp.stack([1 - y, 1 - x]), arrays, [small] * 2, cols * rows, "weight_combine"
    )
    last = [swap(last_a, 4), swap(last_b, 2)]

    def finish(ready):
        ended, ready = lax.optimization_barrier((last, ready))
        (total,) = on_chip(
            finish_kernel,
            jnp.stack([y, x]),
            arrays + ended,
            [jax.ShapeDtypeStruct((rows, cols), jnp.float32)],
            2 * cols * rows,
            "weight_finish",
        )
        return total, ready

    return finish


def input_kernel(*refs):
    *pieces, feature_rows, out = refs
    cols = pieces[0].shape[1]
    total = jnp.zeros(out.shape, jnp.float32)
    for s, piece in enumerate(pieces):
        total = total + lax.dot_general(
            piece[...],
            feature_rows[:, s * cols : (s + 1) * cols],
            (((1,), (1,)), ((), ())),
            preferred_element_type=jnp.float32,
        )
    out[...] = total.astype(out.dtype)


def input_gradient(pieces, feature_rows):
    length, cols = pieces[0].shape
    feats, wide = feature_rows.shape
    step = min(feats, 512)
    return pl.pallas_call(
        input_kernel,
        grid=(feats // step,),
        in_specs=[pl.BlockSpec((length, cols), lambda i: (0, 0))] * len(pieces)
        + [pl.BlockSpec((step, wide), lambda i: (i, 0))],
        out_specs=pl.BlockSpec((length, step), lambda i: (0, i)),
        out_shape=jax.ShapeDtypeStruct((length, feats), jnp.bfloat16),
        cost_estimate=pl.CostEstimate(
            flops=2 * length * feats * wide,
            bytes_accessed=2 * feats * wide + 2 * length * (feats + wide),
            transcendentals=0,
        ),
        compiler_params=pltpu.CompilerParams(vmem_limit_bytes=VMEM_STREAM),
        name="input_gradient",
    )(*pieces, feature_rows)


def make_body(n_dp, n_z):
    ring = [[(z, (z + s) % n_z) for z in range(n_z)] for s in range(n_z)]
    n_pieces = 2

    def body(tokens, queries, d_out, segments, cached, master, moment, second, grad):
        me_dp = lax.axis_index("dp").astype(jnp.int32)
        me_z = lax.axis_index("tensor").astype(jnp.int32)
        length, feats = tokens.shape
        cols = cached.shape[1]
        height = length // n_pieces

        def part(piece, chunk):
            start = jnp.clip(chunk, 0, n_z - 1) * feats
            rows = lax.dynamic_slice_in_dim(cached, start, feats, 0)
            return jnp.dot(piece, rows, preferred_element_type=jnp.float32)

        shape = jax.ShapeDtypeStruct((height, feats), tokens.dtype)
        own = on_chip(
            split_kernel, jnp.zeros((1,), jnp.int32), [tokens], [shape] * n_pieces, 0, "split"
        )
        slots = [(me_z, own)]
        from_low, from_high, merged = own, own, None
        for s in range(1, n_z):
            up = [(z, z + 1) for z in range(s - 1, n_z - 1)]
            down = [(z + 1, z) for z in range(n_z - s)]
            low, high = me_z - s, me_z + s
            if merged is None:
                from_low = [lax.ppermute(piece, "tensor", up) for piece in from_low]
                from_high = [lax.ppermute(piece, "tensor", down) for piece in from_high]
            else:
                merged = [lax.ppermute(piece, "tensor", up + down) for piece in merged]
            if merged is None and 2 * s >= n_z:
                merged = [jnp.where(me_z >= s, a, b) for a, b in zip(from_low, from_high)]
            if merged is None:
                slots += [(low, from_low), (high, from_high)]
            else:
                slots.append((jnp.where(me_z >= s, low, high), merged))
        projected = []
        for p in range(n_pieces):
            total = jnp.zeros((height, cols), jnp.float32)
            for chunk, held in slots:
                total = total + part(held[p], chunk)
            projected.append(total.astype(jnp.bfloat16))
        projected = jnp.concatenate(projected, axis=0)

        later = cached
        if n_z > 1:
            later, master, _ = lax.optimization_barrier((cached, master, slots[1][1][0]))

        master_new, moment_new, second_new, own_new = optimizer(
            cached, master, moment, second, grad
        )
        new_cache = lax.all_gather(own_new, "dp", axis=0, tiled=True)

        share = feats // n_dp

        def block_for(z):
            return lax.dynamic_slice_in_dim(later, z * feats + me_dp * share, share, 0)

        blocks = [block_for(me_z)]
        for s in range(1, n_z):
            blocks.append(lax.ppermute(block_for((me_z + s) % n_z), "tensor", ring[s]))
        feature_rows = lax.all_gather(jnp.concatenate(blocks, axis=1), "dp", axis=0, tiled=True)

        d_queries, d_projected = attention_backward(projected, queries, d_out, segments[0])

        pieces = [d_projected] + [
            lax.ppermute(d_projected, "tensor", ring[s]) for s in range(1, n_z)
        ]
        if n_dp == 8 and n_z == 4:
            finish = weight_sum(slots, d_projected, n_z)
            new_grad, d_tokens = finish(input_gradient(pieces, feature_rows))
        else:
            d_tokens = input_gradient(pieces, feature_rows)
            partial = jnp.zeros((n_z + 1, feats, cols), jnp.bfloat16)
            for chunk, held in slots:
                product = lax.dot_general(
                    jnp.concatenate(held, axis=0),
                    d_projected,
                    (((0,), (0,)), ((), ())),
                    preferred_element_type=jnp.float32,
                )
                slot = jnp.where((chunk >= 0) & (chunk < n_z), chunk, n_z)
                partial = lax.dynamic_update_slice(
                    partial, product.astype(jnp.bfloat16)[None], (slot, 0, 0)
                )
            new_grad = lax.psum_scatter(
                partial[:n_z].reshape(n_z * feats, cols), "dp", scatter_dimension=0, tiled=True
            ).astype(jnp.float32)
        return (master_new, moment_new, second_new, new_cache, new_grad, d_queries, d_tokens)

    return body


def solution(mesh):
    in_specs = (
        P("dp", "tensor"),
        P("dp", "tensor"),
        P("dp", "tensor"),
        P("dp", None),
        P(None, "tensor"),
        P("dp", "tensor"),
        P("dp", "tensor"),
        P("dp", "tensor"),
        P("dp", "tensor"),
    )
    out_specs = (
        P("dp", "tensor"),
        P("dp", "tensor"),
        P("dp", "tensor"),
        P(None, "tensor"),
        P("dp", "tensor"),
        P("dp", "tensor"),
        P("dp", "tensor"),
    )
    body = make_body(mesh.shape["dp"], mesh.shape["tensor"])
    return jax.shard_map(body, mesh=mesh, in_specs=in_specs, out_specs=out_specs, check_vma=False)
```

```python
import math

import jax
import jax.numpy as jnp
from jax import lax
from jax.experimental import pallas as pl
from jax.experimental.pallas import tpu as pltpu
from jax.sharding import PartitionSpec as P

HD = 128
VMEM_STREAM = 56 * 1024 * 1024
VMEM_PART = 40 * 1024 * 1024
VMEM_WHOLE = 24 * 1024 * 1024


beta_first = 0.9
beta_second = 0.95
learn_rate = 0.0003
weight_decay = 0.1
adam_epsilon = 1e-08
first_fix = 1.0 - 0.9**40
second_fix = 1.0 - 0.95**40


def optimizer_kernel(
    place, cached, master, moment, second, grad, master_out, moment_out, second_out, cache_out
):
    moment_new = beta_first * moment[...] + (1.0 - beta_first) * grad[...]
    second_new = beta_second * second[...] + (1.0 - beta_second) * grad[...] * grad[...]
    update = moment_new / first_fix / (jnp.sqrt(second_new / second_fix) + adam_epsilon)
    master_new = master[...] - learn_rate * (update + weight_decay * master[...])
    moment_out[...] = moment_new
    second_out[...] = second_new
    master_out[...] = master_new
    for start in range(0, cached.shape[1], HD):
        block = slice(start, start + HD)
        own_cache = cached[:, block].astype(jnp.float32)
        delta = master_new[:, block] - own_cache
        largest = jnp.max(jnp.abs(delta), axis=1, keepdims=True)
        scale = (largest + 1e-06).astype(jnp.bfloat16).astype(jnp.float32)
        codes = (delta / scale).astype(jnp.bfloat16)
        cache_out[:, block] = (own_cache + codes.astype(jnp.float32) * scale).astype(jnp.bfloat16)


def optimizer(cached, master, moment, second, grad):
    rows, cols = master.shape
    step = min(rows, 256)
    steps = rows // step
    own = pl.BlockSpec((step, cols), lambda i, place: (i, 0))
    full = jax.ShapeDtypeStruct((rows, cols), jnp.float32)
    return pl.pallas_call(
        optimizer_kernel,
        grid_spec=pltpu.PrefetchScalarGridSpec(
            num_scalar_prefetch=1,
            grid=(steps,),
            in_specs=[pl.BlockSpec((step, cols), lambda i, place: (place[0] * steps + i, 0))]
            + [own] * 4,
            out_specs=[own] * 4,
        ),
        out_shape=[full, full, full, jax.ShapeDtypeStruct((rows, cols), jnp.bfloat16)],
        cost_estimate=pl.CostEstimate(
            flops=40 * rows * cols, bytes_accessed=32 * rows * cols, transcendentals=rows * cols
        ),
        compiler_params=pltpu.CompilerParams(vmem_limit_bytes=VMEM_STREAM),
        name="optimizer",
    )(lax.axis_index("dp").astype(jnp.int32).reshape(1), cached, master, moment, second, grad)


def on_chip(kernel, place, arrays, out_shape, flops, name):
    vmem = pl.BlockSpec(memory_space=pltpu.VMEM)
    size = sum(a.size * a.dtype.itemsize for a in arrays)
    size += sum(s.size * s.dtype.itemsize for s in out_shape)
    return pl.pallas_call(
        kernel,
        in_specs=[pl.BlockSpec(memory_space=pltpu.SMEM)] + [vmem] * len(arrays),
        out_specs=[vmem] * len(out_shape),
        out_shape=out_shape,
        cost_estimate=pl.CostEstimate(flops=flops, bytes_accessed=size, transcendentals=0),
        compiler_params=pltpu.CompilerParams(vmem_limit_bytes=VMEM_WHOLE),
        name=name,
    )(place, *arrays)


def absorb_kernel(place, chunk, cached, total, held, total_out, held_out):
    @pl.when(pl.program_id(0) == 0)
    def _():
        total_out[...] = total[...]

    total_out[...] += jnp.dot(chunk[...], cached[...], preferred_element_type=jnp.float32)
    held_out[0] = chunk[...].T


def absorb(chunk, index, cached, total, held, n_chunks):
    length, feats = chunk.shape
    cols = cached.shape[1]
    step = min(feats, 512)
    steps = feats // step
    inside = (index >= 0) & (index < n_chunks)
    place = jnp.stack([jnp.clip(index, 0, n_chunks - 1), jnp.where(inside, index, n_chunks)])
    shape = jax.ShapeDtypeStruct((n_chunks + 1, feats, length), chunk.dtype)
    out_total = jax.ShapeDtypeStruct(total.shape, jnp.float32)
    whole = pl.BlockSpec((length, cols), lambda i, place: (0, 0))
    operands = [chunk, cached, total] + ([] if held is None else [held])

    def kernel(place, chunk, cached, total, *refs):
        absorb_kernel(place, chunk, cached, total, None, *refs[-2:])

    return pl.pallas_call(
        kernel,
        grid_spec=pltpu.PrefetchScalarGridSpec(
            num_scalar_prefetch=1,
            grid=(steps,),
            in_specs=[
                pl.BlockSpec((length, step), lambda i, place: (0, i)),
                pl.BlockSpec((step, cols), lambda i, place: (place[0] * steps + i, 0)),
                whole,
            ]
            + ([] if held is None else [pl.BlockSpec(memory_space=pl.ANY)]),
            out_specs=[
                whole,
                pl.BlockSpec((1, step, length), lambda i, place: (place[1], i, 0)),
            ],
        ),
        out_shape=[out_total, shape],
        input_output_aliases={} if held is None else {4: 1},
        cost_estimate=pl.CostEstimate(
            flops=2 * length * feats * cols,
            bytes_accessed=4 * length * feats + 2 * feats * cols,
            transcendentals=0,
        ),
        compiler_params=pltpu.CompilerParams(vmem_limit_bytes=VMEM_PART),
        name="absorb",
    )(place, *operands)


def attention_kernel(place, projected, queries, d_out, allowed, d_queries, d_projected):
    factor = 1.0 / math.sqrt(HD)
    across = (((1,), (1,)), ((), ()))
    for head in range(projected.shape[1] // (2 * HD)):
        start = 2 * HD * head
        keys = projected[:, start : start + HD]
        values = projected[:, start + HD : start + 2 * HD]
        group = queries.shape[1] // HD // (projected.shape[1] // (2 * HD))
        d_keys = jnp.zeros(keys.shape, jnp.float32)
        d_values = jnp.zeros(keys.shape, jnp.float32)
        kept = allowed[...] > 0
        for g in range(head * group, (head + 1) * group):
            columns = slice(g * HD, (g + 1) * HD)
            query, grad = queries[:, columns], d_out[:, columns]
            scores = (
                lax.dot_general(keys, query, across, preferred_element_type=jnp.float32) * factor
            )
            scores = jnp.where(kept, scores, -1e30)
            weights = jnp.exp(scores - jnp.max(scores, axis=0, keepdims=True))
            probs = weights / jnp.sum(weights, axis=0, keepdims=True)
            probs_low = probs.astype(jnp.bfloat16)
            d_probs = lax.dot_general(values, grad, across, preferred_element_type=jnp.float32)
            rowdot = jnp.sum(probs_low.astype(jnp.float32) * d_probs, axis=0, keepdims=True)
            d_scores = (probs * (d_probs - rowdot) * factor).astype(jnp.bfloat16)
            d_queries[:, columns] = lax.dot_general(
                d_scores, keys, (((0,), (0,)), ((), ())), preferred_element_type=jnp.float32
            ).astype(jnp.bfloat16)
            d_keys = d_keys + jnp.dot(d_scores, query, preferred_element_type=jnp.float32)
            d_values = d_values + jnp.dot(probs_low, grad, preferred_element_type=jnp.float32)
        d_projected[:, start : start + HD] = d_keys.astype(jnp.bfloat16)
        d_projected[:, start + HD : start + 2 * HD] = d_values.astype(jnp.bfloat16)


def attention_backward(projected, queries, d_out, allowed):
    return on_chip(
        attention_kernel,
        jnp.zeros((1,), jnp.int32),
        [projected, queries, d_out, allowed],
        [jax.ShapeDtypeStruct(a.shape, jnp.bfloat16) for a in (queries, projected)],
        12 * allowed.size * queries.shape[1],
        "attention",
    )


def weight_kernel(place, chunk_a, chunk_b, d_projected, *refs):
    *added, out_a, out_b = refs
    half = out_a.shape[2]
    for side, (chunk, out) in enumerate(((chunk_a, out_a), (chunk_b, out_b))):
        columns = d_projected[:, side * half : (side + 1) * half]
        total = jnp.dot(chunk[0], columns, preferred_element_type=jnp.float32)
        if added:
            total = total + added[side][0].astype(jnp.float32)
        out[0] = total.astype(out.dtype)


def weight_parts(held, d_projected, place, added, dtype, name):
    length, cols = d_projected.shape
    rows = held.shape[1] // 2
    half = cols // 2
    out = pl.BlockSpec((1, rows, half), lambda k, place: (k, 0, 0))
    shape = jax.ShapeDtypeStruct((2, rows, half), dtype)
    return pl.pallas_call(
        weight_kernel,
        grid_spec=pltpu.PrefetchScalarGridSpec(
            num_scalar_prefetch=1,
            grid=(2,),
            in_specs=[
                pl.BlockSpec((1, rows, length), lambda k, place: (place[k], place[4], 0)),
                pl.BlockSpec((1, rows, length), lambda k, place: (place[2 + k], place[4], 0)),
                pl.BlockSpec((length, cols), lambda k, place: (0, 0)),
            ]
            + [out] * len(added),
            out_specs=[out, out],
        ),
        out_shape=[shape, shape],
        cost_estimate=pl.CostEstimate(
            flops=4 * length * rows * cols, bytes_accessed=8 * rows * cols, transcendentals=0
        ),
        compiler_params=pltpu.CompilerParams(vmem_limit_bytes=VMEM_PART),
        name=name,
    )(place, held, held, d_projected, *added)


def combine_kernel(place, keep_a, got_a, keep_b, got_b, out_a, out_b):
    sides = ((keep_a, got_a, out_a), (keep_b, got_b, out_b))
    for side, (keep, got, out) in enumerate(sides):
        which = place[side]
        out[...] = (keep[which] + got[which].astype(jnp.float32)).astype(out.dtype)


def finish_kernel(place, keep_a, got_a, keep_b, got_b, last_a, last_b, out):
    half = last_a.shape[1]
    sides = ((keep_a, got_a, last_a), (keep_b, got_b, last_b))
    for side, (keep, got, last) in enumerate(sides):
        which = place[side]
        total = keep[which] + got[which].astype(jnp.float32) + last[...].astype(jnp.float32)
        out[:, side * half : (side + 1) * half] = total


def plane():
    index = lax.axis_index("dp").astype(jnp.int32)

    def swap(value, bit):
        return lax.ppermute(value, "dp", [(i, i ^ bit) for i in range(8)])

    return index % 2, (index // 2) % 2, index // 4, swap


def weight_sum(held, d_projected):
    core, x, y, swap = plane()
    rows, cols = held.shape[1] // 2, d_projected.shape[1]
    send = [1 - x, 3 - x, 2 - 2 * y, 3 - 2 * y]
    keep = [x, 2 + x, 2 * y, 2 * y + 1]

    def parts(chunks, which, added, dtype, name):
        place = jnp.stack(chunks + [which])
        return weight_parts(held, d_projected, place, added, dtype, name)

    theirs = parts(send, 1 - core, [], jnp.bfloat16, "weight_send_other")
    theirs = [swap(part, 1) for part in theirs]
    rest = parts(keep, 1 - core, [], jnp.bfloat16, "weight_keep_other")
    rest = [swap(part, 1) for part in rest]
    send_a, send_b = parts(send, core, theirs, jnp.bfloat16, "weight_send")
    got_a, got_b = swap(send_a, 2), swap(send_b, 4)
    keep_a, keep_b = parts(keep, core, rest, jnp.float32, "weight_keep")

    small = jax.ShapeDtypeStruct((rows, cols // 2), jnp.bfloat16)
    arrays = [keep_a, got_a, keep_b, got_b]
    last_a, last_b = on_chip(
        combine_kernel, jnp.stack([1 - y, 1 - x]), arrays, [small] * 2, cols * rows, "weight_combine"
    )
    last = [swap(last_a, 4), swap(last_b, 2)]

    def finish(ready):
        ended, ready = lax.optimization_barrier((last, ready))
        (total,) = on_chip(
            finish_kernel,
            jnp.stack([y, x]),
            arrays + ended,
            [jax.ShapeDtypeStruct((rows, cols), jnp.float32)],
            2 * cols * rows,
            "weight_finish",
        )
        return total, ready

    return finish


def gather_plane(own_cache, own_rows):
    _, _, _, swap = plane()
    cache, rows = {0: own_cache}, {0: own_rows}
    for bit in (2, 4):
        cache[bit] = swap(own_cache, bit)
        rows[bit] = swap(own_rows, bit)
    cache[6] = swap(cache[4], 2)
    rows[6] = swap(rows[2], 4)
    for bits in (0, 2, 4, 6):
        cache[bits + 1] = swap(cache[bits], 1)
        rows[bits + 1] = swap(rows[bits], 1)
    return [cache[k] for k in range(8)], [rows[k] for k in range(8)]


def place_rows_kernel(place, *refs):
    *pieces, out, sems = refs
    height = pieces[0].shape[0]
    copies = []
    for k, piece in enumerate(pieces):
        start = pl.multiple_of((place[0] ^ k) * height, height)
        copies.append(
            pltpu.make_async_copy(piece, out.at[pl.ds(start, height), :], sems.at[k])
        )
    for copy in copies:
        copy.start()
    for copy in copies:
        copy.wait()


def place_rows(pieces):
    height, cols = pieces[0].shape
    anywhere = pl.BlockSpec(memory_space=pl.ANY)
    return pl.pallas_call(
        place_rows_kernel,
        in_specs=[pl.BlockSpec(memory_space=pltpu.SMEM)] + [anywhere] * len(pieces),
        out_specs=anywhere,
        out_shape=jax.ShapeDtypeStruct((height * len(pieces), cols), pieces[0].dtype),
        scratch_shapes=[pltpu.SemaphoreType.DMA((len(pieces),))],
        cost_estimate=pl.CostEstimate(
            flops=0, bytes_accessed=4 * height * cols * len(pieces), transcendentals=0
        ),
        compiler_params=pltpu.CompilerParams(vmem_limit_bytes=VMEM_WHOLE),
        name="place_rows",
    )(lax.axis_index("dp").astype(jnp.int32).reshape(1), *pieces)


def input_kernel(place, *refs):
    *arrays, out = refs
    n_blocks = place.shape[0] - 1
    pieces, rows = arrays[:n_blocks], arrays[n_blocks:]
    share = rows[0].shape[0] // n_blocks
    for k, held in enumerate(rows):
        total = jnp.zeros((out.shape[0], share), jnp.float32)
        for s, piece in enumerate(pieces):
            total = total + lax.dot_general(
                piece[...],
                held[s * share : (s + 1) * share, :],
                (((1,), (1,)), ((), ())),
                preferred_element_type=jnp.float32,
            )
        start = pl.multiple_of((place[0] ^ k) * share, share)
        out[:, pl.ds(start, share)] = total.astype(out.dtype)


def input_gradient(pieces, rows):
    length, cols = pieces[0].shape
    feats = sum(held.shape[0] for held in rows) // len(pieces)
    place = jnp.broadcast_to(lax.axis_index("dp").astype(jnp.int32), (len(pieces) + 1,))
    (d_tokens,) = on_chip(
        input_kernel,
        place,
        pieces + rows,
        [jax.ShapeDtypeStruct((length, feats), jnp.bfloat16)],
        2 * length * feats * cols * len(pieces),
        "input_gradient",
    )
    return d_tokens


def make_body(n_dp, n_z):
    ring = [[(z, (z + s) % n_z) for z in range(n_z)] for s in range(n_z)]
    tuned = n_dp == 8 and n_z == 4

    def body(tokens, queries, d_out, segments, cached, master, moment, second, grad):
        me_dp = lax.axis_index("dp").astype(jnp.int32)
        me_z = lax.axis_index("tensor").astype(jnp.int32)
        length, feats = tokens.shape
        cols = cached.shape[1]

        share = feats // n_dp

        def block_for(z):
            return lax.dynamic_slice_in_dim(cached, z * feats + me_dp * share, share, 0)

        blocks = [block_for(me_z)]
        for s in range(1, n_z):
            blocks.append(lax.ppermute(block_for((me_z + s) % n_z), "tensor", ring[s]))
        own_rows = jnp.concatenate(blocks, axis=0)

        master_new, moment_new, second_new, own_cache = optimizer(
            cached, master, moment, second, grad
        )

        total = jnp.zeros((length, cols), jnp.float32)
        total, held = absorb(tokens, me_z, cached, total, None, n_z)
        from_low, from_high, merged = tokens, tokens, None
        for s in range(1, n_z):
            up = [(z, z + 1) for z in range(s - 1, n_z - 1)]
            down = [(z + 1, z) for z in range(n_z - s)]
            low, high = me_z - s, me_z + s
            if merged is None:
                from_low = lax.ppermute(from_low, "tensor", up)
                from_high = lax.ppermute(from_high, "tensor", down)
            else:
                merged = lax.ppermute(merged, "tensor", up + down)
            if s == 1:
                from_low, from_high, own_cache, own_rows = lax.optimization_barrier(
                    (from_low, from_high, own_cache, own_rows)
                )
            if merged is None and 2 * s >= n_z:
                merged = jnp.where(me_z >= s, from_low, from_high)
            if merged is None:
                total, held = absorb(from_low, low, cached, total, held, n_z)
                total, held = absorb(from_high, high, cached, total, held, n_z)
            else:
                origin = jnp.where(me_z >= s, low, high)
                total, held = absorb(merged, origin, cached, total, held, n_z)

        doc_ids = segments[0]
        position = jnp.arange(length)
        allowed = (doc_ids[:, None] == doc_ids[None, :]) & (position[:, None] <= position[None, :])
        allowed = allowed.astype(jnp.float32)

        if tuned:
            cache_pieces, row_pieces = gather_plane(own_cache, own_rows)
            new_cache = place_rows(cache_pieces)
            total, new_cache, row_pieces = lax.optimization_barrier((total, new_cache, row_pieces))
        else:
            new_cache = lax.all_gather(own_cache, "dp", axis=0, tiled=True)
            row_pieces = lax.all_gather(own_rows, "dp", axis=0)

        d_queries, d_projected = attention_backward(
            total.astype(jnp.bfloat16), queries, d_out, allowed
        )

        pieces = [d_projected] + [
            lax.ppermute(d_projected, "tensor", ring[s]) for s in range(1, n_z)
        ]
        if tuned:
            finish = weight_sum(held, d_projected)
            new_grad, d_tokens = finish(input_gradient(pieces, row_pieces))
        else:
            rows = row_pieces.reshape(n_dp, n_z, share, cols)
            d_tokens = jnp.einsum(
                "slc,ksfc->lkf", jnp.stack(pieces), rows, preferred_element_type=jnp.float32
            )
            d_tokens = d_tokens.astype(jnp.bfloat16).reshape(length, feats)
            partial = lax.dot_general(
                held[:n_z].reshape(n_z * feats, length),
                d_projected,
                (((1,), (0,)), ((), ())),
                preferred_element_type=jnp.float32,
            )
            new_grad = lax.psum_scatter(
                partial.astype(jnp.bfloat16), "dp", scatter_dimension=0, tiled=True
            ).astype(jnp.float32)
        return (master_new, moment_new, second_new, new_cache, new_grad, d_queries, d_tokens)

    return body


def solution(mesh):
    in_specs = (
        P("dp", "tensor"),
        P("dp", "tensor"),
        P("dp", "tensor"),
        P("dp", None),
        P(None, "tensor"),
        P("dp", "tensor"),
        P("dp", "tensor"),
        P("dp", "tensor"),
        P("dp", "tensor"),
    )
    out_specs = (
        P("dp", "tensor"),
        P("dp", "tensor"),
        P("dp", "tensor"),
        P(None, "tensor"),
        P("dp", "tensor"),
        P("dp", "tensor"),
        P("dp", "tensor"),
    )
    body = make_body(mesh.shape["dp"], mesh.shape["tensor"])
    return jax.shard_map(body, mesh=mesh, in_specs=in_specs, out_specs=out_specs, check_vma=False)
```

```python
import math

import jax
import jax.numpy as jnp
from jax import lax
from jax.experimental import pallas as pl
from jax.experimental.pallas import tpu as pltpu
from jax.sharding import PartitionSpec as P

HD = 128
VMEM_STREAM = 56 * 1024 * 1024
VMEM_PART = 40 * 1024 * 1024
VMEM_WHOLE = 24 * 1024 * 1024


beta_first = 0.9
beta_second = 0.95
learn_rate = 0.0003
weight_decay = 0.1
adam_epsilon = 1e-08
first_fix = 1.0 - 0.9**40
second_fix = 1.0 - 0.95**40


def optimizer_kernel(
    place, cached, master, moment, second, grad, master_out, moment_out, second_out, cache_out
):
    moment_new = beta_first * moment[...] + (1.0 - beta_first) * grad[...]
    second_new = beta_second * second[...] + (1.0 - beta_second) * grad[...] * grad[...]
    update = moment_new / first_fix / (jnp.sqrt(second_new / second_fix) + adam_epsilon)
    master_new = master[...] - learn_rate * (update + weight_decay * master[...])
    moment_out[...] = moment_new
    second_out[...] = second_new
    master_out[...] = master_new
    for start in range(0, cached.shape[1], HD):
        block = slice(start, start + HD)
        own_cache = cached[:, block].astype(jnp.float32)
        delta = master_new[:, block] - own_cache
        largest = jnp.max(jnp.abs(delta), axis=1, keepdims=True)
        scale = (largest + 1e-06).astype(jnp.bfloat16).astype(jnp.float32)
        codes = (delta / scale).astype(jnp.bfloat16)
        cache_out[:, block] = (own_cache + codes.astype(jnp.float32) * scale).astype(jnp.bfloat16)


def optimizer(cached, master, moment, second, grad):
    rows, cols = master.shape
    step = min(rows, 256)
    steps = rows // step
    own = pl.BlockSpec((step, cols), lambda i, place: (i, 0))
    full = jax.ShapeDtypeStruct((rows, cols), jnp.float32)
    return pl.pallas_call(
        optimizer_kernel,
        grid_spec=pltpu.PrefetchScalarGridSpec(
            num_scalar_prefetch=1,
            grid=(steps,),
            in_specs=[pl.BlockSpec((step, cols), lambda i, place: (place[0] * steps + i, 0))]
            + [own] * 4,
            out_specs=[own] * 4,
        ),
        out_shape=[full, full, full, jax.ShapeDtypeStruct((rows, cols), jnp.bfloat16)],
        cost_estimate=pl.CostEstimate(
            flops=40 * rows * cols, bytes_accessed=32 * rows * cols, transcendentals=rows * cols
        ),
        compiler_params=pltpu.CompilerParams(vmem_limit_bytes=VMEM_STREAM),
        name="optimizer",
    )(lax.axis_index("dp").astype(jnp.int32).reshape(1), cached, master, moment, second, grad)


def on_chip(kernel, place, arrays, out_shape, flops, name):
    vmem = pl.BlockSpec(memory_space=pltpu.VMEM)
    size = sum(a.size * a.dtype.itemsize for a in arrays)
    size += sum(s.size * s.dtype.itemsize for s in out_shape)
    return pl.pallas_call(
        kernel,
        in_specs=[pl.BlockSpec(memory_space=pltpu.SMEM)] + [vmem] * len(arrays),
        out_specs=[vmem] * len(out_shape),
        out_shape=out_shape,
        cost_estimate=pl.CostEstimate(flops=flops, bytes_accessed=size, transcendentals=0),
        compiler_params=pltpu.CompilerParams(vmem_limit_bytes=VMEM_WHOLE),
        name=name,
    )(place, *arrays)


def split_kernel(place, whole, *pieces):
    rows = pieces[0].shape[0]
    for p, piece in enumerate(pieces):
        piece[...] = whole[p * rows : (p + 1) * rows, :]


def absorb_kernel(place, piece, cached, total, *refs):
    *_, total_out, held_out = refs

    @pl.when(pl.program_id(0) == 0)
    def _():
        total_out[...] = total[...]

    total_out[...] += jnp.dot(piece[...], cached[...], preferred_element_type=jnp.float32)
    held_out[0] = piece[...].T


def absorb(piece, p, n_pieces, index, cached, total, held, n_chunks):
    height, feats = piece.shape
    cols = cached.shape[1]
    step = min(feats, 1024)
    steps = feats // step
    inside = (index >= 0) & (index < n_chunks)
    place = jnp.stack([jnp.clip(index, 0, n_chunks - 1), jnp.where(inside, index, n_chunks)])
    shape = jax.ShapeDtypeStruct((n_chunks + 1, feats, height * n_pieces), piece.dtype)
    whole = pl.BlockSpec((height, cols), lambda i, place: (0, 0))
    return pl.pallas_call(
        absorb_kernel,
        grid_spec=pltpu.PrefetchScalarGridSpec(
            num_scalar_prefetch=1,
            grid=(steps,),
            in_specs=[
                pl.BlockSpec((height, step), lambda i, place: (0, i)),
                pl.BlockSpec((step, cols), lambda i, place: (place[0] * steps + i, 0)),
                whole,
            ]
            + ([] if held is None else [pl.BlockSpec(memory_space=pl.ANY)]),
            out_specs=[
                whole,
                pl.BlockSpec((1, step, height), lambda i, place: (place[1], i, p)),
            ],
        ),
        out_shape=[jax.ShapeDtypeStruct(total.shape, jnp.float32), shape],
        input_output_aliases={} if held is None else {4: 1},
        cost_estimate=pl.CostEstimate(
            flops=2 * height * feats * cols,
            bytes_accessed=4 * height * feats + 2 * feats * cols,
            transcendentals=0,
        ),
        compiler_params=pltpu.CompilerParams(vmem_limit_bytes=VMEM_PART),
        name="absorb",
    )(place, piece, cached, total, *([] if held is None else [held]))


def attention_kernel(place, projected, queries, d_out, allowed, d_queries, d_projected):
    factor = 1.0 / math.sqrt(HD)
    across = (((1,), (1,)), ((), ()))
    for head in range(projected.shape[1] // (2 * HD)):
        start = 2 * HD * head
        keys = projected[:, start : start + HD]
        values = projected[:, start + HD : start + 2 * HD]
        group = queries.shape[1] // HD // (projected.shape[1] // (2 * HD))
        d_keys = jnp.zeros(keys.shape, jnp.float32)
        d_values = jnp.zeros(keys.shape, jnp.float32)
        kept = allowed[...] > 0
        for g in range(head * group, (head + 1) * group):
            columns = slice(g * HD, (g + 1) * HD)
            query, grad = queries[:, columns], d_out[:, columns]
            scores = (
                lax.dot_general(keys, query, across, preferred_element_type=jnp.float32) * factor
            )
            scores = jnp.where(kept, scores, -1e30)
            weights = jnp.exp(scores - jnp.max(scores, axis=0, keepdims=True))
            probs = weights / jnp.sum(weights, axis=0, keepdims=True)
            probs_low = probs.astype(jnp.bfloat16)
            d_probs = lax.dot_general(values, grad, across, preferred_element_type=jnp.float32)
            rowdot = jnp.sum(probs_low.astype(jnp.float32) * d_probs, axis=0, keepdims=True)
            d_scores = (probs * (d_probs - rowdot) * factor).astype(jnp.bfloat16)
            d_queries[:, columns] = lax.dot_general(
                d_scores, keys, (((0,), (0,)), ((), ())), preferred_element_type=jnp.float32
            ).astype(jnp.bfloat16)
            d_keys = d_keys + jnp.dot(d_scores, query, preferred_element_type=jnp.float32)
            d_values = d_values + jnp.dot(probs_low, grad, preferred_element_type=jnp.float32)
        d_projected[:, start : start + HD] = d_keys.astype(jnp.bfloat16)
        d_projected[:, start + HD : start + 2 * HD] = d_values.astype(jnp.bfloat16)


def attention_backward(projected, queries, d_out, allowed):
    return on_chip(
        attention_kernel,
        jnp.zeros((1,), jnp.int32),
        [projected, queries, d_out, allowed],
        [jax.ShapeDtypeStruct(a.shape, jnp.bfloat16) for a in (queries, projected)],
        12 * allowed.size * queries.shape[1],
        "attention",
    )


def weight_kernel(place, chunk, d_projected, send_a, send_b, keep_a, keep_b):
    k = pl.program_id(0)
    half = send_a.shape[2]
    total = jnp.dot(chunk[0], d_projected[...], preferred_element_type=jnp.float32)

    @pl.when(k < 2)
    def _():
        send_a[0] = total[:, :half].astype(send_a.dtype)

    @pl.when(k >= 2)
    def _():
        keep_a[0] = total[:, :half].astype(keep_a.dtype)

    @pl.when(k % 2 == 0)
    def _():
        send_b[0] = total[:, half:].astype(send_b.dtype)

    @pl.when(k % 2 == 1)
    def _():
        keep_b[0] = total[:, half:].astype(keep_b.dtype)


def weight_parts(held, d_projected, place, dtype, name):
    length, cols = d_projected.shape
    rows = held.shape[1] // 2
    half = cols // 2
    first = pl.BlockSpec((1, rows, half), lambda k, place: (jnp.minimum(k, 1), 0, 0))
    second = pl.BlockSpec((1, rows, half), lambda k, place: (jnp.maximum(k, 2) - 2, 0, 0))
    pairs = pl.BlockSpec((1, rows, half), lambda k, place: (k // 2, 0, 0))
    return pl.pallas_call(
        weight_kernel,
        grid_spec=pltpu.PrefetchScalarGridSpec(
            num_scalar_prefetch=1,
            grid=(4,),
            in_specs=[
                pl.BlockSpec((1, rows, length), lambda k, place: (place[k], place[4], 0)),
                pl.BlockSpec((length, cols), lambda k, place: (0, 0)),
            ],
            out_specs=[first, pairs, second, pairs],
        ),
        out_shape=[jax.ShapeDtypeStruct((2, rows, half), dtype)] * 4,
        cost_estimate=pl.CostEstimate(
            flops=8 * length * rows * cols, bytes_accessed=16 * rows * cols, transcendentals=0
        ),
        compiler_params=pltpu.CompilerParams(vmem_limit_bytes=VMEM_STREAM),
        name=name,
    )(place, held, d_projected)


def add_kernel(place, mine_a, mine_b, other_a, other_b, out_a, out_b):
    for mine, other, out in ((mine_a, other_a, out_a), (mine_b, other_b, out_b)):
        out[...] = (mine[...] + other[...].astype(jnp.float32)).astype(out.dtype)


def combine_kernel(place, keep_a, got_a, keep_b, got_b, out_a, out_b):
    for keep, got, out in ((keep_a, got_a, out_a), (keep_b, got_b, out_b)):
        out[...] = (keep[0] + got[0].astype(jnp.float32)).astype(out.dtype)


def finish_kernel(place, keep_a, got_a, keep_b, got_b, last_a, last_b, out):
    half = last_a.shape[1]
    sides = ((keep_a, got_a, last_a), (keep_b, got_b, last_b))
    for side, (keep, got, last) in enumerate(sides):
        total = keep[1] + got[1].astype(jnp.float32) + last[...].astype(jnp.float32)
        out[:, side * half : (side + 1) * half] = total


def plane():
    index = lax.axis_index("dp").astype(jnp.int32)

    def swap(value, bit):
        return lax.ppermute(value, "dp", [(i, i ^ bit) for i in range(8)])

    return index % 2, (index // 2) % 2, index // 4, swap


def weight_sum(held, d_projected, beside):
    core, x, y, swap = plane()
    rows, cols = held.shape[1] // 2, d_projected.shape[1]
    none = jnp.zeros((1,), jnp.int32)
    chunks = [3 - x - 2 * y, 1 - x + 2 * y, x + 2 - 2 * y, x + 2 * y]

    def parts(which, dtype, name):
        return weight_parts(held, d_projected, jnp.stack(chunks + [which]), dtype, name)

    def add(mine, other, dtype, name):
        shape = jax.ShapeDtypeStruct(mine[0].shape, dtype)
        return on_chip(add_kernel, none, list(mine) + other, [shape] * 2, 2 * cols * rows, name)

    theirs = [swap(part, 1) for part in parts(1 - core, jnp.bfloat16, "weight_other")]
    mine = parts(core, jnp.float32, "weight_own")
    send_a, send_b = add(mine[:2], theirs[:2], jnp.bfloat16, "weight_add_send")
    got_a, got_b = swap(send_a, 2), swap(send_b, 4)
    keep_a, keep_b = add(mine[2:], theirs[2:], jnp.float32, "weight_add_keep")
    got_a, got_b, beside = lax.optimization_barrier((got_a, got_b, beside))

    small = jax.ShapeDtypeStruct((rows, cols // 2), jnp.bfloat16)
    arrays = [keep_a, got_a, keep_b, got_b]
    last_a, last_b = on_chip(
        combine_kernel, none, arrays, [small] * 2, cols * rows, "weight_combine"
    )
    last = [swap(last_a, 4), swap(last_b, 2)]

    def finish(ready):
        ended, ready = lax.optimization_barrier((last, ready))
        (total,) = on_chip(
            finish_kernel,
            none,
            arrays + ended,
            [jax.ShapeDtypeStruct((rows, cols), jnp.float32)],
            2 * cols * rows,
            "weight_finish",
        )
        return total, ready

    return finish, beside


def gather_plane(own_cache, own_rows, gate):
    _, _, _, swap = plane()
    cache, rows = {0: own_cache}, {0: own_rows}
    for bit in (2, 4):
        cache[bit] = swap(own_cache, bit)
        rows[bit] = swap(own_rows, bit)
    cache, rows, _ = lax.optimization_barrier((cache, rows, gate))
    cache[6] = swap(cache[4], 2)
    rows[6] = swap(rows[2], 4)
    for bits in (0, 2, 4, 6):
        cache[bits + 1] = swap(cache[bits], 1)
        rows[bits + 1] = swap(rows[bits], 1)
    return [cache[k] for k in range(8)], [rows[k] for k in range(8)]


def place_rows_kernel(place, *refs):
    *pieces, out, sems = refs
    height = pieces[0].shape[0]
    copies = []
    for k, piece in enumerate(pieces):
        start = pl.multiple_of((place[0] ^ k) * height, height)
        copies.append(
            pltpu.make_async_copy(piece, out.at[pl.ds(start, height), :], sems.at[k])
        )
    for copy in copies:
        copy.start()
    for copy in copies:
        copy.wait()


def place_rows(pieces):
    height, cols = pieces[0].shape
    return pl.pallas_call(
        place_rows_kernel,
        in_specs=[pl.BlockSpec(memory_space=pltpu.SMEM)]
        + [pl.BlockSpec(memory_space=pltpu.VMEM)] * len(pieces),
        out_specs=pl.BlockSpec(memory_space=pl.ANY),
        out_shape=jax.ShapeDtypeStruct((height * len(pieces), cols), pieces[0].dtype),
        scratch_shapes=[pltpu.SemaphoreType.DMA((len(pieces),))],
        cost_estimate=pl.CostEstimate(
            flops=0, bytes_accessed=4 * height * cols * len(pieces), transcendentals=0
        ),
        compiler_params=pltpu.CompilerParams(vmem_limit_bytes=VMEM_WHOLE),
        name="place_rows",
    )(lax.axis_index("dp").astype(jnp.int32).reshape(1), *pieces)


def input_kernel(place, *refs):
    *arrays, out = refs
    n_blocks = place.shape[0] - 1
    pieces, rows = arrays[:n_blocks], arrays[n_blocks:]
    share = rows[0].shape[0] // n_blocks
    for k, held in enumerate(rows):
        total = jnp.zeros((out.shape[0], share), jnp.float32)
        for s, piece in enumerate(pieces):
            total = total + lax.dot_general(
                piece[...],
                held[s * share : (s + 1) * share, :],
                (((1,), (1,)), ((), ())),
                preferred_element_type=jnp.float32,
            )
        start = pl.multiple_of((place[0] ^ k) * share, share)
        out[:, pl.ds(start, share)] = total.astype(out.dtype)


def input_gradient(pieces, rows):
    length, cols = pieces[0].shape
    feats = sum(held.shape[0] for held in rows) // len(pieces)
    place = jnp.broadcast_to(lax.axis_index("dp").astype(jnp.int32), (len(pieces) + 1,))
    (d_tokens,) = on_chip(
        input_kernel,
        place,
        pieces + rows,
        [jax.ShapeDtypeStruct((length, feats), jnp.bfloat16)],
        2 * length * feats * cols * len(pieces),
        "input_gradient",
    )
    return d_tokens


def make_body(n_dp, n_z):
    ring = [[(z, (z + s) % n_z) for z in range(n_z)] for s in range(n_z)]
    tuned = n_dp == 8 and n_z == 4
    n_pieces = 2

    def body(tokens, queries, d_out, segments, cached, master, moment, second, grad):
        me_dp = lax.axis_index("dp").astype(jnp.int32)
        me_z = lax.axis_index("tensor").astype(jnp.int32)
        length, feats = tokens.shape
        cols = cached.shape[1]

        share = feats // n_dp

        def block_for(z):
            return lax.dynamic_slice_in_dim(cached, z * feats + me_dp * share, share, 0)

        blocks = [block_for(me_z)]
        for s in range(1, n_z):
            blocks.append(lax.ppermute(block_for((me_z + s) % n_z), "tensor", ring[s]))
        own_rows = jnp.concatenate(blocks, axis=0)

        master_new, moment_new, second_new, own_cache = optimizer(
            cached, master, moment, second, grad
        )

        shape = jax.ShapeDtypeStruct((length // n_pieces, feats), tokens.dtype)
        own = on_chip(
            split_kernel, jnp.zeros((1,), jnp.int32), [tokens], [shape] * n_pieces, 0, "split"
        )
        totals = [jnp.zeros((length // n_pieces, cols), jnp.float32) for _ in range(n_pieces)]
        held = None

        def take(pieces, index, held):
            for p, piece in enumerate(pieces):
                totals[p], held = absorb(
                    piece, p, n_pieces, index, cached, totals[p], held, n_z
                )
            return held

        held = take(own, me_z, held)
        from_low, from_high, merged = own, own, None
        gates, after = [], held
        for s in range(1, n_z):
            up = [(z, z + 1) for z in range(s - 1, n_z - 1)]
            down = [(z + 1, z) for z in range(n_z - s)]
            low, high = me_z - s, me_z + s
            if merged is None:
                from_low = [lax.ppermute(piece, "tensor", up) for piece in from_low]
                from_high = [lax.ppermute(piece, "tensor", down) for piece in from_high]
            else:
                merged = [lax.ppermute(piece, "tensor", up + down) for piece in merged]
            if merged is None and 2 * s >= n_z:
                merged = [jnp.where(me_z >= s, a, b) for a, b in zip(from_low, from_high)]
            if merged is None:
                held = take(from_low, low, held)
                held = take(from_high, high, held)
            else:
                held = take(merged, jnp.where(me_z >= s, low, high), held)
            arrived = (from_low[0], from_high[0]) if merged is None else merged[0]
            gates.append((arrived, after))
            after = held

        doc_ids = segments[0]
        position = jnp.arange(length)
        allowed = (doc_ids[:, None] == doc_ids[None, :]) & (position[:, None] <= position[None, :])
        allowed = allowed.astype(jnp.float32)

        if tuned:
            own_cache, own_rows, _ = lax.optimization_barrier((own_cache, own_rows, gates[0]))
            cache_pieces, row_pieces = gather_plane(own_cache, own_rows, gates[1])
            totals, cache_pieces, row_pieces = lax.optimization_barrier(
                (totals, cache_pieces, row_pieces)
            )
        else:
            new_cache = lax.all_gather(own_cache, "dp", axis=0, tiled=True)
            row_pieces = lax.all_gather(own_rows, "dp", axis=0)

        d_queries, d_projected = attention_backward(
            jnp.concatenate(totals, axis=0).astype(jnp.bfloat16), queries, d_out, allowed
        )

        pieces = [d_projected] + [
            lax.ppermute(d_projected, "tensor", ring[s]) for s in range(1, n_z)
        ]
        if tuned:
            new_cache = place_rows(cache_pieces)
            finish, (pieces, new_cache) = weight_sum(held, d_projected, (pieces, new_cache))
            new_grad, d_tokens = finish(input_gradient(pieces, row_pieces))
        else:
            rows = row_pieces.reshape(n_dp, n_z, share, cols)
            d_tokens = jnp.einsum(
                "slc,ksfc->lkf", jnp.stack(pieces), rows, preferred_element_type=jnp.float32
            )
            d_tokens = d_tokens.astype(jnp.bfloat16).reshape(length, feats)
            partial = lax.dot_general(
                held[:n_z].reshape(n_z * feats, length),
                d_projected,
                (((1,), (0,)), ((), ())),
                preferred_element_type=jnp.float32,
            )
            new_grad = lax.psum_scatter(
                partial.astype(jnp.bfloat16), "dp", scatter_dimension=0, tiled=True
            ).astype(jnp.float32)
        return (master_new, moment_new, second_new, new_cache, new_grad, d_queries, d_tokens)

    return body


def solution(mesh):
    in_specs = (
        P("dp", "tensor"),
        P("dp", "tensor"),
        P("dp", "tensor"),
        P("dp", None),
        P(None, "tensor"),
        P("dp", "tensor"),
        P("dp", "tensor"),
        P("dp", "tensor"),
        P("dp", "tensor"),
    )
    out_specs = (
        P("dp", "tensor"),
        P("dp", "tensor"),
        P("dp", "tensor"),
        P(None, "tensor"),
        P("dp", "tensor"),
        P("dp", "tensor"),
        P("dp", "tensor"),
    )
    body = make_body(mesh.shape["dp"], mesh.shape["tensor"])
    return jax.shard_map(body, mesh=mesh, in_specs=in_specs, out_specs=out_specs, check_vma=False)
```

```python
import functools
import math

import jax
import jax.numpy as jnp
from jax import lax
from jax.experimental import pallas as pl
from jax.experimental.pallas import tpu as pltpu
from jax.sharding import PartitionSpec as P

HD = 128
VMEM_STREAM = 60 * 1024 * 1024
VMEM_WHOLE = 24 * 1024 * 1024


beta_first = 0.9
beta_second = 0.95
learn_rate = 0.0003
weight_decay = 0.1
adam_epsilon = 1e-08
first_fix = 1.0 - 0.9**40
second_fix = 1.0 - 0.95**40


def optimizer_kernel(
    place, cached, master, moment, second, grad, master_out, moment_out, second_out, cache_out
):
    moment_new = beta_first * moment[...] + (1.0 - beta_first) * grad[...]
    second_new = beta_second * second[...] + (1.0 - beta_second) * grad[...] * grad[...]
    update = moment_new / first_fix / (jnp.sqrt(second_new / second_fix) + adam_epsilon)
    master_new = master[...] - learn_rate * (update + weight_decay * master[...])
    moment_out[...] = moment_new
    second_out[...] = second_new
    master_out[...] = master_new
    for start in range(0, cached.shape[1], HD):
        block = slice(start, start + HD)
        own_cache = cached[:, block].astype(jnp.float32)
        delta = master_new[:, block] - own_cache
        largest = jnp.max(jnp.abs(delta), axis=1, keepdims=True)
        scale = (largest + 1e-06).astype(jnp.bfloat16).astype(jnp.float32)
        codes = (delta / scale).astype(jnp.bfloat16)
        cache_out[:, block] = (own_cache + codes.astype(jnp.float32) * scale).astype(jnp.bfloat16)


def optimizer(cached, master, moment, second, grad):
    rows, cols = master.shape
    step = min(rows, 256)
    steps = rows // step
    own = pl.BlockSpec((step, cols), lambda i, place: (i, 0))
    full = jax.ShapeDtypeStruct((rows, cols), jnp.float32)
    return pl.pallas_call(
        optimizer_kernel,
        grid_spec=pltpu.PrefetchScalarGridSpec(
            num_scalar_prefetch=1,
            grid=(steps,),
            in_specs=[pl.BlockSpec((step, cols), lambda i, place: (place[0] * steps + i, 0))]
            + [own] * 4,
            out_specs=[own] * 4,
        ),
        out_shape=[full, full, full, jax.ShapeDtypeStruct((rows, cols), jnp.bfloat16)],
        cost_estimate=pl.CostEstimate(
            flops=40 * rows * cols, bytes_accessed=32 * rows * cols, transcendentals=rows * cols
        ),
        compiler_params=pltpu.CompilerParams(vmem_limit_bytes=VMEM_STREAM),
        name="optimizer",
    )(lax.axis_index("dp").astype(jnp.int32).reshape(1), cached, master, moment, second, grad)


def on_chip(kernel, place, arrays, out_shape, flops, name):
    vmem = pl.BlockSpec(memory_space=pltpu.VMEM)
    size = sum(a.size * a.dtype.itemsize for a in arrays)
    size += sum(s.size * s.dtype.itemsize for s in out_shape)
    return pl.pallas_call(
        kernel,
        in_specs=[pl.BlockSpec(memory_space=pltpu.SMEM)] + [vmem] * len(arrays),
        out_specs=[vmem] * len(out_shape),
        out_shape=out_shape,
        cost_estimate=pl.CostEstimate(flops=flops, bytes_accessed=size, transcendentals=0),
        compiler_params=pltpu.CompilerParams(vmem_limit_bytes=VMEM_WHOLE),
        name=name,
    )(place, *arrays)


def absorb_kernel(place, chunk, cached, total, *refs):
    *_, total_out, held_out = refs

    @pl.when(pl.program_id(0) == 0)
    def _():
        total_out[...] = total[...]

    total_out[...] += jnp.dot(chunk[...], cached[...], preferred_element_type=jnp.float32)
    held_out[0] = chunk[...].T


def absorb(chunk, index, cached, total, held, n_chunks):
    length, feats = chunk.shape
    cols = cached.shape[1]
    step = min(feats, 1024)
    steps = feats // step
    inside = (index >= 0) & (index < n_chunks)
    place = jnp.stack([jnp.clip(index, 0, n_chunks - 1), jnp.where(inside, index, n_chunks)])
    shape = jax.ShapeDtypeStruct((8 * n_chunks, feats, length), chunk.dtype)
    whole = pl.BlockSpec((length, cols), lambda i, place: (0, 0))
    return pl.pallas_call(
        absorb_kernel,
        grid_spec=pltpu.PrefetchScalarGridSpec(
            num_scalar_prefetch=1,
            grid=(steps,),
            in_specs=[
                pl.BlockSpec((length, step), lambda i, place: (0, i)),
                pl.BlockSpec((step, cols), lambda i, place: (place[0] * steps + i, 0)),
                whole,
            ]
            + ([] if held is None else [pl.BlockSpec(memory_space=pl.ANY)]),
            out_specs=[
                whole,
                pl.BlockSpec((1, step, length), lambda i, place: (place[1], i, 0)),
            ],
        ),
        out_shape=[jax.ShapeDtypeStruct(total.shape, jnp.float32), shape],
        input_output_aliases={} if held is None else {4: 1},
        cost_estimate=pl.CostEstimate(
            flops=2 * length * feats * cols,
            bytes_accessed=4 * length * feats + 2 * feats * cols,
            transcendentals=0,
        ),
        compiler_params=pltpu.CompilerParams(vmem_limit_bytes=VMEM_STREAM),
        name="absorb",
    )(place, chunk, cached, total, *([] if held is None else [held]))


def attention_kernel(place, projected, queries, d_out, allowed, d_queries, d_projected):
    factor = 1.0 / math.sqrt(HD)
    across = (((1,), (1,)), ((), ()))
    for head in range(projected.shape[1] // (2 * HD)):
        start = 2 * HD * head
        keys = projected[:, start : start + HD]
        values = projected[:, start + HD : start + 2 * HD]
        group = queries.shape[1] // HD // (projected.shape[1] // (2 * HD))
        d_keys = jnp.zeros(keys.shape, jnp.float32)
        d_values = jnp.zeros(keys.shape, jnp.float32)
        kept = allowed[...] > 0
        for g in range(head * group, (head + 1) * group):
            columns = slice(g * HD, (g + 1) * HD)
            query, grad = queries[:, columns], d_out[:, columns]
            scores = (
                lax.dot_general(keys, query, across, preferred_element_type=jnp.float32) * factor
            )
            scores = jnp.where(kept, scores, -1e30)
            weights = jnp.exp(scores - jnp.max(scores, axis=0, keepdims=True))
            probs = weights / jnp.sum(weights, axis=0, keepdims=True)
            probs_low = probs.astype(jnp.bfloat16)
            d_probs = lax.dot_general(values, grad, across, preferred_element_type=jnp.float32)
            rowdot = jnp.sum(probs_low.astype(jnp.float32) * d_probs, axis=0, keepdims=True)
            d_scores = (probs * (d_probs - rowdot) * factor).astype(jnp.bfloat16)
            d_queries[:, columns] = lax.dot_general(
                d_scores, keys, (((0,), (0,)), ((), ())), preferred_element_type=jnp.float32
            ).astype(jnp.bfloat16)
            d_keys = d_keys + jnp.dot(d_scores, query, preferred_element_type=jnp.float32)
            d_values = d_values + jnp.dot(probs_low, grad, preferred_element_type=jnp.float32)
        d_projected[:, start : start + HD] = d_keys.astype(jnp.bfloat16)
        d_projected[:, start + HD : start + 2 * HD] = d_values.astype(jnp.bfloat16)


def attention_backward(projected, queries, d_out, allowed):
    return on_chip(
        attention_kernel,
        jnp.zeros((1,), jnp.int32),
        [projected, queries, d_out, allowed],
        [jax.ShapeDtypeStruct(a.shape, jnp.bfloat16) for a in (queries, projected)],
        12 * allowed.size * queries.shape[1],
        "attention",
    )


SENT = ((0, 0, 0), (0, 1, 0), (1, 0, 1), (2, 1, 1))
KEPT = ((1, 1, 0), (2, 0, 0), (3, 0, 1), (3, 1, 1))


def weight_kernel(groups, place, held, d_projected, *refs):
    *refs, buffer, sems = refs
    n_out = 2 * len(groups)
    added, outs = refs[:-n_out], refs[-n_out:]
    rows = buffer.shape[1]
    half = d_projected.shape[1] // 2
    block = min(rows, 256)
    start = pl.multiple_of(place[4] * rows, rows)
    chunks = sorted({chunk for group in groups for chunk, _, _ in group})
    copies = {}
    for chunk in chunks:
        copies[chunk] = pltpu.make_async_copy(
            held.at[place[chunk], pl.ds(start, rows), :], buffer.at[chunk], sems.at[chunk]
        )
        copies[chunk].start()
    for chunk in chunks:
        copies[chunk].wait()
        for r in range(0, rows, block):
            wanted = [
                (side, 2 * g + side, position)
                for g, group in enumerate(groups)
                for which, side, position in group
                if which == chunk
            ]
            first, last = min(w[0] for w in wanted), max(w[0] for w in wanted)
            total = jnp.dot(
                buffer[chunk, r : r + block, :],
                d_projected[:, first * half : (last + 1) * half],
                preferred_element_type=jnp.float32,
            )
            for side, n, position in wanted:
                part = total[:, (side - first) * half : (side - first + 1) * half]
                if added:
                    part = part + added[n][position, r : r + block, :].astype(jnp.float32)
                outs[n][position, r : r + block, :] = part.astype(outs[n].dtype)


def weight_parts(held, d_projected, place, groups, added, dtype, name):
    length, cols = d_projected.shape
    rows = held.shape[1] // 2
    shape = jax.ShapeDtypeStruct((2, rows, cols // 2), dtype)
    vmem = pl.BlockSpec(memory_space=pltpu.VMEM)
    n_out = 2 * len(groups)
    return pl.pallas_call(
        functools.partial(weight_kernel, groups),
        in_specs=[pl.BlockSpec(memory_space=pltpu.SMEM), pl.BlockSpec(memory_space=pl.ANY)]
        + [vmem] * (1 + len(added)),
        out_specs=[vmem] * n_out,
        out_shape=[shape] * n_out,
        scratch_shapes=[
            pltpu.VMEM((4, rows, length), held.dtype),
            pltpu.SemaphoreType.DMA((4,)),
        ],
        cost_estimate=pl.CostEstimate(
            flops=4 * length * rows * cols * len(groups),
            bytes_accessed=8 * rows * cols * len(groups),
            transcendentals=0,
        ),
        compiler_params=pltpu.CompilerParams(vmem_limit_bytes=VMEM_WHOLE),
        name=name,
    )(place, held, d_projected, *added)


def combine_kernel(place, keep_a, got_a, keep_b, got_b, out_a, out_b):
    for keep, got, out in ((keep_a, got_a, out_a), (keep_b, got_b, out_b)):
        out[...] = (keep[0] + got[0].astype(jnp.float32)).astype(out.dtype)


def finish_kernel(place, keep_a, got_a, keep_b, got_b, last_a, last_b, out):
    half = last_a.shape[1]
    sides = ((keep_a, got_a, last_a), (keep_b, got_b, last_b))
    for side, (keep, got, last) in enumerate(sides):
        total = keep[1] + got[1].astype(jnp.float32) + last[...].astype(jnp.float32)
        out[:, side * half : (side + 1) * half] = total


def plane():
    index = lax.axis_index("dp").astype(jnp.int32)

    def swap(value, bit):
        return lax.ppermute(value, "dp", [(i, i ^ bit) for i in range(8)])

    return index % 2, (index // 2) % 2, index // 4, swap


def weight_sum(held, d_projected, beside):
    core, x, y, swap = plane()
    rows, cols = held.shape[1] // 2, d_projected.shape[1]
    none = jnp.zeros((1,), jnp.int32)
    chunks = [3 - x - 2 * y, 1 - x + 2 * y, x + 2 - 2 * y, x + 2 * y]

    def parts(which, groups, added, dtype, name):
        place = jnp.stack(chunks + [which])
        return weight_parts(held, d_projected, place, groups, added, dtype, name)

    theirs = parts(1 - core, (SENT, KEPT), [], jnp.bfloat16, "weight_other")
    theirs = [swap(part, 1) for part in theirs]
    send_a, send_b = parts(core, (SENT,), theirs[:2], jnp.bfloat16, "weight_send")
    got_a, got_b = swap(send_a, 2), swap(send_b, 4)
    keep_a, keep_b = parts(core, (KEPT,), theirs[2:], jnp.float32, "weight_keep")
    got_a, got_b, beside = lax.optimization_barrier((got_a, got_b, beside))

    small = jax.ShapeDtypeStruct((rows, cols // 2), jnp.bfloat16)
    arrays = [keep_a, got_a, keep_b, got_b]
    last_a, last_b = on_chip(
        combine_kernel, none, arrays, [small] * 2, cols * rows, "weight_combine"
    )
    last = [swap(last_a, 4), swap(last_b, 2)]

    def finish(ready):
        ended, ready = lax.optimization_barrier((last, ready))
        (total,) = on_chip(
            finish_kernel,
            none,
            arrays + ended,
            [jax.ShapeDtypeStruct((rows, cols), jnp.float32)],
            2 * cols * rows,
            "weight_finish",
        )
        return total, ready

    return finish, beside


def gather_plane(own, gate):
    _, _, _, swap = plane()
    half = own.shape[0] // 2
    got = {0: own, 2: swap(own, 2), 4: swap(own, 4)}
    got[1] = swap(own, 1)
    (got, _) = lax.optimization_barrier((got, gate))
    top, bottom = swap(got[4][:half], 2), swap(got[2][half:], 4)
    got[3], got[5] = swap(got[2], 1), swap(got[4], 1)
    near = [(got[k], got[k]) for k in range(6)]
    return near + [(top, bottom), (swap(top, 1), swap(bottom, 1))]


def place_rows_kernel(height, place, *refs):
    *pieces, out, sems = refs
    copies = []
    for k, piece in enumerate(pieces):
        start = pl.multiple_of((place[0] ^ k) * height, height)
        copies.append(
            pltpu.make_async_copy(
                piece.at[pl.ds(0, height), :], out.at[pl.ds(start, height), :], sems.at[k]
            )
        )
    for copy in copies:
        copy.start()
    for copy in copies:
        copy.wait()


def place_rows(pieces, height):
    cols = pieces[0].shape[1]
    return pl.pallas_call(
        functools.partial(place_rows_kernel, height),
        in_specs=[pl.BlockSpec(memory_space=pltpu.SMEM)]
        + [pl.BlockSpec(memory_space=pltpu.VMEM)] * len(pieces),
        out_specs=pl.BlockSpec(memory_space=pl.ANY),
        out_shape=jax.ShapeDtypeStruct((height * len(pieces), cols), pieces[0].dtype),
        scratch_shapes=[pltpu.SemaphoreType.DMA((len(pieces),))],
        cost_estimate=pl.CostEstimate(
            flops=0, bytes_accessed=4 * height * cols * len(pieces), transcendentals=0
        ),
        compiler_params=pltpu.CompilerParams(vmem_limit_bytes=VMEM_WHOLE),
        name="place_rows",
    )(lax.axis_index("dp").astype(jnp.int32).reshape(1), *pieces)


def input_kernel(offsets, place, *refs):
    *arrays, out = refs
    n_blocks = place.shape[0] - 1
    pieces, rows = arrays[:n_blocks], arrays[n_blocks:]
    share = out.shape[1] // len(rows)
    for k, (held, offset) in enumerate(zip(rows, offsets)):
        total = jnp.zeros((out.shape[0], share), jnp.float32)
        for s, piece in enumerate(pieces):
            total = total + lax.dot_general(
                piece[...],
                held[offset + s * share : offset + (s + 1) * share, :],
                (((1,), (1,)), ((), ())),
                preferred_element_type=jnp.float32,
            )
        start = pl.multiple_of((place[0] ^ k) * share, share)
        out[:, pl.ds(start, share)] = total.astype(out.dtype)


def input_gradient(pieces, rows, offsets, feats):
    length, cols = pieces[0].shape
    place = jnp.broadcast_to(lax.axis_index("dp").astype(jnp.int32), (len(pieces) + 1,))
    (d_tokens,) = on_chip(
        functools.partial(input_kernel, offsets),
        place,
        pieces + rows,
        [jax.ShapeDtypeStruct((length, feats), jnp.bfloat16)],
        2 * length * feats * cols * len(pieces),
        "input_gradient",
    )
    return d_tokens


def make_body(n_dp, n_z):
    tuned = n_dp == 8 and n_z == 4

    def pair(value, s):
        return lax.ppermute(value, "tensor", [(z, z ^ s) for z in range(n_z)])

    def body(tokens, queries, d_out, segments, cached, master, moment, second, grad):
        me_dp = lax.axis_index("dp").astype(jnp.int32)
        me_z = lax.axis_index("tensor").astype(jnp.int32)
        length, feats = tokens.shape
        cols = cached.shape[1]

        share = feats // n_dp

        def block_for(z):
            return lax.dynamic_slice_in_dim(cached, z * feats + me_dp * share, share, 0)

        blocks = [block_for(me_z)] + [pair(block_for(me_z ^ s), s) for s in range(1, n_z)]

        master_new, moment_new, second_new, own_cache = optimizer(
            cached, master, moment, second, grad
        )

        total = jnp.zeros((length, cols), jnp.float32)
        total, held = absorb(tokens, me_z, cached, total, None, n_z)
        if tuned:
            bundle = jnp.concatenate([own_cache] + blocks, axis=0)
        from_low, from_high, merged = tokens, tokens, None
        for s in range(1, n_z):
            up = [(z, z + 1) for z in range(s - 1, n_z - 1)]
            down = [(z + 1, z) for z in range(n_z - s)]
            low, high = me_z - s, me_z + s
            if merged is None:
                from_low = lax.ppermute(from_low, "tensor", up)
                from_high = lax.ppermute(from_high, "tensor", down)
            else:
                merged = lax.ppermute(merged, "tensor", up + down)
            if merged is None and 2 * s >= n_z:
                merged = jnp.where(me_z >= s, from_low, from_high)
            if tuned and s == 1:
                from_low, from_high, held, bundle = lax.optimization_barrier(
                    (from_low, from_high, held, bundle)
                )
            if tuned and s == n_z - 1:
                gathered = gather_plane(bundle, merged)
                new_cache = place_rows([cache for cache, _ in gathered], own_cache.shape[0])
                total, new_cache, gathered = lax.optimization_barrier((total, new_cache, gathered))
            if merged is None:
                total, held = absorb(from_low, low, cached, total, held, n_z)
                total, held = absorb(from_high, high, cached, total, held, n_z)
            else:
                origin = jnp.where(me_z >= s, low, high)
                total, held = absorb(merged, origin, cached, total, held, n_z)

        doc_ids = segments[0]
        position = jnp.arange(length)
        allowed = (doc_ids[:, None] == doc_ids[None, :]) & (position[:, None] <= position[None, :])
        allowed = allowed.astype(jnp.float32)

        d_queries, d_projected = attention_backward(
            total.astype(jnp.bfloat16), queries, d_out, allowed
        )

        pieces = [d_projected]
        s = 1
        while s < n_z:
            pieces = pieces + [pair(piece, s) for piece in pieces]
            s *= 2
        if tuned:
            finish, pieces = weight_sum(held, d_projected, pieces)
            rows = [rows for _, rows in gathered]
            offsets = [array.shape[0] - n_z * share for array in rows]
            new_grad, d_tokens = finish(input_gradient(pieces, rows, offsets, feats))
        else:
            new_cache = lax.all_gather(own_cache, "dp", axis=0, tiled=True)
            rows = lax.all_gather(jnp.stack(blocks), "dp", axis=0)
            d_tokens = jnp.einsum(
                "slc,ksfc->lkf", jnp.stack(pieces), rows, preferred_element_type=jnp.float32
            )
            d_tokens = d_tokens.astype(jnp.bfloat16).reshape(length, feats)
            partial = lax.dot_general(
                held[:n_z].reshape(n_z * feats, length),
                d_projected,
                (((1,), (0,)), ((), ())),
                preferred_element_type=jnp.float32,
            )
            new_grad = lax.psum_scatter(
                partial.astype(jnp.bfloat16), "dp", scatter_dimension=0, tiled=True
            ).astype(jnp.float32)
        return (master_new, moment_new, second_new, new_cache, new_grad, d_queries, d_tokens)

    return body


def solution(mesh):
    in_specs = (
        P("dp", "tensor"),
        P("dp", "tensor"),
        P("dp", "tensor"),
        P("dp", None),
        P(None, "tensor"),
        P("dp", "tensor"),
        P("dp", "tensor"),
        P("dp", "tensor"),
        P("dp", "tensor"),
    )
    out_specs = (
        P("dp", "tensor"),
        P("dp", "tensor"),
        P("dp", "tensor"),
        P(None, "tensor"),
        P("dp", "tensor"),
        P("dp", "tensor"),
        P("dp", "tensor"),
    )
    body = make_body(mesh.shape["dp"], mesh.shape["tensor"])
    return jax.shard_map(body, mesh=mesh, in_specs=in_specs, out_specs=out_specs, check_vma=False)
```

```python
import functools
import math

import jax
import jax.numpy as jnp
from jax import lax
from jax.experimental import pallas as pl
from jax.experimental.pallas import tpu as pltpu
from jax.sharding import PartitionSpec as P

HD = 128
VMEM_STREAM = 60 * 1024 * 1024
VMEM_WHOLE = 24 * 1024 * 1024


beta_first = 0.9
beta_second = 0.95
learn_rate = 0.0003
weight_decay = 0.1
adam_epsilon = 1e-08
first_fix = 1.0 - 0.9**40
second_fix = 1.0 - 0.95**40


def optimizer_kernel(
    place, cached, master, moment, second, grad, master_out, moment_out, second_out, cache_out
):
    moment_new = beta_first * moment[...] + (1.0 - beta_first) * grad[...]
    second_new = beta_second * second[...] + (1.0 - beta_second) * grad[...] * grad[...]
    update = moment_new / first_fix / (jnp.sqrt(second_new / second_fix) + adam_epsilon)
    master_new = master[...] - learn_rate * (update + weight_decay * master[...])
    moment_out[...] = moment_new
    second_out[...] = second_new
    master_out[...] = master_new
    for start in range(0, cached.shape[1], HD):
        block = slice(start, start + HD)
        own_cache = cached[:, block].astype(jnp.float32)
        delta = master_new[:, block] - own_cache
        largest = jnp.max(jnp.abs(delta), axis=1, keepdims=True)
        scale = (largest + 1e-06).astype(jnp.bfloat16).astype(jnp.float32)
        codes = (delta / scale).astype(jnp.bfloat16)
        cache_out[:, block] = (own_cache + codes.astype(jnp.float32) * scale).astype(jnp.bfloat16)


def optimizer(cached, master, moment, second, grad):
    rows, cols = master.shape
    step = min(rows, 256)
    steps = rows // step
    own = pl.BlockSpec((step, cols), lambda i, place: (i, 0))
    full = jax.ShapeDtypeStruct((rows, cols), jnp.float32)
    return pl.pallas_call(
        optimizer_kernel,
        grid_spec=pltpu.PrefetchScalarGridSpec(
            num_scalar_prefetch=1,
            grid=(steps,),
            in_specs=[pl.BlockSpec((step, cols), lambda i, place: (place[0] * steps + i, 0))]
            + [own] * 4,
            out_specs=[own] * 4,
        ),
        out_shape=[full, full, full, jax.ShapeDtypeStruct((rows, cols), jnp.bfloat16)],
        cost_estimate=pl.CostEstimate(
            flops=40 * rows * cols, bytes_accessed=32 * rows * cols, transcendentals=rows * cols
        ),
        compiler_params=pltpu.CompilerParams(vmem_limit_bytes=VMEM_STREAM),
        name="optimizer",
    )(lax.axis_index("dp").astype(jnp.int32).reshape(1), cached, master, moment, second, grad)


def on_chip(kernel, place, arrays, out_shape, flops, name):
    vmem = pl.BlockSpec(memory_space=pltpu.VMEM)
    size = sum(a.size * a.dtype.itemsize for a in arrays)
    size += sum(s.size * s.dtype.itemsize for s in out_shape)
    return pl.pallas_call(
        kernel,
        in_specs=[pl.BlockSpec(memory_space=pltpu.SMEM)] + [vmem] * len(arrays),
        out_specs=[vmem] * len(out_shape),
        out_shape=out_shape,
        cost_estimate=pl.CostEstimate(flops=flops, bytes_accessed=size, transcendentals=0),
        compiler_params=pltpu.CompilerParams(vmem_limit_bytes=VMEM_WHOLE),
        name=name,
    )(place, *arrays)


def absorb_kernel(place, chunk, total, cached, *refs):
    *_, total_out, held, rows, turned, sems = refs
    height = rows.shape[0]
    start = pl.multiple_of(place[0] * height, height)
    fetch = pltpu.make_async_copy(cached.at[pl.ds(start, height), :], rows, sems.at[0])
    fetch.start()
    turned[...] = chunk[...].T
    keep = pltpu.make_async_copy(turned, held.at[place[1]], sems.at[1])
    keep.start()
    fetch.wait()
    total_out[...] = total[...] + jnp.dot(
        chunk[...], rows[...], preferred_element_type=jnp.float32
    )
    keep.wait()


def absorb(chunk, index, cached, total, held, n_chunks):
    length, feats = chunk.shape
    cols = cached.shape[1]
    inside = (index >= 0) & (index < n_chunks)
    place = jnp.stack([jnp.clip(index, 0, n_chunks - 1), jnp.where(inside, index, n_chunks)])
    shape = jax.ShapeDtypeStruct((8 * n_chunks, feats, length), chunk.dtype)
    vmem, anywhere = pl.BlockSpec(memory_space=pltpu.VMEM), pl.BlockSpec(memory_space=pl.ANY)
    return pl.pallas_call(
        absorb_kernel,
        in_specs=[pl.BlockSpec(memory_space=pltpu.SMEM), vmem, vmem, anywhere]
        + ([] if held is None else [anywhere]),
        out_specs=[vmem, anywhere],
        out_shape=[jax.ShapeDtypeStruct(total.shape, jnp.float32), shape],
        scratch_shapes=[
            pltpu.VMEM((feats, cols), cached.dtype),
            pltpu.VMEM((feats, length), chunk.dtype),
            pltpu.SemaphoreType.DMA((2,)),
        ],
        input_output_aliases={} if held is None else {4: 1},
        cost_estimate=pl.CostEstimate(
            flops=2 * length * feats * cols,
            bytes_accessed=4 * length * feats + 2 * feats * cols,
            transcendentals=0,
        ),
        compiler_params=pltpu.CompilerParams(vmem_limit_bytes=VMEM_WHOLE),
        name="absorb",
    )(place, chunk, total, cached, *([] if held is None else [held]))


def attention_kernel(n_totals, *refs):
    totals, (allowed, queries_in, d_out_in) = refs[:n_totals], refs[n_totals : n_totals + 3]
    d_queries, d_projected, queries, d_out, sems = refs[n_totals + 3 :]
    copies = [
        pltpu.make_async_copy(queries_in, queries, sems.at[0]),
        pltpu.make_async_copy(d_out_in, d_out, sems.at[1]),
    ]
    for copy in copies:
        copy.start()
    projected = jnp.concatenate([total[...].astype(jnp.bfloat16) for total in totals], axis=0)
    kept = allowed[...] > 0
    for copy in copies:
        copy.wait()
    factor = 1.0 / math.sqrt(HD)
    across = (((1,), (1,)), ((), ()))
    heads = projected.shape[1] // (2 * HD)
    group = queries.shape[1] // HD // heads
    for head in range(heads):
        start = 2 * HD * head
        keys = projected[:, start : start + HD]
        values = projected[:, start + HD : start + 2 * HD]
        d_keys = jnp.zeros(keys.shape, jnp.float32)
        d_values = jnp.zeros(keys.shape, jnp.float32)
        for g in range(head * group, (head + 1) * group):
            columns = slice(g * HD, (g + 1) * HD)
            query, grad = queries[:, columns], d_out[:, columns]
            scores = (
                lax.dot_general(keys, query, across, preferred_element_type=jnp.float32) * factor
            )
            scores = jnp.where(kept, scores, -1e30)
            weights = jnp.exp(scores - jnp.max(scores, axis=0, keepdims=True))
            probs = weights / jnp.sum(weights, axis=0, keepdims=True)
            probs_low = probs.astype(jnp.bfloat16)
            d_probs = lax.dot_general(values, grad, across, preferred_element_type=jnp.float32)
            rowdot = jnp.sum(probs_low.astype(jnp.float32) * d_probs, axis=0, keepdims=True)
            d_scores = (probs * (d_probs - rowdot) * factor).astype(jnp.bfloat16)
            d_queries[:, columns] = lax.dot_general(
                d_scores, keys, (((0,), (0,)), ((), ())), preferred_element_type=jnp.float32
            ).astype(jnp.bfloat16)
            d_keys = d_keys + jnp.dot(d_scores, query, preferred_element_type=jnp.float32)
            d_values = d_values + jnp.dot(probs_low, grad, preferred_element_type=jnp.float32)
        d_projected[:, start : start + HD] = d_keys.astype(jnp.bfloat16)
        d_projected[:, start + HD : start + 2 * HD] = d_values.astype(jnp.bfloat16)


def attention_backward(totals, queries, d_out, allowed):
    length, cols = queries.shape[0], totals[0].shape[1]
    vmem, anywhere = pl.BlockSpec(memory_space=pltpu.VMEM), pl.BlockSpec(memory_space=pl.ANY)
    return pl.pallas_call(
        functools.partial(attention_kernel, len(totals)),
        in_specs=[vmem] * (len(totals) + 1) + [anywhere] * 2,
        out_specs=[vmem] * 2,
        out_shape=[
            jax.ShapeDtypeStruct(queries.shape, jnp.bfloat16),
            jax.ShapeDtypeStruct((length, cols), jnp.bfloat16),
        ],
        scratch_shapes=[
            pltpu.VMEM(queries.shape, queries.dtype),
            pltpu.VMEM(d_out.shape, d_out.dtype),
            pltpu.SemaphoreType.DMA((2,)),
        ],
        cost_estimate=pl.CostEstimate(
            flops=12 * allowed.size * queries.shape[1],
            bytes_accessed=8 * queries.size,
            transcendentals=allowed.size * queries.shape[1] // HD,
        ),
        compiler_params=pltpu.CompilerParams(vmem_limit_bytes=VMEM_STREAM),
        name="attention",
    )(*totals, allowed, queries, d_out)


SENT = ((0, 0, 0), (0, 1, 0), (1, 0, 1), (2, 1, 1))
KEPT = ((1, 1, 0), (2, 0, 0), (3, 0, 1), (3, 1, 1))


def weight_kernel(groups, place, held, d_projected, *refs):
    *refs, buffer, sems = refs
    joined = len(groups) > 1
    n_out = len(groups) if joined else 2
    added, outs = refs[:-n_out], refs[-n_out:]
    rows = buffer.shape[1]
    half = d_projected.shape[1] // 2
    start = pl.multiple_of(place[4] * rows, rows)
    chunks = sorted({chunk for group in groups for chunk, _, _ in group})
    copies = {}
    for chunk in chunks:
        copies[chunk] = pltpu.make_async_copy(
            held.at[place[chunk], pl.ds(start, rows), :], buffer.at[chunk], sems.at[chunk]
        )
        copies[chunk].start()
    for chunk in chunks:
        copies[chunk].wait()
        wanted = [
            (g, side, position)
            for g, group in enumerate(groups)
            for which, side, position in group
            if which == chunk
        ]
        first, last = min(w[1] for w in wanted), max(w[1] for w in wanted)
        total = jnp.dot(
            buffer[chunk],
            d_projected[:, first * half : (last + 1) * half],
            preferred_element_type=jnp.float32,
        )
        for g, side, position in wanted:
            part = total[:, (side - first) * half : (side - first + 1) * half]
            if added:
                part = part + added[0][2 * side + position].astype(jnp.float32)
            if joined:
                outs[g][2 * side + position] = part.astype(outs[g].dtype)
            else:
                outs[side][position] = part.astype(outs[side].dtype)


def weight_parts(held, d_projected, place, groups, added, dtype, name):
    length, cols = d_projected.shape
    rows = held.shape[1] // 2
    vmem = pl.BlockSpec(memory_space=pltpu.VMEM)
    depth = 4 if len(groups) > 1 else 2
    shape = jax.ShapeDtypeStruct((depth, rows, cols // 2), dtype)
    return pl.pallas_call(
        functools.partial(weight_kernel, groups),
        in_specs=[pl.BlockSpec(memory_space=pltpu.SMEM), pl.BlockSpec(memory_space=pl.ANY)]
        + [vmem] * (1 + len(added)),
        out_specs=[vmem] * 2,
        out_shape=[shape] * 2,
        scratch_shapes=[
            pltpu.VMEM((4, rows, length), held.dtype),
            pltpu.SemaphoreType.DMA((4,)),
        ],
        cost_estimate=pl.CostEstimate(
            flops=4 * length * rows * cols * len(groups),
            bytes_accessed=8 * rows * cols * len(groups),
            transcendentals=0,
        ),
        compiler_params=pltpu.CompilerParams(vmem_limit_bytes=VMEM_WHOLE),
        name=name,
    )(place, held, d_projected, *added)


def combine_kernel(place, keep_a, got_a, keep_b, got_b, out_a, out_b):
    for keep, got, out in ((keep_a, got_a, out_a), (keep_b, got_b, out_b)):
        out[...] = (keep[0] + got[0].astype(jnp.float32)).astype(out.dtype)


def finish_kernel(place, keep_a, got_a, keep_b, got_b, last_a, last_b, out):
    half = last_a.shape[1]
    sides = ((keep_a, got_a, last_a), (keep_b, got_b, last_b))
    for side, (keep, got, last) in enumerate(sides):
        total = keep[1] + got[1].astype(jnp.float32) + last[...].astype(jnp.float32)
        out[:, side * half : (side + 1) * half] = total


def plane():
    index = lax.axis_index("dp").astype(jnp.int32)

    def swap(value, bit):
        return lax.ppermute(value, "dp", [(i, i ^ bit) for i in range(8)])

    return index % 2, (index // 2) % 2, index // 4, swap


def weight_sum(held, d_projected, pieces, beside):
    core, x, y, swap = plane()
    rows, cols = held.shape[1] // 2, d_projected.shape[1]
    none = jnp.zeros((1,), jnp.int32)
    chunks = [3 - x - 2 * y, 1 - x + 2 * y, x + 2 - 2 * y, x + 2 * y]

    def parts(which, groups, added, dtype, name):
        place = jnp.stack(chunks + [which])
        return weight_parts(held, d_projected, place, groups, added, dtype, name)

    sent, kept = parts(1 - core, (SENT, KEPT), [], jnp.bfloat16, "weight_other")
    sent, kept = swap(sent, 1), swap(kept, 1)
    sent, pieces[1] = lax.optimization_barrier((sent, pieces[1]))
    send_a, send_b = parts(core, (SENT,), [sent], jnp.bfloat16, "weight_send")
    got_a, got_b = swap(send_a, 2), swap(send_b, 4)
    keep_a, keep_b = parts(core, (KEPT,), [kept], jnp.float32, "weight_keep")
    got_a, got_b, pieces, beside = lax.optimization_barrier((got_a, got_b, pieces, beside))

    small = jax.ShapeDtypeStruct((rows, cols // 2), jnp.bfloat16)
    arrays = [keep_a, got_a, keep_b, got_b]
    last_a, last_b = on_chip(
        combine_kernel, none, arrays, [small] * 2, cols * rows, "weight_combine"
    )
    last = [swap(last_a, 4), swap(last_b, 2)]

    def finish(ready):
        ended, ready = lax.optimization_barrier((last, ready))
        (total,) = on_chip(
            finish_kernel,
            none,
            arrays + ended,
            [jax.ShapeDtypeStruct((rows, cols), jnp.float32)],
            2 * cols * rows,
            "weight_finish",
        )
        return total, ready

    return finish, pieces, beside


class PlaneGather:
    def __init__(self, own):
        self.got = {0: own}

    def first(self):
        own, swap = self.got[0], plane()[3]
        self.got.update({bit: swap(own, bit) for bit in (2, 4, 1)})
        return self.got

    def second(self):
        got, swap, half = self.got, plane()[3], self.got[0].shape[0] // 2
        self.far = [swap(got[4][:half], 2), swap(got[2][half:], 4)]
        got[3], got[5] = swap(got[2], 1), swap(got[4], 1)
        return self.far, got[3], got[5]

    def third(self):
        swap = plane()[3]
        self.far_other = [swap(value, 1) for value in self.far]
        return self.far_other

    def where(self, bits):
        return lax.axis_index("dp").astype(jnp.int32) ^ jnp.array(bits, dtype=jnp.int32)

    def lay(self, height, rows):
        arrays = [self.got[k] for k in range(6)]
        return place_rows(arrays, self.where(list(range(6))), height, rows, [])

    def lay_far(self, height, laid):
        arrays = [self.far[0], self.far_other[0]]
        return place_rows(arrays, self.where([6, 7]), height, laid.shape[0], [laid])

    def last(self):
        arrays = [self.got[k] for k in range(6)] + [self.far[1], self.far_other[1]]
        return arrays, self.where(list(range(8)))


def place_rows_kernel(height, n_arrays, place, *refs):
    arrays, (out, sems) = refs[:n_arrays], refs[-2:]
    copies = []
    for k, array in enumerate(arrays):
        start = pl.multiple_of(place[k] * height, height)
        copies.append(
            pltpu.make_async_copy(
                array.at[pl.ds(0, height), :], out.at[pl.ds(start, height), :], sems.at[k]
            )
        )
    for copy in copies:
        copy.start()
    for copy in copies:
        copy.wait()


def place_rows(arrays, place, height, rows, into):
    cols = arrays[0].shape[1]
    anywhere = pl.BlockSpec(memory_space=pl.ANY)
    return pl.pallas_call(
        functools.partial(place_rows_kernel, height, len(arrays)),
        in_specs=[pl.BlockSpec(memory_space=pltpu.SMEM)]
        + [pl.BlockSpec(memory_space=pltpu.VMEM)] * len(arrays)
        + [anywhere] * len(into),
        out_specs=anywhere,
        out_shape=jax.ShapeDtypeStruct((rows, cols), arrays[0].dtype),
        scratch_shapes=[pltpu.SemaphoreType.DMA((len(arrays),))],
        input_output_aliases={1 + len(arrays): 0} if into else {},
        cost_estimate=pl.CostEstimate(
            flops=0, bytes_accessed=4 * height * cols * len(arrays), transcendentals=0
        ),
        compiler_params=pltpu.CompilerParams(vmem_limit_bytes=VMEM_WHOLE),
        name="place_rows",
    )(place, *arrays, *into)


def input_kernel(n_blocks, place, *refs):
    *arrays, out = refs
    pieces, rows = arrays[:n_blocks], arrays[n_blocks:]
    share = out.shape[1] // len(rows)
    for k, held in enumerate(rows):
        first = held.shape[0] - n_blocks * share
        total = jnp.zeros((out.shape[0], share), jnp.float32)
        for s, piece in enumerate(pieces):
            total = total + lax.dot_general(
                piece[...],
                held[first + s * share : first + (s + 1) * share, :],
                (((1,), (1,)), ((), ())),
                preferred_element_type=jnp.float32,
            )
        start = pl.multiple_of(place[k] * share, share)
        out[:, pl.ds(start, share)] = total.astype(out.dtype)


def input_gradient(pieces, arrays, place, feats):
    length, cols = pieces[0].shape
    (d_tokens,) = on_chip(
        functools.partial(input_kernel, len(pieces)),
        place,
        pieces + arrays,
        [jax.ShapeDtypeStruct((length, feats), jnp.bfloat16)],
        2 * length * feats * cols * len(pieces),
        "input_gradient",
    )
    return d_tokens


def make_body(n_dp, n_z):
    tuned = n_dp == 8 and n_z == 4

    def pair(value, s):
        return lax.ppermute(value, "tensor", [(z, z ^ s) for z in range(n_z)])

    def body(tokens, queries, d_out, segments, cached, master, moment, second, grad):
        me_dp = lax.axis_index("dp").astype(jnp.int32)
        me_z = lax.axis_index("tensor").astype(jnp.int32)
        length, feats = tokens.shape
        cols = cached.shape[1]

        master_new, moment_new, second_new, own_cache = optimizer(
            cached, master, moment, second, grad
        )

        share = feats // n_dp

        def block_for(z):
            return lax.dynamic_slice_in_dim(cached, z * feats + me_dp * share, share, 0)

        blocks = [block_for(me_z)] + [pair(block_for(me_z ^ s), s) for s in range(1, n_z)]

        total = jnp.zeros((length, cols), jnp.float32)
        total, held = absorb(tokens, me_z, cached, total, None, n_z)
        if tuned:
            gather = PlaneGather(jnp.concatenate([own_cache] + blocks, axis=0))
        from_low, from_high, merged = tokens, tokens, None
        for s in range(1, n_z):
            up = [(z, z + 1) for z in range(s - 1, n_z - 1)]
            down = [(z + 1, z) for z in range(n_z - s)]
            low, high = me_z - s, me_z + s
            if merged is None:
                from_low = lax.ppermute(from_low, "tensor", up)
                from_high = lax.ppermute(from_high, "tensor", down)
                arrived = from_low, from_high
            else:
                merged = lax.ppermute(merged, "tensor", up + down)
                arrived = merged
            if tuned:
                if s == 1:
                    rounds = gather.got
                elif s == 2:
                    rounds = gather.first()
                elif s == 3:
                    rounds = gather.second()
                    laid = gather.lay(own_cache.shape[0], cached.shape[0])
                    rounds = (rounds, laid)
                arrived, held, rounds = lax.optimization_barrier((arrived, held, rounds))
                if s < 3:
                    gather.got = rounds
                else:
                    (gather.far, gather.got[3], gather.got[5]), laid = rounds
            if merged is None:
                from_low, from_high = arrived
            else:
                merged = arrived
            if merged is None and 2 * s >= n_z:
                merged = jnp.where(me_z >= s, from_low, from_high)
            if merged is None:
                total, held = absorb(from_low, low, cached, total, held, n_z)
                total, held = absorb(from_high, high, cached, total, held, n_z)
            else:
                total, held = absorb(
                    merged, jnp.where(me_z >= s, low, high), cached, total, held, n_z
                )

        doc_ids = segments[0]
        position = jnp.arange(length)
        allowed = (doc_ids[:, None] == doc_ids[None, :]) & (position[:, None] <= position[None, :])
        allowed = allowed.astype(jnp.float32)

        d_queries, d_projected = attention_backward([total], queries, d_out, allowed)

        pieces = [d_projected]
        s = 1
        while s < n_z:
            pieces = pieces + [pair(piece, s) for piece in pieces]
            s *= 2
        if tuned:
            d_projected, gather.far_other = lax.optimization_barrier((d_projected, gather.third()))
            pieces[0] = d_projected
            new_cache = gather.lay_far(own_cache.shape[0], laid)
            finish, pieces, new_cache = weight_sum(held, d_projected, pieces, new_cache)
            new_grad, d_tokens = finish(input_gradient(pieces, *gather.last(), feats))
        else:
            new_cache = lax.all_gather(own_cache, "dp", axis=0, tiled=True)
            rows = lax.all_gather(jnp.stack(blocks), "dp", axis=0)
            d_tokens = jnp.einsum(
                "slc,ksfc->lkf", jnp.stack(pieces), rows, preferred_element_type=jnp.float32
            )
            d_tokens = d_tokens.astype(jnp.bfloat16).reshape(length, feats)
            partial = lax.dot_general(
                held[:n_z].reshape(n_z * feats, length),
                d_projected,
                (((1,), (0,)), ((), ())),
                preferred_element_type=jnp.float32,
            )
            new_grad = lax.psum_scatter(
                partial.astype(jnp.bfloat16), "dp", scatter_dimension=0, tiled=True
            ).astype(jnp.float32)
        return (master_new, moment_new, second_new, new_cache, new_grad, d_queries, d_tokens)

    return body


def solution(mesh):
    in_specs = (
        P("dp", "tensor"),
        P("dp", "tensor"),
        P("dp", "tensor"),
        P("dp", None),
        P(None, "tensor"),
        P("dp", "tensor"),
        P("dp", "tensor"),
        P("dp", "tensor"),
        P("dp", "tensor"),
    )
    out_specs = (
        P("dp", "tensor"),
        P("dp", "tensor"),
        P("dp", "tensor"),
        P(None, "tensor"),
        P("dp", "tensor"),
        P("dp", "tensor"),
        P("dp", "tensor"),
    )
    body = make_body(mesh.shape["dp"], mesh.shape["tensor"])
    return jax.shard_map(body, mesh=mesh, in_specs=in_specs, out_specs=out_specs, check_vma=False)
```

```python
import functools
import math

import jax
import jax.numpy as jnp
from jax import lax
from jax.experimental import pallas as pl
from jax.experimental.pallas import tpu as pltpu
from jax.sharding import PartitionSpec as P

HD = 128
VMEM_STREAM = 60 * 1024 * 1024
VMEM_WHOLE = 24 * 1024 * 1024


beta_first = 0.9
beta_second = 0.95
learn_rate = 0.0003
weight_decay = 0.1
adam_epsilon = 1e-08
first_fix = 1.0 - 0.9**40
second_fix = 1.0 - 0.95**40


def optimizer_kernel(
    place, cached, master, moment, second, grad, master_out, moment_out, second_out, cache_out
):
    moment_new = beta_first * moment[...] + (1.0 - beta_first) * grad[...]
    second_new = beta_second * second[...] + (1.0 - beta_second) * grad[...] * grad[...]
    update = moment_new / first_fix / (jnp.sqrt(second_new / second_fix) + adam_epsilon)
    master_new = master[...] - learn_rate * (update + weight_decay * master[...])
    moment_out[...] = moment_new
    second_out[...] = second_new
    master_out[...] = master_new
    for start in range(0, cached.shape[1], HD):
        block = slice(start, start + HD)
        own_cache = cached[:, block].astype(jnp.float32)
        delta = master_new[:, block] - own_cache
        largest = jnp.max(jnp.abs(delta), axis=1, keepdims=True)
        scale = (largest + 1e-06).astype(jnp.bfloat16).astype(jnp.float32)
        codes = (delta / scale).astype(jnp.bfloat16)
        cache_out[:, block] = (own_cache + codes.astype(jnp.float32) * scale).astype(jnp.bfloat16)


def optimizer(cached, master, moment, second, grad):
    rows, cols = master.shape
    step = min(rows, 256)
    steps = rows // step
    own = pl.BlockSpec((step, cols), lambda i, place: (i, 0))
    full = jax.ShapeDtypeStruct((rows, cols), jnp.float32)
    return pl.pallas_call(
        optimizer_kernel,
        grid_spec=pltpu.PrefetchScalarGridSpec(
            num_scalar_prefetch=1,
            grid=(steps,),
            in_specs=[pl.BlockSpec((step, cols), lambda i, place: (place[0] * steps + i, 0))]
            + [own] * 4,
            out_specs=[own] * 4,
        ),
        out_shape=[full, full, full, jax.ShapeDtypeStruct((rows, cols), jnp.bfloat16)],
        cost_estimate=pl.CostEstimate(
            flops=40 * rows * cols, bytes_accessed=32 * rows * cols, transcendentals=rows * cols
        ),
        compiler_params=pltpu.CompilerParams(vmem_limit_bytes=VMEM_STREAM),
        name="optimizer",
    )(lax.axis_index("dp").astype(jnp.int32).reshape(1), cached, master, moment, second, grad)


def on_chip(kernel, place, arrays, out_shape, flops, name):
    vmem = pl.BlockSpec(memory_space=pltpu.VMEM)
    size = sum(a.size * a.dtype.itemsize for a in arrays)
    size += sum(s.size * s.dtype.itemsize for s in out_shape)
    return pl.pallas_call(
        kernel,
        in_specs=[pl.BlockSpec(memory_space=pltpu.SMEM)] + [vmem] * len(arrays),
        out_specs=[vmem] * len(out_shape),
        out_shape=out_shape,
        cost_estimate=pl.CostEstimate(flops=flops, bytes_accessed=size, transcendentals=0),
        compiler_params=pltpu.CompilerParams(vmem_limit_bytes=VMEM_WHOLE),
        name=name,
    )(place, *arrays)


def fetch_chunk(place, chunks, chunk, sem):
    for n, source in enumerate(chunks):

        @pl.when(place[2] == n)
        def _():
            pltpu.make_async_copy(source, chunk, sem).start()

    return pltpu.make_async_copy(chunks[0], chunk, sem)


def fetch_rows(place, cached, rows, sem):
    height = rows.shape[0]
    start = pl.multiple_of(place[0] * height, height)
    copy = pltpu.make_async_copy(cached.at[pl.ds(start, height), :], rows, sem)
    copy.start()
    return copy


def absorb_kernel(n_chunks, place, *refs):
    chunks, (total, cached) = refs[:n_chunks], refs[n_chunks : n_chunks + 2]
    total_out, held, chunk, rows, turned, sems = refs[-6:]
    chunk_copy = fetch_chunk(place, chunks, chunk, sems.at[0])
    rows_copy = fetch_rows(place, cached, rows, sems.at[1])
    chunk_copy.wait()
    turned[...] = chunk[...].T
    keep = pltpu.make_async_copy(turned, held.at[place[1]], sems.at[2])
    keep.start()
    rows_copy.wait()
    total_out[...] = total[...] + jnp.dot(
        chunk[...], rows[...], preferred_element_type=jnp.float32
    )
    keep.wait()


def absorb_place(index, which, n_chunks):
    inside = (index >= 0) & (index < n_chunks)
    return jnp.stack(
        [jnp.clip(index, 0, n_chunks - 1), jnp.where(inside, index, n_chunks), which]
    ).astype(jnp.int32)


def absorb_scratch(chunk, cached, n_sems):
    length, feats = chunk.shape
    return [
        pltpu.VMEM((length, feats), chunk.dtype),
        pltpu.VMEM((feats, cached.shape[1]), cached.dtype),
        pltpu.VMEM((feats, length), chunk.dtype),
        pltpu.SemaphoreType.DMA((n_sems,)),
    ]


def absorb(chunks, which, index, cached, total, held, n_chunks):
    length, feats = chunks[0].shape
    cols = cached.shape[1]
    shape = jax.ShapeDtypeStruct((8 * n_chunks, feats, length), chunks[0].dtype)
    vmem, anywhere = pl.BlockSpec(memory_space=pltpu.VMEM), pl.BlockSpec(memory_space=pl.ANY)
    return pl.pallas_call(
        functools.partial(absorb_kernel, len(chunks)),
        in_specs=[pl.BlockSpec(memory_space=pltpu.SMEM)]
        + [anywhere] * len(chunks)
        + [vmem, anywhere]
        + ([] if held is None else [anywhere]),
        out_specs=[vmem, anywhere],
        out_shape=[jax.ShapeDtypeStruct(total.shape, jnp.float32), shape],
        scratch_shapes=absorb_scratch(chunks[0], cached, 3),
        input_output_aliases={} if held is None else {3 + len(chunks): 1},
        cost_estimate=pl.CostEstimate(
            flops=2 * length * feats * cols,
            bytes_accessed=4 * length * feats + 2 * feats * cols,
            transcendentals=0,
        ),
        compiler_params=pltpu.CompilerParams(vmem_limit_bytes=VMEM_STREAM),
        name="absorb",
    )(
        absorb_place(index, which, n_chunks),
        *chunks,
        total,
        cached,
        *([] if held is None else [held]),
    )


def attend_kernel(n_chunks, place, *refs):
    chunks, refs = refs[:n_chunks], refs[n_chunks:]
    total, cached, _, allowed, queries_in, d_out_in = refs[:6]
    held, d_queries, d_projected, chunk, rows, turned, sems, queries, d_out = refs[6:]
    chunk_copy = fetch_chunk(place, chunks, chunk, sems.at[0])
    rows_copy = fetch_rows(place, cached, rows, sems.at[1])
    others = [
        pltpu.make_async_copy(queries_in, queries, sems.at[3]),
        pltpu.make_async_copy(d_out_in, d_out, sems.at[4]),
    ]
    for copy in others:
        copy.start()
    chunk_copy.wait()
    turned[...] = chunk[...].T
    keep = pltpu.make_async_copy(turned, held.at[place[1]], sems.at[2])
    keep.start()
    rows_copy.wait()
    projected = (
        total[...] + jnp.dot(chunk[...], rows[...], preferred_element_type=jnp.float32)
    ).astype(jnp.bfloat16)
    kept = allowed[...] > 0
    for copy in others:
        copy.wait()
    factor = 1.0 / math.sqrt(HD)
    across = (((1,), (1,)), ((), ()))
    heads = projected.shape[1] // (2 * HD)
    group = queries.shape[1] // HD // heads
    for head in range(heads):
        start = 2 * HD * head
        keys = projected[:, start : start + HD]
        values = projected[:, start + HD : start + 2 * HD]
        d_keys = jnp.zeros(keys.shape, jnp.float32)
        d_values = jnp.zeros(keys.shape, jnp.float32)
        for g in range(head * group, (head + 1) * group):
            columns = slice(g * HD, (g + 1) * HD)
            query, grad = queries[:, columns], d_out[:, columns]
            scores = (
                lax.dot_general(keys, query, across, preferred_element_type=jnp.float32) * factor
            )
            scores = jnp.where(kept, scores, -1e30)
            weights = jnp.exp(scores - jnp.max(scores, axis=0, keepdims=True))
            probs = weights / jnp.sum(weights, axis=0, keepdims=True)
            probs_low = probs.astype(jnp.bfloat16)
            d_probs = lax.dot_general(values, grad, across, preferred_element_type=jnp.float32)
            rowdot = jnp.sum(probs_low.astype(jnp.float32) * d_probs, axis=0, keepdims=True)
            d_scores = (probs * (d_probs - rowdot) * factor).astype(jnp.bfloat16)
            d_queries[:, columns] = lax.dot_general(
                d_scores, keys, (((0,), (0,)), ((), ())), preferred_element_type=jnp.float32
            ).astype(jnp.bfloat16)
            d_keys = d_keys + jnp.dot(d_scores, query, preferred_element_type=jnp.float32)
            d_values = d_values + jnp.dot(probs_low, grad, preferred_element_type=jnp.float32)
        d_projected[:, start : start + HD] = d_keys.astype(jnp.bfloat16)
        d_projected[:, start + HD : start + 2 * HD] = d_values.astype(jnp.bfloat16)
    keep.wait()


def attend(chunks, which, index, cached, total, held, queries, d_out, allowed, n_chunks):
    vmem, anywhere = pl.BlockSpec(memory_space=pltpu.VMEM), pl.BlockSpec(memory_space=pl.ANY)
    return pl.pallas_call(
        functools.partial(attend_kernel, len(chunks)),
        in_specs=[pl.BlockSpec(memory_space=pltpu.SMEM)]
        + [anywhere] * len(chunks)
        + [vmem, anywhere, anywhere, vmem, anywhere, anywhere],
        out_specs=[anywhere, vmem, vmem],
        out_shape=[
            jax.ShapeDtypeStruct(held.shape, held.dtype),
            jax.ShapeDtypeStruct(queries.shape, jnp.bfloat16),
            jax.ShapeDtypeStruct(total.shape, jnp.bfloat16),
        ],
        scratch_shapes=absorb_scratch(chunks[0], cached, 5)
        + [pltpu.VMEM(queries.shape, queries.dtype), pltpu.VMEM(d_out.shape, d_out.dtype)],
        input_output_aliases={3 + len(chunks): 0},
        cost_estimate=pl.CostEstimate(
            flops=12 * allowed.size * queries.shape[1],
            bytes_accessed=8 * queries.size,
            transcendentals=allowed.size * queries.shape[1] // HD,
        ),
        compiler_params=pltpu.CompilerParams(vmem_limit_bytes=VMEM_STREAM),
        name="attend",
    )(
        absorb_place(index, which, n_chunks),
        *chunks,
        total,
        cached,
        held,
        allowed,
        queries,
        d_out,
    )


SENT = ((0, 0, 0), (0, 1, 0), (1, 0, 1), (2, 1, 1))
KEPT = ((1, 1, 0), (2, 0, 0), (3, 0, 1), (3, 1, 1))


def weight_kernel(groups, place, held, d_projected, *refs):
    *refs, buffer, sems = refs
    joined = len(groups) > 1
    n_out = len(groups) if joined else 2
    added, outs = refs[:-n_out], refs[-n_out:]
    rows = buffer.shape[1]
    half = d_projected.shape[1] // 2
    block = min(rows, 256)
    start = pl.multiple_of(place[4] * rows, rows)
    chunks = sorted({chunk for group in groups for chunk, _, _ in group})
    copies = {}
    for chunk in chunks:
        copies[chunk] = pltpu.make_async_copy(
            held.at[place[chunk], pl.ds(start, rows), :], buffer.at[chunk], sems.at[chunk]
        )
        copies[chunk].start()
    for chunk in chunks:
        copies[chunk].wait()
        wanted = [
            (g, side, position)
            for g, group in enumerate(groups)
            for which, side, position in group
            if which == chunk
        ]
        first, last = min(w[1] for w in wanted), max(w[1] for w in wanted)
        for r in range(0, rows, block):
            here = slice(r, r + block)
            total = jnp.dot(
                buffer[chunk, here, :],
                d_projected[:, first * half : (last + 1) * half],
                preferred_element_type=jnp.float32,
            )
            for g, side, position in wanted:
                part = total[:, (side - first) * half : (side - first + 1) * half]
                if added:
                    part = part + added[0][2 * side + position, here, :].astype(jnp.float32)
                if joined:
                    outs[g][2 * side + position, here, :] = part.astype(outs[g].dtype)
                else:
                    outs[side][position, here, :] = part.astype(outs[side].dtype)


def weight_parts(held, d_projected, place, groups, added, dtype, name):
    length, cols = d_projected.shape
    rows = held.shape[1] // 2
    vmem = pl.BlockSpec(memory_space=pltpu.VMEM)
    depth = 4 if len(groups) > 1 else 2
    shape = jax.ShapeDtypeStruct((depth, rows, cols // 2), dtype)
    return pl.pallas_call(
        functools.partial(weight_kernel, groups),
        in_specs=[pl.BlockSpec(memory_space=pltpu.SMEM), pl.BlockSpec(memory_space=pl.ANY)]
        + [vmem] * (1 + len(added)),
        out_specs=[vmem] * 2,
        out_shape=[shape] * 2,
        scratch_shapes=[
            pltpu.VMEM((4, rows, length), held.dtype),
            pltpu.SemaphoreType.DMA((4,)),
        ],
        cost_estimate=pl.CostEstimate(
            flops=4 * length * rows * cols * len(groups),
            bytes_accessed=8 * rows * cols * len(groups),
            transcendentals=0,
        ),
        compiler_params=pltpu.CompilerParams(vmem_limit_bytes=VMEM_WHOLE),
        name=name,
    )(place, held, d_projected, *added)


def combine_kernel(place, keep_a, got_a, keep_b, got_b, out_a, out_b):
    for keep, got, out in ((keep_a, got_a, out_a), (keep_b, got_b, out_b)):
        out[...] = (keep[0] + got[0].astype(jnp.float32)).astype(out.dtype)


def finish_kernel(place, keep_a, got_a, keep_b, got_b, last_a, last_b, out):
    half = last_a.shape[1]
    sides = ((keep_a, got_a, last_a), (keep_b, got_b, last_b))
    for side, (keep, got, last) in enumerate(sides):
        total = keep[1] + got[1].astype(jnp.float32) + last[...].astype(jnp.float32)
        out[:, side * half : (side + 1) * half] = total


def plane():
    index = lax.axis_index("dp").astype(jnp.int32)

    def swap(value, bit):
        return lax.ppermute(value, "dp", [(i, i ^ bit) for i in range(8)])

    return index % 2, (index // 2) % 2, index // 4, swap


def weight_sum(held, d_projected, pieces, beside):
    core, x, y, swap = plane()
    rows, cols = held.shape[1] // 2, d_projected.shape[1]
    none = jnp.zeros((1,), jnp.int32)
    chunks = [3 - x - 2 * y, 1 - x + 2 * y, x + 2 - 2 * y, x + 2 * y]

    def parts(which, groups, added, dtype, name):
        place = jnp.stack(chunks + [which])
        return weight_parts(held, d_projected, place, groups, added, dtype, name)

    sent, kept = parts(1 - core, (SENT, KEPT), [], jnp.bfloat16, "weight_other")
    sent, kept = swap(sent, 1), swap(kept, 1)
    sent, beside = lax.optimization_barrier((sent, beside))
    send_a, send_b = parts(core, (SENT,), [sent], jnp.bfloat16, "weight_send")
    got_a, got_b = swap(send_a, 2), swap(send_b, 4)
    keep_a, keep_b = parts(core, (KEPT,), [kept], jnp.float32, "weight_keep")
    got_a, got_b, pieces = lax.optimization_barrier((got_a, got_b, pieces))

    small = jax.ShapeDtypeStruct((rows, cols // 2), jnp.bfloat16)
    arrays = [keep_a, got_a, keep_b, got_b]
    last_a, last_b = on_chip(
        combine_kernel, none, arrays, [small] * 2, cols * rows, "weight_combine"
    )
    last = [swap(last_a, 4), swap(last_b, 2)]

    def finish(ready):
        ended, ready = lax.optimization_barrier((last, ready))
        (total,) = on_chip(
            finish_kernel,
            none,
            arrays + ended,
            [jax.ShapeDtypeStruct((rows, cols), jnp.float32)],
            2 * cols * rows,
            "weight_finish",
        )
        return total, ready

    return finish, pieces, beside


class PlaneGather:
    def __init__(self, own):
        self.got = {0: own}

    def first(self):
        own, swap = self.got[0], plane()[3]
        self.got.update({bit: swap(own, bit) for bit in (2, 4, 1)})
        return self.got

    def second(self):
        got, swap, half = self.got, plane()[3], self.got[0].shape[0] // 2
        self.far = [swap(got[4][:half], 2), swap(got[2][half:], 4)]
        got[3], got[5] = swap(got[2], 1), swap(got[4], 1)
        return self.far, got[3], got[5]

    def third(self):
        swap = plane()[3]
        self.far_other = [swap(value, 1) for value in self.far]
        return self.far_other

    def where(self, bits):
        return lax.axis_index("dp").astype(jnp.int32) ^ jnp.array(bits, dtype=jnp.int32)

    def lay(self, height, rows):
        arrays = [self.got[k] for k in range(6)]
        return place_rows(arrays, self.where(list(range(6))), height, rows, [])

    def lay_far(self, height, laid):
        arrays = [self.far[0], self.far_other[0]]
        return place_rows(arrays, self.where([6, 7]), height, laid.shape[0], [laid])

    def last(self):
        arrays = [self.got[k] for k in range(6)] + [self.far[1], self.far_other[1]]
        return arrays, self.where(list(range(8)))


def place_rows_kernel(height, n_arrays, place, *refs):
    arrays, (out, sems) = refs[:n_arrays], refs[-2:]
    copies = []
    for k, array in enumerate(arrays):
        start = pl.multiple_of(place[k] * height, height)
        copies.append(
            pltpu.make_async_copy(
                array.at[pl.ds(0, height), :], out.at[pl.ds(start, height), :], sems.at[k]
            )
        )
    for copy in copies:
        copy.start()
    for copy in copies:
        copy.wait()


def place_rows(arrays, place, height, rows, into):
    cols = arrays[0].shape[1]
    anywhere = pl.BlockSpec(memory_space=pl.ANY)
    return pl.pallas_call(
        functools.partial(place_rows_kernel, height, len(arrays)),
        in_specs=[pl.BlockSpec(memory_space=pltpu.SMEM)]
        + [pl.BlockSpec(memory_space=pltpu.VMEM)] * len(arrays)
        + [anywhere] * len(into),
        out_specs=anywhere,
        out_shape=jax.ShapeDtypeStruct((rows, cols), arrays[0].dtype),
        scratch_shapes=[pltpu.SemaphoreType.DMA((len(arrays),))],
        input_output_aliases={1 + len(arrays): 0} if into else {},
        cost_estimate=pl.CostEstimate(
            flops=0, bytes_accessed=4 * height * cols * len(arrays), transcendentals=0
        ),
        compiler_params=pltpu.CompilerParams(vmem_limit_bytes=VMEM_WHOLE),
        name="place_rows",
    )(place, *arrays, *into)


def input_kernel(n_blocks, place, *refs):
    *arrays, out = refs
    pieces, rows = arrays[:n_blocks], arrays[n_blocks:]
    share = out.shape[1] // len(rows)
    for k, held in enumerate(rows):
        first = held.shape[0] - n_blocks * share
        total = jnp.zeros((out.shape[0], share), jnp.float32)
        for s, piece in enumerate(pieces):
            total = total + lax.dot_general(
                piece[...],
                held[first + s * share : first + (s + 1) * share, :],
                (((1,), (1,)), ((), ())),
                preferred_element_type=jnp.float32,
            )
        start = pl.multiple_of(place[k] * share, share)
        out[:, pl.ds(start, share)] = total.astype(out.dtype)


def input_gradient(pieces, arrays, place, feats):
    length, cols = pieces[0].shape
    (d_tokens,) = on_chip(
        functools.partial(input_kernel, len(pieces)),
        place,
        pieces + arrays,
        [jax.ShapeDtypeStruct((length, feats), jnp.bfloat16)],
        2 * length * feats * cols * len(pieces),
        "input_gradient",
    )
    return d_tokens


def make_body(n_dp, n_z):
    tuned = n_dp == 8 and n_z == 4

    def pair(value, s):
        return lax.ppermute(value, "tensor", [(z, z ^ s) for z in range(n_z)])

    def body(tokens, queries, d_out, segments, cached, master, moment, second, grad):
        me_dp = lax.axis_index("dp").astype(jnp.int32)
        me_z = lax.axis_index("tensor").astype(jnp.int32)
        length, feats = tokens.shape
        cols = cached.shape[1]

        master_new, moment_new, second_new, own_cache = optimizer(
            cached, master, moment, second, grad
        )

        share = feats // n_dp

        def block_for(z):
            return lax.dynamic_slice_in_dim(cached, z * feats + me_dp * share, share, 0)

        blocks = [block_for(me_z)] + [pair(block_for(me_z ^ s), s) for s in range(1, n_z)]

        doc_ids = segments[0]
        position = jnp.arange(length)
        allowed = (doc_ids[:, None] == doc_ids[None, :]) & (position[:, None] <= position[None, :])
        allowed = allowed.astype(jnp.float32)

        total = jnp.zeros((length, cols), jnp.float32)
        zero = 0 * me_z
        total, held = absorb([tokens], zero, me_z, cached, total, None, n_z)
        if tuned:
            gather = PlaneGather(jnp.concatenate([own_cache] + blocks, axis=0))
        from_low, from_high = tokens, tokens
        for s in range(1, n_z):
            low, high = me_z - s, me_z + s
            from_low = lax.ppermute(
                from_low, "tensor", [(z, z + 1) for z in range(s - 1, n_z - 1)]
            )
            from_high = lax.ppermute(from_high, "tensor", [(z + 1, z) for z in range(n_z - s)])
            if tuned:
                if s == 1:
                    rounds, allowed = lax.optimization_barrier((gather.got, allowed))
                elif s == 2:
                    rounds = gather.first()
                else:
                    rounds = gather.second()
                    laid = gather.lay(own_cache.shape[0], cached.shape[0])
                    rounds = (rounds, laid)
                from_low, from_high, held, rounds = lax.optimization_barrier(
                    (from_low, from_high, held, rounds)
                )
                if s < 3:
                    gather.got = rounds
                else:
                    (gather.far, gather.got[3], gather.got[5]), laid = rounds
            chunks, which = [from_low, from_high], (me_z < s).astype(jnp.int32)
            index = jnp.where(me_z < s, high, low)
            if 2 * s < n_z:
                total, held = absorb([from_low], zero, low, cached, total, held, n_z)
                chunks, which, index = [from_high], zero, high
            if s < n_z - 1:
                total, held = absorb(chunks, which, index, cached, total, held, n_z)

        held, d_queries, d_projected = attend(
            chunks, which, index, cached, total, held, queries, d_out, allowed, n_z
        )

        pieces = [d_projected] + [pair(d_projected, s) for s in range(1, n_z)]
        if tuned:
            d_projected, gather.far_other = lax.optimization_barrier((d_projected, gather.third()))
            pieces[0] = d_projected
            new_cache = gather.lay_far(own_cache.shape[0], laid)
            finish, pieces, new_cache = weight_sum(held, d_projected, pieces, new_cache)
            new_grad, d_tokens = finish(input_gradient(pieces, *gather.last(), feats))
        else:
            new_cache = lax.all_gather(own_cache, "dp", axis=0, tiled=True)
            rows = lax.all_gather(jnp.stack(blocks), "dp", axis=0)
            d_tokens = jnp.einsum(
                "slc,ksfc->lkf", jnp.stack(pieces), rows, preferred_element_type=jnp.float32
            )
            d_tokens = d_tokens.astype(jnp.bfloat16).reshape(length, feats)
            partial = lax.dot_general(
                held[:n_z].reshape(n_z * feats, length),
                d_projected,
                (((1,), (0,)), ((), ())),
                preferred_element_type=jnp.float32,
            )
            new_grad = lax.psum_scatter(
                partial.astype(jnp.bfloat16), "dp", scatter_dimension=0, tiled=True
            ).astype(jnp.float32)
        return (master_new, moment_new, second_new, new_cache, new_grad, d_queries, d_tokens)

    return body


def solution(mesh):
    in_specs = (
        P("dp", "tensor"),
        P("dp", "tensor"),
        P("dp", "tensor"),
        P("dp", None),
        P(None, "tensor"),
        P("dp", "tensor"),
        P("dp", "tensor"),
        P("dp", "tensor"),
        P("dp", "tensor"),
    )
    out_specs = (
        P("dp", "tensor"),
        P("dp", "tensor"),
        P("dp", "tensor"),
        P(None, "tensor"),
        P("dp", "tensor"),
        P("dp", "tensor"),
        P("dp", "tensor"),
    )
    body = make_body(mesh.shape["dp"], mesh.shape["tensor"])
    return jax.shard_map(body, mesh=mesh, in_specs=in_specs, out_specs=out_specs, check_vma=False)
```

```python
import functools
import math

import jax
import jax.numpy as jnp
from jax import lax
from jax.experimental import pallas as pl
from jax.experimental.pallas import tpu as pltpu
from jax.sharding import PartitionSpec as P

HD = 128
VMEM_STREAM = 60 * 1024 * 1024
VMEM_WHOLE = 24 * 1024 * 1024


beta_first = 0.9
beta_second = 0.95
learn_rate = 0.0003
weight_decay = 0.1
adam_epsilon = 1e-08
first_fix = 1.0 - 0.9**40
second_fix = 1.0 - 0.95**40


def optimizer_kernel(
    place, cached, master, moment, second, grad, master_out, moment_out, second_out, cache_out
):
    moment_new = beta_first * moment[...] + (1.0 - beta_first) * grad[...]
    second_new = beta_second * second[...] + (1.0 - beta_second) * grad[...] * grad[...]
    update = moment_new / first_fix / (jnp.sqrt(second_new / second_fix) + adam_epsilon)
    master_new = master[...] - learn_rate * (update + weight_decay * master[...])
    moment_out[...] = moment_new
    second_out[...] = second_new
    master_out[...] = master_new
    for start in range(0, cached.shape[1], HD):
        block = slice(start, start + HD)
        own_cache = cached[:, block].astype(jnp.float32)
        delta = master_new[:, block] - own_cache
        largest = jnp.max(jnp.abs(delta), axis=1, keepdims=True)
        scale = (largest + 1e-06).astype(jnp.bfloat16).astype(jnp.float32)
        codes = (delta / scale).astype(jnp.bfloat16)
        cache_out[:, block] = (own_cache + codes.astype(jnp.float32) * scale).astype(jnp.bfloat16)


def optimizer(cached, master, moment, second, grad):
    rows, cols = master.shape
    step = min(rows, 256)
    steps = rows // step
    own = pl.BlockSpec((step, cols), lambda i, place: (i, 0))
    full = jax.ShapeDtypeStruct((rows, cols), jnp.float32)
    return pl.pallas_call(
        optimizer_kernel,
        grid_spec=pltpu.PrefetchScalarGridSpec(
            num_scalar_prefetch=1,
            grid=(steps,),
            in_specs=[pl.BlockSpec((step, cols), lambda i, place: (place[0] * steps + i, 0))]
            + [own] * 4,
            out_specs=[own] * 4,
        ),
        out_shape=[full, full, full, jax.ShapeDtypeStruct((rows, cols), jnp.bfloat16)],
        cost_estimate=pl.CostEstimate(
            flops=40 * rows * cols, bytes_accessed=32 * rows * cols, transcendentals=rows * cols
        ),
        compiler_params=pltpu.CompilerParams(vmem_limit_bytes=VMEM_STREAM),
        name="optimizer",
    )(lax.axis_index("dp").astype(jnp.int32).reshape(1), cached, master, moment, second, grad)


def on_chip(kernel, place, arrays, out_shape, flops, name):
    vmem = pl.BlockSpec(memory_space=pltpu.VMEM)
    size = sum(a.size * a.dtype.itemsize for a in arrays)
    size += sum(s.size * s.dtype.itemsize for s in out_shape)
    return pl.pallas_call(
        kernel,
        in_specs=[pl.BlockSpec(memory_space=pltpu.SMEM)] + [vmem] * len(arrays),
        out_specs=[vmem] * len(out_shape),
        out_shape=out_shape,
        cost_estimate=pl.CostEstimate(flops=flops, bytes_accessed=size, transcendentals=0),
        compiler_params=pltpu.CompilerParams(vmem_limit_bytes=VMEM_WHOLE),
        name=name,
    )(place, *arrays)


def fetch_chunk(place, chunks, chunk, sem):
    for n, source in enumerate(chunks):

        @pl.when(place[2] == n)
        def _():
            pltpu.make_async_copy(source, chunk, sem).start()

    return pltpu.make_async_copy(chunks[0], chunk, sem)


def fetch_rows(place, cached, rows, sem):
    height = rows.shape[0]
    start = pl.multiple_of(place[0] * height, height)
    copy = pltpu.make_async_copy(cached.at[pl.ds(start, height), :], rows, sem)
    copy.start()
    return copy


def absorb_kernel(n_chunks, place, *refs):
    chunks, (total, cached) = refs[:n_chunks], refs[n_chunks : n_chunks + 2]
    total_out, held, chunk, rows, turned, sems = refs[-6:]
    chunk_copy = fetch_chunk(place, chunks, chunk, sems.at[0])
    rows_copy = fetch_rows(place, cached, rows, sems.at[1])
    chunk_copy.wait()
    turned[...] = chunk[...].T
    keep = pltpu.make_async_copy(turned, held.at[place[1]], sems.at[2])
    keep.start()
    rows_copy.wait()
    total_out[...] = total[...] + jnp.dot(
        chunk[...], rows[...], preferred_element_type=jnp.float32
    )
    keep.wait()


def absorb_place(index, which, n_chunks):
    inside = (index >= 0) & (index < n_chunks)
    return jnp.stack(
        [jnp.clip(index, 0, n_chunks - 1), jnp.where(inside, index, n_chunks), which]
    ).astype(jnp.int32)


def absorb_scratch(chunk, cached, n_sems):
    length, feats = chunk.shape
    return [
        pltpu.VMEM((length, feats), chunk.dtype),
        pltpu.VMEM((feats, cached.shape[1]), cached.dtype),
        pltpu.VMEM((feats, length), chunk.dtype),
        pltpu.SemaphoreType.DMA((n_sems,)),
    ]


def absorb(chunks, which, index, cached, total, held, n_chunks):
    length, feats = chunks[0].shape
    cols = cached.shape[1]
    shape = jax.ShapeDtypeStruct((8 * n_chunks, feats, length), chunks[0].dtype)
    vmem, anywhere = pl.BlockSpec(memory_space=pltpu.VMEM), pl.BlockSpec(memory_space=pl.ANY)
    return pl.pallas_call(
        functools.partial(absorb_kernel, len(chunks)),
        in_specs=[pl.BlockSpec(memory_space=pltpu.SMEM)]
        + [anywhere] * len(chunks)
        + [vmem, anywhere]
        + ([] if held is None else [anywhere]),
        out_specs=[vmem, anywhere],
        out_shape=[jax.ShapeDtypeStruct(total.shape, jnp.float32), shape],
        scratch_shapes=absorb_scratch(chunks[0], cached, 3),
        input_output_aliases={} if held is None else {3 + len(chunks): 1},
        cost_estimate=pl.CostEstimate(
            flops=2 * length * feats * cols,
            bytes_accessed=4 * length * feats + 2 * feats * cols,
            transcendentals=0,
        ),
        compiler_params=pltpu.CompilerParams(vmem_limit_bytes=VMEM_STREAM),
        name="absorb",
    )(
        absorb_place(index, which, n_chunks),
        *chunks,
        total,
        cached,
        *([] if held is None else [held]),
    )


def attend_kernel(n_chunks, place, order, *refs):
    chunks, refs = refs[:n_chunks], refs[n_chunks:]
    total, cached, _, allowed, queries_in, d_out_in = refs[:6]
    held, d_queries, d_projected, sent, kept, *refs = refs[6:]
    chunk, rows, turned, sems, queries, d_out, buffer, part_sems = refs
    chunk_copy = fetch_chunk(place, chunks, chunk, sems.at[0])
    rows_copy = fetch_rows(place, cached, rows, sems.at[1])
    others = [
        pltpu.make_async_copy(queries_in, queries, sems.at[3]),
        pltpu.make_async_copy(d_out_in, d_out, sems.at[4]),
    ]
    for copy in others:
        copy.start()
    chunk_copy.wait()
    turned[...] = chunk[...].T
    keep = pltpu.make_async_copy(turned, held.at[place[1]], sems.at[2])
    keep.start()
    rows_copy.wait()
    projected = (
        total[...] + jnp.dot(chunk[...], rows[...], preferred_element_type=jnp.float32)
    ).astype(jnp.bfloat16)
    seen = allowed[...] > 0
    for copy in others:
        copy.wait()
    factor = 1.0 / math.sqrt(HD)
    across = (((1,), (1,)), ((), ()))
    heads = projected.shape[1] // (2 * HD)
    group = queries.shape[1] // HD // heads
    for head in range(heads):
        start = 2 * HD * head
        keys = projected[:, start : start + HD]
        values = projected[:, start + HD : start + 2 * HD]
        d_keys = jnp.zeros(keys.shape, jnp.float32)
        d_values = jnp.zeros(keys.shape, jnp.float32)
        for g in range(head * group, (head + 1) * group):
            if g == heads * group // 2:
                keep.wait()
                copies = fetch_parts(order, held, range(4), buffer, part_sems)
            columns = slice(g * HD, (g + 1) * HD)
            query, grad = queries[:, columns], d_out[:, columns]
            scores = (
                lax.dot_general(keys, query, across, preferred_element_type=jnp.float32) * factor
            )
            scores = jnp.where(seen, scores, -1e30)
            weights = jnp.exp(scores - jnp.max(scores, axis=0, keepdims=True))
            probs = weights / jnp.sum(weights, axis=0, keepdims=True)
            probs_low = probs.astype(jnp.bfloat16)
            d_probs = lax.dot_general(values, grad, across, preferred_element_type=jnp.float32)
            rowdot = jnp.sum(probs_low.astype(jnp.float32) * d_probs, axis=0, keepdims=True)
            d_scores = (probs * (d_probs - rowdot) * factor).astype(jnp.bfloat16)
            d_queries[:, columns] = lax.dot_general(
                d_scores, keys, (((0,), (0,)), ((), ())), preferred_element_type=jnp.float32
            ).astype(jnp.bfloat16)
            d_keys = d_keys + jnp.dot(d_scores, query, preferred_element_type=jnp.float32)
            d_values = d_values + jnp.dot(probs_low, grad, preferred_element_type=jnp.float32)
        d_projected[:, start : start + HD] = d_keys.astype(jnp.bfloat16)
        d_projected[:, start + HD : start + 2 * HD] = d_values.astype(jnp.bfloat16)

    def give(g, side, position, here, part):
        out = (sent, kept)[g]
        out[2 * side + position, here, :] = part.astype(out.dtype)

    weight_products(copies, (SENT, KEPT), buffer, d_projected, give)


def attend(chunks, which, index, cached, total, held, queries, d_out, allowed, order, n_chunks):
    feats, length = held.shape[1:]
    parts = jax.ShapeDtypeStruct((4, feats // 2, total.shape[1] // 2), jnp.bfloat16)
    vmem, anywhere = pl.BlockSpec(memory_space=pltpu.VMEM), pl.BlockSpec(memory_space=pl.ANY)
    return pl.pallas_call(
        functools.partial(attend_kernel, len(chunks)),
        in_specs=[pl.BlockSpec(memory_space=pltpu.SMEM)] * 2
        + [anywhere] * len(chunks)
        + [vmem, anywhere, anywhere, vmem, anywhere, anywhere],
        out_specs=[anywhere] + [vmem] * 4,
        out_shape=[
            jax.ShapeDtypeStruct(held.shape, held.dtype),
            jax.ShapeDtypeStruct(queries.shape, jnp.bfloat16),
            jax.ShapeDtypeStruct(total.shape, jnp.bfloat16),
            parts,
            parts,
        ],
        scratch_shapes=absorb_scratch(chunks[0], cached, 5)
        + [
            pltpu.VMEM(queries.shape, queries.dtype),
            pltpu.VMEM(d_out.shape, d_out.dtype),
            pltpu.VMEM((4, feats // 2, length), held.dtype),
            pltpu.SemaphoreType.DMA((4,)),
        ],
        input_output_aliases={4 + len(chunks): 0},
        cost_estimate=pl.CostEstimate(
            flops=12 * allowed.size * queries.shape[1],
            bytes_accessed=8 * queries.size,
            transcendentals=allowed.size * queries.shape[1] // HD,
        ),
        compiler_params=pltpu.CompilerParams(vmem_limit_bytes=VMEM_STREAM),
        name="attend",
    )(
        absorb_place(index, which, n_chunks),
        order,
        *chunks,
        total,
        cached,
        held,
        allowed,
        queries,
        d_out,
    )


SENT = ((0, 0, 0), (0, 1, 0), (1, 0, 1), (2, 1, 1))
KEPT = ((1, 1, 0), (2, 0, 0), (3, 0, 1), (3, 1, 1))


def fetch_parts(place, held, chunks, buffer, sems):
    rows = buffer.shape[1]
    start = pl.multiple_of(place[4] * rows, rows)
    copies = {}
    for chunk in chunks:
        copies[chunk] = pltpu.make_async_copy(
            held.at[place[chunk], pl.ds(start, rows), :], buffer.at[chunk], sems.at[chunk]
        )
        copies[chunk].start()
    return copies


def weight_products(copies, groups, buffer, d_projected, give):
    rows = buffer.shape[1]
    half = d_projected.shape[1] // 2
    block = min(rows, 256)
    for chunk, copy in copies.items():
        copy.wait()
        wanted = [
            (g, side, position)
            for g, group in enumerate(groups)
            for which, side, position in group
            if which == chunk
        ]
        first, last = min(w[1] for w in wanted), max(w[1] for w in wanted)
        for r in range(0, rows, block):
            here = slice(r, r + block)
            total = jnp.dot(
                buffer[chunk, here, :],
                d_projected[:, first * half : (last + 1) * half],
                preferred_element_type=jnp.float32,
            )
            for g, side, position in wanted:
                part = total[:, (side - first) * half : (side - first + 1) * half]
                give(g, side, position, here, part)


def weight_kernel(group, place, held, d_projected, *refs):
    *added, out_a, out_b, buffer, sems = refs
    copies = fetch_parts(place, held, sorted({part[0] for part in group}), buffer, sems)

    def give(_, side, position, here, part):
        if added:
            part = part + added[0][2 * side + position, here, :].astype(jnp.float32)
        out = (out_a, out_b)[side]
        out[position, here, :] = part.astype(out.dtype)

    weight_products(copies, (group,), buffer, d_projected, give)


def weight_parts(held, d_projected, place, group, added, dtype, name):
    length, cols = d_projected.shape
    rows = held.shape[1] // 2
    vmem = pl.BlockSpec(memory_space=pltpu.VMEM)
    return pl.pallas_call(
        functools.partial(weight_kernel, group),
        in_specs=[pl.BlockSpec(memory_space=pltpu.SMEM), pl.BlockSpec(memory_space=pl.ANY)]
        + [vmem] * (1 + len(added)),
        out_specs=[vmem] * 2,
        out_shape=[jax.ShapeDtypeStruct((2, rows, cols // 2), dtype)] * 2,
        scratch_shapes=[
            pltpu.VMEM((4, rows, length), held.dtype),
            pltpu.SemaphoreType.DMA((4,)),
        ],
        cost_estimate=pl.CostEstimate(
            flops=4 * length * rows * cols, bytes_accessed=8 * rows * cols, transcendentals=0
        ),
        compiler_params=pltpu.CompilerParams(vmem_limit_bytes=VMEM_WHOLE),
        name=name,
    )(place, held, d_projected, *added)


def add_kernel(place, own_a, own_b, other, out_a, out_b):
    depth = own_a.shape[0]
    for side, (own, out) in enumerate(((own_a, out_a), (own_b, out_b))):
        other_here = other[side * depth : (side + 1) * depth]
        out[...] = (own[...] + other_here.astype(jnp.float32)).astype(out.dtype)


def combine_kernel(place, keep_a, got_a, keep_b, got_b, out_a, out_b):
    for keep, got, out in ((keep_a, got_a, out_a), (keep_b, got_b, out_b)):
        out[...] = (keep[0] + got[0].astype(jnp.float32)).astype(out.dtype)


def finish_kernel(place, keep_a, got_a, keep_b, got_b, last_a, last_b, out):
    half = last_a.shape[1]
    sides = ((keep_a, got_a, last_a), (keep_b, got_b, last_b))
    for side, (keep, got, last) in enumerate(sides):
        total = keep[1] + got[1].astype(jnp.float32) + last[...].astype(jnp.float32)
        out[:, side * half : (side + 1) * half] = total


def plane():
    index = lax.axis_index("dp").astype(jnp.int32)

    def swap(value, bit):
        return lax.ppermute(value, "dp", [(i, i ^ bit) for i in range(8)])

    return index % 2, (index // 2) % 2, index // 4, swap


def weight_order(other):
    core, x, y, _ = plane()
    chunks = [3 - x - 2 * y, 1 - x + 2 * y, x + 2 - 2 * y, x + 2 * y]
    return jnp.stack(chunks + [1 - core if other else core])


def weight_sum(held, d_projected, sent, kept, pieces, beside):
    swap = plane()[3]
    rows, cols = held.shape[1] // 2, d_projected.shape[1]
    none = jnp.zeros((1,), jnp.int32)
    order = weight_order(False)
    sent, kept = swap(sent, 1), swap(kept, 1)
    own = weight_parts(held, d_projected, order, SENT, [], jnp.float32, "weight_send")
    shape = jax.ShapeDtypeStruct(own[0].shape, jnp.bfloat16)
    send_a, send_b = on_chip(
        add_kernel, none, list(own) + [sent], [shape] * 2, 2 * cols * rows, "weight_add"
    )
    got_a, got_b = swap(send_a, 2), swap(send_b, 4)
    keep_a, keep_b = weight_parts(
        held, d_projected, order, KEPT, [kept], jnp.float32, "weight_keep"
    )
    got_a, got_b, pieces, beside = lax.optimization_barrier((got_a, got_b, pieces, beside))

    small = jax.ShapeDtypeStruct((rows, cols // 2), jnp.bfloat16)
    arrays = [keep_a, got_a, keep_b, got_b]
    last_a, last_b = on_chip(
        combine_kernel, none, arrays, [small] * 2, cols * rows, "weight_combine"
    )
    last = [swap(last_a, 4), swap(last_b, 2)]

    def finish(ready):
        ended, ready = lax.optimization_barrier((last, ready))
        (total,) = on_chip(
            finish_kernel,
            none,
            arrays + ended,
            [jax.ShapeDtypeStruct((rows, cols), jnp.float32)],
            2 * cols * rows,
            "weight_finish",
        )
        return total, ready

    return finish, pieces, beside


class PlaneGather:
    def __init__(self, own):
        self.got = {0: own}

    def first(self):
        own, swap = self.got[0], plane()[3]
        self.got.update({bit: swap(own, bit) for bit in (2, 4, 1)})
        return self.got

    def second(self):
        got, swap, half = self.got, plane()[3], self.got[0].shape[0] // 2
        self.far = [swap(got[4][:half], 2), swap(got[2][half:], 4)]
        got[3], got[5] = swap(got[2], 1), swap(got[4], 1)
        return self.far, got[3], got[5]

    def third(self):
        swap = plane()[3]
        self.far_other = [swap(value, 1) for value in self.far]
        return self.far_other

    def where(self, bits):
        return lax.axis_index("dp").astype(jnp.int32) ^ jnp.array(bits, dtype=jnp.int32)

    def lay(self, height, rows):
        arrays = [self.got[k] for k in range(6)]
        return place_rows(arrays, self.where(list(range(6))), height, rows, [])

    def lay_far(self, height, laid):
        arrays = [self.far[0], self.far_other[0]]
        return place_rows(arrays, self.where([6, 7]), height, laid.shape[0], [laid])

    def last(self):
        arrays = [self.got[k] for k in range(6)] + [self.far[1], self.far_other[1]]
        return arrays, self.where(list(range(8)))


def place_rows_kernel(height, n_arrays, place, *refs):
    arrays, (out, sems) = refs[:n_arrays], refs[-2:]
    copies = []
    for k, array in enumerate(arrays):
        start = pl.multiple_of(place[k] * height, height)
        copies.append(
            pltpu.make_async_copy(
                array.at[pl.ds(0, height), :], out.at[pl.ds(start, height), :], sems.at[k]
            )
        )
    for copy in copies:
        copy.start()
    for copy in copies:
        copy.wait()


def place_rows(arrays, place, height, rows, into):
    cols = arrays[0].shape[1]
    anywhere = pl.BlockSpec(memory_space=pl.ANY)
    return pl.pallas_call(
        functools.partial(place_rows_kernel, height, len(arrays)),
        in_specs=[pl.BlockSpec(memory_space=pltpu.SMEM)]
        + [pl.BlockSpec(memory_space=pltpu.VMEM)] * len(arrays)
        + [anywhere] * len(into),
        out_specs=anywhere,
        out_shape=jax.ShapeDtypeStruct((rows, cols), arrays[0].dtype),
        scratch_shapes=[pltpu.SemaphoreType.DMA((len(arrays),))],
        input_output_aliases={1 + len(arrays): 0} if into else {},
        cost_estimate=pl.CostEstimate(
            flops=0, bytes_accessed=4 * height * cols * len(arrays), transcendentals=0
        ),
        compiler_params=pltpu.CompilerParams(vmem_limit_bytes=VMEM_WHOLE),
        name="place_rows",
    )(place, *arrays, *into)


def input_kernel(n_blocks, place, *refs):
    *arrays, out = refs
    pieces, rows = arrays[:n_blocks], arrays[n_blocks:]
    share = out.shape[1] // len(rows)
    for k, held in enumerate(rows):
        first = held.shape[0] - n_blocks * share
        total = jnp.zeros((out.shape[0], share), jnp.float32)
        for s, piece in enumerate(pieces):
            total = total + lax.dot_general(
                piece[...],
                held[first + s * share : first + (s + 1) * share, :],
                (((1,), (1,)), ((), ())),
                preferred_element_type=jnp.float32,
            )
        start = pl.multiple_of(place[k] * share, share)
        out[:, pl.ds(start, share)] = total.astype(out.dtype)


def input_gradient(pieces, arrays, place, feats):
    length, cols = pieces[0].shape
    (d_tokens,) = on_chip(
        functools.partial(input_kernel, len(pieces)),
        place,
        pieces + arrays,
        [jax.ShapeDtypeStruct((length, feats), jnp.bfloat16)],
        2 * length * feats * cols * len(pieces),
        "input_gradient",
    )
    return d_tokens


def make_body(n_dp, n_z):
    tuned = n_dp == 8 and n_z == 4

    def pair(value, s):
        return lax.ppermute(value, "tensor", [(z, z ^ s) for z in range(n_z)])

    def body(tokens, queries, d_out, segments, cached, master, moment, second, grad):
        me_dp = lax.axis_index("dp").astype(jnp.int32)
        me_z = lax.axis_index("tensor").astype(jnp.int32)
        length, feats = tokens.shape
        cols = cached.shape[1]

        master_new, moment_new, second_new, own_cache = optimizer(
            cached, master, moment, second, grad
        )

        share = feats // n_dp

        def block_for(z):
            return lax.dynamic_slice_in_dim(cached, z * feats + me_dp * share, share, 0)

        blocks = [block_for(me_z)] + [pair(block_for(me_z ^ s), s) for s in range(1, n_z)]

        doc_ids = segments[0]
        position = jnp.arange(length)
        allowed = (doc_ids[:, None] == doc_ids[None, :]) & (position[:, None] <= position[None, :])
        allowed = allowed.astype(jnp.float32)

        total = jnp.zeros((length, cols), jnp.float32)
        zero = 0 * me_z
        total, held = absorb([tokens], zero, me_z, cached, total, None, n_z)
        if tuned:
            gather = PlaneGather(jnp.concatenate([own_cache] + blocks, axis=0))
        from_low, from_high = tokens, tokens
        for s in range(1, n_z):
            low, high = me_z - s, me_z + s
            from_low = lax.ppermute(
                from_low, "tensor", [(z, z + 1) for z in range(s - 1, n_z - 1)]
            )
            from_high = lax.ppermute(from_high, "tensor", [(z + 1, z) for z in range(n_z - s)])
            if tuned:
                if s == 1:
                    rounds, allowed = lax.optimization_barrier((gather.got, allowed))
                elif s == 2:
                    rounds = gather.first()
                else:
                    rounds = gather.second()
                    laid = gather.lay(own_cache.shape[0], cached.shape[0])
                    rounds = (rounds, laid)
                from_low, from_high, held, rounds = lax.optimization_barrier(
                    (from_low, from_high, held, rounds)
                )
                if s < 3:
                    gather.got = rounds
                else:
                    (gather.far, gather.got[3], gather.got[5]), laid = rounds
            chunks, which = [from_low, from_high], (me_z < s).astype(jnp.int32)
            index = jnp.where(me_z < s, high, low)
            if 2 * s < n_z:
                total, held = absorb([from_low], zero, low, cached, total, held, n_z)
                chunks, which, index = [from_high], zero, high
            if s < n_z - 1:
                total, held = absorb(chunks, which, index, cached, total, held, n_z)

        order = weight_order(True) if tuned else jnp.zeros((5,), jnp.int32)
        held, d_queries, d_projected, sent, kept = attend(
            chunks, which, index, cached, total, held, queries, d_out, allowed, order, n_z
        )

        pieces = [d_projected] + [pair(d_projected, s) for s in range(1, n_z)]
        if tuned:
            sent, gather.far_other = lax.optimization_barrier((sent, gather.third()))
            new_cache = gather.lay_far(own_cache.shape[0], laid)
            finish, pieces, new_cache = weight_sum(
                held, d_projected, sent, kept, pieces, new_cache
            )
            new_grad, d_tokens = finish(input_gradient(pieces, *gather.last(), feats))
        else:
            new_cache = lax.all_gather(own_cache, "dp", axis=0, tiled=True)
            rows = lax.all_gather(jnp.stack(blocks), "dp", axis=0)
            d_tokens = jnp.einsum(
                "slc,ksfc->lkf", jnp.stack(pieces), rows, preferred_element_type=jnp.float32
            )
            d_tokens = d_tokens.astype(jnp.bfloat16).reshape(length, feats)
            partial = lax.dot_general(
                held[:n_z].reshape(n_z * feats, length),
                d_projected,
                (((1,), (0,)), ((), ())),
                preferred_element_type=jnp.float32,
            )
            new_grad = lax.psum_scatter(
                partial.astype(jnp.bfloat16), "dp", scatter_dimension=0, tiled=True
            ).astype(jnp.float32)
        return (master_new, moment_new, second_new, new_cache, new_grad, d_queries, d_tokens)

    return body


def solution(mesh):
    in_specs = (
        P("dp", "tensor"),
        P("dp", "tensor"),
        P("dp", "tensor"),
        P("dp", None),
        P(None, "tensor"),
        P("dp", "tensor"),
        P("dp", "tensor"),
        P("dp", "tensor"),
        P("dp", "tensor"),
    )
    out_specs = (
        P("dp", "tensor"),
        P("dp", "tensor"),
        P("dp", "tensor"),
        P(None, "tensor"),
        P("dp", "tensor"),
        P("dp", "tensor"),
        P("dp", "tensor"),
    )
    body = make_body(mesh.shape["dp"], mesh.shape["tensor"])
    return jax.shard_map(body, mesh=mesh, in_specs=in_specs, out_specs=out_specs, check_vma=False)
```

```python
import functools
import math

import jax
import jax.numpy as jnp
from jax import lax
from jax.experimental import pallas as pl
from jax.experimental.pallas import tpu as pltpu
from jax.sharding import PartitionSpec as P

HD = 128
VMEM_STREAM = 60 * 1024 * 1024
VMEM_WHOLE = 24 * 1024 * 1024


beta_first = 0.9
beta_second = 0.95
learn_rate = 0.0003
weight_decay = 0.1
adam_epsilon = 1e-08
first_fix = 1.0 - 0.9**40
second_fix = 1.0 - 0.95**40


def optimizer_kernel(
    place, cached, master, moment, second, grad, master_out, moment_out, second_out, cache_out
):
    moment_new = beta_first * moment[...] + (1.0 - beta_first) * grad[...]
    second_new = beta_second * second[...] + (1.0 - beta_second) * grad[...] * grad[...]
    update = moment_new / first_fix / (jnp.sqrt(second_new / second_fix) + adam_epsilon)
    master_new = master[...] - learn_rate * (update + weight_decay * master[...])
    moment_out[...] = moment_new
    second_out[...] = second_new
    master_out[...] = master_new
    for start in range(0, cached.shape[1], HD):
        block = slice(start, start + HD)
        own_cache = cached[:, block].astype(jnp.float32)
        delta = master_new[:, block] - own_cache
        largest = jnp.max(jnp.abs(delta), axis=1, keepdims=True)
        scale = (largest + 1e-06).astype(jnp.bfloat16).astype(jnp.float32)
        codes = (delta / scale).astype(jnp.bfloat16)
        cache_out[:, block] = (own_cache + codes.astype(jnp.float32) * scale).astype(jnp.bfloat16)


def optimizer(cached, master, moment, second, grad):
    rows, cols = master.shape
    step = min(rows, 256)
    steps = rows // step
    own = pl.BlockSpec((step, cols), lambda i, place: (i, 0))
    full = jax.ShapeDtypeStruct((rows, cols), jnp.float32)
    return pl.pallas_call(
        optimizer_kernel,
        grid_spec=pltpu.PrefetchScalarGridSpec(
            num_scalar_prefetch=1,
            grid=(steps,),
            in_specs=[pl.BlockSpec((step, cols), lambda i, place: (place[0] * steps + i, 0))]
            + [own] * 4,
            out_specs=[own] * 4,
        ),
        out_shape=[full, full, full, jax.ShapeDtypeStruct((rows, cols), jnp.bfloat16)],
        cost_estimate=pl.CostEstimate(
            flops=40 * rows * cols, bytes_accessed=32 * rows * cols, transcendentals=rows * cols
        ),
        compiler_params=pltpu.CompilerParams(vmem_limit_bytes=VMEM_STREAM),
        name="optimizer",
    )(lax.axis_index("dp").astype(jnp.int32).reshape(1), cached, master, moment, second, grad)


def on_chip(kernel, place, arrays, out_shape, flops, name):
    vmem = pl.BlockSpec(memory_space=pltpu.VMEM)
    size = sum(a.size * a.dtype.itemsize for a in arrays)
    size += sum(s.size * s.dtype.itemsize for s in out_shape)
    return pl.pallas_call(
        kernel,
        in_specs=[pl.BlockSpec(memory_space=pltpu.SMEM)] + [vmem] * len(arrays),
        out_specs=[vmem] * len(out_shape),
        out_shape=out_shape,
        cost_estimate=pl.CostEstimate(flops=flops, bytes_accessed=size, transcendentals=0),
        compiler_params=pltpu.CompilerParams(vmem_limit_bytes=VMEM_WHOLE),
        name=name,
    )(place, *arrays)


def fetch_chunk(place, chunks, chunk, sem):
    for n, source in enumerate(chunks):

        @pl.when(place[2] == n)
        def _():
            pltpu.make_async_copy(source, chunk, sem).start()

    return pltpu.make_async_copy(chunks[0], chunk, sem)


def fetch_rows(place, cached, rows, sem):
    height = rows.shape[0]
    start = pl.multiple_of(place[0] * height, height)
    copy = pltpu.make_async_copy(cached.at[pl.ds(start, height), :], rows, sem)
    copy.start()
    return copy


def absorb_kernel(n_chunks, place, *refs):
    chunks, (total, cached) = refs[:n_chunks], refs[n_chunks : n_chunks + 2]
    total_out, held, chunk, rows, turned, sems = refs[-6:]
    chunk_copy = fetch_chunk(place, chunks, chunk, sems.at[0])
    rows_copy = fetch_rows(place, cached, rows, sems.at[1])
    chunk_copy.wait()
    turned[...] = chunk[...].T
    keep = pltpu.make_async_copy(turned, held.at[place[1]], sems.at[2])
    keep.start()
    rows_copy.wait()
    total_out[...] = total[...] + jnp.dot(
        chunk[...], rows[...], preferred_element_type=jnp.float32
    )
    keep.wait()


def absorb_place(index, which, n_chunks):
    inside = (index >= 0) & (index < n_chunks)
    return jnp.stack(
        [jnp.clip(index, 0, n_chunks - 1), jnp.where(inside, index, n_chunks), which]
    ).astype(jnp.int32)


def absorb_scratch(chunk, cached, n_sems):
    length, feats = chunk.shape
    return [
        pltpu.VMEM((length, feats), chunk.dtype),
        pltpu.VMEM((feats, cached.shape[1]), cached.dtype),
        pltpu.VMEM((feats, length), chunk.dtype),
        pltpu.SemaphoreType.DMA((n_sems,)),
    ]


def absorb(chunks, which, index, cached, total, held, n_chunks):
    length, feats = chunks[0].shape
    cols = cached.shape[1]
    shape = jax.ShapeDtypeStruct((8 * n_chunks, feats, length), chunks[0].dtype)
    vmem, anywhere = pl.BlockSpec(memory_space=pltpu.VMEM), pl.BlockSpec(memory_space=pl.ANY)
    return pl.pallas_call(
        functools.partial(absorb_kernel, len(chunks)),
        in_specs=[pl.BlockSpec(memory_space=pltpu.SMEM)]
        + [anywhere] * len(chunks)
        + [vmem, anywhere]
        + ([] if held is None else [anywhere]),
        out_specs=[vmem, anywhere],
        out_shape=[jax.ShapeDtypeStruct(total.shape, jnp.float32), shape],
        scratch_shapes=absorb_scratch(chunks[0], cached, 3),
        input_output_aliases={} if held is None else {3 + len(chunks): 1},
        cost_estimate=pl.CostEstimate(
            flops=2 * length * feats * cols,
            bytes_accessed=4 * length * feats + 2 * feats * cols,
            transcendentals=0,
        ),
        compiler_params=pltpu.CompilerParams(vmem_limit_bytes=VMEM_STREAM),
        name="absorb",
    )(
        absorb_place(index, which, n_chunks),
        *chunks,
        total,
        cached,
        *([] if held is None else [held]),
    )


def attend_kernel(n_chunks, place, order, *refs):
    chunks, refs = refs[:n_chunks], refs[n_chunks:]
    total, cached, _, allowed, queries_in, d_out_in = refs[:6]
    held, d_queries, d_projected, sent, kept, *refs = refs[6:]
    chunk, rows, turned, sems, queries, d_out, buffer, part_sems = refs
    chunk_copy = fetch_chunk(place, chunks, chunk, sems.at[0])
    rows_copy = fetch_rows(place, cached, rows, sems.at[1])
    others = [
        pltpu.make_async_copy(queries_in, queries, sems.at[3]),
        pltpu.make_async_copy(d_out_in, d_out, sems.at[4]),
    ]
    for copy in others:
        copy.start()
    keep = pltpu.make_async_copy(turned, held.at[place[1]], sems.at[2])
    for copy in [chunk_copy, rows_copy] + others:
        copy.wait()
    turned[...] = chunk[...].T
    projected = (
        total[...] + jnp.dot(chunk[...], rows[...], preferred_element_type=jnp.float32)
    ).astype(jnp.bfloat16)
    seen = allowed[...] > 0
    factor = 1.0 / math.sqrt(HD)
    across = (((1,), (1,)), ((), ()))
    heads = projected.shape[1] // (2 * HD)
    group = queries.shape[1] // HD // heads
    for head in range(heads):
        start = 2 * HD * head
        keys = projected[:, start : start + HD]
        values = projected[:, start + HD : start + 2 * HD]
        d_keys = jnp.zeros(keys.shape, jnp.float32)
        d_values = jnp.zeros(keys.shape, jnp.float32)
        for g in range(head * group, (head + 1) * group):
            if g == heads * group // 4:
                keep.start()
            if g == heads * group * 3 // 4:
                keep.wait()
                copies = fetch_parts(order, held, range(4), buffer, part_sems)
            columns = slice(g * HD, (g + 1) * HD)
            query, grad = queries[:, columns], d_out[:, columns]
            scores = (
                lax.dot_general(keys, query, across, preferred_element_type=jnp.float32) * factor
            )
            scores = jnp.where(seen, scores, -1e30)
            weights = jnp.exp(scores - jnp.max(scores, axis=0, keepdims=True))
            probs = weights / jnp.sum(weights, axis=0, keepdims=True)
            probs_low = probs.astype(jnp.bfloat16)
            d_probs = lax.dot_general(values, grad, across, preferred_element_type=jnp.float32)
            rowdot = jnp.sum(probs_low.astype(jnp.float32) * d_probs, axis=0, keepdims=True)
            d_scores = (probs * (d_probs - rowdot) * factor).astype(jnp.bfloat16)
            d_queries[:, columns] = lax.dot_general(
                d_scores, keys, (((0,), (0,)), ((), ())), preferred_element_type=jnp.float32
            ).astype(jnp.bfloat16)
            d_keys = d_keys + jnp.dot(d_scores, query, preferred_element_type=jnp.float32)
            d_values = d_values + jnp.dot(probs_low, grad, preferred_element_type=jnp.float32)
        d_projected[:, start : start + HD] = d_keys.astype(jnp.bfloat16)
        d_projected[:, start + HD : start + 2 * HD] = d_values.astype(jnp.bfloat16)

    def give(g, side, position, here, part):
        out = (sent, kept)[g]
        out[2 * side + position, here, :] = part.astype(out.dtype)

    weight_products(copies, (SENT, KEPT), buffer, d_projected, give)


def attend(chunks, which, index, cached, total, held, queries, d_out, allowed, order, n_chunks):
    feats, length = held.shape[1:]
    parts = jax.ShapeDtypeStruct((4, feats // 2, total.shape[1] // 2), jnp.bfloat16)
    vmem, anywhere = pl.BlockSpec(memory_space=pltpu.VMEM), pl.BlockSpec(memory_space=pl.ANY)
    return pl.pallas_call(
        functools.partial(attend_kernel, len(chunks)),
        in_specs=[pl.BlockSpec(memory_space=pltpu.SMEM)] * 2
        + [anywhere] * len(chunks)
        + [vmem, anywhere, anywhere, vmem, anywhere, anywhere],
        out_specs=[anywhere] + [vmem] * 4,
        out_shape=[
            jax.ShapeDtypeStruct(held.shape, held.dtype),
            jax.ShapeDtypeStruct(queries.shape, jnp.bfloat16),
            jax.ShapeDtypeStruct(total.shape, jnp.bfloat16),
            parts,
            parts,
        ],
        scratch_shapes=absorb_scratch(chunks[0], cached, 5)
        + [
            pltpu.VMEM(queries.shape, queries.dtype),
            pltpu.VMEM(d_out.shape, d_out.dtype),
            pltpu.VMEM((4, feats // 2, length), held.dtype),
            pltpu.SemaphoreType.DMA((4,)),
        ],
        input_output_aliases={4 + len(chunks): 0},
        cost_estimate=pl.CostEstimate(
            flops=12 * allowed.size * queries.shape[1],
            bytes_accessed=8 * queries.size,
            transcendentals=allowed.size * queries.shape[1] // HD,
        ),
        compiler_params=pltpu.CompilerParams(vmem_limit_bytes=VMEM_STREAM),
        name="attend",
    )(
        absorb_place(index, which, n_chunks),
        order,
        *chunks,
        total,
        cached,
        held,
        allowed,
        queries,
        d_out,
    )


SENT = ((0, 0, 0), (0, 1, 0), (1, 0, 1), (2, 1, 1))
KEPT = ((1, 1, 0), (2, 0, 0), (3, 0, 1), (3, 1, 1))


def fetch_parts(place, held, chunks, buffer, sems):
    rows = buffer.shape[1]
    start = pl.multiple_of(place[4] * rows, rows)
    copies = {}
    for chunk in chunks:
        copies[chunk] = pltpu.make_async_copy(
            held.at[place[chunk], pl.ds(start, rows), :], buffer.at[chunk], sems.at[chunk]
        )
        copies[chunk].start()
    return copies


def weight_products(copies, groups, buffer, d_projected, give):
    rows = buffer.shape[1]
    half = d_projected.shape[1] // 2
    block = min(rows, 256)
    for chunk, copy in copies.items():
        copy.wait()
        wanted = [
            (g, side, position)
            for g, group in enumerate(groups)
            for which, side, position in group
            if which == chunk
        ]
        first, last = min(w[1] for w in wanted), max(w[1] for w in wanted)
        for r in range(0, rows, block):
            here = slice(r, r + block)
            total = jnp.dot(
                buffer[chunk, here, :],
                d_projected[:, first * half : (last + 1) * half],
                preferred_element_type=jnp.float32,
            )
            for g, side, position in wanted:
                part = total[:, (side - first) * half : (side - first + 1) * half]
                give(g, side, position, here, part)


def weight_kernel(group, place, held, d_projected, *refs):
    *added, out_a, out_b, buffer, sems = refs
    copies = fetch_parts(place, held, sorted({part[0] for part in group}), buffer, sems)

    def give(_, side, position, here, part):
        if added:
            part = part + added[0][2 * side + position, here, :].astype(jnp.float32)
        out = (out_a, out_b)[side]
        out[position, here, :] = part.astype(out.dtype)

    weight_products(copies, (group,), buffer, d_projected, give)


def weight_parts(held, d_projected, place, group, added, dtype, name):
    length, cols = d_projected.shape
    rows = held.shape[1] // 2
    vmem = pl.BlockSpec(memory_space=pltpu.VMEM)
    return pl.pallas_call(
        functools.partial(weight_kernel, group),
        in_specs=[pl.BlockSpec(memory_space=pltpu.SMEM), pl.BlockSpec(memory_space=pl.ANY)]
        + [vmem] * (1 + len(added)),
        out_specs=[vmem] * 2,
        out_shape=[jax.ShapeDtypeStruct((2, rows, cols // 2), dtype)] * 2,
        scratch_shapes=[
            pltpu.VMEM((4, rows, length), held.dtype),
            pltpu.SemaphoreType.DMA((4,)),
        ],
        cost_estimate=pl.CostEstimate(
            flops=4 * length * rows * cols, bytes_accessed=8 * rows * cols, transcendentals=0
        ),
        compiler_params=pltpu.CompilerParams(vmem_limit_bytes=VMEM_WHOLE),
        name=name,
    )(place, held, d_projected, *added)


def add_kernel(place, own_a, own_b, other, out_a, out_b):
    depth = own_a.shape[0]
    for side, (own, out) in enumerate(((own_a, out_a), (own_b, out_b))):
        other_here = other[side * depth : (side + 1) * depth]
        out[...] = (own[...] + other_here.astype(jnp.float32)).astype(out.dtype)


def combine_kernel(place, keep_a, got_a, keep_b, got_b, out_a, out_b):
    for keep, got, out in ((keep_a, got_a, out_a), (keep_b, got_b, out_b)):
        out[...] = (keep[0] + got[0].astype(jnp.float32)).astype(out.dtype)


def finish_kernel(place, keep_a, got_a, keep_b, got_b, last_a, last_b, out):
    half = last_a.shape[1]
    sides = ((keep_a, got_a, last_a), (keep_b, got_b, last_b))
    for side, (keep, got, last) in enumerate(sides):
        total = keep[1] + got[1].astype(jnp.float32) + last[...].astype(jnp.float32)
        out[:, side * half : (side + 1) * half] = total


def plane():
    index = lax.axis_index("dp").astype(jnp.int32)

    def swap(value, bit):
        return lax.ppermute(value, "dp", [(i, i ^ bit) for i in range(8)])

    return index % 2, (index // 2) % 2, index // 4, swap


def weight_orders():
    core, x, y, _ = plane()
    chunks = [3 - x - 2 * y, 1 - x + 2 * y, x + 2 - 2 * y, x + 2 * y]
    return [jnp.stack(chunks + [half]) for half in (1 - core, core)]


def weight_sum(held, d_projected, order, sent, kept, pieces, beside):
    swap = plane()[3]
    rows, cols = held.shape[1] // 2, d_projected.shape[1]
    none = jnp.zeros((1,), jnp.int32)
    sent, kept = swap(sent, 1), swap(kept, 1)
    own = weight_parts(held, d_projected, order, SENT, [], jnp.float32, "weight_send")
    shape = jax.ShapeDtypeStruct(own[0].shape, jnp.bfloat16)
    send_a, send_b = on_chip(
        add_kernel, none, list(own) + [sent], [shape] * 2, 2 * cols * rows, "weight_add"
    )
    got_a, got_b = swap(send_a, 2), swap(send_b, 4)
    keep_a, keep_b = weight_parts(
        held, d_projected, order, KEPT, [kept], jnp.float32, "weight_keep"
    )
    got_a, got_b, pieces, beside = lax.optimization_barrier((got_a, got_b, pieces, beside))

    small = jax.ShapeDtypeStruct((rows, cols // 2), jnp.bfloat16)
    arrays = [keep_a, got_a, keep_b, got_b]
    last_a, last_b = on_chip(
        combine_kernel, none, arrays, [small] * 2, cols * rows, "weight_combine"
    )
    last = [swap(last_a, 4), swap(last_b, 2)]

    def finish(ready):
        ended, ready = lax.optimization_barrier((last, ready))
        (total,) = on_chip(
            finish_kernel,
            none,
            arrays + ended,
            [jax.ShapeDtypeStruct((rows, cols), jnp.float32)],
            2 * cols * rows,
            "weight_finish",
        )
        return total, ready

    return finish, pieces, beside


class PlaneGather:
    def __init__(self, own, split):
        self.got, self.split = {0: own}, split

    def first(self):
        own, swap = self.got[0], plane()[3]
        self.got.update({bit: swap(own, bit) for bit in (2, 4, 1)})
        return self.got

    def second(self):
        got, swap = self.got, plane()[3]
        self.far = [swap(got[4][: self.split], 2), swap(got[2][self.split :], 4)]
        got[3], got[5] = swap(got[2], 1), swap(got[4], 1)
        return self.far, got[3], got[5]

    def third(self):
        swap = plane()[3]
        self.far_other = [swap(value, 1) for value in self.far]
        return self.far_other

    def where(self, bits):
        return lax.axis_index("dp").astype(jnp.int32) ^ jnp.array(bits, dtype=jnp.int32)

    def lay(self, height, rows):
        arrays = [self.got[k] for k in range(6)]
        return place_rows(arrays, self.where(list(range(6))), height, rows, [])

    def lay_far(self, height, laid):
        arrays = [self.far[0], self.far_other[0]]
        return place_rows(arrays, self.where([6, 7]), height, laid.shape[0], [laid])

    def last(self):
        arrays = [self.got[k] for k in range(6)] + [self.far[1], self.far_other[1]]
        return arrays, self.where(list(range(8)))


def place_rows_kernel(height, n_arrays, place, *refs):
    arrays, (out, sems) = refs[:n_arrays], refs[-2:]
    copies = []
    for k, array in enumerate(arrays):
        start = pl.multiple_of(place[k] * height, height)
        copies.append(
            pltpu.make_async_copy(
                array.at[pl.ds(0, height), :], out.at[pl.ds(start, height), :], sems.at[k]
            )
        )
    for copy in copies:
        copy.start()
    for copy in copies:
        copy.wait()


def place_rows(arrays, place, height, rows, into):
    cols = arrays[0].shape[1]
    anywhere = pl.BlockSpec(memory_space=pl.ANY)
    return pl.pallas_call(
        functools.partial(place_rows_kernel, height, len(arrays)),
        in_specs=[pl.BlockSpec(memory_space=pltpu.SMEM)]
        + [pl.BlockSpec(memory_space=pltpu.VMEM)] * len(arrays)
        + [anywhere] * len(into),
        out_specs=anywhere,
        out_shape=jax.ShapeDtypeStruct((rows, cols), arrays[0].dtype),
        scratch_shapes=[pltpu.SemaphoreType.DMA((len(arrays),))],
        input_output_aliases={1 + len(arrays): 0} if into else {},
        cost_estimate=pl.CostEstimate(
            flops=0, bytes_accessed=4 * height * cols * len(arrays), transcendentals=0
        ),
        compiler_params=pltpu.CompilerParams(vmem_limit_bytes=VMEM_WHOLE),
        name="place_rows",
    )(place, *arrays, *into)


def input_kernel(n_blocks, place, *refs):
    *arrays, out = refs
    pieces, here, rows = arrays[:n_blocks], arrays[n_blocks], arrays[n_blocks + 1 :]
    share = out.shape[1] // len(rows)
    for k, held in enumerate(rows):
        start = pl.multiple_of(place[k] * share, share)
        first = held.shape[0] - n_blocks * share
        total = jnp.zeros((out.shape[0], share), jnp.float32)
        for s, piece in enumerate(pieces):
            if s:
                block = held[first + s * share : first + (s + 1) * share, :]
            else:
                block = here[pl.ds(start, share), :]
            total = total + lax.dot_general(
                piece[...], block, (((1,), (1,)), ((), ())), preferred_element_type=jnp.float32
            )
        out[:, pl.ds(start, share)] = total.astype(out.dtype)


def input_gradient(pieces, here, arrays, place):
    length, cols = pieces[0].shape
    feats = here.shape[0]
    (d_tokens,) = on_chip(
        functools.partial(input_kernel, len(pieces)),
        place,
        pieces + [here] + arrays,
        [jax.ShapeDtypeStruct((length, feats), jnp.bfloat16)],
        2 * length * feats * cols * len(pieces),
        "input_gradient",
    )
    return d_tokens


def make_body(n_dp, n_z):
    tuned = n_dp == 8 and n_z == 4

    def pair(value, s):
        return lax.ppermute(value, "tensor", [(z, z ^ s) for z in range(n_z)])

    def body(tokens, queries, d_out, segments, cached, master, moment, second, grad):
        me_dp = lax.axis_index("dp").astype(jnp.int32)
        me_z = lax.axis_index("tensor").astype(jnp.int32)
        length, feats = tokens.shape
        cols = cached.shape[1]

        master_new, moment_new, second_new, own_cache = optimizer(
            cached, master, moment, second, grad
        )

        share = feats // n_dp

        def block_for(z):
            return lax.dynamic_slice_in_dim(cached, z * feats + me_dp * share, share, 0)

        blocks = [pair(block_for(me_z ^ s), s) for s in range(1, n_z)]
        here = lax.dynamic_slice_in_dim(cached, me_z * feats, feats, 0)

        doc_ids = segments[0]
        position = jnp.arange(length)
        allowed = (doc_ids[:, None] == doc_ids[None, :]) & (position[:, None] <= position[None, :])
        allowed = allowed.astype(jnp.float32)

        total = jnp.zeros((length, cols), jnp.float32)
        zero = 0 * me_z
        orders = weight_orders() if tuned else [jnp.zeros((5,), jnp.int32)]
        total, held = absorb([tokens], zero, me_z, cached, total, None, n_z)
        if tuned:
            gather = PlaneGather(jnp.concatenate([own_cache] + blocks, axis=0), own_cache.shape[0])
        from_low, from_high = tokens, tokens
        for s in range(1, n_z):
            low, high = me_z - s, me_z + s
            from_high = lax.ppermute(from_high, "tensor", [(z + 1, z) for z in range(n_z - s)])
            from_low = lax.ppermute(
                from_low, "tensor", [(z, z + 1) for z in range(s - 1, n_z - 1)]
            )
            if tuned:
                if s == 1:
                    rounds, allowed, orders, here = lax.optimization_barrier(
                        (gather.got, allowed, orders, here)
                    )
                elif s == 2:
                    rounds = gather.first()
                else:
                    rounds = gather.second()
                    laid = gather.lay(own_cache.shape[0], cached.shape[0])
                    rounds = (rounds, laid)
                from_low, from_high, held, rounds = lax.optimization_barrier(
                    (from_low, from_high, held, rounds)
                )
                if s < 3:
                    gather.got = rounds
                else:
                    (gather.far, gather.got[3], gather.got[5]), laid = rounds
            chunks, which = [from_low, from_high], (me_z < s).astype(jnp.int32)
            index = jnp.where(me_z < s, high, low)
            if 2 * s < n_z:
                total, held = absorb([from_low], zero, low, cached, total, held, n_z)
                chunks, which, index = [from_high], zero, high
            if s < n_z - 1:
                total, held = absorb(chunks, which, index, cached, total, held, n_z)

        held, d_queries, d_projected, sent, kept = attend(
            chunks, which, index, cached, total, held, queries, d_out, allowed, orders[0], n_z
        )

        pieces = [d_projected] + [pair(d_projected, s) for s in range(1, n_z)]
        if tuned:
            sent, gather.far_other = lax.optimization_barrier((sent, gather.third()))
            new_cache = gather.lay_far(own_cache.shape[0], laid)
            finish, pieces, new_cache = weight_sum(
                held, d_projected, orders[1], sent, kept, pieces, new_cache
            )
            new_grad, d_tokens = finish(input_gradient(pieces, here, *gather.last()))
        else:
            new_cache = lax.all_gather(own_cache, "dp", axis=0, tiled=True)
            rows = lax.all_gather(jnp.stack([block_for(me_z)] + blocks), "dp", axis=0)
            d_tokens = jnp.einsum(
                "slc,ksfc->lkf", jnp.stack(pieces), rows, preferred_element_type=jnp.float32
            )
            d_tokens = d_tokens.astype(jnp.bfloat16).reshape(length, feats)
            partial = lax.dot_general(
                held[:n_z].reshape(n_z * feats, length),
                d_projected,
                (((1,), (0,)), ((), ())),
                preferred_element_type=jnp.float32,
            )
            new_grad = lax.psum_scatter(
                partial.astype(jnp.bfloat16), "dp", scatter_dimension=0, tiled=True
            ).astype(jnp.float32)
        return (master_new, moment_new, second_new, new_cache, new_grad, d_queries, d_tokens)

    return body


def solution(mesh):
    in_specs = (
        P("dp", "tensor"),
        P("dp", "tensor"),
        P("dp", "tensor"),
        P("dp", None),
        P(None, "tensor"),
        P("dp", "tensor"),
        P("dp", "tensor"),
        P("dp", "tensor"),
        P("dp", "tensor"),
    )
    out_specs = (
        P("dp", "tensor"),
        P("dp", "tensor"),
        P("dp", "tensor"),
        P(None, "tensor"),
        P("dp", "tensor"),
        P("dp", "tensor"),
        P("dp", "tensor"),
    )
    body = make_body(mesh.shape["dp"], mesh.shape["tensor"])
    return jax.shard_map(body, mesh=mesh, in_specs=in_specs, out_specs=out_specs, check_vma=False)
```

```python
import functools
import math

import jax
import jax.numpy as jnp
from jax import lax
from jax.experimental import pallas as pl
from jax.experimental.pallas import tpu as pltpu
from jax.sharding import PartitionSpec as P

HD = 128
VMEM_STREAM = 60 * 1024 * 1024
VMEM_WHOLE = 24 * 1024 * 1024


beta_first = 0.9
beta_second = 0.95
learn_rate = 0.0003
weight_decay = 0.1
adam_epsilon = 1e-08
first_fix = 1.0 - 0.9**40
second_fix = 1.0 - 0.95**40


def optimizer_kernel(
    place, cached, master, moment, second, grad, master_out, moment_out, second_out, cache_out
):
    moment_new = beta_first * moment[...] + (1.0 - beta_first) * grad[...]
    second_new = beta_second * second[...] + (1.0 - beta_second) * grad[...] * grad[...]
    update = moment_new / first_fix / (jnp.sqrt(second_new / second_fix) + adam_epsilon)
    master_new = master[...] - learn_rate * (update + weight_decay * master[...])
    moment_out[...] = moment_new
    second_out[...] = second_new
    master_out[...] = master_new
    for start in range(0, cached.shape[1], HD):
        block = slice(start, start + HD)
        own_cache = cached[:, block].astype(jnp.float32)
        delta = master_new[:, block] - own_cache
        largest = jnp.max(jnp.abs(delta), axis=1, keepdims=True)
        scale = (largest + 1e-06).astype(jnp.bfloat16).astype(jnp.float32)
        codes = (delta / scale).astype(jnp.bfloat16)
        cache_out[:, block] = (own_cache + codes.astype(jnp.float32) * scale).astype(jnp.bfloat16)


def optimizer(cached, master, moment, second, grad):
    rows, cols = master.shape
    step = min(rows, 256)
    steps = rows // step
    own = pl.BlockSpec((step, cols), lambda i, place: (i, 0))
    full = jax.ShapeDtypeStruct((rows, cols), jnp.float32)
    return pl.pallas_call(
        optimizer_kernel,
        grid_spec=pltpu.PrefetchScalarGridSpec(
            num_scalar_prefetch=1,
            grid=(steps,),
            in_specs=[pl.BlockSpec((step, cols), lambda i, place: (place[0] * steps + i, 0))]
            + [own] * 4,
            out_specs=[own] * 4,
        ),
        out_shape=[full, full, full, jax.ShapeDtypeStruct((rows, cols), jnp.bfloat16)],
        cost_estimate=pl.CostEstimate(
            flops=40 * rows * cols, bytes_accessed=32 * rows * cols, transcendentals=rows * cols
        ),
        compiler_params=pltpu.CompilerParams(vmem_limit_bytes=VMEM_STREAM),
        name="optimizer",
    )(lax.axis_index("dp").astype(jnp.int32).reshape(1), cached, master, moment, second, grad)


def on_chip(kernel, place, arrays, out_shape, flops, name):
    vmem = pl.BlockSpec(memory_space=pltpu.VMEM)
    size = sum(a.size * a.dtype.itemsize for a in arrays)
    size += sum(s.size * s.dtype.itemsize for s in out_shape)
    return pl.pallas_call(
        kernel,
        in_specs=[pl.BlockSpec(memory_space=pltpu.SMEM)] + [vmem] * len(arrays),
        out_specs=[vmem] * len(out_shape),
        out_shape=out_shape,
        cost_estimate=pl.CostEstimate(flops=flops, bytes_accessed=size, transcendentals=0),
        compiler_params=pltpu.CompilerParams(vmem_limit_bytes=VMEM_WHOLE),
        name=name,
    )(place, *arrays)


def fetch_chunk(place, chunks, chunk, sem):
    for n, source in enumerate(chunks):

        @pl.when(place[2] == n)
        def _():
            pltpu.make_async_copy(source, chunk, sem).start()

    return pltpu.make_async_copy(chunks[0], chunk, sem)


def fetch_rows(place, cached, rows, sem):
    height = rows.shape[0]
    start = pl.multiple_of(place[0] * height, height)
    copy = pltpu.make_async_copy(cached.at[pl.ds(start, height), :], rows, sem)
    copy.start()
    return copy


def absorb_kernel(n_chunks, place, *refs):
    chunks, (total, cached) = refs[:n_chunks], refs[n_chunks : n_chunks + 2]
    total_out, held, chunk, rows, turned, sems = refs[-6:]
    chunk_copy = fetch_chunk(place, chunks, chunk, sems.at[0])
    rows_copy = fetch_rows(place, cached, rows, sems.at[1])
    chunk_copy.wait()
    turned[...] = chunk[...].T
    keep = pltpu.make_async_copy(turned, held.at[place[1]], sems.at[2])
    keep.start()
    rows_copy.wait()
    total_out[...] = total[...] + jnp.dot(
        chunk[...], rows[...], preferred_element_type=jnp.float32
    )
    keep.wait()


def absorb_place(index, which, n_chunks):
    inside = (index >= 0) & (index < n_chunks)
    return jnp.stack(
        [jnp.clip(index, 0, n_chunks - 1), jnp.where(inside, index, n_chunks), which]
    ).astype(jnp.int32)


def absorb_scratch(chunk, cached, n_sems):
    length, feats = chunk.shape
    return [
        pltpu.VMEM((length, feats), chunk.dtype),
        pltpu.VMEM((feats, cached.shape[1]), cached.dtype),
        pltpu.VMEM((feats, length), chunk.dtype),
        pltpu.SemaphoreType.DMA((n_sems,)),
    ]


def absorb(chunks, which, index, cached, total, held, n_chunks):
    length, feats = chunks[0].shape
    cols = cached.shape[1]
    shape = jax.ShapeDtypeStruct((8 * n_chunks, feats, length), chunks[0].dtype)
    vmem, anywhere = pl.BlockSpec(memory_space=pltpu.VMEM), pl.BlockSpec(memory_space=pl.ANY)
    return pl.pallas_call(
        functools.partial(absorb_kernel, len(chunks)),
        in_specs=[pl.BlockSpec(memory_space=pltpu.SMEM)]
        + [anywhere] * len(chunks)
        + [vmem, anywhere]
        + ([] if held is None else [anywhere]),
        out_specs=[vmem, anywhere],
        out_shape=[jax.ShapeDtypeStruct(total.shape, jnp.float32), shape],
        scratch_shapes=absorb_scratch(chunks[0], cached, 3),
        input_output_aliases={} if held is None else {3 + len(chunks): 1},
        cost_estimate=pl.CostEstimate(
            flops=2 * length * feats * cols,
            bytes_accessed=4 * length * feats + 2 * feats * cols,
            transcendentals=0,
        ),
        compiler_params=pltpu.CompilerParams(vmem_limit_bytes=VMEM_STREAM),
        name="absorb",
    )(
        absorb_place(index, which, n_chunks),
        *chunks,
        total,
        cached,
        *([] if held is None else [held]),
    )


def attend_kernel(n_chunks, place, order, *refs):
    chunks, refs = refs[:n_chunks], refs[n_chunks:]
    total, cached, _, allowed, queries_in, d_out_in = refs[:6]
    held, d_queries, d_projected, sent, kept, *refs = refs[6:]
    chunk, rows, turned, sems, queries, d_out, buffer, part_sems = refs
    chunk_copy = fetch_chunk(place, chunks, chunk, sems.at[0])
    rows_copy = fetch_rows(place, cached, rows, sems.at[1])
    others = [
        pltpu.make_async_copy(queries_in, queries, sems.at[3]),
        pltpu.make_async_copy(d_out_in, d_out, sems.at[4]),
    ]
    for copy in others:
        copy.start()
    chunk_copy.wait()
    turned[...] = chunk[...].T
    keep = pltpu.make_async_copy(turned, held.at[place[1]], sems.at[2])
    keep.start()
    rows_copy.wait()
    projected = (
        total[...] + jnp.dot(chunk[...], rows[...], preferred_element_type=jnp.float32)
    ).astype(jnp.bfloat16)
    seen = allowed[...] > 0
    for copy in others:
        copy.wait()
    factor = 1.0 / math.sqrt(HD)
    across = (((1,), (1,)), ((), ()))
    heads = projected.shape[1] // (2 * HD)
    group = queries.shape[1] // HD // heads
    for head in range(heads):
        start = 2 * HD * head
        keys = projected[:, start : start + HD]
        values = projected[:, start + HD : start + 2 * HD]
        d_keys = jnp.zeros(keys.shape, jnp.float32)
        d_values = jnp.zeros(keys.shape, jnp.float32)
        for g in range(head * group, (head + 1) * group):
            if g == heads * group // 2:
                keep.wait()
                copies = fetch_parts(order, held, range(4), buffer, part_sems)
            columns = slice(g * HD, (g + 1) * HD)
            query, grad = queries[:, columns], d_out[:, columns]
            scores = (
                lax.dot_general(keys, query, across, preferred_element_type=jnp.float32) * factor
            )
            scores = jnp.where(seen, scores, -1e30)
            weights = jnp.exp(scores - jnp.max(scores, axis=0, keepdims=True))
            probs = weights / jnp.sum(weights, axis=0, keepdims=True)
            probs_low = probs.astype(jnp.bfloat16)
            d_probs = lax.dot_general(values, grad, across, preferred_element_type=jnp.float32)
            rowdot = jnp.sum(probs_low.astype(jnp.float32) * d_probs, axis=0, keepdims=True)
            d_scores = (probs * (d_probs - rowdot) * factor).astype(jnp.bfloat16)
            d_queries[:, columns] = lax.dot_general(
                d_scores, keys, (((0,), (0,)), ((), ())), preferred_element_type=jnp.float32
            ).astype(jnp.bfloat16)
            d_keys = d_keys + jnp.dot(d_scores, query, preferred_element_type=jnp.float32)
            d_values = d_values + jnp.dot(probs_low, grad, preferred_element_type=jnp.float32)
        d_projected[:, start : start + HD] = d_keys.astype(jnp.bfloat16)
        d_projected[:, start + HD : start + 2 * HD] = d_values.astype(jnp.bfloat16)

    def give(g, side, position, here, part):
        out = (sent, kept)[g]
        out[2 * side + position, here, :] = part.astype(out.dtype)

    weight_products(copies, (SENT, KEPT), buffer, d_projected, give)


def attend(chunks, which, index, cached, total, held, queries, d_out, allowed, order, n_chunks):
    feats, length = held.shape[1:]
    parts = jax.ShapeDtypeStruct((4, feats // 2, total.shape[1] // 2), jnp.bfloat16)
    vmem, anywhere = pl.BlockSpec(memory_space=pltpu.VMEM), pl.BlockSpec(memory_space=pl.ANY)
    return pl.pallas_call(
        functools.partial(attend_kernel, len(chunks)),
        in_specs=[pl.BlockSpec(memory_space=pltpu.SMEM)] * 2
        + [anywhere] * len(chunks)
        + [vmem, anywhere, anywhere, vmem, anywhere, anywhere],
        out_specs=[anywhere] + [vmem] * 4,
        out_shape=[
            jax.ShapeDtypeStruct(held.shape, held.dtype),
            jax.ShapeDtypeStruct(queries.shape, jnp.bfloat16),
            jax.ShapeDtypeStruct(total.shape, jnp.bfloat16),
            parts,
            parts,
        ],
        scratch_shapes=absorb_scratch(chunks[0], cached, 5)
        + [
            pltpu.VMEM(queries.shape, queries.dtype),
            pltpu.VMEM(d_out.shape, d_out.dtype),
            pltpu.VMEM((4, feats // 2, length), held.dtype),
            pltpu.SemaphoreType.DMA((4,)),
        ],
        input_output_aliases={4 + len(chunks): 0},
        cost_estimate=pl.CostEstimate(
            flops=12 * allowed.size * queries.shape[1],
            bytes_accessed=8 * queries.size,
            transcendentals=allowed.size * queries.shape[1] // HD,
        ),
        compiler_params=pltpu.CompilerParams(vmem_limit_bytes=VMEM_STREAM),
        name="attend",
    )(
        absorb_place(index, which, n_chunks),
        order,
        *chunks,
        total,
        cached,
        held,
        allowed,
        queries,
        d_out,
    )


SENT = ((0, 0, 0), (0, 1, 0), (1, 0, 1), (2, 1, 1))
KEPT = ((1, 1, 0), (2, 0, 0), (3, 0, 1), (3, 1, 1))


def fetch_parts(place, held, chunks, buffer, sems):
    rows = buffer.shape[1]
    start = pl.multiple_of(place[4] * rows, rows)
    copies = {}
    for chunk in chunks:
        copies[chunk] = pltpu.make_async_copy(
            held.at[place[chunk], pl.ds(start, rows), :], buffer.at[chunk], sems.at[chunk]
        )
        copies[chunk].start()
    return copies


def weight_products(copies, groups, buffer, d_projected, give):
    rows = buffer.shape[1]
    half = d_projected.shape[1] // 2
    block = min(rows, 256)
    for chunk, copy in copies.items():
        copy.wait()
        wanted = [
            (g, side, position)
            for g, group in enumerate(groups)
            for which, side, position in group
            if which == chunk
        ]
        first, last = min(w[1] for w in wanted), max(w[1] for w in wanted)
        for r in range(0, rows, block):
            here = slice(r, r + block)
            total = jnp.dot(
                buffer[chunk, here, :],
                d_projected[:, first * half : (last + 1) * half],
                preferred_element_type=jnp.float32,
            )
            for g, side, position in wanted:
                part = total[:, (side - first) * half : (side - first + 1) * half]
                give(g, side, position, here, part)


def weight_kernel(group, place, held, d_projected, *refs):
    *added, out_a, out_b, buffer, sems = refs
    copies = fetch_parts(place, held, sorted({part[0] for part in group}), buffer, sems)

    def give(_, side, position, here, part):
        if added:
            part = part + added[0][2 * side + position, here, :].astype(jnp.float32)
        out = (out_a, out_b)[side]
        out[position, here, :] = part.astype(out.dtype)

    weight_products(copies, (group,), buffer, d_projected, give)


def weight_parts(held, d_projected, place, group, added, dtype, name):
    length, cols = d_projected.shape
    rows = held.shape[1] // 2
    vmem = pl.BlockSpec(memory_space=pltpu.VMEM)
    return pl.pallas_call(
        functools.partial(weight_kernel, group),
        in_specs=[pl.BlockSpec(memory_space=pltpu.SMEM), pl.BlockSpec(memory_space=pl.ANY)]
        + [vmem] * (1 + len(added)),
        out_specs=[vmem] * 2,
        out_shape=[jax.ShapeDtypeStruct((2, rows, cols // 2), dtype)] * 2,
        scratch_shapes=[
            pltpu.VMEM((4, rows, length), held.dtype),
            pltpu.SemaphoreType.DMA((4,)),
        ],
        cost_estimate=pl.CostEstimate(
            flops=4 * length * rows * cols, bytes_accessed=8 * rows * cols, transcendentals=0
        ),
        compiler_params=pltpu.CompilerParams(vmem_limit_bytes=VMEM_WHOLE),
        name=name,
    )(place, held, d_projected, *added)


def add_kernel(place, own_a, own_b, other, out_a, out_b):
    depth = own_a.shape[0]
    for side, (own, out) in enumerate(((own_a, out_a), (own_b, out_b))):
        other_here = other[side * depth : (side + 1) * depth]
        out[...] = (own[...] + other_here.astype(jnp.float32)).astype(out.dtype)


def combine_kernel(place, keep_a, got_a, keep_b, got_b, out_a, out_b):
    for keep, got, out in ((keep_a, got_a, out_a), (keep_b, got_b, out_b)):
        out[...] = (keep[0] + got[0].astype(jnp.float32)).astype(out.dtype)


def finish_kernel(place, keep_a, got_a, keep_b, got_b, last_a, last_b, out):
    half = last_a.shape[1]
    sides = ((keep_a, got_a, last_a), (keep_b, got_b, last_b))
    for side, (keep, got, last) in enumerate(sides):
        total = keep[1] + got[1].astype(jnp.float32) + last[...].astype(jnp.float32)
        out[:, side * half : (side + 1) * half] = total


def plane():
    index = lax.axis_index("dp").astype(jnp.int32)

    def swap(value, bit):
        return lax.ppermute(value, "dp", [(i, i ^ bit) for i in range(8)])

    return index % 2, (index // 2) % 2, index // 4, swap


def weight_orders():
    core, x, y, _ = plane()
    chunks = [3 - x - 2 * y, 1 - x + 2 * y, x + 2 - 2 * y, x + 2 * y]
    return [jnp.stack(chunks + [half]) for half in (1 - core, core)]


def weight_sum(held, d_projected, order, sent, kept, pieces, beside):
    swap = plane()[3]
    rows, cols = held.shape[1] // 2, d_projected.shape[1]
    none = jnp.zeros((1,), jnp.int32)
    sent, kept = swap(sent, 1), swap(kept, 1)
    own = weight_parts(held, d_projected, order, SENT, [], jnp.float32, "weight_send")
    shape = jax.ShapeDtypeStruct(own[0].shape, jnp.bfloat16)
    send_a, send_b = on_chip(
        add_kernel, none, list(own) + [sent], [shape] * 2, 2 * cols * rows, "weight_add"
    )
    got_a, got_b = swap(send_a, 2), swap(send_b, 4)
    keep_a, keep_b = weight_parts(
        held, d_projected, order, KEPT, [kept], jnp.float32, "weight_keep"
    )
    got_a, got_b, pieces, beside = lax.optimization_barrier((got_a, got_b, pieces, beside))

    small = jax.ShapeDtypeStruct((rows, cols // 2), jnp.bfloat16)
    arrays = [keep_a, got_a, keep_b, got_b]
    last_a, last_b = on_chip(
        combine_kernel, none, arrays, [small] * 2, cols * rows, "weight_combine"
    )
    last = [swap(last_a, 4), swap(last_b, 2)]

    def finish(ready):
        ended, ready = lax.optimization_barrier((last, ready))
        (total,) = on_chip(
            finish_kernel,
            none,
            arrays + ended,
            [jax.ShapeDtypeStruct((rows, cols), jnp.float32)],
            2 * cols * rows,
            "weight_finish",
        )
        return total, ready

    return finish, pieces, beside


class PlaneGather:
    def __init__(self, own, split):
        self.got, self.split = {0: own}, split

    def first(self):
        own, swap = self.got[0], plane()[3]
        self.got.update({bit: swap(own, bit) for bit in (2, 4, 1)})
        return self.got

    def second(self):
        got, swap = self.got, plane()[3]
        self.far = [swap(got[4][: self.split], 2), swap(got[2][self.split :], 4)]
        got[3], got[5] = swap(got[2], 1), swap(got[4], 1)
        return self.far, got[3], got[5]

    def third(self):
        swap = plane()[3]
        self.far_other = [swap(value, 1) for value in self.far]
        return self.far_other

    def where(self, bits):
        return lax.axis_index("dp").astype(jnp.int32) ^ jnp.array(bits, dtype=jnp.int32)

    def lay(self, height, rows):
        arrays = [self.got[k] for k in range(6)]
        return place_rows(arrays, self.where(list(range(6))), height, rows, [])

    def lay_far(self, height, laid):
        arrays = [self.far[0], self.far_other[0]]
        return place_rows(arrays, self.where([6, 7]), height, laid.shape[0], [laid])

    def last(self):
        arrays = [self.got[k] for k in range(6)] + [self.far[1], self.far_other[1]]
        return arrays, self.where(list(range(8)))


def place_rows_kernel(height, n_arrays, place, *refs):
    arrays, (out, sems) = refs[:n_arrays], refs[-2:]
    copies = []
    for k, array in enumerate(arrays):
        start = pl.multiple_of(place[k] * height, height)
        copies.append(
            pltpu.make_async_copy(
                array.at[pl.ds(0, height), :], out.at[pl.ds(start, height), :], sems.at[k]
            )
        )
    for copy in copies:
        copy.start()
    for copy in copies:
        copy.wait()


def place_rows(arrays, place, height, rows, into):
    cols = arrays[0].shape[1]
    anywhere = pl.BlockSpec(memory_space=pl.ANY)
    return pl.pallas_call(
        functools.partial(place_rows_kernel, height, len(arrays)),
        in_specs=[pl.BlockSpec(memory_space=pltpu.SMEM)]
        + [pl.BlockSpec(memory_space=pltpu.VMEM)] * len(arrays)
        + [anywhere] * len(into),
        out_specs=anywhere,
        out_shape=jax.ShapeDtypeStruct((rows, cols), arrays[0].dtype),
        scratch_shapes=[pltpu.SemaphoreType.DMA((len(arrays),))],
        input_output_aliases={1 + len(arrays): 0} if into else {},
        cost_estimate=pl.CostEstimate(
            flops=0, bytes_accessed=4 * height * cols * len(arrays), transcendentals=0
        ),
        compiler_params=pltpu.CompilerParams(vmem_limit_bytes=VMEM_WHOLE),
        name="place_rows",
    )(place, *arrays, *into)


def input_kernel(n_blocks, place, *refs):
    *arrays, out = refs
    pieces, here, rows = arrays[:n_blocks], arrays[n_blocks], arrays[n_blocks + 1 :]
    share = out.shape[1] // len(rows)
    for k, held in enumerate(rows):
        start = pl.multiple_of(place[k] * share, share)
        first = held.shape[0] - n_blocks * share
        total = jnp.zeros((out.shape[0], share), jnp.float32)
        for s, piece in enumerate(pieces):
            if s:
                block = held[first + s * share : first + (s + 1) * share, :]
            else:
                block = here[pl.ds(start, share), :]
            total = total + lax.dot_general(
                piece[...], block, (((1,), (1,)), ((), ())), preferred_element_type=jnp.float32
            )
        out[:, pl.ds(start, share)] = total.astype(out.dtype)


def input_gradient(pieces, here, arrays, place):
    length, cols = pieces[0].shape
    feats = here.shape[0]
    (d_tokens,) = on_chip(
        functools.partial(input_kernel, len(pieces)),
        place,
        pieces + [here] + arrays,
        [jax.ShapeDtypeStruct((length, feats), jnp.bfloat16)],
        2 * length * feats * cols * len(pieces),
        "input_gradient",
    )
    return d_tokens


def make_body(n_dp, n_z):
    tuned = n_dp == 8 and n_z == 4

    def pair(value, s):
        return lax.ppermute(value, "tensor", [(z, z ^ s) for z in range(n_z)])

    def body(tokens, queries, d_out, segments, cached, master, moment, second, grad):
        me_dp = lax.axis_index("dp").astype(jnp.int32)
        me_z = lax.axis_index("tensor").astype(jnp.int32)
        length, feats = tokens.shape
        cols = cached.shape[1]

        master_new, moment_new, second_new, own_cache = optimizer(
            cached, master, moment, second, grad
        )

        share = feats // n_dp

        def block_for(z):
            return lax.dynamic_slice_in_dim(cached, z * feats + me_dp * share, share, 0)

        blocks = [pair(block_for(me_z ^ s), s) for s in range(1, n_z)]
        here = lax.dynamic_slice_in_dim(cached, me_z * feats, feats, 0)

        doc_ids = segments[0]
        position = jnp.arange(length)
        allowed = (doc_ids[:, None] == doc_ids[None, :]) & (position[:, None] <= position[None, :])
        allowed = allowed.astype(jnp.float32)

        total = jnp.zeros((length, cols), jnp.float32)
        zero = 0 * me_z
        orders = weight_orders() if tuned else [jnp.zeros((5,), jnp.int32)]
        total, held = absorb([tokens], zero, me_z, cached, total, None, n_z)
        if tuned:
            gather = PlaneGather(jnp.concatenate([own_cache] + blocks, axis=0), own_cache.shape[0])
        from_low, from_high = tokens, tokens
        for s in range(1, n_z):
            low, high = me_z - s, me_z + s
            from_high = lax.ppermute(from_high, "tensor", [(z + 1, z) for z in range(n_z - s)])
            from_low = lax.ppermute(
                from_low, "tensor", [(z, z + 1) for z in range(s - 1, n_z - 1)]
            )
            if tuned:
                if s == 1:
                    held, allowed, orders, here = lax.optimization_barrier(
                        (held, allowed, orders, here)
                    )
                    rounds = None
                elif s == 2:
                    rounds = gather.first()
                else:
                    rounds = gather.second()
                    laid = gather.lay(own_cache.shape[0], cached.shape[0])
                    rounds = (rounds, laid)
                if s > 1:
                    from_low, from_high, held, rounds = lax.optimization_barrier(
                        (from_low, from_high, held, rounds)
                    )
                if s == 2:
                    gather.got = rounds
                if s == 3:
                    (gather.far, gather.got[3], gather.got[5]), laid = rounds
            chunks, which = [from_low, from_high], (me_z < s).astype(jnp.int32)
            index = jnp.where(me_z < s, high, low)
            if 2 * s < n_z:
                total, held = absorb([from_low], zero, low, cached, total, held, n_z)
                chunks, which, index = [from_high], zero, high
            if s < n_z - 1:
                total, held = absorb(chunks, which, index, cached, total, held, n_z)

        held, d_queries, d_projected, sent, kept = attend(
            chunks, which, index, cached, total, held, queries, d_out, allowed, orders[0], n_z
        )

        pieces = [d_projected] + [pair(d_projected, s) for s in range(1, n_z)]
        if tuned:
            sent, gather.far_other = lax.optimization_barrier((sent, gather.third()))
            new_cache = gather.lay_far(own_cache.shape[0], laid)
            finish, pieces, new_cache = weight_sum(
                held, d_projected, orders[1], sent, kept, pieces, new_cache
            )
            new_grad, d_tokens = finish(input_gradient(pieces, here, *gather.last()))
        else:
            new_cache = lax.all_gather(own_cache, "dp", axis=0, tiled=True)
            rows = lax.all_gather(jnp.stack([block_for(me_z)] + blocks), "dp", axis=0)
            d_tokens = jnp.einsum(
                "slc,ksfc->lkf", jnp.stack(pieces), rows, preferred_element_type=jnp.float32
            )
            d_tokens = d_tokens.astype(jnp.bfloat16).reshape(length, feats)
            partial = lax.dot_general(
                held[:n_z].reshape(n_z * feats, length),
                d_projected,
                (((1,), (0,)), ((), ())),
                preferred_element_type=jnp.float32,
            )
            new_grad = lax.psum_scatter(
                partial.astype(jnp.bfloat16), "dp", scatter_dimension=0, tiled=True
            ).astype(jnp.float32)
        return (master_new, moment_new, second_new, new_cache, new_grad, d_queries, d_tokens)

    return body


def solution(mesh):
    in_specs = (
        P("dp", "tensor"),
        P("dp", "tensor"),
        P("dp", "tensor"),
        P("dp", None),
        P(None, "tensor"),
        P("dp", "tensor"),
        P("dp", "tensor"),
        P("dp", "tensor"),
        P("dp", "tensor"),
    )
    out_specs = (
        P("dp", "tensor"),
        P("dp", "tensor"),
        P("dp", "tensor"),
        P(None, "tensor"),
        P("dp", "tensor"),
        P("dp", "tensor"),
        P("dp", "tensor"),
    )
    body = make_body(mesh.shape["dp"], mesh.shape["tensor"])
    return jax.shard_map(body, mesh=mesh, in_specs=in_specs, out_specs=out_specs, check_vma=False)
```

```python
import functools
import math

import jax
import jax.numpy as jnp
from jax import lax
from jax.experimental import pallas as pl
from jax.experimental.pallas import tpu as pltpu
from jax.sharding import PartitionSpec as P

HD = 128
VMEM_STREAM = 60 * 1024 * 1024
VMEM_WHOLE = 24 * 1024 * 1024


beta_first = 0.9
beta_second = 0.95
learn_rate = 0.0003
weight_decay = 0.1
adam_epsilon = 1e-08
first_fix = 1.0 - 0.9**40
second_fix = 1.0 - 0.95**40


def optimizer_kernel(
    place, cached, master, moment, second, grad, master_out, moment_out, second_out, cache_out
):
    moment_new = beta_first * moment[...] + (1.0 - beta_first) * grad[...]
    second_new = beta_second * second[...] + (1.0 - beta_second) * grad[...] * grad[...]
    update = moment_new / first_fix / (jnp.sqrt(second_new / second_fix) + adam_epsilon)
    master_new = master[...] - learn_rate * (update + weight_decay * master[...])
    moment_out[...] = moment_new
    second_out[...] = second_new
    master_out[...] = master_new
    for start in range(0, cached.shape[1], HD):
        block = slice(start, start + HD)
        own_cache = cached[:, block].astype(jnp.float32)
        delta = master_new[:, block] - own_cache
        largest = jnp.max(jnp.abs(delta), axis=1, keepdims=True)
        scale = (largest + 1e-06).astype(jnp.bfloat16).astype(jnp.float32)
        codes = (delta / scale).astype(jnp.bfloat16)
        cache_out[:, block] = (own_cache + codes.astype(jnp.float32) * scale).astype(jnp.bfloat16)


def optimizer(cached, master, moment, second, grad):
    rows, cols = master.shape
    step = min(rows, 256)
    steps = rows // step
    own = pl.BlockSpec((step, cols), lambda i, place: (i, 0))
    full = jax.ShapeDtypeStruct((rows, cols), jnp.float32)
    return pl.pallas_call(
        optimizer_kernel,
        grid_spec=pltpu.PrefetchScalarGridSpec(
            num_scalar_prefetch=1,
            grid=(steps,),
            in_specs=[pl.BlockSpec((step, cols), lambda i, place: (place[0] * steps + i, 0))]
            + [own] * 4,
            out_specs=[own] * 4,
        ),
        out_shape=[full, full, full, jax.ShapeDtypeStruct((rows, cols), jnp.bfloat16)],
        cost_estimate=pl.CostEstimate(
            flops=40 * rows * cols, bytes_accessed=32 * rows * cols, transcendentals=rows * cols
        ),
        compiler_params=pltpu.CompilerParams(vmem_limit_bytes=VMEM_STREAM),
        name="optimizer",
    )(lax.axis_index("dp").astype(jnp.int32).reshape(1), cached, master, moment, second, grad)


def on_chip(kernel, place, arrays, out_shape, flops, name):
    vmem = pl.BlockSpec(memory_space=pltpu.VMEM)
    size = sum(a.size * a.dtype.itemsize for a in arrays)
    size += sum(s.size * s.dtype.itemsize for s in out_shape)
    return pl.pallas_call(
        kernel,
        in_specs=[pl.BlockSpec(memory_space=pltpu.SMEM)] + [vmem] * len(arrays),
        out_specs=[vmem] * len(out_shape),
        out_shape=out_shape,
        cost_estimate=pl.CostEstimate(flops=flops, bytes_accessed=size, transcendentals=0),
        compiler_params=pltpu.CompilerParams(vmem_limit_bytes=VMEM_WHOLE),
        name=name,
    )(place, *arrays)


def fetch_chunk(place, chunks, chunk, sem):
    for n, source in enumerate(chunks):

        @pl.when(place[2] == n)
        def _():
            pltpu.make_async_copy(source, chunk, sem).start()

    return pltpu.make_async_copy(chunks[0], chunk, sem)


def fetch_rows(place, cached, rows, sem):
    height = rows.shape[0]
    start = pl.multiple_of(place[0] * height, height)
    copy = pltpu.make_async_copy(cached.at[pl.ds(start, height), :], rows, sem)
    copy.start()
    return copy


def absorb_kernel(n_chunks, place, *refs):
    chunks, (total, cached) = refs[:n_chunks], refs[n_chunks : n_chunks + 2]
    total_out, held, chunk, rows, turned, sems = refs[-6:]
    chunk_copy = fetch_chunk(place, chunks, chunk, sems.at[0])
    rows_copy = fetch_rows(place, cached, rows, sems.at[1])
    chunk_copy.wait()
    turned[...] = chunk[...].T
    keep = pltpu.make_async_copy(turned, held.at[place[1]], sems.at[2])
    keep.start()
    rows_copy.wait()
    total_out[...] = total[...] + jnp.dot(
        chunk[...], rows[...], preferred_element_type=jnp.float32
    )
    keep.wait()


def absorb_place(index, which, n_chunks):
    inside = (index >= 0) & (index < n_chunks)
    return jnp.stack(
        [jnp.clip(index, 0, n_chunks - 1), jnp.where(inside, index, n_chunks), which]
    ).astype(jnp.int32)


def absorb_scratch(chunk, cached, n_sems):
    length, feats = chunk.shape
    return [
        pltpu.VMEM((length, feats), chunk.dtype),
        pltpu.VMEM((feats, cached.shape[1]), cached.dtype),
        pltpu.VMEM((feats, length), chunk.dtype),
        pltpu.SemaphoreType.DMA((n_sems,)),
    ]


def absorb(chunks, which, index, cached, total, held, n_chunks):
    length, feats = chunks[0].shape
    cols = cached.shape[1]
    shape = jax.ShapeDtypeStruct((8 * n_chunks, feats, length), chunks[0].dtype)
    vmem, anywhere = pl.BlockSpec(memory_space=pltpu.VMEM), pl.BlockSpec(memory_space=pl.ANY)
    return pl.pallas_call(
        functools.partial(absorb_kernel, len(chunks)),
        in_specs=[pl.BlockSpec(memory_space=pltpu.SMEM)]
        + [anywhere] * len(chunks)
        + [vmem, anywhere]
        + ([] if held is None else [anywhere]),
        out_specs=[vmem, anywhere],
        out_shape=[jax.ShapeDtypeStruct(total.shape, jnp.float32), shape],
        scratch_shapes=absorb_scratch(chunks[0], cached, 3),
        input_output_aliases={} if held is None else {3 + len(chunks): 1},
        cost_estimate=pl.CostEstimate(
            flops=2 * length * feats * cols,
            bytes_accessed=4 * length * feats + 2 * feats * cols,
            transcendentals=0,
        ),
        compiler_params=pltpu.CompilerParams(vmem_limit_bytes=VMEM_STREAM),
        name="absorb",
    )(
        absorb_place(index, which, n_chunks),
        *chunks,
        total,
        cached,
        *([] if held is None else [held]),
    )


def attend_kernel(n_chunks, place, order, *refs):
    chunks, refs = refs[:n_chunks], refs[n_chunks:]
    total, cached, _, allowed, queries_in, d_out_in = refs[:6]
    held, d_queries, d_projected, sent, kept, *refs = refs[6:]
    chunk, rows, turned, sems, queries, d_out, buffer, part_sems = refs
    chunk_copy = fetch_chunk(place, chunks, chunk, sems.at[0])
    rows_copy = fetch_rows(place, cached, rows, sems.at[1])
    others = [
        pltpu.make_async_copy(queries_in, queries, sems.at[3]),
        pltpu.make_async_copy(d_out_in, d_out, sems.at[4]),
    ]
    for copy in others:
        copy.start()
    chunk_copy.wait()
    turned[...] = chunk[...].T
    keep = pltpu.make_async_copy(turned, held.at[place[1]], sems.at[2])
    keep.start()
    rows_copy.wait()
    projected = (
        total[...] + jnp.dot(chunk[...], rows[...], preferred_element_type=jnp.float32)
    ).astype(jnp.bfloat16)
    seen = allowed[...] > 0
    for copy in others:
        copy.wait()
    factor = 1.0 / math.sqrt(HD)
    across = (((1,), (1,)), ((), ()))
    heads = projected.shape[1] // (2 * HD)
    group = queries.shape[1] // HD // heads
    for head in range(heads):
        start = 2 * HD * head
        keys = projected[:, start : start + HD]
        values = projected[:, start + HD : start + 2 * HD]
        d_keys = jnp.zeros(keys.shape, jnp.float32)
        d_values = jnp.zeros(keys.shape, jnp.float32)
        for g in range(head * group, (head + 1) * group):
            if g == heads * group // 2:
                keep.wait()
                copies = fetch_parts(order, held, range(4), buffer, part_sems)
            columns = slice(g * HD, (g + 1) * HD)
            query, grad = queries[:, columns], d_out[:, columns]
            scores = (
                lax.dot_general(keys, query, across, preferred_element_type=jnp.float32) * factor
            )
            scores = jnp.where(seen, scores, -1e30)
            weights = jnp.exp(scores - jnp.max(scores, axis=0, keepdims=True))
            probs = weights / jnp.sum(weights, axis=0, keepdims=True)
            probs_low = probs.astype(jnp.bfloat16)
            d_probs = lax.dot_general(values, grad, across, preferred_element_type=jnp.float32)
            rowdot = jnp.sum(probs_low.astype(jnp.float32) * d_probs, axis=0, keepdims=True)
            d_scores = (probs * (d_probs - rowdot) * factor).astype(jnp.bfloat16)
            d_queries[:, columns] = lax.dot_general(
                d_scores, keys, (((0,), (0,)), ((), ())), preferred_element_type=jnp.float32
            ).astype(jnp.bfloat16)
            d_keys = d_keys + jnp.dot(d_scores, query, preferred_element_type=jnp.float32)
            d_values = d_values + jnp.dot(probs_low, grad, preferred_element_type=jnp.float32)
        d_projected[:, start : start + HD] = d_keys.astype(jnp.bfloat16)
        d_projected[:, start + HD : start + 2 * HD] = d_values.astype(jnp.bfloat16)

    def give(g, side, position, here, part):
        out = (sent, kept)[g]
        out[2 * side + position, here, :] = part.astype(out.dtype)

    weight_products(copies, (SENT, KEPT), buffer, d_projected, give)


def attend(chunks, which, index, cached, total, held, queries, d_out, allowed, order, n_chunks):
    feats, length = held.shape[1:]
    parts = jax.ShapeDtypeStruct((4, feats // 2, total.shape[1] // 2), jnp.bfloat16)
    vmem, anywhere = pl.BlockSpec(memory_space=pltpu.VMEM), pl.BlockSpec(memory_space=pl.ANY)
    return pl.pallas_call(
        functools.partial(attend_kernel, len(chunks)),
        in_specs=[pl.BlockSpec(memory_space=pltpu.SMEM)] * 2
        + [anywhere] * len(chunks)
        + [vmem, anywhere, anywhere, vmem, anywhere, anywhere],
        out_specs=[anywhere] + [vmem] * 4,
        out_shape=[
            jax.ShapeDtypeStruct(held.shape, held.dtype),
            jax.ShapeDtypeStruct(queries.shape, jnp.bfloat16),
            jax.ShapeDtypeStruct(total.shape, jnp.bfloat16),
            parts,
            parts,
        ],
        scratch_shapes=absorb_scratch(chunks[0], cached, 5)
        + [
            pltpu.VMEM(queries.shape, queries.dtype),
            pltpu.VMEM(d_out.shape, d_out.dtype),
            pltpu.VMEM((4, feats // 2, length), held.dtype),
            pltpu.SemaphoreType.DMA((4,)),
        ],
        input_output_aliases={4 + len(chunks): 0},
        cost_estimate=pl.CostEstimate(
            flops=12 * allowed.size * queries.shape[1],
            bytes_accessed=8 * queries.size,
            transcendentals=allowed.size * queries.shape[1] // HD,
        ),
        compiler_params=pltpu.CompilerParams(vmem_limit_bytes=VMEM_STREAM),
        name="attend",
    )(
        absorb_place(index, which, n_chunks),
        order,
        *chunks,
        total,
        cached,
        held,
        allowed,
        queries,
        d_out,
    )


SENT = ((0, 0, 0), (0, 1, 0), (1, 0, 1), (2, 1, 1))
KEPT = ((1, 1, 0), (2, 0, 0), (3, 0, 1), (3, 1, 1))


def fetch_parts(place, held, chunks, buffer, sems):
    rows = buffer.shape[1]
    start = pl.multiple_of(place[4] * rows, rows)
    copies = {}
    for chunk in chunks:
        copies[chunk] = pltpu.make_async_copy(
            held.at[place[chunk], pl.ds(start, rows), :], buffer.at[chunk], sems.at[chunk]
        )
        copies[chunk].start()
    return copies


def weight_products(copies, groups, buffer, d_projected, give):
    rows = buffer.shape[1]
    half = d_projected.shape[1] // 2
    block = min(rows, 256)
    for chunk, copy in copies.items():
        copy.wait()
        wanted = [
            (g, side, position)
            for g, group in enumerate(groups)
            for which, side, position in group
            if which == chunk
        ]
        first, last = min(w[1] for w in wanted), max(w[1] for w in wanted)
        for r in range(0, rows, block):
            here = slice(r, r + block)
            total = jnp.dot(
                buffer[chunk, here, :],
                d_projected[:, first * half : (last + 1) * half],
                preferred_element_type=jnp.float32,
            )
            for g, side, position in wanted:
                part = total[:, (side - first) * half : (side - first + 1) * half]
                give(g, side, position, here, part)


def weight_kernel(group, place, held, d_projected, *refs):
    *added, out_a, out_b, buffer, sems = refs
    copies = fetch_parts(place, held, sorted({part[0] for part in group}), buffer, sems)

    def give(_, side, position, here, part):
        if added:
            part = part + added[0][2 * side + position, here, :].astype(jnp.float32)
        out = (out_a, out_b)[side]
        out[position, here, :] = part.astype(out.dtype)

    weight_products(copies, (group,), buffer, d_projected, give)


def weight_parts(held, d_projected, place, group, added, dtype, name):
    length, cols = d_projected.shape
    rows = held.shape[1] // 2
    vmem = pl.BlockSpec(memory_space=pltpu.VMEM)
    return pl.pallas_call(
        functools.partial(weight_kernel, group),
        in_specs=[pl.BlockSpec(memory_space=pltpu.SMEM), pl.BlockSpec(memory_space=pl.ANY)]
        + [vmem] * (1 + len(added)),
        out_specs=[vmem] * 2,
        out_shape=[jax.ShapeDtypeStruct((2, rows, cols // 2), dtype)] * 2,
        scratch_shapes=[
            pltpu.VMEM((4, rows, length), held.dtype),
            pltpu.SemaphoreType.DMA((4,)),
        ],
        cost_estimate=pl.CostEstimate(
            flops=4 * length * rows * cols, bytes_accessed=8 * rows * cols, transcendentals=0
        ),
        compiler_params=pltpu.CompilerParams(vmem_limit_bytes=VMEM_WHOLE),
        name=name,
    )(place, held, d_projected, *added)


def add_kernel(place, own_a, own_b, other, out_a, out_b):
    depth = own_a.shape[0]
    for side, (own, out) in enumerate(((own_a, out_a), (own_b, out_b))):
        other_here = other[side * depth : (side + 1) * depth]
        out[...] = (own[...] + other_here.astype(jnp.float32)).astype(out.dtype)


def combine_kernel(place, keep_a, got_a, keep_b, got_b, out_a, out_b):
    for keep, got, out in ((keep_a, got_a, out_a), (keep_b, got_b, out_b)):
        out[...] = (keep[0] + got[0].astype(jnp.float32)).astype(out.dtype)


def finish_kernel(place, keep_a, got_a, keep_b, got_b, last_a, last_b, out):
    half = last_a.shape[1]
    sides = ((keep_a, got_a, last_a), (keep_b, got_b, last_b))
    for side, (keep, got, last) in enumerate(sides):
        total = keep[1] + got[1].astype(jnp.float32) + last[...].astype(jnp.float32)
        out[:, side * half : (side + 1) * half] = total


def plane():
    index = lax.axis_index("dp").astype(jnp.int32)

    def swap(value, bit):
        return lax.ppermute(value, "dp", [(i, i ^ bit) for i in range(8)])

    return index % 2, (index // 2) % 2, index // 4, swap


def weight_orders():
    core, x, y, _ = plane()
    chunks = [3 - x - 2 * y, 1 - x + 2 * y, x + 2 - 2 * y, x + 2 * y]
    return [jnp.stack(chunks + [half]) for half in (1 - core, core)]


def weight_sum(held, d_projected, order, sent, kept, pieces, beside):
    swap = plane()[3]
    rows, cols = held.shape[1] // 2, d_projected.shape[1]
    none = jnp.zeros((1,), jnp.int32)
    sent, kept = swap(sent, 1), swap(kept, 1)
    own = weight_parts(held, d_projected, order, SENT, [], jnp.float32, "weight_send")
    shape = jax.ShapeDtypeStruct(own[0].shape, jnp.bfloat16)
    send_a, send_b = on_chip(
        add_kernel, none, list(own) + [sent], [shape] * 2, 2 * cols * rows, "weight_add"
    )
    got_a, got_b = swap(send_a, 2), swap(send_b, 4)
    keep_a, keep_b = weight_parts(
        held, d_projected, order, KEPT, [kept], jnp.float32, "weight_keep"
    )
    got_a, got_b, pieces, beside = lax.optimization_barrier((got_a, got_b, pieces, beside))

    small = jax.ShapeDtypeStruct((rows, cols // 2), jnp.bfloat16)
    arrays = [keep_a, got_a, keep_b, got_b]
    last_a, last_b = on_chip(
        combine_kernel, none, arrays, [small] * 2, cols * rows, "weight_combine"
    )
    last = [swap(last_a, 4), swap(last_b, 2)]

    def finish(ready):
        ended, ready = lax.optimization_barrier((last, ready))
        (total,) = on_chip(
            finish_kernel,
            none,
            arrays + ended,
            [jax.ShapeDtypeStruct((rows, cols), jnp.float32)],
            2 * cols * rows,
            "weight_finish",
        )
        return total, ready

    return finish, pieces, beside


class PlaneGather:
    def __init__(self, own_cache, own_rows):
        self.own = own_cache, own_rows
        self.both = jnp.concatenate([own_cache, own_rows], axis=0)

    def first(self):
        swap = plane()[3]
        return swap(self.own[1], 2), swap(self.own[0], 4), swap(self.both, 1)

    def second(self):
        swap = plane()[3]
        rows_x, cache_y, _ = self.got
        packs = (
            swap(jnp.concatenate([self.own[0], cache_y], axis=0), 2),
            swap(jnp.concatenate([self.own[1], rows_x], axis=0), 4),
        )
        return packs, (swap(rows_x, 1), swap(cache_y, 1))

    def third(self):
        swap = plane()[3]
        return swap(self.packs[0], 1), swap(self.packs[1], 1)

    def where(self, bits):
        return lax.axis_index("dp").astype(jnp.int32) ^ jnp.array(bits, dtype=jnp.int32)

    def lay(self, swapped, n_rows):
        arrays = [self.own[0], self.got[2], self.got[1], swapped[1]]
        return place_rows(arrays, [(k, 0) for k in range(4)], self.where([0, 1, 4, 5]),
                          self.own[0].shape[0], n_rows, [])

    def lay_rest(self, laid):
        height = self.own[0].shape[0]
        parts = [(0, 0), (0, height), (1, 0), (1, height)]
        arrays = [self.packs[0], self.packs_other[0]]
        return place_rows(
            arrays, parts, self.where([2, 6, 3, 7]), height, laid.shape[0], [laid]
        )

    def feature_rows(self):
        height, count = self.own[0].shape[0], self.own[1].shape[0]
        arrays = [self.own[1], self.got[2], self.got[0], self.swapped[0]]
        arrays += [self.packs[1], self.packs_other[1]]
        parts = [(0, 0), (1, height), (2, 0), (3, 0), (4, 0), (4, count), (5, 0), (5, count)]
        return arrays, parts, self.where([0, 1, 2, 3, 4, 6, 5, 7])


def place_rows_kernel(height, parts, place, *refs):
    out, sems = refs[-2:]
    copies = []
    for k, (which, row) in enumerate(parts):
        start = pl.multiple_of(place[k] * height, height)
        copies.append(
            pltpu.make_async_copy(
                refs[which].at[pl.ds(row, height), :],
                out.at[pl.ds(start, height), :],
                sems.at[k],
            )
        )
    for copy in copies:
        copy.start()
    for copy in copies:
        copy.wait()


def place_rows(arrays, parts, place, height, rows, into):
    cols = arrays[0].shape[1]
    anywhere = pl.BlockSpec(memory_space=pl.ANY)
    return pl.pallas_call(
        functools.partial(place_rows_kernel, height, parts),
        in_specs=[pl.BlockSpec(memory_space=pltpu.SMEM)]
        + [pl.BlockSpec(memory_space=pltpu.VMEM)] * len(arrays)
        + [anywhere] * len(into),
        out_specs=anywhere,
        out_shape=jax.ShapeDtypeStruct((rows, cols), arrays[0].dtype),
        scratch_shapes=[pltpu.SemaphoreType.DMA((len(parts),))],
        input_output_aliases={1 + len(arrays): 0} if into else {},
        cost_estimate=pl.CostEstimate(
            flops=0, bytes_accessed=4 * height * cols * len(parts), transcendentals=0
        ),
        compiler_params=pltpu.CompilerParams(vmem_limit_bytes=VMEM_WHOLE),
        name="place_rows",
    )(place, *arrays, *into)


def input_kernel(n_blocks, parts, place, *refs):
    *arrays, out = refs
    pieces, here, arrays = arrays[:n_blocks], arrays[n_blocks], arrays[n_blocks + 1 :]
    share = out.shape[1] // len(parts)
    for k, (which, row) in enumerate(parts):
        start = pl.multiple_of(place[k] * share, share)
        total = jnp.zeros((out.shape[0], share), jnp.float32)
        for s, piece in enumerate(pieces):
            if s:
                block = arrays[which][row + (s - 1) * share : row + s * share, :]
            else:
                block = here[pl.ds(start, share), :]
            total = total + lax.dot_general(
                piece[...], block, (((1,), (1,)), ((), ())), preferred_element_type=jnp.float32
            )
        out[:, pl.ds(start, share)] = total.astype(out.dtype)


def input_gradient(pieces, here, arrays, parts, place):
    length, cols = pieces[0].shape
    feats = here.shape[0]
    (d_tokens,) = on_chip(
        functools.partial(input_kernel, len(pieces), parts),
        place,
        pieces + [here] + arrays,
        [jax.ShapeDtypeStruct((length, feats), jnp.bfloat16)],
        2 * length * feats * cols * len(pieces),
        "input_gradient",
    )
    return d_tokens


def make_body(n_dp, n_z):
    tuned = n_dp == 8 and n_z == 4

    def pair(value, s):
        return lax.ppermute(value, "tensor", [(z, z ^ s) for z in range(n_z)])

    def body(tokens, queries, d_out, segments, cached, master, moment, second, grad):
        me_dp = lax.axis_index("dp").astype(jnp.int32)
        me_z = lax.axis_index("tensor").astype(jnp.int32)
        length, feats = tokens.shape
        cols = cached.shape[1]

        master_new, moment_new, second_new, own_cache = optimizer(
            cached, master, moment, second, grad
        )

        share = feats // n_dp

        def block_for(z):
            return lax.dynamic_slice_in_dim(cached, z * feats + me_dp * share, share, 0)

        blocks = [pair(block_for(me_z ^ s), s) for s in range(1, n_z)]
        here = lax.dynamic_slice_in_dim(cached, me_z * feats, feats, 0)

        doc_ids = segments[0]
        position = jnp.arange(length)
        allowed = (doc_ids[:, None] == doc_ids[None, :]) & (position[:, None] <= position[None, :])
        allowed = allowed.astype(jnp.float32)

        total = jnp.zeros((length, cols), jnp.float32)
        zero = 0 * me_z
        orders = weight_orders() if tuned else [jnp.zeros((5,), jnp.int32)]
        total, held = absorb([tokens], zero, me_z, cached, total, None, n_z)
        if tuned:
            gather = PlaneGather(own_cache, jnp.concatenate(blocks, axis=0))
        from_low, from_high = tokens, tokens
        for s in range(1, n_z):
            low, high = me_z - s, me_z + s
            from_high = lax.ppermute(from_high, "tensor", [(z + 1, z) for z in range(n_z - s)])
            from_low = lax.ppermute(
                from_low, "tensor", [(z, z + 1) for z in range(s - 1, n_z - 1)]
            )
            if tuned and s == 1:
                from_low, from_high, held, allowed, orders, here = lax.optimization_barrier(
                    (from_low, from_high, held, allowed, orders, here)
                )
            elif tuned and s == 2:
                from_low, from_high, held, gather.got = lax.optimization_barrier(
                    (from_low, from_high, held, gather.first())
                )
            elif tuned:
                packs, swapped = gather.second()
                laid = gather.lay(swapped, cached.shape[0])
                from_low, from_high, held, gather.packs, gather.swapped, laid = (
                    lax.optimization_barrier((from_low, from_high, held, packs, swapped, laid))
                )
            chunks, which = [from_low, from_high], (me_z < s).astype(jnp.int32)
            index = jnp.where(me_z < s, high, low)
            if 2 * s < n_z:
                total, held = absorb([from_low], zero, low, cached, total, held, n_z)
                chunks, which, index = [from_high], zero, high
            if s < n_z - 1:
                total, held = absorb(chunks, which, index, cached, total, held, n_z)

        held, d_queries, d_projected, sent, kept = attend(
            chunks, which, index, cached, total, held, queries, d_out, allowed, orders[0], n_z
        )

        pieces = [d_projected] + [pair(d_projected, s) for s in range(1, n_z)]
        if tuned:
            sent, gather.packs_other = lax.optimization_barrier((sent, gather.third()))
            new_cache = gather.lay_rest(laid)
            finish, pieces, new_cache = weight_sum(
                held, d_projected, orders[1], sent, kept, pieces, new_cache
            )
            new_grad, d_tokens = finish(input_gradient(pieces, here, *gather.feature_rows()))
        else:
            new_cache = lax.all_gather(own_cache, "dp", axis=0, tiled=True)
            rows = lax.all_gather(jnp.stack([block_for(me_z)] + blocks), "dp", axis=0)
            d_tokens = jnp.einsum(
                "slc,ksfc->lkf", jnp.stack(pieces), rows, preferred_element_type=jnp.float32
            )
            d_tokens = d_tokens.astype(jnp.bfloat16).reshape(length, feats)
            partial = lax.dot_general(
                held[:n_z].reshape(n_z * feats, length),
                d_projected,
                (((1,), (0,)), ((), ())),
                preferred_element_type=jnp.float32,
            )
            new_grad = lax.psum_scatter(
                partial.astype(jnp.bfloat16), "dp", scatter_dimension=0, tiled=True
            ).astype(jnp.float32)
        return (master_new, moment_new, second_new, new_cache, new_grad, d_queries, d_tokens)

    return body


def solution(mesh):
    in_specs = (
        P("dp", "tensor"),
        P("dp", "tensor"),
        P("dp", "tensor"),
        P("dp", None),
        P(None, "tensor"),
        P("dp", "tensor"),
        P("dp", "tensor"),
        P("dp", "tensor"),
        P("dp", "tensor"),
    )
    out_specs = (
        P("dp", "tensor"),
        P("dp", "tensor"),
        P("dp", "tensor"),
        P(None, "tensor"),
        P("dp", "tensor"),
        P("dp", "tensor"),
        P("dp", "tensor"),
    )
    body = make_body(mesh.shape["dp"], mesh.shape["tensor"])
    return jax.shard_map(body, mesh=mesh, in_specs=in_specs, out_specs=out_specs, check_vma=False)
```

```python
import functools
import math

import jax
import jax.numpy as jnp
from jax import lax
from jax.experimental import pallas as pl
from jax.experimental.pallas import tpu as pltpu
from jax.sharding import PartitionSpec as P

HD = 128
VMEM_STREAM = 60 * 1024 * 1024
VMEM_WHOLE = 24 * 1024 * 1024


beta_first = 0.9
beta_second = 0.95
learn_rate = 0.0003
weight_decay = 0.1
adam_epsilon = 1e-08
first_fix = 1.0 - 0.9**40
second_fix = 1.0 - 0.95**40


def optimizer_kernel(
    place, cached, master, moment, second, grad, master_out, moment_out, second_out, cache_out
):
    moment_new = beta_first * moment[...] + (1.0 - beta_first) * grad[...]
    second_new = beta_second * second[...] + (1.0 - beta_second) * grad[...] * grad[...]
    update = moment_new / first_fix / (jnp.sqrt(second_new / second_fix) + adam_epsilon)
    master_new = master[...] - learn_rate * (update + weight_decay * master[...])
    moment_out[...] = moment_new
    second_out[...] = second_new
    master_out[...] = master_new
    for start in range(0, cached.shape[1], HD):
        block = slice(start, start + HD)
        own_cache = cached[:, block].astype(jnp.float32)
        delta = master_new[:, block] - own_cache
        largest = jnp.max(jnp.abs(delta), axis=1, keepdims=True)
        scale = (largest + 1e-06).astype(jnp.bfloat16).astype(jnp.float32)
        codes = (delta / scale).astype(jnp.bfloat16)
        cache_out[:, block] = (own_cache + codes.astype(jnp.float32) * scale).astype(jnp.bfloat16)


def optimizer(cached, master, moment, second, grad):
    rows, cols = master.shape
    step = min(rows, 256)
    steps = rows // step
    own = pl.BlockSpec((step, cols), lambda i, place: (i, 0))
    full = jax.ShapeDtypeStruct((rows, cols), jnp.float32)
    return pl.pallas_call(
        optimizer_kernel,
        grid_spec=pltpu.PrefetchScalarGridSpec(
            num_scalar_prefetch=1,
            grid=(steps,),
            in_specs=[pl.BlockSpec((step, cols), lambda i, place: (place[0] * steps + i, 0))]
            + [own] * 4,
            out_specs=[own] * 4,
        ),
        out_shape=[full, full, full, jax.ShapeDtypeStruct((rows, cols), jnp.bfloat16)],
        cost_estimate=pl.CostEstimate(
            flops=40 * rows * cols, bytes_accessed=32 * rows * cols, transcendentals=rows * cols
        ),
        compiler_params=pltpu.CompilerParams(vmem_limit_bytes=VMEM_STREAM),
        name="optimizer",
    )(lax.axis_index("dp").astype(jnp.int32).reshape(1), cached, master, moment, second, grad)


def on_chip(kernel, place, arrays, out_shape, flops, name):
    vmem = pl.BlockSpec(memory_space=pltpu.VMEM)
    size = sum(a.size * a.dtype.itemsize for a in arrays)
    size += sum(s.size * s.dtype.itemsize for s in out_shape)
    return pl.pallas_call(
        kernel,
        in_specs=[pl.BlockSpec(memory_space=pltpu.SMEM)] + [vmem] * len(arrays),
        out_specs=[vmem] * len(out_shape),
        out_shape=out_shape,
        cost_estimate=pl.CostEstimate(flops=flops, bytes_accessed=size, transcendentals=0),
        compiler_params=pltpu.CompilerParams(vmem_limit_bytes=VMEM_WHOLE),
        name=name,
    )(place, *arrays)


def fetch_chunk(place, chunks, chunk, sem):
    for n, source in enumerate(chunks):

        @pl.when(place[2] == n)
        def _():
            pltpu.make_async_copy(source, chunk, sem).start()

    return pltpu.make_async_copy(chunks[0], chunk, sem)


def fetch_rows(place, cached, rows, sem):
    height = rows.shape[0]
    start = pl.multiple_of(place[0] * height, height)
    copy = pltpu.make_async_copy(cached.at[pl.ds(start, height), :], rows, sem)
    copy.start()
    return copy


def absorb_kernel(n_chunks, place, *refs):
    chunks, (total, cached) = refs[:n_chunks], refs[n_chunks : n_chunks + 2]
    total_out, held, chunk, rows, turned, sems = refs[-6:]
    chunk_copy = fetch_chunk(place, chunks, chunk, sems.at[0])
    rows_copy = fetch_rows(place, cached, rows, sems.at[1])
    chunk_copy.wait()
    turned[...] = chunk[...].T
    keep = pltpu.make_async_copy(turned, held.at[place[1]], sems.at[2])
    keep.start()
    rows_copy.wait()
    total_out[...] = total[...] + jnp.dot(
        chunk[...], rows[...], preferred_element_type=jnp.float32
    )
    keep.wait()


def absorb_place(index, which, n_chunks):
    inside = (index >= 0) & (index < n_chunks)
    return jnp.stack(
        [jnp.clip(index, 0, n_chunks - 1), jnp.where(inside, index, n_chunks), which]
    ).astype(jnp.int32)


def absorb_scratch(chunk, cached, n_sems):
    length, feats = chunk.shape
    return [
        pltpu.VMEM((length, feats), chunk.dtype),
        pltpu.VMEM((feats, cached.shape[1]), cached.dtype),
        pltpu.VMEM((feats, length), chunk.dtype),
        pltpu.SemaphoreType.DMA((n_sems,)),
    ]


def absorb(chunks, which, index, cached, total, held, n_chunks):
    length, feats = chunks[0].shape
    cols = cached.shape[1]
    shape = jax.ShapeDtypeStruct((8 * n_chunks, feats, length), chunks[0].dtype)
    vmem, anywhere = pl.BlockSpec(memory_space=pltpu.VMEM), pl.BlockSpec(memory_space=pl.ANY)
    return pl.pallas_call(
        functools.partial(absorb_kernel, len(chunks)),
        in_specs=[pl.BlockSpec(memory_space=pltpu.SMEM)]
        + [anywhere] * len(chunks)
        + [vmem, anywhere]
        + ([] if held is None else [anywhere]),
        out_specs=[vmem, anywhere],
        out_shape=[jax.ShapeDtypeStruct(total.shape, jnp.float32), shape],
        scratch_shapes=absorb_scratch(chunks[0], cached, 3),
        input_output_aliases={} if held is None else {3 + len(chunks): 1},
        cost_estimate=pl.CostEstimate(
            flops=2 * length * feats * cols,
            bytes_accessed=4 * length * feats + 2 * feats * cols,
            transcendentals=0,
        ),
        compiler_params=pltpu.CompilerParams(vmem_limit_bytes=VMEM_STREAM),
        name="absorb",
    )(
        absorb_place(index, which, n_chunks),
        *chunks,
        total,
        cached,
        *([] if held is None else [held]),
    )


def attend_kernel(n_chunks, place, order, *refs):
    chunks, refs = refs[:n_chunks], refs[n_chunks:]
    total, cached, _, allowed, queries_in, d_out_in = refs[:6]
    held, d_queries, d_projected, sent, kept, *refs = refs[6:]
    chunk, rows, turned, sems, queries, d_out, buffer, part_sems = refs
    chunk_copy = fetch_chunk(place, chunks, chunk, sems.at[0])
    rows_copy = fetch_rows(place, cached, rows, sems.at[1])
    others = [
        pltpu.make_async_copy(queries_in, queries, sems.at[3]),
        pltpu.make_async_copy(d_out_in, d_out, sems.at[4]),
    ]
    for copy in others:
        copy.start()
    chunk_copy.wait()
    turned[...] = chunk[...].T
    keep = pltpu.make_async_copy(turned, held.at[place[1]], sems.at[2])
    keep.start()
    rows_copy.wait()
    projected = (
        total[...] + jnp.dot(chunk[...], rows[...], preferred_element_type=jnp.float32)
    ).astype(jnp.bfloat16)
    seen = allowed[...] > 0
    for copy in others:
        copy.wait()
    factor = 1.0 / math.sqrt(HD)
    across = (((1,), (1,)), ((), ()))
    heads = projected.shape[1] // (2 * HD)
    group = queries.shape[1] // HD // heads
    for head in range(heads):
        start = 2 * HD * head
        keys = projected[:, start : start + HD]
        values = projected[:, start + HD : start + 2 * HD]
        d_keys = jnp.zeros(keys.shape, jnp.float32)
        d_values = jnp.zeros(keys.shape, jnp.float32)
        for g in range(head * group, (head + 1) * group):
            if g == heads * group // 2:
                keep.wait()
                copies = fetch_parts(order, held, range(4), buffer, part_sems)
            columns = slice(g * HD, (g + 1) * HD)
            query, grad = queries[:, columns], d_out[:, columns]
            scores = (
                lax.dot_general(keys, query, across, preferred_element_type=jnp.float32) * factor
            )
            scores = jnp.where(seen, scores, -1e30)
            weights = jnp.exp(scores - jnp.max(scores, axis=0, keepdims=True))
            probs = weights / jnp.sum(weights, axis=0, keepdims=True)
            probs_low = probs.astype(jnp.bfloat16)
            d_probs = lax.dot_general(values, grad, across, preferred_element_type=jnp.float32)
            rowdot = jnp.sum(probs_low.astype(jnp.float32) * d_probs, axis=0, keepdims=True)
            d_scores = (probs * (d_probs - rowdot) * factor).astype(jnp.bfloat16)
            d_queries[:, columns] = lax.dot_general(
                d_scores, keys, (((0,), (0,)), ((), ())), preferred_element_type=jnp.float32
            ).astype(jnp.bfloat16)
            d_keys = d_keys + jnp.dot(d_scores, query, preferred_element_type=jnp.float32)
            d_values = d_values + jnp.dot(probs_low, grad, preferred_element_type=jnp.float32)
        d_projected[:, start : start + HD] = d_keys.astype(jnp.bfloat16)
        d_projected[:, start + HD : start + 2 * HD] = d_values.astype(jnp.bfloat16)

    def give(g, side, position, here, part):
        out = (sent, kept)[g]
        out[2 * side + position, here, :] = part.astype(out.dtype)

    weight_products(copies, (SENT, KEPT), buffer, d_projected, give)


def attend(chunks, which, index, cached, total, held, queries, d_out, allowed, order, n_chunks):
    feats, length = held.shape[1:]
    parts = jax.ShapeDtypeStruct((4, feats // 2, total.shape[1] // 2), jnp.bfloat16)
    vmem, anywhere = pl.BlockSpec(memory_space=pltpu.VMEM), pl.BlockSpec(memory_space=pl.ANY)
    return pl.pallas_call(
        functools.partial(attend_kernel, len(chunks)),
        in_specs=[pl.BlockSpec(memory_space=pltpu.SMEM)] * 2
        + [anywhere] * len(chunks)
        + [vmem, anywhere, anywhere, vmem, anywhere, anywhere],
        out_specs=[anywhere] + [vmem] * 4,
        out_shape=[
            jax.ShapeDtypeStruct(held.shape, held.dtype),
            jax.ShapeDtypeStruct(queries.shape, jnp.bfloat16),
            jax.ShapeDtypeStruct(total.shape, jnp.bfloat16),
            parts,
            parts,
        ],
        scratch_shapes=absorb_scratch(chunks[0], cached, 5)
        + [
            pltpu.VMEM(queries.shape, queries.dtype),
            pltpu.VMEM(d_out.shape, d_out.dtype),
            pltpu.VMEM((4, feats // 2, length), held.dtype),
            pltpu.SemaphoreType.DMA((4,)),
        ],
        input_output_aliases={4 + len(chunks): 0},
        cost_estimate=pl.CostEstimate(
            flops=12 * allowed.size * queries.shape[1],
            bytes_accessed=8 * queries.size,
            transcendentals=allowed.size * queries.shape[1] // HD,
        ),
        compiler_params=pltpu.CompilerParams(vmem_limit_bytes=VMEM_STREAM),
        name="attend",
    )(
        absorb_place(index, which, n_chunks),
        order,
        *chunks,
        total,
        cached,
        held,
        allowed,
        queries,
        d_out,
    )


SENT = ((0, 0, 0), (0, 1, 0), (1, 0, 1), (2, 1, 1))
KEPT = ((1, 1, 0), (2, 0, 0), (3, 0, 1), (3, 1, 1))


def fetch_parts(place, held, chunks, buffer, sems):
    rows = buffer.shape[1]
    start = pl.multiple_of(place[4] * rows, rows)
    copies = {}
    for chunk in chunks:
        copies[chunk] = pltpu.make_async_copy(
            held.at[place[chunk], pl.ds(start, rows), :], buffer.at[chunk], sems.at[chunk]
        )
        copies[chunk].start()
    return copies


def weight_products(copies, groups, buffer, d_projected, give):
    rows = buffer.shape[1]
    half = d_projected.shape[1] // 2
    block = min(rows, 256)
    for chunk, copy in copies.items():
        copy.wait()
        wanted = [
            (g, side, position)
            for g, group in enumerate(groups)
            for which, side, position in group
            if which == chunk
        ]
        first, last = min(w[1] for w in wanted), max(w[1] for w in wanted)
        for r in range(0, rows, block):
            here = slice(r, r + block)
            total = jnp.dot(
                buffer[chunk, here, :],
                d_projected[:, first * half : (last + 1) * half],
                preferred_element_type=jnp.float32,
            )
            for g, side, position in wanted:
                part = total[:, (side - first) * half : (side - first + 1) * half]
                give(g, side, position, here, part)


def weight_kernel(group, place, held, d_projected, *refs):
    *added, out_a, out_b, buffer, sems = refs
    copies = fetch_parts(place, held, sorted({part[0] for part in group}), buffer, sems)

    def give(_, side, position, here, part):
        if added:
            part = part + added[0][2 * side + position, here, :].astype(jnp.float32)
        out = (out_a, out_b)[side]
        out[position, here, :] = part.astype(out.dtype)

    weight_products(copies, (group,), buffer, d_projected, give)


def weight_parts(held, d_projected, place, group, added, dtype, name):
    length, cols = d_projected.shape
    rows = held.shape[1] // 2
    vmem = pl.BlockSpec(memory_space=pltpu.VMEM)
    return pl.pallas_call(
        functools.partial(weight_kernel, group),
        in_specs=[pl.BlockSpec(memory_space=pltpu.SMEM), pl.BlockSpec(memory_space=pl.ANY)]
        + [vmem] * (1 + len(added)),
        out_specs=[vmem] * 2,
        out_shape=[jax.ShapeDtypeStruct((2, rows, cols // 2), dtype)] * 2,
        scratch_shapes=[
            pltpu.VMEM((4, rows, length), held.dtype),
            pltpu.SemaphoreType.DMA((4,)),
        ],
        cost_estimate=pl.CostEstimate(
            flops=4 * length * rows * cols, bytes_accessed=8 * rows * cols, transcendentals=0
        ),
        compiler_params=pltpu.CompilerParams(vmem_limit_bytes=VMEM_WHOLE),
        name=name,
    )(place, held, d_projected, *added)


def add_kernel(place, own_a, own_b, other, out_a, out_b):
    depth = own_a.shape[0]
    for side, (own, out) in enumerate(((own_a, out_a), (own_b, out_b))):
        other_here = other[side * depth : (side + 1) * depth]
        out[...] = (own[...] + other_here.astype(jnp.float32)).astype(out.dtype)


def combine_kernel(place, keep_a, got_a, keep_b, got_b, out_a, out_b):
    for keep, got, out in ((keep_a, got_a, out_a), (keep_b, got_b, out_b)):
        out[...] = (keep[0] + got[0].astype(jnp.float32)).astype(out.dtype)


def finish_kernel(place, keep_a, got_a, keep_b, got_b, last_a, last_b, out):
    half = last_a.shape[1]
    sides = ((keep_a, got_a, last_a), (keep_b, got_b, last_b))
    for side, (keep, got, last) in enumerate(sides):
        total = keep[1] + got[1].astype(jnp.float32) + last[...].astype(jnp.float32)
        out[:, side * half : (side + 1) * half] = total


def plane():
    index = lax.axis_index("dp").astype(jnp.int32)

    def swap(value, bit):
        return lax.ppermute(value, "dp", [(i, i ^ bit) for i in range(8)])

    return index % 2, (index // 2) % 2, index // 4, swap


def weight_orders():
    core, x, y, _ = plane()
    chunks = [3 - x - 2 * y, 1 - x + 2 * y, x + 2 - 2 * y, x + 2 * y]
    return [jnp.stack(chunks + [half]) for half in (1 - core, core)]


def weight_sum(held, d_projected, order, sent, kept, pieces, beside):
    swap = plane()[3]
    rows, cols = held.shape[1] // 2, d_projected.shape[1]
    none = jnp.zeros((1,), jnp.int32)
    sent, kept = swap(sent, 1), swap(kept, 1)
    own = weight_parts(held, d_projected, order, SENT, [], jnp.float32, "weight_send")
    shape = jax.ShapeDtypeStruct(own[0].shape, jnp.bfloat16)
    send_a, send_b = on_chip(
        add_kernel, none, list(own) + [sent], [shape] * 2, 2 * cols * rows, "weight_add"
    )
    got_a, got_b = swap(send_a, 2), swap(send_b, 4)
    keep_a, keep_b = weight_parts(
        held, d_projected, order, KEPT, [kept], jnp.float32, "weight_keep"
    )
    pieces, got_a, got_b, beside = lax.optimization_barrier((pieces[::-1], got_a, got_b, beside))
    pieces = pieces[::-1]

    small = jax.ShapeDtypeStruct((rows, cols // 2), jnp.bfloat16)
    arrays = [keep_a, got_a, keep_b, got_b]
    last_a, last_b = on_chip(
        combine_kernel, none, arrays, [small] * 2, cols * rows, "weight_combine"
    )
    last = [swap(last_a, 4), swap(last_b, 2)]

    def finish(ready):
        ended, ready = lax.optimization_barrier((last, ready))
        (total,) = on_chip(
            finish_kernel,
            none,
            arrays + ended,
            [jax.ShapeDtypeStruct((rows, cols), jnp.float32)],
            2 * cols * rows,
            "weight_finish",
        )
        return total, ready

    return finish, pieces, beside


class PlaneGather:
    def __init__(self, own_cache, own_rows):
        self.own = own_cache, own_rows
        self.both = jnp.concatenate([own_cache, own_rows], axis=0)

    def first(self):
        swap = plane()[3]
        return swap(self.own[1], 2), swap(self.own[0], 4), swap(self.both, 1)

    def second(self):
        swap = plane()[3]
        rows_x, cache_y, _ = self.got
        packs = (
            swap(jnp.concatenate([self.own[0], cache_y], axis=0), 2),
            swap(jnp.concatenate([self.own[1], rows_x], axis=0), 4),
        )
        return packs, (swap(rows_x, 1), swap(cache_y, 1))

    def third(self):
        swap = plane()[3]
        return swap(self.packs[0], 1), swap(self.packs[1], 1)

    def where(self, bits):
        return lax.axis_index("dp").astype(jnp.int32) ^ jnp.array(bits, dtype=jnp.int32)

    def lay(self, swapped, n_rows):
        arrays = [self.own[0], self.got[2], self.got[1], swapped[1]]
        return place_rows(arrays, [(k, 0) for k in range(4)], self.where([0, 1, 4, 5]),
                          self.own[0].shape[0], n_rows, [])

    def lay_rest(self, laid):
        height = self.own[0].shape[0]
        parts = [(0, 0), (0, height), (1, 0), (1, height)]
        arrays = [self.packs[0], self.packs_other[0]]
        return place_rows(
            arrays, parts, self.where([2, 6, 3, 7]), height, laid.shape[0], [laid]
        )

    def feature_rows(self):
        height, count = self.own[0].shape[0], self.own[1].shape[0]
        arrays = [self.own[1], self.got[2], self.got[0], self.swapped[0]]
        arrays += [self.packs[1], self.packs_other[1]]
        parts = [(0, 0), (1, height), (2, 0), (3, 0), (4, 0), (4, count), (5, 0), (5, count)]
        return arrays, parts, self.where([0, 1, 2, 3, 4, 6, 5, 7])


def place_rows_kernel(height, parts, place, *refs):
    out, sems = refs[-2:]
    copies = []
    for k, (which, row) in enumerate(parts):
        start = pl.multiple_of(place[k] * height, height)
        copies.append(
            pltpu.make_async_copy(
                refs[which].at[pl.ds(row, height), :],
                out.at[pl.ds(start, height), :],
                sems.at[k],
            )
        )
    for copy in copies:
        copy.start()
    for copy in copies:
        copy.wait()


def place_rows(arrays, parts, place, height, rows, into):
    cols = arrays[0].shape[1]
    anywhere = pl.BlockSpec(memory_space=pl.ANY)
    return pl.pallas_call(
        functools.partial(place_rows_kernel, height, parts),
        in_specs=[pl.BlockSpec(memory_space=pltpu.SMEM)]
        + [pl.BlockSpec(memory_space=pltpu.VMEM)] * len(arrays)
        + [anywhere] * len(into),
        out_specs=anywhere,
        out_shape=jax.ShapeDtypeStruct((rows, cols), arrays[0].dtype),
        scratch_shapes=[pltpu.SemaphoreType.DMA((len(parts),))],
        input_output_aliases={1 + len(arrays): 0} if into else {},
        cost_estimate=pl.CostEstimate(
            flops=0, bytes_accessed=4 * height * cols * len(parts), transcendentals=0
        ),
        compiler_params=pltpu.CompilerParams(vmem_limit_bytes=VMEM_WHOLE),
        name="place_rows",
    )(place, *arrays, *into)


def input_kernel(n_blocks, parts, place, *refs):
    *arrays, out = refs
    pieces, here, arrays = arrays[:n_blocks], arrays[n_blocks], arrays[n_blocks + 1 :]
    share = out.shape[1] // len(parts)
    for k, (which, row) in enumerate(parts):
        start = pl.multiple_of(place[k] * share, share)
        total = jnp.zeros((out.shape[0], share), jnp.float32)
        for s, piece in enumerate(pieces):
            if s:
                block = arrays[which][row + (s - 1) * share : row + s * share, :]
            else:
                block = here[pl.ds(start, share), :]
            total = total + lax.dot_general(
                piece[...], block, (((1,), (1,)), ((), ())), preferred_element_type=jnp.float32
            )
        out[:, pl.ds(start, share)] = total.astype(out.dtype)


def input_gradient(pieces, here, arrays, parts, place):
    length, cols = pieces[0].shape
    feats = here.shape[0]
    (d_tokens,) = on_chip(
        functools.partial(input_kernel, len(pieces), parts),
        place,
        pieces + [here] + arrays,
        [jax.ShapeDtypeStruct((length, feats), jnp.bfloat16)],
        2 * length * feats * cols * len(pieces),
        "input_gradient",
    )
    return d_tokens


def make_body(n_dp, n_z):
    tuned = n_dp == 8 and n_z == 4

    def pair(value, s):
        return lax.ppermute(value, "tensor", [(z, z ^ s) for z in range(n_z)])

    def body(tokens, queries, d_out, segments, cached, master, moment, second, grad):
        me_dp = lax.axis_index("dp").astype(jnp.int32)
        me_z = lax.axis_index("tensor").astype(jnp.int32)
        length, feats = tokens.shape
        cols = cached.shape[1]

        master_new, moment_new, second_new, own_cache = optimizer(
            cached, master, moment, second, grad
        )

        share = feats // n_dp

        def block_for(z):
            return lax.dynamic_slice_in_dim(cached, z * feats + me_dp * share, share, 0)

        blocks = [pair(block_for(me_z ^ s), s) for s in range(1, n_z)]
        here = lax.dynamic_slice_in_dim(cached, me_z * feats, feats, 0)

        doc_ids = segments[0]
        position = jnp.arange(length)
        allowed = (doc_ids[:, None] == doc_ids[None, :]) & (position[:, None] <= position[None, :])
        allowed = allowed.astype(jnp.float32)

        total = jnp.zeros((length, cols), jnp.float32)
        zero = 0 * me_z
        orders = weight_orders() if tuned else [jnp.zeros((5,), jnp.int32)]
        total, held = absorb([tokens], zero, me_z, cached, total, None, n_z)
        if tuned:
            gather = PlaneGather(own_cache, jnp.concatenate(blocks, axis=0))
        from_low, from_high = tokens, tokens
        for s in range(1, n_z):
            low, high = me_z - s, me_z + s
            from_high = lax.ppermute(from_high, "tensor", [(z + 1, z) for z in range(n_z - s)])
            from_low = lax.ppermute(
                from_low, "tensor", [(z, z + 1) for z in range(s - 1, n_z - 1)]
            )
            if tuned and s == 1:
                from_high, from_low, held, allowed, orders, here = lax.optimization_barrier(
                    (from_high, from_low, held, allowed, orders, here)
                )
            elif tuned and s == 2:
                from_high, from_low, held, gather.got = lax.optimization_barrier(
                    (from_high, from_low, held, gather.first())
                )
            elif tuned:
                packs, swapped = gather.second()
                laid = gather.lay(swapped, cached.shape[0])
                from_high, from_low, held, gather.packs, gather.swapped, laid = (
                    lax.optimization_barrier((from_high, from_low, held, packs, swapped, laid))
                )
            chunks, which = [from_low, from_high], (me_z < s).astype(jnp.int32)
            index = jnp.where(me_z < s, high, low)
            if 2 * s < n_z:
                total, held = absorb([from_low], zero, low, cached, total, held, n_z)
                chunks, which, index = [from_high], zero, high
            if s < n_z - 1:
                total, held = absorb(chunks, which, index, cached, total, held, n_z)

        held, d_queries, d_projected, sent, kept = attend(
            chunks, which, index, cached, total, held, queries, d_out, allowed, orders[0], n_z
        )

        pieces = [pair(d_projected, s) for s in range(n_z - 1, 0, -1)]
        pieces = [d_projected] + pieces[::-1]
        if tuned:
            sent, gather.packs_other = lax.optimization_barrier((sent, gather.third()))
            new_cache = gather.lay_rest(laid)
            finish, pieces, new_cache = weight_sum(
                held, d_projected, orders[1], sent, kept, pieces, new_cache
            )
            new_grad, d_tokens = finish(input_gradient(pieces, here, *gather.feature_rows()))
        else:
            new_cache = lax.all_gather(own_cache, "dp", axis=0, tiled=True)
            rows = lax.all_gather(jnp.stack([block_for(me_z)] + blocks), "dp", axis=0)
            d_tokens = jnp.einsum(
                "slc,ksfc->lkf", jnp.stack(pieces), rows, preferred_element_type=jnp.float32
            )
            d_tokens = d_tokens.astype(jnp.bfloat16).reshape(length, feats)
            partial = lax.dot_general(
                held[:n_z].reshape(n_z * feats, length),
                d_projected,
                (((1,), (0,)), ((), ())),
                preferred_element_type=jnp.float32,
            )
            new_grad = lax.psum_scatter(
                partial.astype(jnp.bfloat16), "dp", scatter_dimension=0, tiled=True
            ).astype(jnp.float32)
        return (master_new, moment_new, second_new, new_cache, new_grad, d_queries, d_tokens)

    return body


def solution(mesh):
    in_specs = (
        P("dp", "tensor"),
        P("dp", "tensor"),
        P("dp", "tensor"),
        P("dp", None),
        P(None, "tensor"),
        P("dp", "tensor"),
        P("dp", "tensor"),
        P("dp", "tensor"),
        P("dp", "tensor"),
    )
    out_specs = (
        P("dp", "tensor"),
        P("dp", "tensor"),
        P("dp", "tensor"),
        P(None, "tensor"),
        P("dp", "tensor"),
        P("dp", "tensor"),
        P("dp", "tensor"),
    )
    body = make_body(mesh.shape["dp"], mesh.shape["tensor"])
    return jax.shard_map(body, mesh=mesh, in_specs=in_specs, out_specs=out_specs, check_vma=False)
```

```python
import functools
import math

import jax
import jax.numpy as jnp
from jax import lax
from jax.experimental import pallas as pl
from jax.experimental.pallas import tpu as pltpu
from jax.sharding import PartitionSpec as P

HD = 128
VMEM_STREAM = 60 * 1024 * 1024
VMEM_WHOLE = 24 * 1024 * 1024


beta_first = 0.9
beta_second = 0.95
learn_rate = 0.0003
weight_decay = 0.1
adam_epsilon = 1e-08
first_fix = 1.0 - 0.9**40
second_fix = 1.0 - 0.95**40


def optimizer_kernel(
    place, cached, master, moment, second, grad, master_out, moment_out, second_out, cache_out
):
    moment_new = beta_first * moment[...] + (1.0 - beta_first) * grad[...]
    second_new = beta_second * second[...] + (1.0 - beta_second) * grad[...] * grad[...]
    update = moment_new / first_fix / (jnp.sqrt(second_new / second_fix) + adam_epsilon)
    master_new = master[...] - learn_rate * (update + weight_decay * master[...])
    moment_out[...] = moment_new
    second_out[...] = second_new
    master_out[...] = master_new
    for start in range(0, cached.shape[1], HD):
        block = slice(start, start + HD)
        own_cache = cached[:, block].astype(jnp.float32)
        delta = master_new[:, block] - own_cache
        largest = jnp.max(jnp.abs(delta), axis=1, keepdims=True)
        scale = (largest + 1e-06).astype(jnp.bfloat16).astype(jnp.float32)
        codes = (delta / scale).astype(jnp.bfloat16)
        cache_out[:, block] = (own_cache + codes.astype(jnp.float32) * scale).astype(jnp.bfloat16)


def optimizer(cached, master, moment, second, grad):
    rows, cols = master.shape
    step = min(rows, 256)
    steps = rows // step
    own = pl.BlockSpec((step, cols), lambda i, place: (i, 0))
    full = jax.ShapeDtypeStruct((rows, cols), jnp.float32)
    return pl.pallas_call(
        optimizer_kernel,
        grid_spec=pltpu.PrefetchScalarGridSpec(
            num_scalar_prefetch=1,
            grid=(steps,),
            in_specs=[pl.BlockSpec((step, cols), lambda i, place: (place[0] * steps + i, 0))]
            + [own] * 4,
            out_specs=[own] * 4,
        ),
        out_shape=[full, full, full, jax.ShapeDtypeStruct((rows, cols), jnp.bfloat16)],
        cost_estimate=pl.CostEstimate(
            flops=40 * rows * cols, bytes_accessed=32 * rows * cols, transcendentals=rows * cols
        ),
        compiler_params=pltpu.CompilerParams(vmem_limit_bytes=VMEM_STREAM),
        name="optimizer",
    )(lax.axis_index("dp").astype(jnp.int32).reshape(1), cached, master, moment, second, grad)


def on_chip(kernel, place, arrays, out_shape, flops, name):
    vmem = pl.BlockSpec(memory_space=pltpu.VMEM)
    size = sum(a.size * a.dtype.itemsize for a in arrays)
    size += sum(s.size * s.dtype.itemsize for s in out_shape)
    return pl.pallas_call(
        kernel,
        in_specs=[pl.BlockSpec(memory_space=pltpu.SMEM)] + [vmem] * len(arrays),
        out_specs=[vmem] * len(out_shape),
        out_shape=out_shape,
        cost_estimate=pl.CostEstimate(flops=flops, bytes_accessed=size, transcendentals=0),
        compiler_params=pltpu.CompilerParams(vmem_limit_bytes=VMEM_WHOLE),
        name=name,
    )(place, *arrays)


def fetch_chunk(place, chunks, chunk, sem):
    for n, source in enumerate(chunks):

        @pl.when(place[2] == n)
        def _():
            pltpu.make_async_copy(source, chunk, sem).start()

    return pltpu.make_async_copy(chunks[0], chunk, sem)


def fetch_rows(place, cached, rows, sem):
    height = rows.shape[0]
    start = pl.multiple_of(place[0] * height, height)
    copy = pltpu.make_async_copy(cached.at[pl.ds(start, height), :], rows, sem)
    copy.start()
    return copy


def absorb_kernel(n_chunks, place, *refs):
    chunks, (total, cached) = refs[:n_chunks], refs[n_chunks : n_chunks + 2]
    total_out, held, chunk, rows, turned, sems = refs[-6:]
    chunk_copy = fetch_chunk(place, chunks, chunk, sems.at[0])
    rows_copy = fetch_rows(place, cached, rows, sems.at[1])
    chunk_copy.wait()
    turned[...] = chunk[...].T
    keep = pltpu.make_async_copy(turned, held.at[place[1]], sems.at[2])
    keep.start()
    rows_copy.wait()
    total_out[...] = total[...] + jnp.dot(
        chunk[...], rows[...], preferred_element_type=jnp.float32
    )
    keep.wait()


def absorb_place(index, which, n_chunks):
    inside = (index >= 0) & (index < n_chunks)
    return jnp.stack(
        [jnp.clip(index, 0, n_chunks - 1), jnp.where(inside, index, n_chunks), which]
    ).astype(jnp.int32)


def absorb_scratch(chunk, cached, n_sems):
    length, feats = chunk.shape
    return [
        pltpu.VMEM((length, feats), chunk.dtype),
        pltpu.VMEM((feats, cached.shape[1]), cached.dtype),
        pltpu.VMEM((feats, length), chunk.dtype),
        pltpu.SemaphoreType.DMA((n_sems,)),
    ]


def absorb(chunks, which, index, cached, total, held, n_chunks):
    length, feats = chunks[0].shape
    cols = cached.shape[1]
    shape = jax.ShapeDtypeStruct((8 * n_chunks, feats, length), chunks[0].dtype)
    vmem, anywhere = pl.BlockSpec(memory_space=pltpu.VMEM), pl.BlockSpec(memory_space=pl.ANY)
    return pl.pallas_call(
        functools.partial(absorb_kernel, len(chunks)),
        in_specs=[pl.BlockSpec(memory_space=pltpu.SMEM)]
        + [anywhere] * len(chunks)
        + [vmem, anywhere]
        + ([] if held is None else [anywhere]),
        out_specs=[vmem, anywhere],
        out_shape=[jax.ShapeDtypeStruct(total.shape, jnp.float32), shape],
        scratch_shapes=absorb_scratch(chunks[0], cached, 3),
        input_output_aliases={} if held is None else {3 + len(chunks): 1},
        cost_estimate=pl.CostEstimate(
            flops=2 * length * feats * cols,
            bytes_accessed=4 * length * feats + 2 * feats * cols,
            transcendentals=0,
        ),
        compiler_params=pltpu.CompilerParams(vmem_limit_bytes=VMEM_STREAM),
        name="absorb",
    )(
        absorb_place(index, which, n_chunks),
        *chunks,
        total,
        cached,
        *([] if held is None else [held]),
    )


def attend_kernel(n_chunks, place, order, *refs):
    chunks, refs = refs[:n_chunks], refs[n_chunks:]
    total, cached, _, allowed, queries_in, d_out_in = refs[:6]
    held, d_queries, d_projected, sent, kept, *refs = refs[6:]
    chunk, rows, turned, sems, queries, d_out, buffer, part_sems = refs
    chunk_copy = fetch_chunk(place, chunks, chunk, sems.at[0])
    rows_copy = fetch_rows(place, cached, rows, sems.at[1])
    others = [
        pltpu.make_async_copy(queries_in, queries, sems.at[3]),
        pltpu.make_async_copy(d_out_in, d_out, sems.at[4]),
    ]
    for copy in others:
        copy.start()
    chunk_copy.wait()
    turned[...] = chunk[...].T
    keep = pltpu.make_async_copy(turned, held.at[place[1]], sems.at[2])
    keep.start()
    rows_copy.wait()
    projected = (
        total[...] + jnp.dot(chunk[...], rows[...], preferred_element_type=jnp.float32)
    ).astype(jnp.bfloat16)
    seen = allowed[...] > 0
    for copy in others:
        copy.wait()
    factor = 1.0 / math.sqrt(HD)
    across = (((1,), (1,)), ((), ()))
    heads = projected.shape[1] // (2 * HD)
    group = queries.shape[1] // HD // heads
    for head in range(heads):
        start = 2 * HD * head
        keys = projected[:, start : start + HD]
        values = projected[:, start + HD : start + 2 * HD]
        d_keys = jnp.zeros(keys.shape, jnp.float32)
        d_values = jnp.zeros(keys.shape, jnp.float32)
        for g in range(head * group, (head + 1) * group):
            if g == heads * group // 2:
                keep.wait()
                copies = fetch_parts(order, held, range(4), buffer, part_sems)
            columns = slice(g * HD, (g + 1) * HD)
            query, grad = queries[:, columns], d_out[:, columns]
            scores = (
                lax.dot_general(keys, query, across, preferred_element_type=jnp.float32) * factor
            )
            scores = jnp.where(seen, scores, -1e30)
            weights = jnp.exp(scores - jnp.max(scores, axis=0, keepdims=True))
            probs = weights / jnp.sum(weights, axis=0, keepdims=True)
            probs_low = probs.astype(jnp.bfloat16)
            d_probs = lax.dot_general(values, grad, across, preferred_element_type=jnp.float32)
            rowdot = jnp.sum(probs_low.astype(jnp.float32) * d_probs, axis=0, keepdims=True)
            d_scores = (probs * (d_probs - rowdot) * factor).astype(jnp.bfloat16)
            d_queries[:, columns] = lax.dot_general(
                d_scores, keys, (((0,), (0,)), ((), ())), preferred_element_type=jnp.float32
            ).astype(jnp.bfloat16)
            d_keys = d_keys + jnp.dot(d_scores, query, preferred_element_type=jnp.float32)
            d_values = d_values + jnp.dot(probs_low, grad, preferred_element_type=jnp.float32)
        d_projected[:, start : start + HD] = d_keys.astype(jnp.bfloat16)
        d_projected[:, start + HD : start + 2 * HD] = d_values.astype(jnp.bfloat16)

    def give(g, side, position, here, part):
        out = (sent, kept)[g]
        out[2 * side + position, here, :] = part.astype(out.dtype)

    weight_products(copies, (SENT, KEPT), buffer, d_projected, give)


def attend(chunks, which, index, cached, total, held, queries, d_out, allowed, order, n_chunks):
    feats, length = held.shape[1:]
    parts = jax.ShapeDtypeStruct((4, feats // 2, total.shape[1] // 2), jnp.bfloat16)
    vmem, anywhere = pl.BlockSpec(memory_space=pltpu.VMEM), pl.BlockSpec(memory_space=pl.ANY)
    return pl.pallas_call(
        functools.partial(attend_kernel, len(chunks)),
        in_specs=[pl.BlockSpec(memory_space=pltpu.SMEM)] * 2
        + [anywhere] * len(chunks)
        + [vmem, anywhere, anywhere, vmem, anywhere, anywhere],
        out_specs=[anywhere] + [vmem] * 4,
        out_shape=[
            jax.ShapeDtypeStruct(held.shape, held.dtype),
            jax.ShapeDtypeStruct(queries.shape, jnp.bfloat16),
            jax.ShapeDtypeStruct(total.shape, jnp.bfloat16),
            parts,
            parts,
        ],
        scratch_shapes=absorb_scratch(chunks[0], cached, 5)
        + [
            pltpu.VMEM(queries.shape, queries.dtype),
            pltpu.VMEM(d_out.shape, d_out.dtype),
            pltpu.VMEM((4, feats // 2, length), held.dtype),
            pltpu.SemaphoreType.DMA((4,)),
        ],
        input_output_aliases={4 + len(chunks): 0},
        cost_estimate=pl.CostEstimate(
            flops=12 * allowed.size * queries.shape[1],
            bytes_accessed=8 * queries.size,
            transcendentals=allowed.size * queries.shape[1] // HD,
        ),
        compiler_params=pltpu.CompilerParams(vmem_limit_bytes=VMEM_STREAM),
        name="attend",
    )(
        absorb_place(index, which, n_chunks),
        order,
        *chunks,
        total,
        cached,
        held,
        allowed,
        queries,
        d_out,
    )


SENT = ((0, 0, 0), (0, 1, 0), (1, 0, 1), (2, 1, 1))
KEPT = ((1, 1, 0), (2, 0, 0), (3, 0, 1), (3, 1, 1))


def fetch_parts(place, held, chunks, buffer, sems):
    rows = buffer.shape[1]
    start = pl.multiple_of(place[4] * rows, rows)
    copies = {}
    for chunk in chunks:
        copies[chunk] = pltpu.make_async_copy(
            held.at[place[chunk], pl.ds(start, rows), :], buffer.at[chunk], sems.at[chunk]
        )
        copies[chunk].start()
    return copies


def weight_products(copies, groups, buffer, d_projected, give):
    rows = buffer.shape[1]
    half = d_projected.shape[1] // 2
    block = min(rows, 256)
    for chunk, copy in copies.items():
        copy.wait()
        wanted = [
            (g, side, position)
            for g, group in enumerate(groups)
            for which, side, position in group
            if which == chunk
        ]
        first, last = min(w[1] for w in wanted), max(w[1] for w in wanted)
        for r in range(0, rows, block):
            here = slice(r, r + block)
            total = jnp.dot(
                buffer[chunk, here, :],
                d_projected[:, first * half : (last + 1) * half],
                preferred_element_type=jnp.float32,
            )
            for g, side, position in wanted:
                part = total[:, (side - first) * half : (side - first + 1) * half]
                give(g, side, position, here, part)


def weight_kernel(group, place, held, d_projected, *refs):
    *added, out_a, out_b, buffer, sems = refs
    copies = fetch_parts(place, held, sorted({part[0] for part in group}), buffer, sems)

    def give(_, side, position, here, part):
        if added:
            part = part + added[0][2 * side + position, here, :].astype(jnp.float32)
        out = (out_a, out_b)[side]
        out[position, here, :] = part.astype(out.dtype)

    weight_products(copies, (group,), buffer, d_projected, give)


def weight_parts(held, d_projected, place, group, added, dtype, name):
    length, cols = d_projected.shape
    rows = held.shape[1] // 2
    vmem = pl.BlockSpec(memory_space=pltpu.VMEM)
    return pl.pallas_call(
        functools.partial(weight_kernel, group),
        in_specs=[pl.BlockSpec(memory_space=pltpu.SMEM), pl.BlockSpec(memory_space=pl.ANY)]
        + [vmem] * (1 + len(added)),
        out_specs=[vmem] * 2,
        out_shape=[jax.ShapeDtypeStruct((2, rows, cols // 2), dtype)] * 2,
        scratch_shapes=[
            pltpu.VMEM((4, rows, length), held.dtype),
            pltpu.SemaphoreType.DMA((4,)),
        ],
        cost_estimate=pl.CostEstimate(
            flops=4 * length * rows * cols, bytes_accessed=8 * rows * cols, transcendentals=0
        ),
        compiler_params=pltpu.CompilerParams(vmem_limit_bytes=VMEM_WHOLE),
        name=name,
    )(place, held, d_projected, *added)


def add_kernel(place, own_a, own_b, other, out_a, out_b):
    depth = own_a.shape[0]
    for side, (own, out) in enumerate(((own_a, out_a), (own_b, out_b))):
        other_here = other[side * depth : (side + 1) * depth]
        out[...] = (own[...] + other_here.astype(jnp.float32)).astype(out.dtype)


def combine_kernel(place, keep_a, got_a, keep_b, got_b, out_a, out_b):
    for keep, got, out in ((keep_a, got_a, out_a), (keep_b, got_b, out_b)):
        out[...] = (keep[0] + got[0].astype(jnp.float32)).astype(out.dtype)


def finish_kernel(place, keep_a, got_a, keep_b, got_b, last_a, last_b, out):
    half = last_a.shape[1]
    sides = ((keep_a, got_a, last_a), (keep_b, got_b, last_b))
    for side, (keep, got, last) in enumerate(sides):
        total = keep[1] + got[1].astype(jnp.float32) + last[...].astype(jnp.float32)
        out[:, side * half : (side + 1) * half] = total


def plane():
    index = lax.axis_index("dp").astype(jnp.int32)

    def swap(value, bit):
        return lax.ppermute(value, "dp", [(i, i ^ bit) for i in range(8)])

    return index % 2, (index // 2) % 2, index // 4, swap


def weight_orders():
    core, x, y, _ = plane()
    chunks = [3 - x - 2 * y, 1 - x + 2 * y, x + 2 - 2 * y, x + 2 * y]
    return [jnp.stack(chunks + [half]) for half in (1 - core, core)]


def weight_sum(held, d_projected, order, sent, kept, pieces, pair, beside):
    swap = plane()[3]
    rows, cols = held.shape[1] // 2, d_projected.shape[1]
    none = jnp.zeros((1,), jnp.int32)
    sent, kept = swap(sent, 1), swap(kept, 1)
    own = weight_parts(held, d_projected, order, SENT, [], jnp.float32, "weight_send")
    shape = jax.ShapeDtypeStruct(own[0].shape, jnp.bfloat16)
    send_a, send_b = on_chip(
        add_kernel, none, list(own) + [sent], [shape] * 2, 2 * cols * rows, "weight_add"
    )
    got_a, got_b = swap(send_a, 2), swap(send_b, 4)
    keep_a, keep_b = weight_parts(
        held, d_projected, order, KEPT, [kept], jnp.float32, "weight_keep"
    )
    pieces[2], keep_a, keep_b, beside = lax.optimization_barrier(
        (pieces[2], keep_a, keep_b, beside)
    )
    pieces = pieces + [pair(pieces[2], 1)]
    pieces, got_a, got_b = lax.optimization_barrier((pieces, got_a, got_b))

    small = jax.ShapeDtypeStruct((rows, cols // 2), jnp.bfloat16)
    arrays = [keep_a, got_a, keep_b, got_b]
    last_a, last_b = on_chip(
        combine_kernel, none, arrays, [small] * 2, cols * rows, "weight_combine"
    )
    last = [swap(last_a, 4), swap(last_b, 2)]

    def finish(ready):
        ended, ready = lax.optimization_barrier((last, ready))
        (total,) = on_chip(
            finish_kernel,
            none,
            arrays + ended,
            [jax.ShapeDtypeStruct((rows, cols), jnp.float32)],
            2 * cols * rows,
            "weight_finish",
        )
        return total, ready

    return finish, pieces, beside


class PlaneGather:
    def __init__(self, own_cache, own_rows):
        self.own = own_cache, own_rows
        self.both = jnp.concatenate([own_cache, own_rows], axis=0)

    def first(self):
        swap = plane()[3]
        return swap(self.own[1], 2), swap(self.own[0], 4), swap(self.both, 1)

    def second(self):
        swap = plane()[3]
        rows_x, cache_y, _ = self.got
        packs = (
            swap(jnp.concatenate([self.own[0], cache_y], axis=0), 2),
            swap(jnp.concatenate([self.own[1], rows_x], axis=0), 4),
        )
        return packs, (swap(rows_x, 1), swap(cache_y, 1))

    def third(self):
        swap = plane()[3]
        return swap(self.packs[0], 1), swap(self.packs[1], 1)

    def where(self, bits):
        return lax.axis_index("dp").astype(jnp.int32) ^ jnp.array(bits, dtype=jnp.int32)

    def lay(self, swapped, n_rows):
        arrays = [self.own[0], self.got[2], self.got[1], swapped[1]]
        return place_rows(arrays, [(k, 0) for k in range(4)], self.where([0, 1, 4, 5]),
                          self.own[0].shape[0], n_rows, [])

    def lay_rest(self, laid):
        height = self.own[0].shape[0]
        parts = [(0, 0), (0, height), (1, 0), (1, height)]
        arrays = [self.packs[0], self.packs_other[0]]
        return place_rows(
            arrays, parts, self.where([2, 6, 3, 7]), height, laid.shape[0], [laid]
        )

    def feature_rows(self):
        height, count = self.own[0].shape[0], self.own[1].shape[0]
        arrays = [self.own[1], self.got[2], self.got[0], self.swapped[0]]
        arrays += [self.packs[1], self.packs_other[1]]
        parts = [(0, 0), (1, height), (2, 0), (3, 0), (4, 0), (4, count), (5, 0), (5, count)]
        return arrays, parts, self.where([0, 1, 2, 3, 4, 6, 5, 7])


def place_rows_kernel(height, parts, place, *refs):
    out, sems = refs[-2:]
    copies = []
    for k, (which, row) in enumerate(parts):
        start = pl.multiple_of(place[k] * height, height)
        copies.append(
            pltpu.make_async_copy(
                refs[which].at[pl.ds(row, height), :],
                out.at[pl.ds(start, height), :],
                sems.at[k],
            )
        )
    for copy in copies:
        copy.start()
    for copy in copies:
        copy.wait()


def place_rows(arrays, parts, place, height, rows, into):
    cols = arrays[0].shape[1]
    anywhere = pl.BlockSpec(memory_space=pl.ANY)
    return pl.pallas_call(
        functools.partial(place_rows_kernel, height, parts),
        in_specs=[pl.BlockSpec(memory_space=pltpu.SMEM)]
        + [pl.BlockSpec(memory_space=pltpu.VMEM)] * len(arrays)
        + [anywhere] * len(into),
        out_specs=anywhere,
        out_shape=jax.ShapeDtypeStruct((rows, cols), arrays[0].dtype),
        scratch_shapes=[pltpu.SemaphoreType.DMA((len(parts),))],
        input_output_aliases={1 + len(arrays): 0} if into else {},
        cost_estimate=pl.CostEstimate(
            flops=0, bytes_accessed=4 * height * cols * len(parts), transcendentals=0
        ),
        compiler_params=pltpu.CompilerParams(vmem_limit_bytes=VMEM_WHOLE),
        name="place_rows",
    )(place, *arrays, *into)


def input_kernel(n_blocks, parts, place, *refs):
    *arrays, out = refs
    pieces, here, arrays = arrays[:n_blocks], arrays[n_blocks], arrays[n_blocks + 1 :]
    share = out.shape[1] // len(parts)
    for k, (which, row) in enumerate(parts):
        start = pl.multiple_of(place[k] * share, share)
        total = jnp.zeros((out.shape[0], share), jnp.float32)
        for s, piece in enumerate(pieces):
            if s:
                block = arrays[which][row + (s - 1) * share : row + s * share, :]
            else:
                block = here[pl.ds(start, share), :]
            total = total + lax.dot_general(
                piece[...], block, (((1,), (1,)), ((), ())), preferred_element_type=jnp.float32
            )
        out[:, pl.ds(start, share)] = total.astype(out.dtype)


def input_gradient(pieces, here, arrays, parts, place):
    length, cols = pieces[0].shape
    feats = here.shape[0]
    (d_tokens,) = on_chip(
        functools.partial(input_kernel, len(pieces), parts),
        place,
        pieces + [here] + arrays,
        [jax.ShapeDtypeStruct((length, feats), jnp.bfloat16)],
        2 * length * feats * cols * len(pieces),
        "input_gradient",
    )
    return d_tokens


def make_body(n_dp, n_z):
    tuned = n_dp == 8 and n_z == 4

    def pair(value, s):
        return lax.ppermute(value, "tensor", [(z, z ^ s) for z in range(n_z)])

    def body(tokens, queries, d_out, segments, cached, master, moment, second, grad):
        me_dp = lax.axis_index("dp").astype(jnp.int32)
        me_z = lax.axis_index("tensor").astype(jnp.int32)
        length, feats = tokens.shape
        cols = cached.shape[1]

        master_new, moment_new, second_new, own_cache = optimizer(
            cached, master, moment, second, grad
        )

        share = feats // n_dp

        def block_for(z):
            return lax.dynamic_slice_in_dim(cached, z * feats + me_dp * share, share, 0)

        blocks = [pair(block_for(me_z ^ s), s) for s in range(1, n_z)]
        here = lax.dynamic_slice_in_dim(cached, me_z * feats, feats, 0)

        doc_ids = segments[0]
        position = jnp.arange(length)
        allowed = (doc_ids[:, None] == doc_ids[None, :]) & (position[:, None] <= position[None, :])
        allowed = allowed.astype(jnp.float32)

        total = jnp.zeros((length, cols), jnp.float32)
        zero = 0 * me_z
        orders = weight_orders() if tuned else [jnp.zeros((5,), jnp.int32)]
        total, held = absorb([tokens], zero, me_z, cached, total, None, n_z)
        if tuned:
            gather = PlaneGather(own_cache, jnp.concatenate(blocks, axis=0))
        from_low, from_high = tokens, tokens
        for s in range(1, n_z):
            low, high = me_z - s, me_z + s
            from_high = lax.ppermute(from_high, "tensor", [(z + 1, z) for z in range(n_z - s)])
            from_low = lax.ppermute(
                from_low, "tensor", [(z, z + 1) for z in range(s - 1, n_z - 1)]
            )
            if tuned and s == 1:
                from_high, from_low, held, allowed, orders, here = lax.optimization_barrier(
                    (from_high, from_low, held, allowed, orders, here)
                )
            elif tuned and s == 2:
                from_high, from_low, held, gather.got = lax.optimization_barrier(
                    (from_high, from_low, held, gather.first())
                )
            elif tuned:
                packs, swapped = gather.second()
                laid = gather.lay(swapped, cached.shape[0])
                from_high, from_low, held, gather.packs, gather.swapped, laid = (
                    lax.optimization_barrier((from_high, from_low, held, packs, swapped, laid))
                )
            chunks, which = [from_low, from_high], (me_z < s).astype(jnp.int32)
            index = jnp.where(me_z < s, high, low)
            if 2 * s < n_z:
                total, held = absorb([from_low], zero, low, cached, total, held, n_z)
                chunks, which, index = [from_high], zero, high
            if s < n_z - 1:
                total, held = absorb(chunks, which, index, cached, total, held, n_z)

        held, d_queries, d_projected, sent, kept = attend(
            chunks, which, index, cached, total, held, queries, d_out, allowed, orders[0], n_z
        )

        if tuned:
            pieces = [d_projected, pair(d_projected, 1), pair(d_projected, 2)]
        else:
            pieces = [d_projected] + [pair(d_projected, s) for s in range(1, n_z)]
        if tuned:
            sent, gather.packs_other = lax.optimization_barrier((sent, gather.third()))
            new_cache = gather.lay_rest(laid)
            finish, pieces, new_cache = weight_sum(
                held, d_projected, orders[1], sent, kept, pieces, pair, new_cache
            )
            new_grad, d_tokens = finish(input_gradient(pieces, here, *gather.feature_rows()))
        else:
            new_cache = lax.all_gather(own_cache, "dp", axis=0, tiled=True)
            rows = lax.all_gather(jnp.stack([block_for(me_z)] + blocks), "dp", axis=0)
            d_tokens = jnp.einsum(
                "slc,ksfc->lkf", jnp.stack(pieces), rows, preferred_element_type=jnp.float32
            )
            d_tokens = d_tokens.astype(jnp.bfloat16).reshape(length, feats)
            partial = lax.dot_general(
                held[:n_z].reshape(n_z * feats, length),
                d_projected,
                (((1,), (0,)), ((), ())),
                preferred_element_type=jnp.float32,
            )
            new_grad = lax.psum_scatter(
                partial.astype(jnp.bfloat16), "dp", scatter_dimension=0, tiled=True
            ).astype(jnp.float32)
        return (master_new, moment_new, second_new, new_cache, new_grad, d_queries, d_tokens)

    return body


def solution(mesh):
    in_specs = (
        P("dp", "tensor"),
        P("dp", "tensor"),
        P("dp", "tensor"),
        P("dp", None),
        P(None, "tensor"),
        P("dp", "tensor"),
        P("dp", "tensor"),
        P("dp", "tensor"),
        P("dp", "tensor"),
    )
    out_specs = (
        P("dp", "tensor"),
        P("dp", "tensor"),
        P("dp", "tensor"),
        P(None, "tensor"),
        P("dp", "tensor"),
        P("dp", "tensor"),
        P("dp", "tensor"),
    )
    body = make_body(mesh.shape["dp"], mesh.shape["tensor"])
    return jax.shard_map(body, mesh=mesh, in_specs=in_specs, out_specs=out_specs, check_vma=False)
```

```python
import functools
import math

import jax
import jax.numpy as jnp
from jax import lax
from jax.experimental import pallas as pl
from jax.experimental.pallas import tpu as pltpu
from jax.sharding import PartitionSpec as P

HD = 128
VMEM_STREAM = 60 * 1024 * 1024
VMEM_WHOLE = 24 * 1024 * 1024


beta_first = 0.9
beta_second = 0.95
learn_rate = 0.0003
weight_decay = 0.1
adam_epsilon = 1e-08
first_fix = 1.0 - 0.9**40
second_fix = 1.0 - 0.95**40


def optimizer_kernel(
    place, cached, master, moment, second, grad, master_out, moment_out, second_out, cache_out
):
    moment_new = beta_first * moment[...] + (1.0 - beta_first) * grad[...]
    second_new = beta_second * second[...] + (1.0 - beta_second) * grad[...] * grad[...]
    update = moment_new / first_fix / (jnp.sqrt(second_new / second_fix) + adam_epsilon)
    master_new = master[...] - learn_rate * (update + weight_decay * master[...])
    moment_out[...] = moment_new
    second_out[...] = second_new
    master_out[...] = master_new
    for start in range(0, cached.shape[1], HD):
        block = slice(start, start + HD)
        own_cache = cached[:, block].astype(jnp.float32)
        delta = master_new[:, block] - own_cache
        largest = jnp.max(jnp.abs(delta), axis=1, keepdims=True)
        scale = (largest + 1e-06).astype(jnp.bfloat16).astype(jnp.float32)
        codes = (delta / scale).astype(jnp.bfloat16)
        cache_out[:, block] = (own_cache + codes.astype(jnp.float32) * scale).astype(jnp.bfloat16)


def optimizer(cached, master, moment, second, grad):
    rows, cols = master.shape
    step = min(rows, 256)
    steps = rows // step
    own = pl.BlockSpec((step, cols), lambda i, place: (i, 0))
    full = jax.ShapeDtypeStruct((rows, cols), jnp.float32)
    return pl.pallas_call(
        optimizer_kernel,
        grid_spec=pltpu.PrefetchScalarGridSpec(
            num_scalar_prefetch=1,
            grid=(steps,),
            in_specs=[pl.BlockSpec((step, cols), lambda i, place: (place[0] * steps + i, 0))]
            + [own] * 4,
            out_specs=[own] * 4,
        ),
        out_shape=[full, full, full, jax.ShapeDtypeStruct((rows, cols), jnp.bfloat16)],
        cost_estimate=pl.CostEstimate(
            flops=40 * rows * cols, bytes_accessed=32 * rows * cols, transcendentals=rows * cols
        ),
        compiler_params=pltpu.CompilerParams(vmem_limit_bytes=VMEM_STREAM),
        name="optimizer",
    )(lax.axis_index("dp").astype(jnp.int32).reshape(1), cached, master, moment, second, grad)


def on_chip(kernel, place, arrays, out_shape, flops, name):
    vmem = pl.BlockSpec(memory_space=pltpu.VMEM)
    size = sum(a.size * a.dtype.itemsize for a in arrays)
    size += sum(s.size * s.dtype.itemsize for s in out_shape)
    return pl.pallas_call(
        kernel,
        in_specs=[pl.BlockSpec(memory_space=pltpu.SMEM)] + [vmem] * len(arrays),
        out_specs=[vmem] * len(out_shape),
        out_shape=out_shape,
        cost_estimate=pl.CostEstimate(flops=flops, bytes_accessed=size, transcendentals=0),
        compiler_params=pltpu.CompilerParams(vmem_limit_bytes=VMEM_WHOLE),
        name=name,
    )(place, *arrays)


def fetch_chunk(place, chunks, chunk, sem):
    for n, source in enumerate(chunks):

        @pl.when(place[2] == n)
        def _():
            pltpu.make_async_copy(source, chunk, sem).start()

    return pltpu.make_async_copy(chunks[0], chunk, sem)


def fetch_rows(place, cached, rows, sem):
    height = rows.shape[0]
    start = pl.multiple_of(place[0] * height, height)
    copy = pltpu.make_async_copy(cached.at[pl.ds(start, height), :], rows, sem)
    copy.start()
    return copy


def absorb_kernel(n_chunks, place, *refs):
    chunks, (total, cached) = refs[:n_chunks], refs[n_chunks : n_chunks + 2]
    total_out, held, chunk, rows, turned, sems = refs[-6:]
    chunk_copy = fetch_chunk(place, chunks, chunk, sems.at[0])
    rows_copy = fetch_rows(place, cached, rows, sems.at[1])
    chunk_copy.wait()
    turned[...] = chunk[...].T
    keep = pltpu.make_async_copy(turned, held.at[place[1]], sems.at[2])
    keep.start()
    rows_copy.wait()
    total_out[...] = total[...] + jnp.dot(
        chunk[...], rows[...], preferred_element_type=jnp.float32
    )
    keep.wait()


def absorb_place(index, which, n_chunks):
    inside = (index >= 0) & (index < n_chunks)
    return jnp.stack(
        [jnp.clip(index, 0, n_chunks - 1), jnp.where(inside, index, n_chunks), which]
    ).astype(jnp.int32)


def absorb_scratch(chunk, cached, n_sems):
    length, feats = chunk.shape
    return [
        pltpu.VMEM((length, feats), chunk.dtype),
        pltpu.VMEM((feats, cached.shape[1]), cached.dtype),
        pltpu.VMEM((feats, length), chunk.dtype),
        pltpu.SemaphoreType.DMA((n_sems,)),
    ]


def absorb(chunks, which, index, cached, total, held, n_chunks):
    length, feats = chunks[0].shape
    cols = cached.shape[1]
    shape = jax.ShapeDtypeStruct((8 * n_chunks, feats, length), chunks[0].dtype)
    vmem, anywhere = pl.BlockSpec(memory_space=pltpu.VMEM), pl.BlockSpec(memory_space=pl.ANY)
    return pl.pallas_call(
        functools.partial(absorb_kernel, len(chunks)),
        in_specs=[pl.BlockSpec(memory_space=pltpu.SMEM)]
        + [anywhere] * len(chunks)
        + [vmem, anywhere]
        + ([] if held is None else [anywhere]),
        out_specs=[vmem, anywhere],
        out_shape=[jax.ShapeDtypeStruct(total.shape, jnp.float32), shape],
        scratch_shapes=absorb_scratch(chunks[0], cached, 3),
        input_output_aliases={} if held is None else {3 + len(chunks): 1},
        cost_estimate=pl.CostEstimate(
            flops=2 * length * feats * cols,
            bytes_accessed=4 * length * feats + 2 * feats * cols,
            transcendentals=0,
        ),
        compiler_params=pltpu.CompilerParams(vmem_limit_bytes=VMEM_STREAM),
        name="absorb",
    )(
        absorb_place(index, which, n_chunks),
        *chunks,
        total,
        cached,
        *([] if held is None else [held]),
    )


def attend_kernel(n_chunks, place, order, *refs):
    chunks, refs = refs[:n_chunks], refs[n_chunks:]
    total, cached, _, allowed, queries_in, d_out_in = refs[:6]
    held, d_queries, d_projected, sent, kept, *refs = refs[6:]
    chunk, rows, turned, sems, queries, d_out, buffer, part_sems = refs
    chunk_copy = fetch_chunk(place, chunks, chunk, sems.at[0])
    rows_copy = fetch_rows(place, cached, rows, sems.at[1])
    others = [
        pltpu.make_async_copy(queries_in, queries, sems.at[3]),
        pltpu.make_async_copy(d_out_in, d_out, sems.at[4]),
    ]
    for copy in others:
        copy.start()
    chunk_copy.wait()
    turned[...] = chunk[...].T
    keep = pltpu.make_async_copy(turned, held.at[place[1]], sems.at[2])
    keep.start()
    rows_copy.wait()
    projected = (
        total[...] + jnp.dot(chunk[...], rows[...], preferred_element_type=jnp.float32)
    ).astype(jnp.bfloat16)
    seen = allowed[...] > 0
    for copy in others:
        copy.wait()
    factor = 1.0 / math.sqrt(HD)
    across = (((1,), (1,)), ((), ()))
    heads = projected.shape[1] // (2 * HD)
    group = queries.shape[1] // HD // heads
    for head in range(heads):
        start = 2 * HD * head
        keys = projected[:, start : start + HD]
        values = projected[:, start + HD : start + 2 * HD]
        d_keys = jnp.zeros(keys.shape, jnp.float32)
        d_values = jnp.zeros(keys.shape, jnp.float32)
        for g in range(head * group, (head + 1) * group):
            if g == heads * group // 2:
                keep.wait()
                copies = fetch_parts(order, held, range(4), buffer, part_sems)
            columns = slice(g * HD, (g + 1) * HD)
            query, grad = queries[:, columns], d_out[:, columns]
            scores = lax.dot_general(keys, query, across, preferred_element_type=jnp.float32)
            scores = jnp.where(seen, scores, -1e30)
            highest = jnp.max(scores, axis=0, keepdims=True)
            weights = jnp.exp2((scores - highest) * (factor * math.log2(math.e)))
            share = 1.0 / jnp.sum(weights, axis=0, keepdims=True)
            probs_low = (weights * share).astype(jnp.bfloat16)
            d_probs = lax.dot_general(values, grad, across, preferred_element_type=jnp.float32)
            rowdot = jnp.sum(probs_low.astype(jnp.float32) * d_probs, axis=0, keepdims=True)
            d_scores = (weights * (d_probs - rowdot) * (share * factor)).astype(jnp.bfloat16)
            d_queries[:, columns] = lax.dot_general(
                d_scores, keys, (((0,), (0,)), ((), ())), preferred_element_type=jnp.float32
            ).astype(jnp.bfloat16)
            d_keys = d_keys + jnp.dot(d_scores, query, preferred_element_type=jnp.float32)
            d_values = d_values + jnp.dot(probs_low, grad, preferred_element_type=jnp.float32)
        d_projected[:, start : start + HD] = d_keys.astype(jnp.bfloat16)
        d_projected[:, start + HD : start + 2 * HD] = d_values.astype(jnp.bfloat16)

    def give(g, side, position, here, part):
        out = (sent, kept)[g]
        out[2 * side + position, here, :] = part.astype(out.dtype)

    weight_products(copies, (SENT, KEPT), buffer, d_projected, give)


def attend(chunks, which, index, cached, total, held, queries, d_out, allowed, order, n_chunks):
    feats, length = held.shape[1:]
    parts = jax.ShapeDtypeStruct((4, feats // 2, total.shape[1] // 2), jnp.bfloat16)
    vmem, anywhere = pl.BlockSpec(memory_space=pltpu.VMEM), pl.BlockSpec(memory_space=pl.ANY)
    return pl.pallas_call(
        functools.partial(attend_kernel, len(chunks)),
        in_specs=[pl.BlockSpec(memory_space=pltpu.SMEM)] * 2
        + [anywhere] * len(chunks)
        + [vmem, anywhere, anywhere, vmem, anywhere, anywhere],
        out_specs=[anywhere] + [vmem] * 4,
        out_shape=[
            jax.ShapeDtypeStruct(held.shape, held.dtype),
            jax.ShapeDtypeStruct(queries.shape, jnp.bfloat16),
            jax.ShapeDtypeStruct(total.shape, jnp.bfloat16),
            parts,
            parts,
        ],
        scratch_shapes=absorb_scratch(chunks[0], cached, 5)
        + [
            pltpu.VMEM(queries.shape, queries.dtype),
            pltpu.VMEM(d_out.shape, d_out.dtype),
            pltpu.VMEM((4, feats // 2, length), held.dtype),
            pltpu.SemaphoreType.DMA((4,)),
        ],
        input_output_aliases={4 + len(chunks): 0},
        cost_estimate=pl.CostEstimate(
            flops=12 * allowed.size * queries.shape[1],
            bytes_accessed=8 * queries.size,
            transcendentals=allowed.size * queries.shape[1] // HD,
        ),
        compiler_params=pltpu.CompilerParams(vmem_limit_bytes=VMEM_STREAM),
        name="attend",
    )(
        absorb_place(index, which, n_chunks),
        order,
        *chunks,
        total,
        cached,
        held,
        allowed,
        queries,
        d_out,
    )


SENT = ((0, 0, 0), (0, 1, 0), (1, 0, 1), (2, 1, 1))
KEPT = ((1, 1, 0), (2, 0, 0), (3, 0, 1), (3, 1, 1))


def fetch_parts(place, held, chunks, buffer, sems):
    rows = buffer.shape[1]
    start = pl.multiple_of(place[4] * rows, rows)
    copies = {}
    for chunk in chunks:
        copies[chunk] = pltpu.make_async_copy(
            held.at[place[chunk], pl.ds(start, rows), :], buffer.at[chunk], sems.at[chunk]
        )
        copies[chunk].start()
    return copies


def weight_products(copies, groups, buffer, d_projected, give):
    rows = buffer.shape[1]
    half = d_projected.shape[1] // 2
    block = min(rows, 256)
    for chunk, copy in copies.items():
        copy.wait()
        wanted = [
            (g, side, position)
            for g, group in enumerate(groups)
            for which, side, position in group
            if which == chunk
        ]
        first, last = min(w[1] for w in wanted), max(w[1] for w in wanted)
        for r in range(0, rows, block):
            here = slice(r, r + block)
            total = jnp.dot(
                buffer[chunk, here, :],
                d_projected[:, first * half : (last + 1) * half],
                preferred_element_type=jnp.float32,
            )
            for g, side, position in wanted:
                part = total[:, (side - first) * half : (side - first + 1) * half]
                give(g, side, position, here, part)


def weight_kernel(group, place, held, d_projected, *refs):
    *added, out_a, out_b, buffer, sems = refs
    copies = fetch_parts(place, held, sorted({part[0] for part in group}), buffer, sems)

    def give(_, side, position, here, part):
        if added:
            part = part + added[0][2 * side + position, here, :].astype(jnp.float32)
        out = (out_a, out_b)[side]
        out[position, here, :] = part.astype(out.dtype)

    weight_products(copies, (group,), buffer, d_projected, give)


def weight_parts(held, d_projected, place, group, added, dtype, name):
    length, cols = d_projected.shape
    rows = held.shape[1] // 2
    vmem = pl.BlockSpec(memory_space=pltpu.VMEM)
    return pl.pallas_call(
        functools.partial(weight_kernel, group),
        in_specs=[pl.BlockSpec(memory_space=pltpu.SMEM), pl.BlockSpec(memory_space=pl.ANY)]
        + [vmem] * (1 + len(added)),
        out_specs=[vmem] * 2,
        out_shape=[jax.ShapeDtypeStruct((2, rows, cols // 2), dtype)] * 2,
        scratch_shapes=[
            pltpu.VMEM((4, rows, length), held.dtype),
            pltpu.SemaphoreType.DMA((4,)),
        ],
        cost_estimate=pl.CostEstimate(
            flops=4 * length * rows * cols, bytes_accessed=8 * rows * cols, transcendentals=0
        ),
        compiler_params=pltpu.CompilerParams(vmem_limit_bytes=VMEM_WHOLE),
        name=name,
    )(place, held, d_projected, *added)


def add_kernel(place, own_a, own_b, other, out_a, out_b):
    depth = own_a.shape[0]
    for side, (own, out) in enumerate(((own_a, out_a), (own_b, out_b))):
        other_here = other[side * depth : (side + 1) * depth]
        out[...] = (own[...] + other_here.astype(jnp.float32)).astype(out.dtype)


def combine_kernel(place, keep_a, got_a, keep_b, got_b, out_a, out_b):
    for keep, got, out in ((keep_a, got_a, out_a), (keep_b, got_b, out_b)):
        out[...] = (keep[0] + got[0].astype(jnp.float32)).astype(out.dtype)


def finish_kernel(place, keep_a, got_a, keep_b, got_b, last_a, last_b, out):
    half = last_a.shape[1]
    sides = ((keep_a, got_a, last_a), (keep_b, got_b, last_b))
    for side, (keep, got, last) in enumerate(sides):
        total = keep[1] + got[1].astype(jnp.float32) + last[...].astype(jnp.float32)
        out[:, side * half : (side + 1) * half] = total


def plane():
    index = lax.axis_index("dp").astype(jnp.int32)

    def swap(value, bit):
        return lax.ppermute(value, "dp", [(i, i ^ bit) for i in range(8)])

    return index % 2, (index // 2) % 2, index // 4, swap


def weight_orders():
    core, x, y, _ = plane()
    chunks = [3 - x - 2 * y, 1 - x + 2 * y, x + 2 - 2 * y, x + 2 * y]
    return [jnp.stack(chunks + [half]) for half in (1 - core, core)]


def weight_sum(held, d_projected, order, sent, kept, pieces, beside):
    swap = plane()[3]
    rows, cols = held.shape[1] // 2, d_projected.shape[1]
    none = jnp.zeros((1,), jnp.int32)
    sent, kept = swap(sent, 1), swap(kept, 1)
    own = weight_parts(held, d_projected, order, SENT, [], jnp.float32, "weight_send")
    shape = jax.ShapeDtypeStruct(own[0].shape, jnp.bfloat16)
    send_a, send_b = on_chip(
        add_kernel, none, list(own) + [sent], [shape] * 2, 2 * cols * rows, "weight_add"
    )
    got_a, got_b = swap(send_a, 2), swap(send_b, 4)
    keep_a, keep_b = weight_parts(
        held, d_projected, order, KEPT, [kept], jnp.float32, "weight_keep"
    )
    pieces, got_a, got_b, beside = lax.optimization_barrier((pieces[::-1], got_a, got_b, beside))
    pieces = pieces[::-1]

    small = jax.ShapeDtypeStruct((rows, cols // 2), jnp.bfloat16)
    arrays = [keep_a, got_a, keep_b, got_b]
    last_a, last_b = on_chip(
        combine_kernel, none, arrays, [small] * 2, cols * rows, "weight_combine"
    )
    last = [swap(last_a, 4), swap(last_b, 2)]

    def finish(ready):
        ended, ready = lax.optimization_barrier((last, ready))
        (total,) = on_chip(
            finish_kernel,
            none,
            arrays + ended,
            [jax.ShapeDtypeStruct((rows, cols), jnp.float32)],
            2 * cols * rows,
            "weight_finish",
        )
        return total, ready

    return finish, pieces, beside


class PlaneGather:
    def __init__(self, own_cache, own_rows):
        self.height, self.count = own_cache.shape[0], own_rows.shape[0]
        self.cut = (self.height + self.count) // 2
        self.both = jnp.concatenate([own_cache, own_rows], axis=0)
        short = self.height - self.cut
        self.own = (
            own_cache[: self.cut],
            jnp.concatenate([own_cache[self.cut :], own_rows], axis=0),
        )
        self.short = short

    def first(self):
        swap = plane()[3]
        return swap(self.own[1], 2), swap(self.own[0], 4), swap(self.both, 1)

    def second(self):
        swap = plane()[3]
        second_x, first_y, _ = self.got
        packs = (
            swap(jnp.concatenate([self.own[0], first_y], axis=0), 2),
            swap(jnp.concatenate([self.own[1], second_x], axis=0), 4),
        )
        return packs, (swap(second_x, 1), swap(first_y, 1))

    def third(self):
        swap = plane()[3]
        return swap(self.packs[0], 1), swap(self.packs[1], 1)

    def where(self, bits):
        return lax.axis_index("dp").astype(jnp.int32) ^ jnp.array(bits, dtype=jnp.int32)

    def lay(self, swapped, n_rows):
        arrays = [self.both, self.got[2], self.got[1], swapped[1], self.got[0], swapped[0]]
        cut, short = self.cut, self.short
        parts = [(0, 0, 0, self.height), (1, 0, 0, self.height), (2, 0, 0, cut), (3, 0, 0, cut)]
        parts += [(4, 0, cut, short), (5, 0, cut, short)]
        return place_rows(arrays, parts, self.where([0, 1, 4, 5, 2, 3]), self.height, n_rows, [])

    def lay_rest(self, laid):
        cut, short = self.cut, self.short
        size = self.own[1].shape[0]
        arrays = [self.packs[0], self.packs_other[0], self.packs[1], self.packs_other[1]]
        parts = [(0, 0, 0, cut), (0, cut, 0, cut), (1, 0, 0, cut), (1, cut, 0, cut)]
        parts += [(2, 0, cut, short), (2, size, cut, short)]
        parts += [(3, 0, cut, short), (3, size, cut, short)]
        devices = self.where([2, 6, 3, 7, 4, 6, 5, 7])
        return place_rows(arrays, parts, devices, self.height, laid.shape[0], [laid])

    def feature_rows(self):
        size, short = self.own[1].shape[0], self.short
        arrays = [self.own[1], self.got[2], self.got[0], self.swapped[0]]
        arrays += [self.packs[1], self.packs_other[1]]
        parts = [(0, short), (1, self.height), (2, short), (3, short)]
        parts += [(4, short), (4, size + short), (5, short), (5, size + short)]
        return arrays, parts, self.where([0, 1, 2, 3, 4, 6, 5, 7])


def place_rows_kernel(height, parts, place, *refs):
    out, sems = refs[-2:]
    copies = []
    for k, (which, row, first, count) in enumerate(parts):
        start = pl.multiple_of(place[k] * height + first, math.gcd(height, first or height))
        copies.append(
            pltpu.make_async_copy(
                refs[which].at[pl.ds(row, count), :], out.at[pl.ds(start, count), :], sems.at[k]
            )
        )
    for copy in copies:
        copy.start()
    for copy in copies:
        copy.wait()


def place_rows(arrays, parts, place, height, rows, into):
    cols = arrays[0].shape[1]
    anywhere = pl.BlockSpec(memory_space=pl.ANY)
    return pl.pallas_call(
        functools.partial(place_rows_kernel, height, parts),
        in_specs=[pl.BlockSpec(memory_space=pltpu.SMEM)]
        + [pl.BlockSpec(memory_space=pltpu.VMEM)] * len(arrays)
        + [anywhere] * len(into),
        out_specs=anywhere,
        out_shape=jax.ShapeDtypeStruct((rows, cols), arrays[0].dtype),
        scratch_shapes=[pltpu.SemaphoreType.DMA((len(parts),))],
        input_output_aliases={1 + len(arrays): 0} if into else {},
        cost_estimate=pl.CostEstimate(
            flops=0, bytes_accessed=4 * height * cols * len(parts), transcendentals=0
        ),
        compiler_params=pltpu.CompilerParams(vmem_limit_bytes=VMEM_WHOLE),
        name="place_rows",
    )(place, *arrays, *into)


def input_kernel(n_blocks, parts, place, *refs):
    *arrays, out = refs
    pieces, here, arrays = arrays[:n_blocks], arrays[n_blocks], arrays[n_blocks + 1 :]
    share = out.shape[1] // len(parts)
    for k, (which, row) in enumerate(parts):
        start = pl.multiple_of(place[k] * share, share)
        total = jnp.zeros((out.shape[0], share), jnp.float32)
        for s, piece in enumerate(pieces):
            if s:
                block = arrays[which][row + (s - 1) * share : row + s * share, :]
            else:
                block = here[pl.ds(start, share), :]
            total = total + lax.dot_general(
                piece[...], block, (((1,), (1,)), ((), ())), preferred_element_type=jnp.float32
            )
        out[:, pl.ds(start, share)] = total.astype(out.dtype)


def input_gradient(pieces, here, arrays, parts, place):
    length, cols = pieces[0].shape
    feats = here.shape[0]
    (d_tokens,) = on_chip(
        functools.partial(input_kernel, len(pieces), parts),
        place,
        pieces + [here] + arrays,
        [jax.ShapeDtypeStruct((length, feats), jnp.bfloat16)],
        2 * length * feats * cols * len(pieces),
        "input_gradient",
    )
    return d_tokens


def make_body(n_dp, n_z):
    tuned = n_dp == 8 and n_z == 4

    def pair(value, s):
        return lax.ppermute(value, "tensor", [(z, z ^ s) for z in range(n_z)])

    def body(tokens, queries, d_out, segments, cached, master, moment, second, grad):
        me_dp = lax.axis_index("dp").astype(jnp.int32)
        me_z = lax.axis_index("tensor").astype(jnp.int32)
        length, feats = tokens.shape
        cols = cached.shape[1]

        master_new, moment_new, second_new, own_cache = optimizer(
            cached, master, moment, second, grad
        )

        share = feats // n_dp

        def block_for(z):
            return lax.dynamic_slice_in_dim(cached, z * feats + me_dp * share, share, 0)

        blocks = [pair(block_for(me_z ^ s), s) for s in range(1, n_z)]
        here = lax.dynamic_slice_in_dim(cached, me_z * feats, feats, 0)

        doc_ids = segments[0]
        position = jnp.arange(length)
        allowed = (doc_ids[:, None] == doc_ids[None, :]) & (position[:, None] <= position[None, :])
        allowed = allowed.astype(jnp.float32)

        total = jnp.zeros((length, cols), jnp.float32)
        zero = 0 * me_z
        orders = weight_orders() if tuned else [jnp.zeros((5,), jnp.int32)]
        total, held = absorb([tokens], zero, me_z, cached, total, None, n_z)
        from_low, from_high = tokens, tokens
        for s in range(1, n_z):
            low, high = me_z - s, me_z + s
            from_high = lax.ppermute(from_high, "tensor", [(z + 1, z) for z in range(n_z - s)])
            from_low = lax.ppermute(
                from_low, "tensor", [(z, z + 1) for z in range(s - 1, n_z - 1)]
            )
            if tuned and s == 1:
                from_high, from_low, held, allowed, orders, here = lax.optimization_barrier(
                    (from_high, from_low, held, allowed, orders, here)
                )
                blocks = lax.optimization_barrier((blocks, from_high, from_low))[0]
                gather = PlaneGather(own_cache, jnp.concatenate(blocks, axis=0))
            elif tuned and s == 2:
                from_high, from_low, held, gather.got = lax.optimization_barrier(
                    (from_high, from_low, held, gather.first())
                )
            elif tuned:
                packs, swapped = gather.second()
                laid = gather.lay(swapped, cached.shape[0])
                from_high, from_low, held, gather.packs, gather.swapped, laid = (
                    lax.optimization_barrier((from_high, from_low, held, packs, swapped, laid))
                )
            chunks, which = [from_low, from_high], (me_z < s).astype(jnp.int32)
            index = jnp.where(me_z < s, high, low)
            if 2 * s < n_z:
                total, held = absorb([from_low], zero, low, cached, total, held, n_z)
                chunks, which, index = [from_high], zero, high
            if s < n_z - 1:
                total, held = absorb(chunks, which, index, cached, total, held, n_z)

        held, d_queries, d_projected, sent, kept = attend(
            chunks, which, index, cached, total, held, queries, d_out, allowed, orders[0], n_z
        )

        pieces = [pair(d_projected, s) for s in range(n_z - 1, 0, -1)]
        pieces = [d_projected] + pieces[::-1]
        if tuned:
            sent, gather.packs_other = lax.optimization_barrier((sent, gather.third()))
            new_cache = gather.lay_rest(laid)
            finish, pieces, new_cache = weight_sum(
                held, d_projected, orders[1], sent, kept, pieces, new_cache
            )
            new_grad, d_tokens = finish(input_gradient(pieces, here, *gather.feature_rows()))
        else:
            new_cache = lax.all_gather(own_cache, "dp", axis=0, tiled=True)
            rows = lax.all_gather(jnp.stack([block_for(me_z)] + blocks), "dp", axis=0)
            d_tokens = jnp.einsum(
                "slc,ksfc->lkf", jnp.stack(pieces), rows, preferred_element_type=jnp.float32
            )
            d_tokens = d_tokens.astype(jnp.bfloat16).reshape(length, feats)
            partial = lax.dot_general(
                held[:n_z].reshape(n_z * feats, length),
                d_projected,
                (((1,), (0,)), ((), ())),
                preferred_element_type=jnp.float32,
            )
            new_grad = lax.psum_scatter(
                partial.astype(jnp.bfloat16), "dp", scatter_dimension=0, tiled=True
            ).astype(jnp.float32)
        return (master_new, moment_new, second_new, new_cache, new_grad, d_queries, d_tokens)

    return body


def solution(mesh):
    in_specs = (
        P("dp", "tensor"),
        P("dp", "tensor"),
        P("dp", "tensor"),
        P("dp", None),
        P(None, "tensor"),
        P("dp", "tensor"),
        P("dp", "tensor"),
        P("dp", "tensor"),
        P("dp", "tensor"),
    )
    out_specs = (
        P("dp", "tensor"),
        P("dp", "tensor"),
        P("dp", "tensor"),
        P(None, "tensor"),
        P("dp", "tensor"),
        P("dp", "tensor"),
        P("dp", "tensor"),
    )
    body = make_body(mesh.shape["dp"], mesh.shape["tensor"])
    return jax.shard_map(body, mesh=mesh, in_specs=in_specs, out_specs=out_specs, check_vma=False)
```

```python
import functools
import math

import jax
import jax.numpy as jnp
from jax import lax
from jax.experimental import pallas as pl
from jax.experimental.pallas import tpu as pltpu
from jax.sharding import PartitionSpec as P

HD = 128
VMEM_STREAM = 60 * 1024 * 1024
VMEM_WHOLE = 24 * 1024 * 1024


beta_first = 0.9
beta_second = 0.95
learn_rate = 0.0003
weight_decay = 0.1
adam_epsilon = 1e-08
first_fix = 1.0 - 0.9**40
second_fix = 1.0 - 0.95**40


def optimizer_kernel(
    place, cached, master, moment, second, grad, master_out, moment_out, second_out, cache_out
):
    moment_new = beta_first * moment[...] + (1.0 - beta_first) * grad[...]
    second_new = beta_second * second[...] + (1.0 - beta_second) * grad[...] * grad[...]
    update = moment_new / first_fix / (jnp.sqrt(second_new / second_fix) + adam_epsilon)
    master_new = master[...] - learn_rate * (update + weight_decay * master[...])
    moment_out[...] = moment_new
    second_out[...] = second_new
    master_out[...] = master_new
    for start in range(0, cached.shape[1], HD):
        block = slice(start, start + HD)
        own_cache = cached[:, block].astype(jnp.float32)
        delta = master_new[:, block] - own_cache
        largest = jnp.max(jnp.abs(delta), axis=1, keepdims=True)
        scale = (largest + 1e-06).astype(jnp.bfloat16).astype(jnp.float32)
        codes = (delta / scale).astype(jnp.bfloat16)
        cache_out[:, block] = (own_cache + codes.astype(jnp.float32) * scale).astype(jnp.bfloat16)


def optimizer(cached, master, moment, second, grad):
    rows, cols = master.shape
    step = min(rows, 256)
    steps = rows // step
    own = pl.BlockSpec((step, cols), lambda i, place: (i, 0))
    full = jax.ShapeDtypeStruct((rows, cols), jnp.float32)
    return pl.pallas_call(
        optimizer_kernel,
        grid_spec=pltpu.PrefetchScalarGridSpec(
            num_scalar_prefetch=1,
            grid=(steps,),
            in_specs=[pl.BlockSpec((step, cols), lambda i, place: (place[0] * steps + i, 0))]
            + [own] * 4,
            out_specs=[own] * 4,
        ),
        out_shape=[full, full, full, jax.ShapeDtypeStruct((rows, cols), jnp.bfloat16)],
        cost_estimate=pl.CostEstimate(
            flops=40 * rows * cols, bytes_accessed=32 * rows * cols, transcendentals=rows * cols
        ),
        compiler_params=pltpu.CompilerParams(vmem_limit_bytes=VMEM_STREAM),
        name="optimizer",
    )(lax.axis_index("dp").astype(jnp.int32).reshape(1), cached, master, moment, second, grad)


def on_chip(kernel, place, arrays, out_shape, flops, name):
    vmem = pl.BlockSpec(memory_space=pltpu.VMEM)
    size = sum(a.size * a.dtype.itemsize for a in arrays)
    size += sum(s.size * s.dtype.itemsize for s in out_shape)
    return pl.pallas_call(
        kernel,
        in_specs=[pl.BlockSpec(memory_space=pltpu.SMEM)] + [vmem] * len(arrays),
        out_specs=[vmem] * len(out_shape),
        out_shape=out_shape,
        cost_estimate=pl.CostEstimate(flops=flops, bytes_accessed=size, transcendentals=0),
        compiler_params=pltpu.CompilerParams(vmem_limit_bytes=VMEM_WHOLE),
        name=name,
    )(place, *arrays)


def fetch_chunk(place, chunks, chunk, sem):
    for n, source in enumerate(chunks):

        @pl.when(place[2] == n)
        def _():
            pltpu.make_async_copy(source, chunk, sem).start()

    return pltpu.make_async_copy(chunks[0], chunk, sem)


def fetch_rows(place, cached, rows, sem):
    height = rows.shape[0]
    start = pl.multiple_of(place[0] * height, height)
    copy = pltpu.make_async_copy(cached.at[pl.ds(start, height), :], rows, sem)
    copy.start()
    return copy


def absorb_kernel(n_chunks, place, *refs):
    chunks, (total, cached) = refs[:n_chunks], refs[n_chunks : n_chunks + 2]
    total_out, held, chunk, rows, turned, sems = refs[-6:]
    chunk_copy = fetch_chunk(place, chunks, chunk, sems.at[0])
    rows_copy = fetch_rows(place, cached, rows, sems.at[1])
    chunk_copy.wait()
    turned[...] = chunk[...].T
    keep = pltpu.make_async_copy(turned, held.at[place[1]], sems.at[2])
    keep.start()
    rows_copy.wait()
    total_out[...] = total[...] + jnp.dot(
        chunk[...], rows[...], preferred_element_type=jnp.float32
    )
    keep.wait()


def absorb_place(index, which, n_chunks):
    inside = (index >= 0) & (index < n_chunks)
    return jnp.stack(
        [jnp.clip(index, 0, n_chunks - 1), jnp.where(inside, index, n_chunks), which]
    ).astype(jnp.int32)


def absorb_scratch(chunk, cached, n_sems):
    length, feats = chunk.shape
    return [
        pltpu.VMEM((length, feats), chunk.dtype),
        pltpu.VMEM((feats, cached.shape[1]), cached.dtype),
        pltpu.VMEM((feats, length), chunk.dtype),
        pltpu.SemaphoreType.DMA((n_sems,)),
    ]


def absorb(chunks, which, index, cached, total, held, n_chunks):
    length, feats = chunks[0].shape
    cols = cached.shape[1]
    shape = jax.ShapeDtypeStruct((8 * n_chunks, feats, length), chunks[0].dtype)
    vmem, anywhere = pl.BlockSpec(memory_space=pltpu.VMEM), pl.BlockSpec(memory_space=pl.ANY)
    return pl.pallas_call(
        functools.partial(absorb_kernel, len(chunks)),
        in_specs=[pl.BlockSpec(memory_space=pltpu.SMEM)]
        + [anywhere] * len(chunks)
        + [vmem, anywhere]
        + ([] if held is None else [anywhere]),
        out_specs=[vmem, anywhere],
        out_shape=[jax.ShapeDtypeStruct(total.shape, jnp.float32), shape],
        scratch_shapes=absorb_scratch(chunks[0], cached, 3),
        input_output_aliases={} if held is None else {3 + len(chunks): 1},
        cost_estimate=pl.CostEstimate(
            flops=2 * length * feats * cols,
            bytes_accessed=4 * length * feats + 2 * feats * cols,
            transcendentals=0,
        ),
        compiler_params=pltpu.CompilerParams(vmem_limit_bytes=VMEM_STREAM),
        name="absorb",
    )(
        absorb_place(index, which, n_chunks),
        *chunks,
        total,
        cached,
        *([] if held is None else [held]),
    )


def attend_kernel(n_chunks, place, order, *refs):
    chunks, refs = refs[:n_chunks], refs[n_chunks:]
    total, cached, _, allowed, queries_in, d_out_in = refs[:6]
    held, d_queries, d_projected, sent, kept, *refs = refs[6:]
    chunk, rows, turned, sems, queries, d_out, buffer, part_sems = refs
    chunk_copy = fetch_chunk(place, chunks, chunk, sems.at[0])
    rows_copy = fetch_rows(place, cached, rows, sems.at[1])
    others = [
        pltpu.make_async_copy(queries_in, queries, sems.at[3]),
        pltpu.make_async_copy(d_out_in, d_out, sems.at[4]),
    ]
    for copy in others:
        copy.start()
    chunk_copy.wait()
    turned[...] = chunk[...].T
    keep = pltpu.make_async_copy(turned, held.at[place[1]], sems.at[2])
    keep.start()
    rows_copy.wait()
    projected = (
        total[...] + jnp.dot(chunk[...], rows[...], preferred_element_type=jnp.float32)
    ).astype(jnp.bfloat16)
    seen = allowed[...] > 0
    for copy in others:
        copy.wait()
    factor = 1.0 / math.sqrt(HD)
    across = (((1,), (1,)), ((), ()))
    heads = projected.shape[1] // (2 * HD)
    group = queries.shape[1] // HD // heads
    for head in range(heads):
        start = 2 * HD * head
        keys = projected[:, start : start + HD]
        values = projected[:, start + HD : start + 2 * HD]
        d_keys = jnp.zeros(keys.shape, jnp.float32)
        d_values = jnp.zeros(keys.shape, jnp.float32)
        for g in range(head * group, (head + 1) * group):
            if g == heads * group // 2:
                keep.wait()
                copies = fetch_parts(order, held, range(4), buffer, part_sems)
            columns = slice(g * HD, (g + 1) * HD)
            query, grad = queries[:, columns], d_out[:, columns]
            scores = (
                lax.dot_general(keys, query, across, preferred_element_type=jnp.float32) * factor
            )
            scores = jnp.where(seen, scores, -1e30)
            weights = jnp.exp(scores - jnp.max(scores, axis=0, keepdims=True))
            probs = weights / jnp.sum(weights, axis=0, keepdims=True)
            probs_low = probs.astype(jnp.bfloat16)
            d_probs = lax.dot_general(values, grad, across, preferred_element_type=jnp.float32)
            rowdot = jnp.sum(probs_low.astype(jnp.float32) * d_probs, axis=0, keepdims=True)
            d_scores = (probs * (d_probs - rowdot) * factor).astype(jnp.bfloat16)
            d_queries[:, columns] = lax.dot_general(
                d_scores, keys, (((0,), (0,)), ((), ())), preferred_element_type=jnp.float32
            ).astype(jnp.bfloat16)
            d_keys = d_keys + jnp.dot(d_scores, query, preferred_element_type=jnp.float32)
            d_values = d_values + jnp.dot(probs_low, grad, preferred_element_type=jnp.float32)
        d_projected[:, start : start + HD] = d_keys.astype(jnp.bfloat16)
        d_projected[:, start + HD : start + 2 * HD] = d_values.astype(jnp.bfloat16)

    def give(g, side, position, here, part):
        out = (sent, kept)[g]
        out[2 * side + position, here, :] = part.astype(out.dtype)

    weight_products(copies, (SENT, KEPT), buffer, d_projected, give)


def attend(chunks, which, index, cached, total, held, queries, d_out, allowed, order, n_chunks):
    feats, length = held.shape[1:]
    parts = jax.ShapeDtypeStruct((4, feats // 2, total.shape[1] // 2), jnp.bfloat16)
    vmem, anywhere = pl.BlockSpec(memory_space=pltpu.VMEM), pl.BlockSpec(memory_space=pl.ANY)
    return pl.pallas_call(
        functools.partial(attend_kernel, len(chunks)),
        in_specs=[pl.BlockSpec(memory_space=pltpu.SMEM)] * 2
        + [anywhere] * len(chunks)
        + [vmem, anywhere, anywhere, vmem, anywhere, anywhere],
        out_specs=[anywhere] + [vmem] * 4,
        out_shape=[
            jax.ShapeDtypeStruct(held.shape, held.dtype),
            jax.ShapeDtypeStruct(queries.shape, jnp.bfloat16),
            jax.ShapeDtypeStruct(total.shape, jnp.bfloat16),
            parts,
            parts,
        ],
        scratch_shapes=absorb_scratch(chunks[0], cached, 5)
        + [
            pltpu.VMEM(queries.shape, queries.dtype),
            pltpu.VMEM(d_out.shape, d_out.dtype),
            pltpu.VMEM((4, feats // 2, length), held.dtype),
            pltpu.SemaphoreType.DMA((4,)),
        ],
        input_output_aliases={4 + len(chunks): 0},
        cost_estimate=pl.CostEstimate(
            flops=12 * allowed.size * queries.shape[1],
            bytes_accessed=8 * queries.size,
            transcendentals=allowed.size * queries.shape[1] // HD,
        ),
        compiler_params=pltpu.CompilerParams(vmem_limit_bytes=VMEM_STREAM),
        name="attend",
    )(
        absorb_place(index, which, n_chunks),
        order,
        *chunks,
        total,
        cached,
        held,
        allowed,
        queries,
        d_out,
    )


SENT = ((0, 0, 0), (0, 1, 0), (1, 0, 1), (2, 1, 1))
KEPT = ((1, 1, 0), (2, 0, 0), (3, 0, 1), (3, 1, 1))


def fetch_parts(place, held, chunks, buffer, sems):
    rows = buffer.shape[1]
    start = pl.multiple_of(place[4] * rows, rows)
    copies = {}
    for chunk in chunks:
        copies[chunk] = pltpu.make_async_copy(
            held.at[place[chunk], pl.ds(start, rows), :], buffer.at[chunk], sems.at[chunk]
        )
        copies[chunk].start()
    return copies


def weight_products(copies, groups, buffer, d_projected, give):
    rows = buffer.shape[1]
    half = d_projected.shape[1] // 2
    block = min(rows, 256)
    for chunk, copy in copies.items():
        copy.wait()
        wanted = [
            (g, side, position)
            for g, group in enumerate(groups)
            for which, side, position in group
            if which == chunk
        ]
        first, last = min(w[1] for w in wanted), max(w[1] for w in wanted)
        for r in range(0, rows, block):
            here = slice(r, r + block)
            total = jnp.dot(
                buffer[chunk, here, :],
                d_projected[:, first * half : (last + 1) * half],
                preferred_element_type=jnp.float32,
            )
            for g, side, position in wanted:
                part = total[:, (side - first) * half : (side - first + 1) * half]
                give(g, side, position, here, part)


def weight_kernel(group, place, held, d_projected, *refs):
    *added, out_a, out_b, buffer, sems = refs
    copies = fetch_parts(place, held, sorted({part[0] for part in group}), buffer, sems)

    def give(_, side, position, here, part):
        if added:
            part = part + added[0][2 * side + position, here, :].astype(jnp.float32)
        out = (out_a, out_b)[side]
        out[position, here, :] = part.astype(out.dtype)

    weight_products(copies, (group,), buffer, d_projected, give)


def weight_parts(held, d_projected, place, group, added, dtype, name):
    length, cols = d_projected.shape
    rows = held.shape[1] // 2
    vmem = pl.BlockSpec(memory_space=pltpu.VMEM)
    return pl.pallas_call(
        functools.partial(weight_kernel, group),
        in_specs=[pl.BlockSpec(memory_space=pltpu.SMEM), pl.BlockSpec(memory_space=pl.ANY)]
        + [vmem] * (1 + len(added)),
        out_specs=[vmem] * 2,
        out_shape=[jax.ShapeDtypeStruct((2, rows, cols // 2), dtype)] * 2,
        scratch_shapes=[
            pltpu.VMEM((4, rows, length), held.dtype),
            pltpu.SemaphoreType.DMA((4,)),
        ],
        cost_estimate=pl.CostEstimate(
            flops=4 * length * rows * cols, bytes_accessed=8 * rows * cols, transcendentals=0
        ),
        compiler_params=pltpu.CompilerParams(vmem_limit_bytes=VMEM_WHOLE),
        name=name,
    )(place, held, d_projected, *added)


def add_kernel(place, own_a, own_b, other, out_a, out_b):
    depth = own_a.shape[0]
    for side, (own, out) in enumerate(((own_a, out_a), (own_b, out_b))):
        other_here = other[side * depth : (side + 1) * depth]
        out[...] = (own[...] + other_here.astype(jnp.float32)).astype(out.dtype)


def combine_kernel(place, keep_a, got_a, keep_b, got_b, out_a, out_b):
    for keep, got, out in ((keep_a, got_a, out_a), (keep_b, got_b, out_b)):
        out[...] = (keep[0] + got[0].astype(jnp.float32)).astype(out.dtype)


def finish_kernel(place, keep_a, got_a, keep_b, got_b, last_a, last_b, out):
    half = last_a.shape[1]
    sides = ((keep_a, got_a, last_a), (keep_b, got_b, last_b))
    for side, (keep, got, last) in enumerate(sides):
        total = keep[1] + got[1].astype(jnp.float32) + last[...].astype(jnp.float32)
        out[:, side * half : (side + 1) * half] = total


def plane():
    index = lax.axis_index("dp").astype(jnp.int32)

    def swap(value, bit):
        return lax.ppermute(value, "dp", [(i, i ^ bit) for i in range(8)])

    return index % 2, (index // 2) % 2, index // 4, swap


def weight_orders():
    core, x, y, _ = plane()
    chunks = [3 - x - 2 * y, 1 - x + 2 * y, x + 2 - 2 * y, x + 2 * y]
    return [jnp.stack(chunks + [half]) for half in (1 - core, core)]


def weight_sum(held, d_projected, order, sent, kept, pieces, beside):
    swap = plane()[3]
    rows, cols = held.shape[1] // 2, d_projected.shape[1]
    none = jnp.zeros((1,), jnp.int32)
    sent, kept = swap(sent, 1), swap(kept, 1)
    own = weight_parts(held, d_projected, order, SENT, [], jnp.float32, "weight_send")
    shape = jax.ShapeDtypeStruct(own[0].shape, jnp.bfloat16)
    send_a, send_b = on_chip(
        add_kernel, none, list(own) + [sent], [shape] * 2, 2 * cols * rows, "weight_add"
    )
    got_a, got_b = swap(send_a, 2), swap(send_b, 4)
    keep_a, keep_b = weight_parts(
        held, d_projected, order, KEPT, [kept], jnp.float32, "weight_keep"
    )
    pieces, got_a, got_b, beside = lax.optimization_barrier((pieces[::-1], got_a, got_b, beside))
    pieces = pieces[::-1]

    small = jax.ShapeDtypeStruct((rows, cols // 2), jnp.bfloat16)
    arrays = [keep_a, got_a, keep_b, got_b]
    last_a, last_b = on_chip(
        combine_kernel, none, arrays, [small] * 2, cols * rows, "weight_combine"
    )
    last = [swap(last_a, 4), swap(last_b, 2)]

    def finish(ready):
        ended, ready = lax.optimization_barrier((last, ready))
        (total,) = on_chip(
            finish_kernel,
            none,
            arrays + ended,
            [jax.ShapeDtypeStruct((rows, cols), jnp.float32)],
            2 * cols * rows,
            "weight_finish",
        )
        return total, ready

    return finish, pieces, beside


class PlaneGather:
    def __init__(self, own_cache, own_rows):
        self.own = own_cache, own_rows
        self.both = jnp.concatenate([own_cache, own_rows], axis=0)

    def first(self, held):
        swap = plane()[3]
        rows_x, cache_y = swap(self.own[1], 2), swap(self.own[0], 4)
        rows_x, cache_y, _ = lax.optimization_barrier((rows_x, cache_y, held))
        packs = (
            jnp.concatenate([self.own[0], cache_y], axis=0),
            jnp.concatenate([self.own[1], rows_x], axis=0),
        )
        return rows_x, cache_y, swap(self.both, 1), packs

    def second(self):
        swap = plane()[3]
        rows_x, cache_y, _, packs = self.got
        return (swap(packs[0], 2), swap(packs[1], 4)), (swap(rows_x, 1), swap(cache_y, 1))

    def third(self):
        swap = plane()[3]
        return swap(self.packs[0], 1), swap(self.packs[1], 1)

    def where(self, bits):
        return lax.axis_index("dp").astype(jnp.int32) ^ jnp.array(bits, dtype=jnp.int32)

    def lay(self, swapped, n_rows):
        arrays = [self.own[0], self.got[2], self.got[1], swapped[1]]
        return place_rows(arrays, [(k, 0) for k in range(4)], self.where([0, 1, 4, 5]),
                          self.own[0].shape[0], n_rows, [])

    def lay_rest(self, laid):
        height = self.own[0].shape[0]
        parts = [(0, 0), (0, height), (1, 0), (1, height)]
        arrays = [self.packs[0], self.packs_other[0]]
        return place_rows(
            arrays, parts, self.where([2, 6, 3, 7]), height, laid.shape[0], [laid]
        )

    def feature_rows(self):
        height, count = self.own[0].shape[0], self.own[1].shape[0]
        arrays = [self.own[1], self.got[2], self.got[0], self.swapped[0]]
        arrays += [self.packs[1], self.packs_other[1]]
        parts = [(0, 0), (1, height), (2, 0), (3, 0), (4, 0), (4, count), (5, 0), (5, count)]
        return arrays, parts, self.where([0, 1, 2, 3, 4, 6, 5, 7])


def place_rows_kernel(height, parts, place, *refs):
    out, sems = refs[-2:]
    copies = []
    for k, (which, row) in enumerate(parts):
        start = pl.multiple_of(place[k] * height, height)
        copies.append(
            pltpu.make_async_copy(
                refs[which].at[pl.ds(row, height), :],
                out.at[pl.ds(start, height), :],
                sems.at[k],
            )
        )
    for copy in copies:
        copy.start()
    for copy in copies:
        copy.wait()


def place_rows(arrays, parts, place, height, rows, into):
    cols = arrays[0].shape[1]
    anywhere = pl.BlockSpec(memory_space=pl.ANY)
    return pl.pallas_call(
        functools.partial(place_rows_kernel, height, parts),
        in_specs=[pl.BlockSpec(memory_space=pltpu.SMEM)]
        + [pl.BlockSpec(memory_space=pltpu.VMEM)] * len(arrays)
        + [anywhere] * len(into),
        out_specs=anywhere,
        out_shape=jax.ShapeDtypeStruct((rows, cols), arrays[0].dtype),
        scratch_shapes=[pltpu.SemaphoreType.DMA((len(parts),))],
        input_output_aliases={1 + len(arrays): 0} if into else {},
        cost_estimate=pl.CostEstimate(
            flops=0, bytes_accessed=4 * height * cols * len(parts), transcendentals=0
        ),
        compiler_params=pltpu.CompilerParams(vmem_limit_bytes=VMEM_WHOLE),
        name="place_rows",
    )(place, *arrays, *into)


def input_kernel(n_blocks, parts, place, *refs):
    *arrays, out = refs
    pieces, here, arrays = arrays[:n_blocks], arrays[n_blocks], arrays[n_blocks + 1 :]
    share = out.shape[1] // len(parts)
    for k, (which, row) in enumerate(parts):
        start = pl.multiple_of(place[k] * share, share)
        total = jnp.zeros((out.shape[0], share), jnp.float32)
        for s, piece in enumerate(pieces):
            if s:
                block = arrays[which][row + (s - 1) * share : row + s * share, :]
            else:
                block = here[pl.ds(start, share), :]
            total = total + lax.dot_general(
                piece[...], block, (((1,), (1,)), ((), ())), preferred_element_type=jnp.float32
            )
        out[:, pl.ds(start, share)] = total.astype(out.dtype)


def input_gradient(pieces, here, arrays, parts, place):
    length, cols = pieces[0].shape
    feats = here.shape[0]
    (d_tokens,) = on_chip(
        functools.partial(input_kernel, len(pieces), parts),
        place,
        pieces + [here] + arrays,
        [jax.ShapeDtypeStruct((length, feats), jnp.bfloat16)],
        2 * length * feats * cols * len(pieces),
        "input_gradient",
    )
    return d_tokens


def make_body(n_dp, n_z):
    tuned = n_dp == 8 and n_z == 4

    def pair(value, s):
        return lax.ppermute(value, "tensor", [(z, z ^ s) for z in range(n_z)])

    def body(tokens, queries, d_out, segments, cached, master, moment, second, grad):
        me_dp = lax.axis_index("dp").astype(jnp.int32)
        me_z = lax.axis_index("tensor").astype(jnp.int32)
        length, feats = tokens.shape
        cols = cached.shape[1]

        master_new, moment_new, second_new, own_cache = optimizer(
            cached, master, moment, second, grad
        )

        share = feats // n_dp

        def block_for(z):
            return lax.dynamic_slice_in_dim(cached, z * feats + me_dp * share, share, 0)

        blocks = [pair(block_for(me_z ^ s), s) for s in range(1, n_z)]
        here = lax.dynamic_slice_in_dim(cached, me_z * feats, feats, 0)

        doc_ids = segments[0]
        position = jnp.arange(length)
        allowed = (doc_ids[:, None] == doc_ids[None, :]) & (position[:, None] <= position[None, :])
        allowed = allowed.astype(jnp.float32)

        total = jnp.zeros((length, cols), jnp.float32)
        zero = 0 * me_z
        orders = weight_orders() if tuned else [jnp.zeros((5,), jnp.int32)]
        total, held = absorb([tokens], zero, me_z, cached, total, None, n_z)
        from_low, from_high = tokens, tokens
        for s in range(1, n_z):
            low, high = me_z - s, me_z + s
            from_high = lax.ppermute(from_high, "tensor", [(z + 1, z) for z in range(n_z - s)])
            from_low = lax.ppermute(
                from_low, "tensor", [(z, z + 1) for z in range(s - 1, n_z - 1)]
            )
            if tuned and s == 1:
                from_high, from_low, held, allowed, orders, here = lax.optimization_barrier(
                    (from_high, from_low, held, allowed, orders, here)
                )
                blocks, ready, _, _ = lax.optimization_barrier(
                    (blocks, own_cache, from_high, from_low)
                )
                gather = PlaneGather(ready, jnp.concatenate(blocks, axis=0))
            elif tuned and s == 2:
                from_high, from_low, held, gather.got = lax.optimization_barrier(
                    (from_high, from_low, held, gather.first(held))
                )
            elif tuned:
                packs, swapped = gather.second()
                laid = gather.lay(swapped, cached.shape[0])
                from_high, from_low, held, gather.packs, gather.swapped, laid = (
                    lax.optimization_barrier((from_high, from_low, held, packs, swapped, laid))
                )
            chunks, which = [from_low, from_high], (me_z < s).astype(jnp.int32)
            index = jnp.where(me_z < s, high, low)
            if 2 * s < n_z:
                total, held = absorb([from_low], zero, low, cached, total, held, n_z)
                chunks, which, index = [from_high], zero, high
            if s < n_z - 1:
                total, held = absorb(chunks, which, index, cached, total, held, n_z)

        held, d_queries, d_projected, sent, kept = attend(
            chunks, which, index, cached, total, held, queries, d_out, allowed, orders[0], n_z
        )

        pieces = [pair(d_projected, s) for s in range(n_z - 1, 0, -1)]
        pieces = [d_projected] + pieces[::-1]
        if tuned:
            sent, gather.packs_other = lax.optimization_barrier((sent, gather.third()))
            new_cache = gather.lay_rest(laid)
            finish, pieces, new_cache = weight_sum(
                held, d_projected, orders[1], sent, kept, pieces, new_cache
            )
            new_grad, d_tokens = finish(input_gradient(pieces, here, *gather.feature_rows()))
        else:
            new_cache = lax.all_gather(own_cache, "dp", axis=0, tiled=True)
            rows = lax.all_gather(jnp.stack([block_for(me_z)] + blocks), "dp", axis=0)
            d_tokens = jnp.einsum(
                "slc,ksfc->lkf", jnp.stack(pieces), rows, preferred_element_type=jnp.float32
            )
            d_tokens = d_tokens.astype(jnp.bfloat16).reshape(length, feats)
            partial = lax.dot_general(
                held[:n_z].reshape(n_z * feats, length),
                d_projected,
                (((1,), (0,)), ((), ())),
                preferred_element_type=jnp.float32,
            )
            new_grad = lax.psum_scatter(
                partial.astype(jnp.bfloat16), "dp", scatter_dimension=0, tiled=True
            ).astype(jnp.float32)
        return (master_new, moment_new, second_new, new_cache, new_grad, d_queries, d_tokens)

    return body


def solution(mesh):
    in_specs = (
        P("dp", "tensor"),
        P("dp", "tensor"),
        P("dp", "tensor"),
        P("dp", None),
        P(None, "tensor"),
        P("dp", "tensor"),
        P("dp", "tensor"),
        P("dp", "tensor"),
        P("dp", "tensor"),
    )
    out_specs = (
        P("dp", "tensor"),
        P("dp", "tensor"),
        P("dp", "tensor"),
        P(None, "tensor"),
        P("dp", "tensor"),
        P("dp", "tensor"),
        P("dp", "tensor"),
    )
    body = make_body(mesh.shape["dp"], mesh.shape["tensor"])
    return jax.shard_map(body, mesh=mesh, in_specs=in_specs, out_specs=out_specs, check_vma=False)
```

```python
import functools
import math

import jax
import jax.numpy as jnp
from jax import lax
from jax.experimental import pallas as pl
from jax.experimental.pallas import tpu as pltpu
from jax.sharding import PartitionSpec as P

HD = 128
VMEM_STREAM = 60 * 1024 * 1024
VMEM_WHOLE = 24 * 1024 * 1024


beta_first = 0.9
beta_second = 0.95
learn_rate = 0.0003
weight_decay = 0.1
adam_epsilon = 1e-08
first_fix = 1.0 - 0.9**40
second_fix = 1.0 - 0.95**40


def optimizer_kernel(
    place, cached, master, moment, second, grad, master_out, moment_out, second_out, cache_out
):
    moment_new = beta_first * moment[...] + (1.0 - beta_first) * grad[...]
    second_new = beta_second * second[...] + (1.0 - beta_second) * grad[...] * grad[...]
    update = moment_new / first_fix / (jnp.sqrt(second_new / second_fix) + adam_epsilon)
    master_new = master[...] - learn_rate * (update + weight_decay * master[...])
    moment_out[...] = moment_new
    second_out[...] = second_new
    master_out[...] = master_new
    for start in range(0, cached.shape[1], HD):
        block = slice(start, start + HD)
        own_cache = cached[:, block].astype(jnp.float32)
        delta = master_new[:, block] - own_cache
        largest = jnp.max(jnp.abs(delta), axis=1, keepdims=True)
        scale = (largest + 1e-06).astype(jnp.bfloat16).astype(jnp.float32)
        codes = (delta / scale).astype(jnp.bfloat16)
        cache_out[:, block] = (own_cache + codes.astype(jnp.float32) * scale).astype(jnp.bfloat16)


def optimizer(cached, master, moment, second, grad):
    rows, cols = master.shape
    step = min(rows, 256)
    steps = rows // step
    own = pl.BlockSpec((step, cols), lambda i, place: (i, 0))
    full = jax.ShapeDtypeStruct((rows, cols), jnp.float32)
    return pl.pallas_call(
        optimizer_kernel,
        grid_spec=pltpu.PrefetchScalarGridSpec(
            num_scalar_prefetch=1,
            grid=(steps,),
            in_specs=[pl.BlockSpec((step, cols), lambda i, place: (place[0] * steps + i, 0))]
            + [own] * 4,
            out_specs=[own] * 4,
        ),
        out_shape=[full, full, full, jax.ShapeDtypeStruct((rows, cols), jnp.bfloat16)],
        cost_estimate=pl.CostEstimate(
            flops=40 * rows * cols, bytes_accessed=32 * rows * cols, transcendentals=rows * cols
        ),
        compiler_params=pltpu.CompilerParams(vmem_limit_bytes=VMEM_STREAM),
        name="optimizer",
    )(lax.axis_index("dp").astype(jnp.int32).reshape(1), cached, master, moment, second, grad)


def on_chip(kernel, place, arrays, out_shape, flops, name):
    vmem = pl.BlockSpec(memory_space=pltpu.VMEM)
    size = sum(a.size * a.dtype.itemsize for a in arrays)
    size += sum(s.size * s.dtype.itemsize for s in out_shape)
    return pl.pallas_call(
        kernel,
        in_specs=[pl.BlockSpec(memory_space=pltpu.SMEM)] + [vmem] * len(arrays),
        out_specs=[vmem] * len(out_shape),
        out_shape=out_shape,
        cost_estimate=pl.CostEstimate(flops=flops, bytes_accessed=size, transcendentals=0),
        compiler_params=pltpu.CompilerParams(vmem_limit_bytes=VMEM_WHOLE),
        name=name,
    )(place, *arrays)


def fetch_chunk(place, chunks, chunk, sem):
    for n, source in enumerate(chunks):

        @pl.when(place[2] == n)
        def _():
            pltpu.make_async_copy(source, chunk, sem).start()

    return pltpu.make_async_copy(chunks[0], chunk, sem)


def fetch_rows(place, cached, rows, sem):
    height = rows.shape[0]
    start = pl.multiple_of(place[0] * height, height)
    copy = pltpu.make_async_copy(cached.at[pl.ds(start, height), :], rows, sem)
    copy.start()
    return copy


def absorb_kernel(n_chunks, place, *refs):
    chunks, (total, cached) = refs[:n_chunks], refs[n_chunks : n_chunks + 2]
    total_out, held, chunk, rows, turned, sems = refs[-6:]
    chunk_copy = fetch_chunk(place, chunks, chunk, sems.at[0])
    rows_copy = fetch_rows(place, cached, rows, sems.at[1])
    chunk_copy.wait()
    turned[...] = chunk[...].T
    keep = pltpu.make_async_copy(turned, held.at[place[1]], sems.at[2])
    keep.start()
    rows_copy.wait()
    total_out[...] = total[...] + jnp.dot(
        chunk[...], rows[...], preferred_element_type=jnp.float32
    )
    keep.wait()


def absorb_place(index, which, n_chunks):
    inside = (index >= 0) & (index < n_chunks)
    return jnp.stack(
        [jnp.clip(index, 0, n_chunks - 1), jnp.where(inside, index, n_chunks), which]
    ).astype(jnp.int32)


def absorb_scratch(chunk, cached, n_sems):
    length, feats = chunk.shape
    return [
        pltpu.VMEM((length, feats), chunk.dtype),
        pltpu.VMEM((feats, cached.shape[1]), cached.dtype),
        pltpu.VMEM((feats, length), chunk.dtype),
        pltpu.SemaphoreType.DMA((n_sems,)),
    ]


def absorb(chunks, which, index, cached, total, held, n_chunks):
    length, feats = chunks[0].shape
    cols = cached.shape[1]
    shape = jax.ShapeDtypeStruct((8 * n_chunks, feats, length), chunks[0].dtype)
    vmem, anywhere = pl.BlockSpec(memory_space=pltpu.VMEM), pl.BlockSpec(memory_space=pl.ANY)
    return pl.pallas_call(
        functools.partial(absorb_kernel, len(chunks)),
        in_specs=[pl.BlockSpec(memory_space=pltpu.SMEM)]
        + [anywhere] * len(chunks)
        + [vmem, anywhere]
        + ([] if held is None else [anywhere]),
        out_specs=[vmem, anywhere],
        out_shape=[jax.ShapeDtypeStruct(total.shape, jnp.float32), shape],
        scratch_shapes=absorb_scratch(chunks[0], cached, 3),
        input_output_aliases={} if held is None else {3 + len(chunks): 1},
        cost_estimate=pl.CostEstimate(
            flops=2 * length * feats * cols,
            bytes_accessed=4 * length * feats + 2 * feats * cols,
            transcendentals=0,
        ),
        compiler_params=pltpu.CompilerParams(vmem_limit_bytes=VMEM_STREAM),
        name="absorb",
    )(
        absorb_place(index, which, n_chunks),
        *chunks,
        total,
        cached,
        *([] if held is None else [held]),
    )


def attend_kernel(n_chunks, place, order, *refs):
    chunks, refs = refs[:n_chunks], refs[n_chunks:]
    total, cached, _, allowed, queries_in, d_out_in = refs[:6]
    held, d_queries, d_projected, sent, kept, *refs = refs[6:]
    chunk, rows, turned, sems, queries, d_out, buffer, part_sems = refs
    chunk_copy = fetch_chunk(place, chunks, chunk, sems.at[0])
    rows_copy = fetch_rows(place, cached, rows, sems.at[1])
    others = [
        pltpu.make_async_copy(queries_in, queries, sems.at[3]),
        pltpu.make_async_copy(d_out_in, d_out, sems.at[4]),
    ]
    for copy in others:
        copy.start()
    chunk_copy.wait()
    turned[...] = chunk[...].T
    keep = pltpu.make_async_copy(turned, held.at[place[1]], sems.at[2])
    keep.start()
    rows_copy.wait()
    projected = (
        total[...] + jnp.dot(chunk[...], rows[...], preferred_element_type=jnp.float32)
    ).astype(jnp.bfloat16)
    seen = allowed[...] > 0
    for copy in others:
        copy.wait()
    factor = 1.0 / math.sqrt(HD)
    across = (((1,), (1,)), ((), ()))
    heads = projected.shape[1] // (2 * HD)
    group = queries.shape[1] // HD // heads
    for head in range(heads):
        start = 2 * HD * head
        keys = projected[:, start : start + HD]
        values = projected[:, start + HD : start + 2 * HD]
        d_keys = jnp.zeros(keys.shape, jnp.float32)
        d_values = jnp.zeros(keys.shape, jnp.float32)
        for g in range(head * group, (head + 1) * group):
            if g == heads * group // 2:
                keep.wait()
                copies = fetch_parts(order, held, range(4), buffer, part_sems)
            columns = slice(g * HD, (g + 1) * HD)
            query, grad = queries[:, columns], d_out[:, columns]
            scores = (
                lax.dot_general(keys, query, across, preferred_element_type=jnp.float32) * factor
            )
            scores = jnp.where(seen, scores, -1e30)
            weights = jnp.exp(scores - jnp.max(scores, axis=0, keepdims=True))
            probs = weights / jnp.sum(weights, axis=0, keepdims=True)
            probs_low = probs.astype(jnp.bfloat16)
            d_probs = lax.dot_general(values, grad, across, preferred_element_type=jnp.float32)
            rowdot = jnp.sum(probs_low.astype(jnp.float32) * d_probs, axis=0, keepdims=True)
            d_scores = (probs * (d_probs - rowdot) * factor).astype(jnp.bfloat16)
            d_queries[:, columns] = lax.dot_general(
                d_scores, keys, (((0,), (0,)), ((), ())), preferred_element_type=jnp.float32
            ).astype(jnp.bfloat16)
            d_keys = d_keys + jnp.dot(d_scores, query, preferred_element_type=jnp.float32)
            d_values = d_values + jnp.dot(probs_low, grad, preferred_element_type=jnp.float32)
        d_projected[:, start : start + HD] = d_keys.astype(jnp.bfloat16)
        d_projected[:, start + HD : start + 2 * HD] = d_values.astype(jnp.bfloat16)

    def give(g, side, position, here, part):
        out = (sent, kept)[g]
        out[2 * side + position, here, :] = part.astype(out.dtype)

    save = None
    if held.shape[2] == d_projected.shape[1]:
        save = pltpu.make_async_copy(
            d_projected,
            held.at[held.shape[0] - 1, pl.ds(0, d_projected.shape[0]), :],
            sems.at[2],
        )
        save.start()
    weight_products(copies, (SENT, KEPT), buffer, d_projected, give)
    if save is not None:
        save.wait()


def attend(chunks, which, index, cached, total, held, queries, d_out, allowed, order, n_chunks):
    feats, length = held.shape[1:]
    parts = jax.ShapeDtypeStruct((4, feats // 2, total.shape[1] // 2), jnp.bfloat16)
    vmem, anywhere = pl.BlockSpec(memory_space=pltpu.VMEM), pl.BlockSpec(memory_space=pl.ANY)
    return pl.pallas_call(
        functools.partial(attend_kernel, len(chunks)),
        in_specs=[pl.BlockSpec(memory_space=pltpu.SMEM)] * 2
        + [anywhere] * len(chunks)
        + [vmem, anywhere, anywhere, vmem, anywhere, anywhere],
        out_specs=[anywhere] + [vmem] * 4,
        out_shape=[
            jax.ShapeDtypeStruct(held.shape, held.dtype),
            jax.ShapeDtypeStruct(queries.shape, jnp.bfloat16),
            jax.ShapeDtypeStruct(total.shape, jnp.bfloat16),
            parts,
            parts,
        ],
        scratch_shapes=absorb_scratch(chunks[0], cached, 5)
        + [
            pltpu.VMEM(queries.shape, queries.dtype),
            pltpu.VMEM(d_out.shape, d_out.dtype),
            pltpu.VMEM((4, feats // 2, length), held.dtype),
            pltpu.SemaphoreType.DMA((4,)),
        ],
        input_output_aliases={4 + len(chunks): 0},
        cost_estimate=pl.CostEstimate(
            flops=12 * allowed.size * queries.shape[1],
            bytes_accessed=8 * queries.size,
            transcendentals=allowed.size * queries.shape[1] // HD,
        ),
        compiler_params=pltpu.CompilerParams(vmem_limit_bytes=VMEM_STREAM),
        name="attend",
    )(
        absorb_place(index, which, n_chunks),
        order,
        *chunks,
        total,
        cached,
        held,
        allowed,
        queries,
        d_out,
    )


SENT = ((0, 0, 0), (0, 1, 0), (1, 0, 1), (2, 1, 1))
KEPT = ((1, 1, 0), (2, 0, 0), (3, 0, 1), (3, 1, 1))


def fetch_columns(held, columns, sem):
    length = columns.shape[0]
    return pltpu.make_async_copy(
        held.at[held.shape[0] - 1, pl.ds(0, length), :], columns, sem
    )


def fetch_parts(place, held, chunks, buffer, sems):
    rows = buffer.shape[1]
    start = pl.multiple_of(place[4] * rows, rows)
    copies = {}
    for chunk in chunks:
        copies[chunk] = pltpu.make_async_copy(
            held.at[place[chunk], pl.ds(start, rows), :], buffer.at[chunk], sems.at[chunk]
        )
        copies[chunk].start()
    return copies


def weight_products(copies, groups, buffer, d_projected, give):
    rows = buffer.shape[1]
    half = d_projected.shape[1] // 2
    block = min(rows, 256)
    for chunk, copy in copies.items():
        copy.wait()
        wanted = [
            (g, side, position)
            for g, group in enumerate(groups)
            for which, side, position in group
            if which == chunk
        ]
        first, last = min(w[1] for w in wanted), max(w[1] for w in wanted)
        for r in range(0, rows, block):
            here = slice(r, r + block)
            total = jnp.dot(
                buffer[chunk, here, :],
                d_projected[:, first * half : (last + 1) * half],
                preferred_element_type=jnp.float32,
            )
            for g, side, position in wanted:
                part = total[:, (side - first) * half : (side - first + 1) * half]
                give(g, side, position, here, part)


def weight_kernel(group, place, held, *refs):
    *added, out_a, out_b, buffer, columns, sems, sem = refs
    columns_copy = fetch_columns(held, columns, sem)
    columns_copy.start()
    copies = fetch_parts(place, held, sorted({part[0] for part in group}), buffer, sems)
    columns_copy.wait()

    def give(_, side, position, here, part):
        if added:
            part = part + added[0][2 * side + position, here, :].astype(jnp.float32)
        out = (out_a, out_b)[side]
        out[position, here, :] = part.astype(out.dtype)

    weight_products(copies, (group,), buffer, columns, give)


def weight_parts(held, place, group, added, dtype, name):
    length = cols = held.shape[2]
    rows = held.shape[1] // 2
    vmem = pl.BlockSpec(memory_space=pltpu.VMEM)
    return pl.pallas_call(
        functools.partial(weight_kernel, group),
        in_specs=[pl.BlockSpec(memory_space=pltpu.SMEM), pl.BlockSpec(memory_space=pl.ANY)]
        + [vmem] * len(added),
        out_specs=[vmem] * 2,
        out_shape=[jax.ShapeDtypeStruct((2, rows, cols // 2), dtype)] * 2,
        scratch_shapes=[
            pltpu.VMEM((4, rows, length), held.dtype),
            pltpu.VMEM((length, cols), held.dtype),
            pltpu.SemaphoreType.DMA((4,)),
            pltpu.SemaphoreType.DMA,
        ],
        cost_estimate=pl.CostEstimate(
            flops=4 * length * rows * cols, bytes_accessed=8 * rows * cols, transcendentals=0
        ),
        compiler_params=pltpu.CompilerParams(vmem_limit_bytes=VMEM_WHOLE),
        name=name,
    )(place, held, *added)


def add_kernel(place, own_a, own_b, other, out_a, out_b):
    depth = own_a.shape[0]
    for side, (own, out) in enumerate(((own_a, out_a), (own_b, out_b))):
        other_here = other[side * depth : (side + 1) * depth]
        out[...] = (own[...] + other_here.astype(jnp.float32)).astype(out.dtype)


def combine_kernel(place, keep_a, got_a, keep_b, got_b, out_a, out_b):
    for keep, got, out in ((keep_a, got_a, out_a), (keep_b, got_b, out_b)):
        out[...] = (keep[0] + got[0].astype(jnp.float32)).astype(out.dtype)


def finish_kernel(place, keep_a, got_a, keep_b, got_b, last_a, last_b, out):
    half = last_a.shape[1]
    sides = ((keep_a, got_a, last_a), (keep_b, got_b, last_b))
    for side, (keep, got, last) in enumerate(sides):
        total = keep[1] + got[1].astype(jnp.float32) + last[...].astype(jnp.float32)
        out[:, side * half : (side + 1) * half] = total


def plane():
    index = lax.axis_index("dp").astype(jnp.int32)

    def swap(value, bit):
        return lax.ppermute(value, "dp", [(i, i ^ bit) for i in range(8)])

    return index % 2, (index // 2) % 2, index // 4, swap


def weight_orders():
    core, x, y, _ = plane()
    chunks = [3 - x - 2 * y, 1 - x + 2 * y, x + 2 - 2 * y, x + 2 * y]
    return [jnp.stack(chunks + [half]) for half in (1 - core, core)]


def weight_sum(held, order, sent, kept, pieces, beside):
    swap = plane()[3]
    rows, cols = held.shape[1] // 2, held.shape[2]
    none = jnp.zeros((1,), jnp.int32)
    sent, kept = swap(sent, 1), swap(kept, 1)
    own = weight_parts(held, order, SENT, [], jnp.float32, "weight_send")
    shape = jax.ShapeDtypeStruct(own[0].shape, jnp.bfloat16)
    send_a, send_b = on_chip(
        add_kernel, none, list(own) + [sent], [shape] * 2, 2 * cols * rows, "weight_add"
    )
    got_a, got_b = swap(send_a, 2), swap(send_b, 4)
    keep_a, keep_b = weight_parts(
        held, order, KEPT, [kept], jnp.float32, "weight_keep"
    )
    got_a, got_b, pieces, beside = lax.optimization_barrier((got_a, got_b, pieces, beside))

    small = jax.ShapeDtypeStruct((rows, cols // 2), jnp.bfloat16)
    arrays = [keep_a, got_a, keep_b, got_b]
    last_a, last_b = on_chip(
        combine_kernel, none, arrays, [small] * 2, cols * rows, "weight_combine"
    )
    last = [swap(last_a, 4), swap(last_b, 2)]

    def finish(ready):
        ended, ready = lax.optimization_barrier((last, ready))
        (total,) = on_chip(
            finish_kernel,
            none,
            arrays + ended,
            [jax.ShapeDtypeStruct((rows, cols), jnp.float32)],
            2 * cols * rows,
            "weight_finish",
        )
        return total, ready

    return finish, pieces, beside


class PlaneGather:
    def __init__(self, own_cache, own_rows):
        self.own = own_cache, own_rows
        self.both = jnp.concatenate([own_cache, own_rows], axis=0)

    def first(self, held):
        swap = plane()[3]
        rows_x, cache_y = swap(self.own[1], 2), swap(self.own[0], 4)
        rows_x, cache_y, _ = lax.optimization_barrier((rows_x, cache_y, held))
        packs = (
            jnp.concatenate([self.own[0], cache_y], axis=0),
            jnp.concatenate([self.own[1], rows_x], axis=0),
        )
        return rows_x, cache_y, swap(self.both, 1), packs

    def second(self):
        swap = plane()[3]
        rows_x, cache_y, _, packs = self.got
        return (swap(packs[0], 2), swap(packs[1], 4)), (swap(rows_x, 1), swap(cache_y, 1))

    def third(self):
        swap = plane()[3]
        return swap(self.packs[0], 1), swap(self.packs[1], 1)

    def where(self, bits):
        return lax.axis_index("dp").astype(jnp.int32) ^ jnp.array(bits, dtype=jnp.int32)

    def lay(self, swapped, n_rows):
        arrays = [self.own[0], self.got[2], self.got[1], swapped[1]]
        return place_rows(arrays, [(k, 0) for k in range(4)], self.where([0, 1, 4, 5]),
                          self.own[0].shape[0], n_rows, [])

    def lay_rest(self, laid):
        height = self.own[0].shape[0]
        parts = [(0, 0), (0, height), (1, 0), (1, height)]
        arrays = [self.packs[0], self.packs_other[0]]
        return place_rows(
            arrays, parts, self.where([2, 6, 3, 7]), height, laid.shape[0], [laid]
        )

    def feature_rows(self):
        height, count = self.own[0].shape[0], self.own[1].shape[0]
        arrays = [self.own[1], self.got[2], self.got[0], self.swapped[0]]
        arrays += [self.packs[1], self.packs_other[1]]
        parts = [(0, 0), (1, height), (2, 0), (3, 0), (4, 0), (4, count), (5, 0), (5, count)]
        return arrays, parts, self.where([0, 1, 2, 3, 4, 6, 5, 7])


def place_rows_kernel(height, parts, place, *refs):
    out, sems = refs[-2:]
    copies = []
    for k, (which, row) in enumerate(parts):
        start = pl.multiple_of(place[k] * height, height)
        copies.append(
            pltpu.make_async_copy(
                refs[which].at[pl.ds(row, height), :],
                out.at[pl.ds(start, height), :],
                sems.at[k],
            )
        )
    for copy in copies:
        copy.start()
    for copy in copies:
        copy.wait()


def place_rows(arrays, parts, place, height, rows, into):
    cols = arrays[0].shape[1]
    anywhere = pl.BlockSpec(memory_space=pl.ANY)
    return pl.pallas_call(
        functools.partial(place_rows_kernel, height, parts),
        in_specs=[pl.BlockSpec(memory_space=pltpu.SMEM)]
        + [pl.BlockSpec(memory_space=pltpu.VMEM)] * len(arrays)
        + [anywhere] * len(into),
        out_specs=anywhere,
        out_shape=jax.ShapeDtypeStruct((rows, cols), arrays[0].dtype),
        scratch_shapes=[pltpu.SemaphoreType.DMA((len(parts),))],
        input_output_aliases={1 + len(arrays): 0} if into else {},
        cost_estimate=pl.CostEstimate(
            flops=0, bytes_accessed=4 * height * cols * len(parts), transcendentals=0
        ),
        compiler_params=pltpu.CompilerParams(vmem_limit_bytes=VMEM_WHOLE),
        name="place_rows",
    )(place, *arrays, *into)


def input_kernel(n_blocks, parts, place, *refs):
    *arrays, out = refs
    pieces, here, arrays = arrays[:n_blocks], arrays[n_blocks], arrays[n_blocks + 1 :]
    share = out.shape[1] // len(parts)
    for k, (which, row) in enumerate(parts):
        start = pl.multiple_of(place[k] * share, share)
        total = jnp.zeros((out.shape[0], share), jnp.float32)
        for s, piece in enumerate(pieces):
            if s:
                block = arrays[which][row + (s - 1) * share : row + s * share, :]
            else:
                block = here[pl.ds(start, share), :]
            total = total + lax.dot_general(
                piece[...], block, (((1,), (1,)), ((), ())), preferred_element_type=jnp.float32
            )
        out[:, pl.ds(start, share)] = total.astype(out.dtype)


def input_gradient(pieces, here, arrays, parts, place):
    length, cols = pieces[0].shape
    feats = here.shape[0]
    (d_tokens,) = on_chip(
        functools.partial(input_kernel, len(pieces), parts),
        place,
        pieces + [here] + arrays,
        [jax.ShapeDtypeStruct((length, feats), jnp.bfloat16)],
        2 * length * feats * cols * len(pieces),
        "input_gradient",
    )
    return d_tokens


def make_body(n_dp, n_z):
    mesh_tuned = n_dp == 8 and n_z == 4

    def pair(value, s):
        return lax.ppermute(value, "tensor", [(z, z ^ s) for z in range(n_z)])

    def body(tokens, queries, d_out, segments, cached, master, moment, second, grad):
        me_dp = lax.axis_index("dp").astype(jnp.int32)
        me_z = lax.axis_index("tensor").astype(jnp.int32)
        length, feats = tokens.shape
        cols = cached.shape[1]
        tuned = mesh_tuned and length == cols

        master_new, moment_new, second_new, own_cache = optimizer(
            cached, master, moment, second, grad
        )

        share = feats // n_dp

        def block_for(z):
            return lax.dynamic_slice_in_dim(cached, z * feats + me_dp * share, share, 0)

        blocks = [pair(block_for(me_z ^ s), s) for s in range(1, n_z)]
        here = lax.dynamic_slice_in_dim(cached, me_z * feats, feats, 0)

        doc_ids = segments[0]
        position = jnp.arange(length)
        allowed = (doc_ids[:, None] == doc_ids[None, :]) & (position[:, None] <= position[None, :])
        allowed = allowed.astype(jnp.float32)

        total = jnp.zeros((length, cols), jnp.float32)
        zero = 0 * me_z
        orders = weight_orders() if tuned else [jnp.zeros((5,), jnp.int32)]
        total, held = absorb([tokens], zero, me_z, cached, total, None, n_z)
        from_low, from_high = tokens, tokens
        for s in range(1, n_z):
            low, high = me_z - s, me_z + s
            from_high = lax.ppermute(from_high, "tensor", [(z + 1, z) for z in range(n_z - s)])
            from_low = lax.ppermute(
                from_low, "tensor", [(z, z + 1) for z in range(s - 1, n_z - 1)]
            )
            if tuned and s == 1:
                from_high, from_low, held, allowed, orders, here = lax.optimization_barrier(
                    (from_high, from_low, held, allowed, orders, here)
                )
                blocks, ready, _, _ = lax.optimization_barrier(
                    (blocks, own_cache, from_high, from_low)
                )
                gather = PlaneGather(ready, jnp.concatenate(blocks, axis=0))
            elif tuned and s == 2:
                from_high, from_low, held, gather.got = lax.optimization_barrier(
                    (from_high, from_low, held, gather.first(held))
                )
            elif tuned:
                packs, swapped = gather.second()
                laid = gather.lay(swapped, cached.shape[0])
                from_high, from_low, held, gather.packs, gather.swapped, laid = (
                    lax.optimization_barrier((from_high, from_low, held, packs, swapped, laid))
                )
            chunks, which = [from_low, from_high], (me_z < s).astype(jnp.int32)
            index = jnp.where(me_z < s, high, low)
            if 2 * s < n_z:
                total, held = absorb([from_low], zero, low, cached, total, held, n_z)
                chunks, which, index = [from_high], zero, high
            if s < n_z - 1:
                total, held = absorb(chunks, which, index, cached, total, held, n_z)

        held, d_queries, d_projected, sent, kept = attend(
            chunks, which, index, cached, total, held, queries, d_out, allowed, orders[0], n_z
        )

        pieces = [d_projected] + [pair(d_projected, s) for s in range(1, n_z)]
        if tuned:
            sent, gather.packs_other = lax.optimization_barrier((sent, gather.third()))
            new_cache = gather.lay_rest(laid)
            finish, pieces, new_cache = weight_sum(
                held, orders[1], sent, kept, pieces, new_cache
            )
            new_grad, d_tokens = finish(input_gradient(pieces, here, *gather.feature_rows()))
        else:
            new_cache = lax.all_gather(own_cache, "dp", axis=0, tiled=True)
            rows = lax.all_gather(jnp.stack([block_for(me_z)] + blocks), "dp", axis=0)
            d_tokens = jnp.einsum(
                "slc,ksfc->lkf", jnp.stack(pieces), rows, preferred_element_type=jnp.float32
            )
            d_tokens = d_tokens.astype(jnp.bfloat16).reshape(length, feats)
            partial = lax.dot_general(
                held[:n_z].reshape(n_z * feats, length),
                d_projected,
                (((1,), (0,)), ((), ())),
                preferred_element_type=jnp.float32,
            )
            new_grad = lax.psum_scatter(
                partial.astype(jnp.bfloat16), "dp", scatter_dimension=0, tiled=True
            ).astype(jnp.float32)
        return (master_new, moment_new, second_new, new_cache, new_grad, d_queries, d_tokens)

    return body


def solution(mesh):
    in_specs = (
        P("dp", "tensor"),
        P("dp", "tensor"),
        P("dp", "tensor"),
        P("dp", None),
        P(None, "tensor"),
        P("dp", "tensor"),
        P("dp", "tensor"),
        P("dp", "tensor"),
        P("dp", "tensor"),
    )
    out_specs = (
        P("dp", "tensor"),
        P("dp", "tensor"),
        P("dp", "tensor"),
        P(None, "tensor"),
        P("dp", "tensor"),
        P("dp", "tensor"),
        P("dp", "tensor"),
    )
    body = make_body(mesh.shape["dp"], mesh.shape["tensor"])
    return jax.shard_map(body, mesh=mesh, in_specs=in_specs, out_specs=out_specs, check_vma=False)
```

```python
import functools
import math

import jax
import jax.numpy as jnp
from jax import lax
from jax.experimental import pallas as pl
from jax.experimental.pallas import tpu as pltpu
from jax.sharding import PartitionSpec as P

HD = 128
VMEM_STREAM = 60 * 1024 * 1024
VMEM_WHOLE = 24 * 1024 * 1024


beta_first = 0.9
beta_second = 0.95
learn_rate = 0.0003
weight_decay = 0.1
adam_epsilon = 1e-08
first_fix = 1.0 - 0.9**40
second_fix = 1.0 - 0.95**40


def optimizer_kernel(
    place, cached, master, moment, second, grad, master_out, moment_out, second_out, cache_out
):
    moment_new = beta_first * moment[...] + (1.0 - beta_first) * grad[...]
    second_new = beta_second * second[...] + (1.0 - beta_second) * grad[...] * grad[...]
    update = moment_new / first_fix / (jnp.sqrt(second_new / second_fix) + adam_epsilon)
    master_new = master[...] - learn_rate * (update + weight_decay * master[...])
    moment_out[...] = moment_new
    second_out[...] = second_new
    master_out[...] = master_new
    for start in range(0, cached.shape[1], HD):
        block = slice(start, start + HD)
        own_cache = cached[:, block].astype(jnp.float32)
        delta = master_new[:, block] - own_cache
        largest = jnp.max(jnp.abs(delta), axis=1, keepdims=True)
        scale = (largest + 1e-06).astype(jnp.bfloat16).astype(jnp.float32)
        codes = (delta / scale).astype(jnp.bfloat16)
        cache_out[:, block] = (own_cache + codes.astype(jnp.float32) * scale).astype(jnp.bfloat16)


def optimizer(cached, master, moment, second, grad):
    rows, cols = master.shape
    step = min(rows, 256)
    steps = rows // step
    own = pl.BlockSpec((step, cols), lambda i, place: (i, 0))
    full = jax.ShapeDtypeStruct((rows, cols), jnp.float32)
    return pl.pallas_call(
        optimizer_kernel,
        grid_spec=pltpu.PrefetchScalarGridSpec(
            num_scalar_prefetch=1,
            grid=(steps,),
            in_specs=[pl.BlockSpec((step, cols), lambda i, place: (place[0] * steps + i, 0))]
            + [own] * 4,
            out_specs=[own] * 4,
        ),
        out_shape=[full, full, full, jax.ShapeDtypeStruct((rows, cols), jnp.bfloat16)],
        cost_estimate=pl.CostEstimate(
            flops=40 * rows * cols, bytes_accessed=32 * rows * cols, transcendentals=rows * cols
        ),
        compiler_params=pltpu.CompilerParams(vmem_limit_bytes=VMEM_STREAM),
        name="optimizer",
    )(lax.axis_index("dp").astype(jnp.int32).reshape(1), cached, master, moment, second, grad)


def on_chip(kernel, place, arrays, out_shape, flops, name):
    vmem = pl.BlockSpec(memory_space=pltpu.VMEM)
    size = sum(a.size * a.dtype.itemsize for a in arrays)
    size += sum(s.size * s.dtype.itemsize for s in out_shape)
    return pl.pallas_call(
        kernel,
        in_specs=[pl.BlockSpec(memory_space=pltpu.SMEM)] + [vmem] * len(arrays),
        out_specs=[vmem] * len(out_shape),
        out_shape=out_shape,
        cost_estimate=pl.CostEstimate(flops=flops, bytes_accessed=size, transcendentals=0),
        compiler_params=pltpu.CompilerParams(vmem_limit_bytes=VMEM_WHOLE),
        name=name,
    )(place, *arrays)


def fetch_chunk(place, chunks, chunk, sem):
    for n, source in enumerate(chunks):

        @pl.when(place[2] == n)
        def _():
            pltpu.make_async_copy(source, chunk, sem).start()

    return pltpu.make_async_copy(chunks[0], chunk, sem)


def fetch_rows(place, cached, rows, sem):
    height = rows.shape[0]
    start = pl.multiple_of(place[0] * height, height)
    copy = pltpu.make_async_copy(cached.at[pl.ds(start, height), :], rows, sem)
    copy.start()
    return copy


def absorb_kernel(n_chunks, place, *refs):
    chunks, (total, cached) = refs[:n_chunks], refs[n_chunks : n_chunks + 2]
    total_out, held, chunk, rows, turned, sems = refs[-6:]
    chunk_copy = fetch_chunk(place, chunks, chunk, sems.at[0])
    rows_copy = fetch_rows(place, cached, rows, sems.at[1])
    chunk_copy.wait()
    turned[...] = chunk[...].T
    keep = pltpu.make_async_copy(turned, held.at[place[1]], sems.at[2])
    keep.start()
    rows_copy.wait()
    total_out[...] = total[...] + jnp.dot(
        chunk[...], rows[...], preferred_element_type=jnp.float32
    )
    keep.wait()


def absorb_place(index, which, n_chunks):
    inside = (index >= 0) & (index < n_chunks)
    return jnp.stack(
        [jnp.clip(index, 0, n_chunks - 1), jnp.where(inside, index, n_chunks), which]
    ).astype(jnp.int32)


def absorb_scratch(chunk, cached, n_sems):
    length, feats = chunk.shape
    return [
        pltpu.VMEM((length, feats), chunk.dtype),
        pltpu.VMEM((feats, cached.shape[1]), cached.dtype),
        pltpu.VMEM((feats, length), chunk.dtype),
        pltpu.SemaphoreType.DMA((n_sems,)),
    ]


def absorb(chunks, which, index, cached, total, held, n_chunks):
    length, feats = chunks[0].shape
    cols = cached.shape[1]
    shape = jax.ShapeDtypeStruct((8 * n_chunks, feats, length), chunks[0].dtype)
    vmem, anywhere = pl.BlockSpec(memory_space=pltpu.VMEM), pl.BlockSpec(memory_space=pl.ANY)
    return pl.pallas_call(
        functools.partial(absorb_kernel, len(chunks)),
        in_specs=[pl.BlockSpec(memory_space=pltpu.SMEM)]
        + [anywhere] * len(chunks)
        + [vmem, anywhere]
        + ([] if held is None else [anywhere]),
        out_specs=[vmem, anywhere],
        out_shape=[jax.ShapeDtypeStruct(total.shape, jnp.float32), shape],
        scratch_shapes=absorb_scratch(chunks[0], cached, 3),
        input_output_aliases={} if held is None else {3 + len(chunks): 1},
        cost_estimate=pl.CostEstimate(
            flops=2 * length * feats * cols,
            bytes_accessed=4 * length * feats + 2 * feats * cols,
            transcendentals=0,
        ),
        compiler_params=pltpu.CompilerParams(vmem_limit_bytes=VMEM_STREAM),
        name="absorb",
    )(
        absorb_place(index, which, n_chunks),
        *chunks,
        total,
        cached,
        *([] if held is None else [held]),
    )


def attend_kernel(n_chunks, place, order, *refs):
    chunks, refs = refs[:n_chunks], refs[n_chunks:]
    total, cached, _, allowed, queries_in, d_out_in = refs[:6]
    held, d_queries, d_projected, sent, kept, *refs = refs[6:]
    chunk, rows, turned, sems, queries, d_out, buffer, part_sems = refs
    chunk_copy = fetch_chunk(place, chunks, chunk, sems.at[0])
    rows_copy = fetch_rows(place, cached, rows, sems.at[1])
    others = [
        pltpu.make_async_copy(queries_in, queries, sems.at[3]),
        pltpu.make_async_copy(d_out_in, d_out, sems.at[4]),
    ]
    for copy in others:
        copy.start()
    chunk_copy.wait()
    turned[...] = chunk[...].T
    keep = pltpu.make_async_copy(turned, held.at[place[1]], sems.at[2])
    keep.start()
    rows_copy.wait()
    projected = (
        total[...] + jnp.dot(chunk[...], rows[...], preferred_element_type=jnp.float32)
    ).astype(jnp.bfloat16)
    seen = allowed[...] > 0
    for copy in others:
        copy.wait()
    factor = 1.0 / math.sqrt(HD)
    across = (((1,), (1,)), ((), ()))
    heads = projected.shape[1] // (2 * HD)
    group = queries.shape[1] // HD // heads
    for head in range(heads):
        start = 2 * HD * head
        keys = projected[:, start : start + HD]
        values = projected[:, start + HD : start + 2 * HD]
        d_keys = jnp.zeros(keys.shape, jnp.float32)
        d_values = jnp.zeros(keys.shape, jnp.float32)
        for g in range(head * group, (head + 1) * group):
            if g == heads * group // 2:
                keep.wait()
                copies = fetch_parts(order, held, range(4), buffer, part_sems)
            columns = slice(g * HD, (g + 1) * HD)
            query, grad = queries[:, columns], d_out[:, columns]
            scores = (
                lax.dot_general(keys, query, across, preferred_element_type=jnp.float32) * factor
            )
            scores = jnp.where(seen, scores, -1e30)
            weights = jnp.exp(scores - jnp.max(scores, axis=0, keepdims=True))
            probs = weights / jnp.sum(weights, axis=0, keepdims=True)
            probs_low = probs.astype(jnp.bfloat16)
            d_probs = lax.dot_general(values, grad, across, preferred_element_type=jnp.float32)
            rowdot = jnp.sum(probs_low.astype(jnp.float32) * d_probs, axis=0, keepdims=True)
            d_scores = (probs * (d_probs - rowdot) * factor).astype(jnp.bfloat16)
            d_queries[:, columns] = lax.dot_general(
                d_scores, keys, (((0,), (0,)), ((), ())), preferred_element_type=jnp.float32
            ).astype(jnp.bfloat16)
            d_keys = d_keys + jnp.dot(d_scores, query, preferred_element_type=jnp.float32)
            d_values = d_values + jnp.dot(probs_low, grad, preferred_element_type=jnp.float32)
        d_projected[:, start : start + HD] = d_keys.astype(jnp.bfloat16)
        d_projected[:, start + HD : start + 2 * HD] = d_values.astype(jnp.bfloat16)

    def give(g, side, position, here, part):
        out = (sent, kept)[g]
        out[2 * side + position, here, :] = part.astype(out.dtype)

    save = None
    if held.shape[2] == d_projected.shape[1]:
        save = pltpu.make_async_copy(
            d_projected,
            held.at[held.shape[0] - 1, pl.ds(0, d_projected.shape[0]), :],
            sems.at[2],
        )
        save.start()
    weight_products(copies, (SENT, KEPT), buffer, d_projected, give)
    if save is not None:
        save.wait()


def attend(chunks, which, index, cached, total, held, queries, d_out, allowed, order, n_chunks):
    feats, length = held.shape[1:]
    parts = jax.ShapeDtypeStruct((4, feats // 2, total.shape[1] // 2), jnp.bfloat16)
    vmem, anywhere = pl.BlockSpec(memory_space=pltpu.VMEM), pl.BlockSpec(memory_space=pl.ANY)
    return pl.pallas_call(
        functools.partial(attend_kernel, len(chunks)),
        in_specs=[pl.BlockSpec(memory_space=pltpu.SMEM)] * 2
        + [anywhere] * len(chunks)
        + [vmem, anywhere, anywhere, vmem, anywhere, anywhere],
        out_specs=[anywhere] + [vmem] * 4,
        out_shape=[
            jax.ShapeDtypeStruct(held.shape, held.dtype),
            jax.ShapeDtypeStruct(queries.shape, jnp.bfloat16),
            jax.ShapeDtypeStruct(total.shape, jnp.bfloat16),
            parts,
            parts,
        ],
        scratch_shapes=absorb_scratch(chunks[0], cached, 5)
        + [
            pltpu.VMEM(queries.shape, queries.dtype),
            pltpu.VMEM(d_out.shape, d_out.dtype),
            pltpu.VMEM((4, feats // 2, length), held.dtype),
            pltpu.SemaphoreType.DMA((4,)),
        ],
        input_output_aliases={4 + len(chunks): 0},
        cost_estimate=pl.CostEstimate(
            flops=12 * allowed.size * queries.shape[1],
            bytes_accessed=8 * queries.size,
            transcendentals=allowed.size * queries.shape[1] // HD,
        ),
        compiler_params=pltpu.CompilerParams(vmem_limit_bytes=VMEM_STREAM),
        name="attend",
    )(
        absorb_place(index, which, n_chunks),
        order,
        *chunks,
        total,
        cached,
        held,
        allowed,
        queries,
        d_out,
    )


SENT = ((0, 0, 0), (0, 1, 0), (1, 0, 1), (2, 1, 1))
KEPT = ((1, 1, 0), (2, 0, 0), (3, 0, 1), (3, 1, 1))


def fetch_columns(held, columns, sem):
    length = columns.shape[0]
    return pltpu.make_async_copy(
        held.at[held.shape[0] - 1, pl.ds(0, length), :], columns, sem
    )


def fetch_parts(place, held, chunks, buffer, sems):
    rows = buffer.shape[1]
    start = pl.multiple_of(place[4] * rows, rows)
    copies = {}
    for chunk in chunks:
        copies[chunk] = pltpu.make_async_copy(
            held.at[place[chunk], pl.ds(start, rows), :], buffer.at[chunk], sems.at[chunk]
        )
        copies[chunk].start()
    return copies


def weight_products(copies, groups, buffer, d_projected, give):
    rows = buffer.shape[1]
    half = d_projected.shape[1] // 2
    block = min(rows, 128)
    for chunk, copy in copies.items():
        copy.wait()
        wanted = [
            (g, side, position)
            for g, group in enumerate(groups)
            for which, side, position in group
            if which == chunk
        ]
        first, last = min(w[1] for w in wanted), max(w[1] for w in wanted)
        for r in range(0, rows, block):
            here = slice(r, r + block)
            total = jnp.dot(
                buffer[chunk, here, :],
                d_projected[:, first * half : (last + 1) * half],
                preferred_element_type=jnp.float32,
            )
            for g, side, position in wanted:
                part = total[:, (side - first) * half : (side - first + 1) * half]
                give(g, side, position, here, part)


def weight_kernel(group, place, held, *refs):
    *added, out_a, out_b, buffer, columns, sems, sem = refs
    columns_copy = fetch_columns(held, columns, sem)
    columns_copy.start()
    copies = fetch_parts(place, held, sorted({part[0] for part in group}), buffer, sems)
    columns_copy.wait()

    def give(_, side, position, here, part):
        if added:
            part = part + added[0][2 * side + position, here, :].astype(jnp.float32)
        out = (out_a, out_b)[side]
        out[position, here, :] = part.astype(out.dtype)

    weight_products(copies, (group,), buffer, columns, give)


def weight_parts(held, place, group, added, dtype, name):
    length = cols = held.shape[2]
    rows = held.shape[1] // 2
    vmem = pl.BlockSpec(memory_space=pltpu.VMEM)
    return pl.pallas_call(
        functools.partial(weight_kernel, group),
        in_specs=[pl.BlockSpec(memory_space=pltpu.SMEM), pl.BlockSpec(memory_space=pl.ANY)]
        + [vmem] * len(added),
        out_specs=[vmem] * 2,
        out_shape=[jax.ShapeDtypeStruct((2, rows, cols // 2), dtype)] * 2,
        scratch_shapes=[
            pltpu.VMEM((4, rows, length), held.dtype),
            pltpu.VMEM((length, cols), held.dtype),
            pltpu.SemaphoreType.DMA((4,)),
            pltpu.SemaphoreType.DMA,
        ],
        cost_estimate=pl.CostEstimate(
            flops=4 * length * rows * cols, bytes_accessed=8 * rows * cols, transcendentals=0
        ),
        compiler_params=pltpu.CompilerParams(vmem_limit_bytes=VMEM_WHOLE),
        name=name,
    )(place, held, *added)


def add_kernel(place, own_a, own_b, other, out_a, out_b):
    depth = own_a.shape[0]
    for side, (own, out) in enumerate(((own_a, out_a), (own_b, out_b))):
        other_here = other[side * depth : (side + 1) * depth]
        out[...] = (own[...] + other_here.astype(jnp.float32)).astype(out.dtype)


def combine_kernel(place, keep_a, got_a, keep_b, got_b, out_a, out_b):
    for keep, got, out in ((keep_a, got_a, out_a), (keep_b, got_b, out_b)):
        out[...] = (keep[0] + got[0].astype(jnp.float32)).astype(out.dtype)


def finish_kernel(place, keep_a, got_a, keep_b, got_b, last_a, last_b, out):
    half = last_a.shape[1]
    sides = ((keep_a, got_a, last_a), (keep_b, got_b, last_b))
    for side, (keep, got, last) in enumerate(sides):
        total = keep[1] + got[1].astype(jnp.float32) + last[...].astype(jnp.float32)
        out[:, side * half : (side + 1) * half] = total


def plane():
    index = lax.axis_index("dp").astype(jnp.int32)

    def swap(value, bit):
        return lax.ppermute(value, "dp", [(i, i ^ bit) for i in range(8)])

    return index % 2, (index // 2) % 2, index // 4, swap


def weight_orders():
    core, x, y, _ = plane()
    chunks = [3 - x - 2 * y, 1 - x + 2 * y, x + 2 - 2 * y, x + 2 * y]
    return [jnp.stack(chunks + [half]) for half in (1 - core, core)]


def weight_sum(held, order, sent, kept, pieces, beside):
    swap = plane()[3]
    rows, cols = held.shape[1] // 2, held.shape[2]
    none = jnp.zeros((1,), jnp.int32)
    sent, kept = swap(sent, 1), swap(kept, 1)
    own = weight_parts(held, order, SENT, [], jnp.float32, "weight_send")
    shape = jax.ShapeDtypeStruct(own[0].shape, jnp.bfloat16)
    send_a, send_b = on_chip(
        add_kernel, none, list(own) + [sent], [shape] * 2, 2 * cols * rows, "weight_add"
    )
    got_a, got_b = swap(send_a, 2), swap(send_b, 4)
    keep_a, keep_b = weight_parts(
        held, order, KEPT, [kept], jnp.float32, "weight_keep"
    )
    got_a, got_b, pieces, beside = lax.optimization_barrier((got_a, got_b, pieces, beside))

    small = jax.ShapeDtypeStruct((rows, cols // 2), jnp.bfloat16)
    arrays = [keep_a, got_a, keep_b, got_b]
    last_a, last_b = on_chip(
        combine_kernel, none, arrays, [small] * 2, cols * rows, "weight_combine"
    )
    last = [swap(last_a, 4), swap(last_b, 2)]

    def finish(ready):
        ended, ready = lax.optimization_barrier((last, ready))
        (total,) = on_chip(
            finish_kernel,
            none,
            arrays + ended,
            [jax.ShapeDtypeStruct((rows, cols), jnp.float32)],
            2 * cols * rows,
            "weight_finish",
        )
        return total, ready

    return finish, pieces, beside


class PlaneGather:
    def __init__(self, own_cache, own_rows):
        self.own = own_cache, own_rows
        self.both = jnp.concatenate([own_cache, own_rows], axis=0)

    def first(self, held):
        swap = plane()[3]
        rows_x, cache_y = swap(self.own[1], 2), swap(self.own[0], 4)
        rows_x, cache_y, _ = lax.optimization_barrier((rows_x, cache_y, held))
        packs = (
            jnp.concatenate([self.own[0], cache_y], axis=0),
            jnp.concatenate([self.own[1], rows_x], axis=0),
        )
        return rows_x, cache_y, swap(self.both, 1), packs

    def second(self):
        swap = plane()[3]
        rows_x, cache_y, _, packs = self.got
        return (swap(packs[0], 2), swap(packs[1], 4)), (swap(rows_x, 1), swap(cache_y, 1))

    def third(self):
        swap = plane()[3]
        return swap(self.packs[0], 1), swap(self.packs[1], 1)

    def where(self, bits):
        return lax.axis_index("dp").astype(jnp.int32) ^ jnp.array(bits, dtype=jnp.int32)

    def lay(self, swapped, n_rows):
        arrays = [self.own[0], self.got[2], self.got[1], swapped[1]]
        return place_rows(arrays, [(k, 0) for k in range(4)], self.where([0, 1, 4, 5]),
                          self.own[0].shape[0], n_rows, [])

    def lay_rest(self, laid):
        height = self.own[0].shape[0]
        parts = [(0, 0), (0, height), (1, 0), (1, height)]
        arrays = [self.packs[0], self.packs_other[0]]
        return place_rows(
            arrays, parts, self.where([2, 6, 3, 7]), height, laid.shape[0], [laid]
        )

    def feature_rows(self):
        height, count = self.own[0].shape[0], self.own[1].shape[0]
        arrays = [self.own[1], self.got[2], self.got[0], self.swapped[0]]
        arrays += [self.packs[1], self.packs_other[1]]
        parts = [(0, 0), (1, height), (2, 0), (3, 0), (4, 0), (4, count), (5, 0), (5, count)]
        return arrays, parts, self.where([0, 1, 2, 3, 4, 6, 5, 7])


def place_rows_kernel(height, parts, place, *refs):
    out, sems = refs[-2:]
    copies = []
    for k, (which, row) in enumerate(parts):
        start = pl.multiple_of(place[k] * height, height)
        copies.append(
            pltpu.make_async_copy(
                refs[which].at[pl.ds(row, height), :],
                out.at[pl.ds(start, height), :],
                sems.at[k],
            )
        )
    for copy in copies:
        copy.start()
    for copy in copies:
        copy.wait()


def place_rows(arrays, parts, place, height, rows, into):
    cols = arrays[0].shape[1]
    anywhere = pl.BlockSpec(memory_space=pl.ANY)
    return pl.pallas_call(
        functools.partial(place_rows_kernel, height, parts),
        in_specs=[pl.BlockSpec(memory_space=pltpu.SMEM)]
        + [pl.BlockSpec(memory_space=pltpu.VMEM)] * len(arrays)
        + [anywhere] * len(into),
        out_specs=anywhere,
        out_shape=jax.ShapeDtypeStruct((rows, cols), arrays[0].dtype),
        scratch_shapes=[pltpu.SemaphoreType.DMA((len(parts),))],
        input_output_aliases={1 + len(arrays): 0} if into else {},
        cost_estimate=pl.CostEstimate(
            flops=0, bytes_accessed=4 * height * cols * len(parts), transcendentals=0
        ),
        compiler_params=pltpu.CompilerParams(vmem_limit_bytes=VMEM_WHOLE),
        name="place_rows",
    )(place, *arrays, *into)


def input_kernel(n_blocks, parts, place, *refs):
    *arrays, out = refs
    pieces, here, arrays = arrays[:n_blocks], arrays[n_blocks], arrays[n_blocks + 1 :]
    share = out.shape[1] // len(parts)
    for k, (which, row) in enumerate(parts):
        start = pl.multiple_of(place[k] * share, share)
        total = jnp.zeros((out.shape[0], share), jnp.float32)
        for s, piece in enumerate(pieces):
            if s:
                block = arrays[which][row + (s - 1) * share : row + s * share, :]
            else:
                block = here[pl.ds(start, share), :]
            total = total + lax.dot_general(
                piece[...], block, (((1,), (1,)), ((), ())), preferred_element_type=jnp.float32
            )
        out[:, pl.ds(start, share)] = total.astype(out.dtype)


def input_gradient(pieces, here, arrays, parts, place):
    length, cols = pieces[0].shape
    feats = here.shape[0]
    (d_tokens,) = on_chip(
        functools.partial(input_kernel, len(pieces), parts),
        place,
        pieces + [here] + arrays,
        [jax.ShapeDtypeStruct((length, feats), jnp.bfloat16)],
        2 * length * feats * cols * len(pieces),
        "input_gradient",
    )
    return d_tokens


def make_body(n_dp, n_z):
    mesh_tuned = n_dp == 8 and n_z == 4

    def pair(value, s):
        return lax.ppermute(value, "tensor", [(z, z ^ s) for z in range(n_z)])

    def body(tokens, queries, d_out, segments, cached, master, moment, second, grad):
        me_dp = lax.axis_index("dp").astype(jnp.int32)
        me_z = lax.axis_index("tensor").astype(jnp.int32)
        length, feats = tokens.shape
        cols = cached.shape[1]
        tuned = mesh_tuned and length == cols

        master_new, moment_new, second_new, own_cache = optimizer(
            cached, master, moment, second, grad
        )

        share = feats // n_dp

        def block_for(z):
            return lax.dynamic_slice_in_dim(cached, z * feats + me_dp * share, share, 0)

        blocks = [pair(block_for(me_z ^ s), s) for s in range(1, n_z)]
        here = lax.dynamic_slice_in_dim(cached, me_z * feats, feats, 0)

        doc_ids = segments[0]
        position = jnp.arange(length)
        allowed = (doc_ids[:, None] == doc_ids[None, :]) & (position[:, None] <= position[None, :])
        allowed = allowed.astype(jnp.float32)

        total = jnp.zeros((length, cols), jnp.float32)
        zero = 0 * me_z
        orders = weight_orders() if tuned else [jnp.zeros((5,), jnp.int32)]
        total, held = absorb([tokens], zero, me_z, cached, total, None, n_z)
        from_low, from_high = tokens, tokens
        for s in range(1, n_z):
            low, high = me_z - s, me_z + s
            from_high = lax.ppermute(from_high, "tensor", [(z + 1, z) for z in range(n_z - s)])
            from_low = lax.ppermute(
                from_low, "tensor", [(z, z + 1) for z in range(s - 1, n_z - 1)]
            )
            if tuned and s == 1:
                from_high, from_low, held, allowed, orders, here = lax.optimization_barrier(
                    (from_high, from_low, held, allowed, orders, here)
                )
                blocks, ready, _, _ = lax.optimization_barrier(
                    (blocks, own_cache, from_high, from_low)
                )
                gather = PlaneGather(ready, jnp.concatenate(blocks, axis=0))
            elif tuned and s == 2:
                from_high, from_low, held, gather.got = lax.optimization_barrier(
                    (from_high, from_low, held, gather.first(held))
                )
            elif tuned:
                packs, swapped = gather.second()
                laid = gather.lay(swapped, cached.shape[0])
                from_high, from_low, held, gather.packs, gather.swapped, laid = (
                    lax.optimization_barrier((from_high, from_low, held, packs, swapped, laid))
                )
            chunks, which = [from_low, from_high], (me_z < s).astype(jnp.int32)
            index = jnp.where(me_z < s, high, low)
            if 2 * s < n_z:
                total, held = absorb([from_low], zero, low, cached, total, held, n_z)
                chunks, which, index = [from_high], zero, high
            if s < n_z - 1:
                total, held = absorb(chunks, which, index, cached, total, held, n_z)

        held, d_queries, d_projected, sent, kept = attend(
            chunks, which, index, cached, total, held, queries, d_out, allowed, orders[0], n_z
        )

        pieces = [d_projected] + [pair(d_projected, s) for s in range(1, n_z)]
        if tuned:
            sent, gather.packs_other = lax.optimization_barrier((sent, gather.third()))
            new_cache = gather.lay_rest(laid)
            finish, pieces, new_cache = weight_sum(
                held, orders[1], sent, kept, pieces, new_cache
            )
            new_grad, d_tokens = finish(input_gradient(pieces, here, *gather.feature_rows()))
        else:
            new_cache = lax.all_gather(own_cache, "dp", axis=0, tiled=True)
            rows = lax.all_gather(jnp.stack([block_for(me_z)] + blocks), "dp", axis=0)
            d_tokens = jnp.einsum(
                "slc,ksfc->lkf", jnp.stack(pieces), rows, preferred_element_type=jnp.float32
            )
            d_tokens = d_tokens.astype(jnp.bfloat16).reshape(length, feats)
            partial = lax.dot_general(
                held[:n_z].reshape(n_z * feats, length),
                d_projected,
                (((1,), (0,)), ((), ())),
                preferred_element_type=jnp.float32,
            )
            new_grad = lax.psum_scatter(
                partial.astype(jnp.bfloat16), "dp", scatter_dimension=0, tiled=True
            ).astype(jnp.float32)
        return (master_new, moment_new, second_new, new_cache, new_grad, d_queries, d_tokens)

    return body


def solution(mesh):
    in_specs = (
        P("dp", "tensor"),
        P("dp", "tensor"),
        P("dp", "tensor"),
        P("dp", None),
        P(None, "tensor"),
        P("dp", "tensor"),
        P("dp", "tensor"),
        P("dp", "tensor"),
        P("dp", "tensor"),
    )
    out_specs = (
        P("dp", "tensor"),
        P("dp", "tensor"),
        P("dp", "tensor"),
        P(None, "tensor"),
        P("dp", "tensor"),
        P("dp", "tensor"),
        P("dp", "tensor"),
    )
    body = make_body(mesh.shape["dp"], mesh.shape["tensor"])
    return jax.shard_map(body, mesh=mesh, in_specs=in_specs, out_specs=out_specs, check_vma=False)
```

```python
import functools
import math

import jax
import jax.numpy as jnp
from jax import lax
from jax.experimental import pallas as pl
from jax.experimental.pallas import tpu as pltpu
from jax.sharding import PartitionSpec as P

HD = 128
VMEM_STREAM = 60 * 1024 * 1024
VMEM_WHOLE = 24 * 1024 * 1024


beta_first = 0.9
beta_second = 0.95
learn_rate = 0.0003
weight_decay = 0.1
adam_epsilon = 1e-08
first_fix = 1.0 - 0.9**40
second_fix = 1.0 - 0.95**40


def optimizer_kernel(
    place, cached, master, moment, second, grad, master_out, moment_out, second_out, cache_out
):
    moment_new = beta_first * moment[...] + (1.0 - beta_first) * grad[...]
    second_new = beta_second * second[...] + (1.0 - beta_second) * grad[...] * grad[...]
    update = moment_new / first_fix / (jnp.sqrt(second_new / second_fix) + adam_epsilon)
    master_new = master[...] - learn_rate * (update + weight_decay * master[...])
    moment_out[...] = moment_new
    second_out[...] = second_new
    master_out[...] = master_new
    for start in range(0, cached.shape[1], HD):
        block = slice(start, start + HD)
        own_cache = cached[:, block].astype(jnp.float32)
        delta = master_new[:, block] - own_cache
        largest = jnp.max(jnp.abs(delta), axis=1, keepdims=True)
        scale = (largest + 1e-06).astype(jnp.bfloat16).astype(jnp.float32)
        codes = (delta / scale).astype(jnp.bfloat16)
        cache_out[:, block] = (own_cache + codes.astype(jnp.float32) * scale).astype(jnp.bfloat16)


def optimizer(cached, master, moment, second, grad):
    rows, cols = master.shape
    step = min(rows, 256)
    steps = rows // step
    own = pl.BlockSpec((step, cols), lambda i, place: (i, 0))
    full = jax.ShapeDtypeStruct((rows, cols), jnp.float32)
    return pl.pallas_call(
        optimizer_kernel,
        grid_spec=pltpu.PrefetchScalarGridSpec(
            num_scalar_prefetch=1,
            grid=(steps,),
            in_specs=[pl.BlockSpec((step, cols), lambda i, place: (place[0] * steps + i, 0))]
            + [own] * 4,
            out_specs=[own] * 4,
        ),
        out_shape=[full, full, full, jax.ShapeDtypeStruct((rows, cols), jnp.bfloat16)],
        cost_estimate=pl.CostEstimate(
            flops=40 * rows * cols, bytes_accessed=32 * rows * cols, transcendentals=rows * cols
        ),
        compiler_params=pltpu.CompilerParams(vmem_limit_bytes=VMEM_STREAM),
        name="optimizer",
    )(lax.axis_index("dp").astype(jnp.int32).reshape(1), cached, master, moment, second, grad)


def on_chip(kernel, place, arrays, out_shape, flops, name):
    vmem = pl.BlockSpec(memory_space=pltpu.VMEM)
    size = sum(a.size * a.dtype.itemsize for a in arrays)
    size += sum(s.size * s.dtype.itemsize for s in out_shape)
    return pl.pallas_call(
        kernel,
        in_specs=[pl.BlockSpec(memory_space=pltpu.SMEM)] + [vmem] * len(arrays),
        out_specs=[vmem] * len(out_shape),
        out_shape=out_shape,
        cost_estimate=pl.CostEstimate(flops=flops, bytes_accessed=size, transcendentals=0),
        compiler_params=pltpu.CompilerParams(vmem_limit_bytes=VMEM_WHOLE),
        name=name,
    )(place, *arrays)


def fetch_chunk(place, chunks, chunk, sem):
    for n, source in enumerate(chunks):

        @pl.when(place[2] == n)
        def _():
            pltpu.make_async_copy(source, chunk, sem).start()

    return pltpu.make_async_copy(chunks[0], chunk, sem)


def fetch_rows(place, cached, rows, sem):
    height = rows.shape[0]
    start = pl.multiple_of(place[0] * height, height)
    copy = pltpu.make_async_copy(cached.at[pl.ds(start, height), :], rows, sem)
    copy.start()
    return copy


def absorb_kernel(n_chunks, place, *refs):
    chunks, (total, cached) = refs[:n_chunks], refs[n_chunks : n_chunks + 2]
    total_out, held, chunk, rows, turned, sems = refs[-6:]
    chunk_copy = fetch_chunk(place, chunks, chunk, sems.at[0])
    rows_copy = fetch_rows(place, cached, rows, sems.at[1])
    chunk_copy.wait()
    turned[...] = chunk[...].T
    keep = pltpu.make_async_copy(turned, held.at[place[1]], sems.at[2])
    keep.start()
    rows_copy.wait()
    total_out[...] = total[...] + jnp.dot(
        chunk[...], rows[...], preferred_element_type=jnp.float32
    )
    keep.wait()


def absorb_place(index, which, n_chunks):
    inside = (index >= 0) & (index < n_chunks)
    return jnp.stack(
        [jnp.clip(index, 0, n_chunks - 1), jnp.where(inside, index, n_chunks), which]
    ).astype(jnp.int32)


def absorb_scratch(chunk, cached, n_sems):
    length, feats = chunk.shape
    return [
        pltpu.VMEM((length, feats), chunk.dtype),
        pltpu.VMEM((feats, cached.shape[1]), cached.dtype),
        pltpu.VMEM((feats, length), chunk.dtype),
        pltpu.SemaphoreType.DMA((n_sems,)),
    ]


def absorb(chunks, which, index, cached, total, held, n_chunks):
    length, feats = chunks[0].shape
    cols = cached.shape[1]
    shape = jax.ShapeDtypeStruct((8 * n_chunks, feats, length), chunks[0].dtype)
    vmem, anywhere = pl.BlockSpec(memory_space=pltpu.VMEM), pl.BlockSpec(memory_space=pl.ANY)
    return pl.pallas_call(
        functools.partial(absorb_kernel, len(chunks)),
        in_specs=[pl.BlockSpec(memory_space=pltpu.SMEM)]
        + [anywhere] * len(chunks)
        + [vmem, anywhere]
        + ([] if held is None else [anywhere]),
        out_specs=[vmem, anywhere],
        out_shape=[jax.ShapeDtypeStruct(total.shape, jnp.float32), shape],
        scratch_shapes=absorb_scratch(chunks[0], cached, 3),
        input_output_aliases={} if held is None else {3 + len(chunks): 1},
        cost_estimate=pl.CostEstimate(
            flops=2 * length * feats * cols,
            bytes_accessed=4 * length * feats + 2 * feats * cols,
            transcendentals=0,
        ),
        compiler_params=pltpu.CompilerParams(vmem_limit_bytes=VMEM_STREAM),
        name="absorb",
    )(
        absorb_place(index, which, n_chunks),
        *chunks,
        total,
        cached,
        *([] if held is None else [held]),
    )


def attend_kernel(n_chunks, place, order, *refs):
    chunks, refs = refs[:n_chunks], refs[n_chunks:]
    total, cached, _, allowed, queries_in, d_out_in = refs[:6]
    held, d_queries, d_projected, sent, kept, *refs = refs[6:]
    chunk, rows, turned, sems, queries, d_out, buffer, part_sems = refs
    chunk_copy = fetch_chunk(place, chunks, chunk, sems.at[0])
    rows_copy = fetch_rows(place, cached, rows, sems.at[1])
    others = [
        pltpu.make_async_copy(queries_in, queries, sems.at[3]),
        pltpu.make_async_copy(d_out_in, d_out, sems.at[4]),
    ]
    for copy in others:
        copy.start()
    chunk_copy.wait()
    rows_copy.wait()
    projected = (
        total[...] + jnp.dot(chunk[...], rows[...], preferred_element_type=jnp.float32)
    ).astype(jnp.bfloat16)
    turned[...] = chunk[...].T
    keep = pltpu.make_async_copy(turned, held.at[place[1]], sems.at[2])
    keep.start()
    seen = allowed[...] > 0
    for copy in others:
        copy.wait()
    factor = 1.0 / math.sqrt(HD)
    across = (((1,), (1,)), ((), ()))
    heads = projected.shape[1] // (2 * HD)
    group = queries.shape[1] // HD // heads
    for head in range(heads):
        start = 2 * HD * head
        keys = projected[:, start : start + HD]
        values = projected[:, start + HD : start + 2 * HD]
        d_keys = jnp.zeros(keys.shape, jnp.float32)
        d_values = jnp.zeros(keys.shape, jnp.float32)
        for g in range(head * group, (head + 1) * group):
            if g == heads * group // 2:
                keep.wait()
                copies = fetch_parts(order, held, range(4), buffer, part_sems)
            columns = slice(g * HD, (g + 1) * HD)
            query, grad = queries[:, columns], d_out[:, columns]
            scores = (
                lax.dot_general(keys, query, across, preferred_element_type=jnp.float32) * factor
            )
            scores = jnp.where(seen, scores, -1e30)
            weights = jnp.exp(scores - jnp.max(scores, axis=0, keepdims=True))
            probs = weights / jnp.sum(weights, axis=0, keepdims=True)
            probs_low = probs.astype(jnp.bfloat16)
            d_probs = lax.dot_general(values, grad, across, preferred_element_type=jnp.float32)
            rowdot = jnp.sum(probs_low.astype(jnp.float32) * d_probs, axis=0, keepdims=True)
            d_scores = (probs * (d_probs - rowdot) * factor).astype(jnp.bfloat16)
            d_queries[:, columns] = lax.dot_general(
                d_scores, keys, (((0,), (0,)), ((), ())), preferred_element_type=jnp.float32
            ).astype(jnp.bfloat16)
            d_keys = d_keys + jnp.dot(d_scores, query, preferred_element_type=jnp.float32)
            d_values = d_values + jnp.dot(probs_low, grad, preferred_element_type=jnp.float32)
        d_projected[:, start : start + HD] = d_keys.astype(jnp.bfloat16)
        d_projected[:, start + HD : start + 2 * HD] = d_values.astype(jnp.bfloat16)

    def give(g, side, position, here, part):
        out = (sent, kept)[g]
        out[2 * side + position, here, :] = part.astype(out.dtype)

    save = None
    if held.shape[2] == d_projected.shape[1]:
        save = pltpu.make_async_copy(
            d_projected,
            held.at[held.shape[0] - 1, pl.ds(0, d_projected.shape[0]), :],
            sems.at[2],
        )
        save.start()
    weight_products(copies, (SENT, KEPT), buffer, d_projected, give)
    if save is not None:
        save.wait()


def attend(chunks, which, index, cached, total, held, queries, d_out, allowed, order, n_chunks):
    feats, length = held.shape[1:]
    parts = jax.ShapeDtypeStruct((4, feats // 2, total.shape[1] // 2), jnp.bfloat16)
    vmem, anywhere = pl.BlockSpec(memory_space=pltpu.VMEM), pl.BlockSpec(memory_space=pl.ANY)
    return pl.pallas_call(
        functools.partial(attend_kernel, len(chunks)),
        in_specs=[pl.BlockSpec(memory_space=pltpu.SMEM)] * 2
        + [anywhere] * len(chunks)
        + [vmem, anywhere, anywhere, vmem, anywhere, anywhere],
        out_specs=[anywhere] + [vmem] * 4,
        out_shape=[
            jax.ShapeDtypeStruct(held.shape, held.dtype),
            jax.ShapeDtypeStruct(queries.shape, jnp.bfloat16),
            jax.ShapeDtypeStruct(total.shape, jnp.bfloat16),
            parts,
            parts,
        ],
        scratch_shapes=absorb_scratch(chunks[0], cached, 5)
        + [
            pltpu.VMEM(queries.shape, queries.dtype),
            pltpu.VMEM(d_out.shape, d_out.dtype),
            pltpu.VMEM((4, feats // 2, length), held.dtype),
            pltpu.SemaphoreType.DMA((4,)),
        ],
        input_output_aliases={4 + len(chunks): 0},
        cost_estimate=pl.CostEstimate(
            flops=12 * allowed.size * queries.shape[1],
            bytes_accessed=8 * queries.size,
            transcendentals=allowed.size * queries.shape[1] // HD,
        ),
        compiler_params=pltpu.CompilerParams(vmem_limit_bytes=VMEM_STREAM),
        name="attend",
    )(
        absorb_place(index, which, n_chunks),
        order,
        *chunks,
        total,
        cached,
        held,
        allowed,
        queries,
        d_out,
    )


SENT = ((0, 0, 0), (0, 1, 0), (1, 0, 1), (2, 1, 1))
KEPT = ((1, 1, 0), (2, 0, 0), (3, 0, 1), (3, 1, 1))


def fetch_columns(held, columns, sem):
    length = columns.shape[0]
    return pltpu.make_async_copy(
        held.at[held.shape[0] - 1, pl.ds(0, length), :], columns, sem
    )


def fetch_parts(place, held, chunks, buffer, sems):
    rows = buffer.shape[1]
    start = pl.multiple_of(place[4] * rows, rows)
    copies = {}
    for chunk in chunks:
        copies[chunk] = pltpu.make_async_copy(
            held.at[place[chunk], pl.ds(start, rows), :], buffer.at[chunk], sems.at[chunk]
        )
        copies[chunk].start()
    return copies


def weight_products(copies, groups, buffer, d_projected, give):
    rows = buffer.shape[1]
    half = d_projected.shape[1] // 2
    block = min(rows, 256)
    for chunk, copy in copies.items():
        copy.wait()
        wanted = [
            (g, side, position)
            for g, group in enumerate(groups)
            for which, side, position in group
            if which == chunk
        ]
        first, last = min(w[1] for w in wanted), max(w[1] for w in wanted)
        for r in range(0, rows, block):
            here = slice(r, r + block)
            total = jnp.dot(
                buffer[chunk, here, :],
                d_projected[:, first * half : (last + 1) * half],
                preferred_element_type=jnp.float32,
            )
            for g, side, position in wanted:
                part = total[:, (side - first) * half : (side - first + 1) * half]
                give(g, side, position, here, part)


def weight_kernel(group, place, held, *refs):
    *added, out_a, out_b, buffer, columns, sems, sem = refs
    columns_copy = fetch_columns(held, columns, sem)
    columns_copy.start()
    copies = fetch_parts(place, held, sorted({part[0] for part in group}), buffer, sems)
    columns_copy.wait()

    def give(_, side, position, here, part):
        if added:
            part = part + added[0][2 * side + position, here, :].astype(jnp.float32)
        out = (out_a, out_b)[side]
        out[position, here, :] = part.astype(out.dtype)

    weight_products(copies, (group,), buffer, columns, give)


def weight_parts(held, place, group, added, dtype, name):
    length = cols = held.shape[2]
    rows = held.shape[1] // 2
    vmem = pl.BlockSpec(memory_space=pltpu.VMEM)
    return pl.pallas_call(
        functools.partial(weight_kernel, group),
        in_specs=[pl.BlockSpec(memory_space=pltpu.SMEM), pl.BlockSpec(memory_space=pl.ANY)]
        + [vmem] * len(added),
        out_specs=[vmem] * 2,
        out_shape=[jax.ShapeDtypeStruct((2, rows, cols // 2), dtype)] * 2,
        scratch_shapes=[
            pltpu.VMEM((4, rows, length), held.dtype),
            pltpu.VMEM((length, cols), held.dtype),
            pltpu.SemaphoreType.DMA((4,)),
            pltpu.SemaphoreType.DMA,
        ],
        cost_estimate=pl.CostEstimate(
            flops=4 * length * rows * cols, bytes_accessed=8 * rows * cols, transcendentals=0
        ),
        compiler_params=pltpu.CompilerParams(vmem_limit_bytes=VMEM_WHOLE),
        name=name,
    )(place, held, *added)


def add_kernel(place, own_a, own_b, other, out_a, out_b):
    depth = own_a.shape[0]
    for side, (own, out) in enumerate(((own_a, out_a), (own_b, out_b))):
        other_here = other[side * depth : (side + 1) * depth]
        out[...] = (own[...] + other_here.astype(jnp.float32)).astype(out.dtype)


def combine_kernel(place, keep_a, got_a, keep_b, got_b, out_a, out_b):
    for keep, got, out in ((keep_a, got_a, out_a), (keep_b, got_b, out_b)):
        out[...] = (keep[0] + got[0].astype(jnp.float32)).astype(out.dtype)


def finish_kernel(place, keep_a, got_a, keep_b, got_b, last_a, last_b, out):
    half = last_a.shape[1]
    sides = ((keep_a, got_a, last_a), (keep_b, got_b, last_b))
    for side, (keep, got, last) in enumerate(sides):
        total = keep[1] + got[1].astype(jnp.float32) + last[...].astype(jnp.float32)
        out[:, side * half : (side + 1) * half] = total


def plane():
    index = lax.axis_index("dp").astype(jnp.int32)

    def swap(value, bit):
        return lax.ppermute(value, "dp", [(i, i ^ bit) for i in range(8)])

    return index % 2, (index // 2) % 2, index // 4, swap


def weight_orders():
    core, x, y, _ = plane()
    chunks = [3 - x - 2 * y, 1 - x + 2 * y, x + 2 - 2 * y, x + 2 * y]
    return [jnp.stack(chunks + [half]) for half in (1 - core, core)]


def weight_sum(held, order, sent, kept, pieces, beside):
    swap = plane()[3]
    rows, cols = held.shape[1] // 2, held.shape[2]
    none = jnp.zeros((1,), jnp.int32)
    sent, kept = swap(sent, 1), swap(kept, 1)
    own = weight_parts(held, order, SENT, [], jnp.float32, "weight_send")
    shape = jax.ShapeDtypeStruct(own[0].shape, jnp.bfloat16)
    send_a, send_b = on_chip(
        add_kernel, none, list(own) + [sent], [shape] * 2, 2 * cols * rows, "weight_add"
    )
    got_a, got_b = swap(send_a, 2), swap(send_b, 4)
    keep_a, keep_b = weight_parts(
        held, order, KEPT, [kept], jnp.float32, "weight_keep"
    )
    got_a, got_b, pieces, beside = lax.optimization_barrier((got_a, got_b, pieces, beside))

    small = jax.ShapeDtypeStruct((rows, cols // 2), jnp.bfloat16)
    arrays = [keep_a, got_a, keep_b, got_b]
    last_a, last_b = on_chip(
        combine_kernel, none, arrays, [small] * 2, cols * rows, "weight_combine"
    )
    last = [swap(last_a, 4), swap(last_b, 2)]

    def finish(ready):
        ended, ready = lax.optimization_barrier((last, ready))
        (total,) = on_chip(
            finish_kernel,
            none,
            arrays + ended,
            [jax.ShapeDtypeStruct((rows, cols), jnp.float32)],
            2 * cols * rows,
            "weight_finish",
        )
        return total, ready

    return finish, pieces, beside


class PlaneGather:
    def __init__(self, own_cache, own_rows):
        self.own = own_cache, own_rows
        self.both = jnp.concatenate([own_cache, own_rows], axis=0)

    def first(self, held):
        swap = plane()[3]
        rows_x, cache_y = swap(self.own[1], 2), swap(self.own[0], 4)
        rows_x, cache_y, _ = lax.optimization_barrier((rows_x, cache_y, held))
        packs = (
            jnp.concatenate([self.own[0], cache_y], axis=0),
            jnp.concatenate([self.own[1], rows_x], axis=0),
        )
        return rows_x, cache_y, swap(self.both, 1), packs

    def second(self):
        swap = plane()[3]
        rows_x, cache_y, _, packs = self.got
        return (swap(packs[0], 2), swap(packs[1], 4)), (swap(rows_x, 1), swap(cache_y, 1))

    def third(self):
        swap = plane()[3]
        return swap(self.packs[0], 1), swap(self.packs[1], 1)

    def where(self, bits):
        return lax.axis_index("dp").astype(jnp.int32) ^ jnp.array(bits, dtype=jnp.int32)

    def lay(self, swapped, n_rows):
        arrays = [self.own[0], self.got[2], self.got[1], swapped[1]]
        return place_rows(arrays, [(k, 0) for k in range(4)], self.where([0, 1, 4, 5]),
                          self.own[0].shape[0], n_rows, [])

    def lay_rest(self, laid):
        height = self.own[0].shape[0]
        parts = [(0, 0), (0, height), (1, 0), (1, height)]
        arrays = [self.packs[0], self.packs_other[0]]
        return place_rows(
            arrays, parts, self.where([2, 6, 3, 7]), height, laid.shape[0], [laid]
        )

    def feature_rows(self):
        height, count = self.own[0].shape[0], self.own[1].shape[0]
        arrays = [self.own[1], self.got[2], self.got[0], self.swapped[0]]
        arrays += [self.packs[1], self.packs_other[1]]
        parts = [(0, 0), (1, height), (2, 0), (3, 0), (4, 0), (4, count), (5, 0), (5, count)]
        return arrays, parts, self.where([0, 1, 2, 3, 4, 6, 5, 7])


def place_rows_kernel(height, parts, place, *refs):
    out, sems = refs[-2:]
    copies = []
    for k, (which, row) in enumerate(parts):
        start = pl.multiple_of(place[k] * height, height)
        copies.append(
            pltpu.make_async_copy(
                refs[which].at[pl.ds(row, height), :],
                out.at[pl.ds(start, height), :],
                sems.at[k],
            )
        )
    for copy in copies:
        copy.start()
    for copy in copies:
        copy.wait()


def place_rows(arrays, parts, place, height, rows, into):
    cols = arrays[0].shape[1]
    anywhere = pl.BlockSpec(memory_space=pl.ANY)
    return pl.pallas_call(
        functools.partial(place_rows_kernel, height, parts),
        in_specs=[pl.BlockSpec(memory_space=pltpu.SMEM)]
        + [pl.BlockSpec(memory_space=pltpu.VMEM)] * len(arrays)
        + [anywhere] * len(into),
        out_specs=anywhere,
        out_shape=jax.ShapeDtypeStruct((rows, cols), arrays[0].dtype),
        scratch_shapes=[pltpu.SemaphoreType.DMA((len(parts),))],
        input_output_aliases={1 + len(arrays): 0} if into else {},
        cost_estimate=pl.CostEstimate(
            flops=0, bytes_accessed=4 * height * cols * len(parts), transcendentals=0
        ),
        compiler_params=pltpu.CompilerParams(vmem_limit_bytes=VMEM_WHOLE),
        name="place_rows",
    )(place, *arrays, *into)


def input_kernel(n_blocks, parts, place, *refs):
    *arrays, out = refs
    pieces, here, arrays = arrays[:n_blocks], arrays[n_blocks], arrays[n_blocks + 1 :]
    share = out.shape[1] // len(parts)
    for k, (which, row) in enumerate(parts):
        start = pl.multiple_of(place[k] * share, share)
        total = jnp.zeros((out.shape[0], share), jnp.float32)
        for s, piece in enumerate(pieces):
            if s:
                block = arrays[which][row + (s - 1) * share : row + s * share, :]
            else:
                block = here[pl.ds(start, share), :]
            total = total + lax.dot_general(
                piece[...], block, (((1,), (1,)), ((), ())), preferred_element_type=jnp.float32
            )
        out[:, pl.ds(start, share)] = total.astype(out.dtype)


def input_gradient(pieces, here, arrays, parts, place):
    length, cols = pieces[0].shape
    feats = here.shape[0]
    (d_tokens,) = on_chip(
        functools.partial(input_kernel, len(pieces), parts),
        place,
        pieces + [here] + arrays,
        [jax.ShapeDtypeStruct((length, feats), jnp.bfloat16)],
        2 * length * feats * cols * len(pieces),
        "input_gradient",
    )
    return d_tokens


def make_body(n_dp, n_z):
    mesh_tuned = n_dp == 8 and n_z == 4

    def pair(value, s):
        return lax.ppermute(value, "tensor", [(z, z ^ s) for z in range(n_z)])

    def body(tokens, queries, d_out, segments, cached, master, moment, second, grad):
        me_dp = lax.axis_index("dp").astype(jnp.int32)
        me_z = lax.axis_index("tensor").astype(jnp.int32)
        length, feats = tokens.shape
        cols = cached.shape[1]
        tuned = mesh_tuned and length == cols

        master_new, moment_new, second_new, own_cache = optimizer(
            cached, master, moment, second, grad
        )

        share = feats // n_dp

        def block_for(z):
            return lax.dynamic_slice_in_dim(cached, z * feats + me_dp * share, share, 0)

        blocks = [pair(block_for(me_z ^ s), s) for s in range(1, n_z)]
        here = lax.dynamic_slice_in_dim(cached, me_z * feats, feats, 0)

        doc_ids = segments[0]
        position = jnp.arange(length)
        allowed = (doc_ids[:, None] == doc_ids[None, :]) & (position[:, None] <= position[None, :])
        allowed = allowed.astype(jnp.float32)

        total = jnp.zeros((length, cols), jnp.float32)
        zero = 0 * me_z
        orders = weight_orders() if tuned else [jnp.zeros((5,), jnp.int32)]
        total, held = absorb([tokens], zero, me_z, cached, total, None, n_z)
        from_low, from_high = tokens, tokens
        for s in range(1, n_z):
            low, high = me_z - s, me_z + s
            from_high = lax.ppermute(from_high, "tensor", [(z + 1, z) for z in range(n_z - s)])
            from_low = lax.ppermute(
                from_low, "tensor", [(z, z + 1) for z in range(s - 1, n_z - 1)]
            )
            if tuned and s == 1:
                from_high, from_low, held, allowed, orders, here = lax.optimization_barrier(
                    (from_high, from_low, held, allowed, orders, here)
                )
                blocks, ready, _, _ = lax.optimization_barrier(
                    (blocks, own_cache, from_high, from_low)
                )
                gather = PlaneGather(ready, jnp.concatenate(blocks, axis=0))
            elif tuned and s == 2:
                from_high, from_low, held, gather.got = lax.optimization_barrier(
                    (from_high, from_low, held, gather.first(held))
                )
            elif tuned:
                packs, swapped = gather.second()
                laid = gather.lay(swapped, cached.shape[0])
                from_high, from_low, held, gather.packs, gather.swapped, laid = (
                    lax.optimization_barrier((from_high, from_low, held, packs, swapped, laid))
                )
            chunks, which = [from_low, from_high], (me_z < s).astype(jnp.int32)
            index = jnp.where(me_z < s, high, low)
            if 2 * s < n_z:
                total, held = absorb([from_low], zero, low, cached, total, held, n_z)
                chunks, which, index = [from_high], zero, high
            if s < n_z - 1:
                total, held = absorb(chunks, which, index, cached, total, held, n_z)

        held, d_queries, d_projected, sent, kept = attend(
            chunks, which, index, cached, total, held, queries, d_out, allowed, orders[0], n_z
        )

        pieces = [d_projected] + [pair(d_projected, s) for s in range(1, n_z)]
        if tuned:
            sent, gather.packs_other = lax.optimization_barrier((sent, gather.third()))
            new_cache = gather.lay_rest(laid)
            finish, pieces, new_cache = weight_sum(
                held, orders[1], sent, kept, pieces, new_cache
            )
            new_grad, d_tokens = finish(input_gradient(pieces, here, *gather.feature_rows()))
        else:
            new_cache = lax.all_gather(own_cache, "dp", axis=0, tiled=True)
            rows = lax.all_gather(jnp.stack([block_for(me_z)] + blocks), "dp", axis=0)
            d_tokens = jnp.einsum(
                "slc,ksfc->lkf", jnp.stack(pieces), rows, preferred_element_type=jnp.float32
            )
            d_tokens = d_tokens.astype(jnp.bfloat16).reshape(length, feats)
            partial = lax.dot_general(
                held[:n_z].reshape(n_z * feats, length),
                d_projected,
                (((1,), (0,)), ((), ())),
                preferred_element_type=jnp.float32,
            )
            new_grad = lax.psum_scatter(
                partial.astype(jnp.bfloat16), "dp", scatter_dimension=0, tiled=True
            ).astype(jnp.float32)
        return (master_new, moment_new, second_new, new_cache, new_grad, d_queries, d_tokens)

    return body


def solution(mesh):
    in_specs = (
        P("dp", "tensor"),
        P("dp", "tensor"),
        P("dp", "tensor"),
        P("dp", None),
        P(None, "tensor"),
        P("dp", "tensor"),
        P("dp", "tensor"),
        P("dp", "tensor"),
        P("dp", "tensor"),
    )
    out_specs = (
        P("dp", "tensor"),
        P("dp", "tensor"),
        P("dp", "tensor"),
        P(None, "tensor"),
        P("dp", "tensor"),
        P("dp", "tensor"),
        P("dp", "tensor"),
    )
    body = make_body(mesh.shape["dp"], mesh.shape["tensor"])
    return jax.shard_map(body, mesh=mesh, in_specs=in_specs, out_specs=out_specs, check_vma=False)
```
